32 devices in a mesh: gx: 4 (over z), gy: 8 (over y, x, core).
Axes of the slice: x: 2, y: 2, z: 4, core: 2. Of those that a mesh axis runs over, the one named last changes fastest.
Arguments:
- initial_state: float32 [9, 4, 16, 1024], P(None, None, 'gx', 'gy'), may hold values from -6 to 6
- lame_lambda: float32 [4, 16, 1024], P(None, 'gx', 'gy'), may hold values from 0.5 to 1.5
- shear_modulus: float32 [4, 16, 1024], P(None, 'gx', 'gy'), may hold values from 0.3 to 1
- buoyancy: float32 [4, 16, 1024], P(None, 'gx', 'gy'), may hold values from 0.5 to 1
- source_cells: int32 [2048], P(('gx', 'gy')), may hold values from 0 to 2047
- source_wavelet: float32 [3, 2048], P(None, ('gx', 'gy')), may hold values from -8 to 8
- segment_start: int32 [65536], P(('gx', 'gy')), may hold values from 0 to 1935
- segment_weight: float32 [2, 65536], P(None, ('gx', 'gy')), may hold values from 0.2 to 1
- partial_owner: int32 [65536, 1], P(('gx', 'gy')), may hold values from 0 to 31; in each aligned block of 2048 rows (0 to 2047, 2048 to 4095, ...) at most 128 rows name the same one
- partial_channel: int32 [65536], P(('gx', 'gy')), may hold values from 0 to 1023
- observed_data: float32 [3, 32768], P(None, ('gx', 'gy')), may hold values from -6 to 6
Outputs:
- residuals: float32 [3, 32768], P(None, ('gx', 'gy'))
- gradients: float32 [2, 4, 16, 1024], P(None, None, 'gx', 'gy')
The draws below stay inside these ranges and needn't reach their ends.
Inputs may be any that keep to these rules, and one draw needn't show every extreme that they name: `partial_owner`: each row names the device that owns the segment's channel, counted with gx slowest; the rows of one device name one owner at most 128 times. `partial_channel`: the segment's channel among its owner's 1024 channels. `segment_start`: index of the segment's first cell in its device's grid of starts of shape [4, 4, 121], flattened in that order. `source_cells`: index of the source's cell in its device's tile of shape [4, 4, 128], flattened in that order; cells may repeat.
All inputs are finite; a program needn't handle non-finite values.
Results may differ from the reference program's by a relative error of at most 0.00002.
Values sent between devices are 32-bit elements; how exact they have to be, the bound alone decides.
No kernel may reach another device: no remote copies, remote signals or barrier semaphores. Data moves between devices by JAX's collectives and lax.ppermute only.
A program may use at most 64 MiB of HBM per device.

```python
import math
import jax
import jax.numpy as jnp
import numpy as np

NZ = 4
CX = 4
CY = 128
STEPS = 3
GAUGE = 8
PART_DEV = 2048
CH_DEV = 1024
SRC_DEV = 64
NX = 16
NY = 1024
CAP = 128
PART_TOTAL = 65536
CHANNELS = 32768
SRC_TOTAL = 2048
N_GY = 8
DEVICES = 32


def touch_ends(array, rng, low, high):
    spot = [jax.random.randint(jax.random.fold_in(rng, axis), (), 0, length) for axis, length in enumerate(array.shape)]
    widest = array.shape.index(max(array.shape))
    next_to = spot[:widest] + [(spot[widest] + 1) % array.shape[widest]] + spot[widest + 1:]
    return array.at[tuple(spot)].set(low).at[tuple(next_to)].set(high)


def level_of(own_key, dims, pieces, smallest, top_value):
    loudness, own = 1.0, jax.random.fold_in(own_key, 6)
    for dim, blocks in pieces:
        draws = jnp.exp(jax.random.uniform(jax.random.fold_in(own, dim), (blocks,), jnp.float32, smallest / len(pieces), top_value / len(pieces)))
        loudness = loudness * jnp.repeat(draws, dims[dim] // blocks).reshape([-1 if axis == dim else 1 for axis in range(len(dims))])
    return loudness


def deal_out(own_key, own, number, rows, amount, top, limit, slope):
    order = jax.random.permutation(own_key, amount)
    packed, common = portions_of(amount, rows * top, limit, slope, True), portions_of(amount, rows * top, limit, slope, False)
    places = jnp.arange(amount)

    def named(lengths, offset_by):
        used = int((lengths > 0).sum())
        fixed = max(1, used // 4)
        passed = fixed + (places - fixed + offset_by * (used - fixed)) % max(1, amount - fixed)
        return jnp.zeros((amount,), jnp.int32).at[order[jnp.where(places < fixed, places, passed)]].set(jnp.asarray(lengths, jnp.int32))

    lengths = jnp.where(number % 4 == 0, named(packed, number // 4), named(common, number - number // 4 - 1))
    mixed = jax.random.permutation(jax.random.fold_in(own, 3), amount)
    source_of, receiver = mixed[0:amount // 2 * 2:2], mixed[1:amount // 2 * 2:2]
    room = jnp.minimum(lengths[source_of] - 1, limit - lengths[receiver]) // 2
    room = jnp.where((source_of == order[0]) | (receiver == order[0]) | (lengths[receiver] == 0), 0, jnp.maximum(room, 0))
    passed = jax.random.randint(jax.random.fold_in(own, 4), (amount // 2,), 0, 1 << 20) % (room + 1)
    lengths = lengths.at[source_of].add(-passed).at[receiver].add(passed)
    members = jnp.searchsorted(jnp.cumsum(lengths), jnp.arange(rows * top), side="right").astype(jnp.int32)
    listing = members.reshape(top, rows).T
    listing = listing[jax.random.permutation(jax.random.fold_in(own, 1), rows)]
    offset_by = jax.random.randint(jax.random.fold_in(own, 2), (rows, 1), 0, top)
    return jnp.take_along_axis(listing, (jnp.arange(top)[None, :] + offset_by) % top, axis=1)


def portions_of(count, total, most, slope, full):
    loads = [(1 << 20) // math.isqrt(rank ** slope) + 1 for rank in range(1, count + 1)]
    largest = most if full else min(most, max(-(-total // count), total * loads[0] // sum(loads)))
    least = 1 if total - largest >= count - 1 else 0
    holding, spare = [largest] + [least] * (count - 1), total - largest - least * (count - 1)
    while spare > 0:
        movable = [i for i in range(1, count) if holding[i] < largest] or [i for i in range(1, count) if holding[i] < most]
        whole, left = sum([loads[i] for i in movable]), spare
        for i in movable:
            more = min(most - holding[i], max(1, left * loads[i] // whole), spare)
            holding[i] = holding[i] + more
            spare = spare - more
    return np.array(holding)


def noise(rng, shape, width, most, pieces=(), kind=jnp.bfloat16):
    result = width * jax.random.normal(rng, shape, jnp.float32)
    if pieces:
        result = result * level_of(rng, shape, pieces, -0.22, 0.18)
    return jnp.clip(result, -most, most).astype(kind)


def setup_inputs(seed: int = 0) -> dict:
    seeds = jax.random.split(jax.random.key(seed), 12)
    initial_state = noise(seeds[0], (9, NZ, NX, NY), 1.0, 6.0, ((2, 4), (3, 8)), jnp.float32)
    lame_lambda = jnp.clip(0.5 + 1.0 * jax.random.uniform(seeds[1], (NZ, NX, NY), jnp.float32) ** level_of(seeds[1], (NZ, NX, NY), ((1, 4), (2, 8)), -0.2, 0.2), 0.5, 1.5)
    shear_modulus = jnp.clip(0.3 + 0.7 * jax.random.uniform(seeds[2], (NZ, NX, NY), jnp.float32) ** level_of(seeds[2], (NZ, NX, NY), ((1, 4), (2, 8)), -0.2, 0.2), 0.3, 1.0)
    buoyancy = jnp.clip(0.5 + 0.5 * jax.random.uniform(seeds[3], (NZ, NX, NY), jnp.float32) ** level_of(seeds[3], (NZ, NX, NY), ((1, 4), (2, 8)), -0.2, 0.2), 0.5, 1.0)
    source_cells = touch_ends(jax.random.randint(seeds[4], (SRC_TOTAL,), 0, NZ * CX * CY), jax.random.fold_in(seeds[4], 1), 0, (NZ * CX * CY) - 1).astype(jnp.int32)
    source_wavelet = noise(seeds[5], (STEPS, SRC_TOTAL), 2.0, 8.0, ((1, 32),), jnp.float32)
    segment_start = touch_ends(jax.random.randint(seeds[6], (PART_TOTAL,), 0, NZ * CX * (CY - GAUGE + 1)), jax.random.fold_in(seeds[6], 1), 0, (NZ * CX * (CY - GAUGE + 1)) - 1).astype(jnp.int32)
    segment_weight = jnp.clip(0.2 + 0.8 * jax.random.uniform(seeds[7], (2, PART_TOTAL), jnp.float32) ** level_of(seeds[7], (2, PART_TOTAL), ((1, 32),), -0.2, 0.2), 0.2, 1.0)
    partial_owner_keys = jax.random.split(jax.random.fold_in(seeds[8], 1), PART_TOTAL // PART_DEV)
    partial_owner_turns = jax.random.permutation(jax.random.fold_in(seeds[8], 3), PART_TOTAL // PART_DEV)
    partial_owner = jax.vmap(lambda own, number: deal_out(jax.random.fold_in(seeds[8], 2), own, number, PART_DEV, DEVICES, 1, CAP, 2))(partial_owner_keys, partial_owner_turns).reshape((PART_TOTAL, 1))
    partial_channel = touch_ends(jax.random.randint(seeds[9], (PART_TOTAL,), 0, CH_DEV), jax.random.fold_in(seeds[9], 1), 0, CH_DEV - 1).astype(jnp.int32)
    observed_data = noise(seeds[10], (STEPS, CHANNELS), 1.0, 6.0, ((1, 32),), jnp.float32)
    return {"initial_state": initial_state, "lame_lambda": lame_lambda, "shear_modulus": shear_modulus, "buoyancy": buoyancy, "source_cells": source_cells, "source_wavelet": source_wavelet, "segment_start": segment_start, "segment_weight": segment_weight, "partial_owner": partial_owner, "partial_channel": partial_channel, "observed_data": observed_data}


time_step = 0.25


def crop_rim(values):
    return values[..., 1:-1, 1:-1]


def ahead_x(values):
    return values[..., 2:, 1:-1] - values[..., 1:-1, 1:-1]


def behind_x(values):
    return values[..., 1:-1, 1:-1] - values[..., :-2, 1:-1]


def ahead_y(values):
    return values[..., 1:-1, 2:] - values[..., 1:-1, 1:-1]


def behind_y(values):
    return values[..., 1:-1, 1:-1] - values[..., 1:-1, :-2]


def ahead_z(inner_part):
    return jnp.concatenate([inner_part[..., 1:, :, :], jnp.zeros_like(inner_part[..., :1, :, :])], axis=-3) - inner_part


def behind_z(inner_part):
    return inner_part - jnp.concatenate([jnp.zeros_like(inner_part[..., :1, :, :]), inner_part[..., :-1, :, :]], axis=-3)


def velocity_update(velocity, stress_pad, buoyancy):
    accel_x = ahead_x(stress_pad[0]) + behind_y(stress_pad[3]) + behind_z(crop_rim(stress_pad[4]))
    accel_y = behind_x(stress_pad[3]) + ahead_y(stress_pad[1]) + behind_z(crop_rim(stress_pad[5]))
    accel_z = behind_x(stress_pad[4]) + behind_y(stress_pad[5]) + ahead_z(crop_rim(stress_pad[2]))
    return velocity + time_step * buoyancy * jnp.stack([accel_x, accel_y, accel_z])


def strain_rates(velocity_pad):
    along_x = velocity_pad[0]
    along_y = velocity_pad[1]
    along_z = velocity_pad[2]
    return jnp.stack([behind_x(along_x), behind_y(along_y), behind_z(crop_rim(along_z)),
                      ahead_y(along_x) + ahead_x(along_y),
                      ahead_z(crop_rim(along_x)) + ahead_x(along_z),
                      ahead_z(crop_rim(along_y)) + ahead_y(along_z)])


def stress_update(stress, strains, lame_lambda, shear_modulus):
    dilation = strains[0] + strains[1] + strains[2]
    normal = stress[:3] + time_step * (lame_lambda * dilation + 2.0 * shear_modulus * strains[:3])
    sheared = stress[3:] + time_step * shear_modulus * strains[3:]
    return jnp.concatenate([normal, sheared])


def gradient_terms(forward, adjoint):
    products = forward * adjoint
    lambda_term = (forward[0] + forward[1] + forward[2]) * (adjoint[0] + adjoint[1] + adjoint[2])
    shear_term = 2.0 * (products[0] + products[1] + products[2]) + products[3] + products[4] + products[5]
    return jnp.stack([lambda_term, shear_term])


def window_sums(values, gauge_len):
    span_len = values.shape[-1] - gauge_len + 1
    running = values[..., 0:span_len]
    for offset in range(1, gauge_len):
        running = running + values[..., offset:offset + span_len]
    return running


def spread_back(values, gauge_len):
    widths = [(0, 0)] * (values.ndim - 1)
    running = jnp.pad(values, widths + [(0, gauge_len - 1)])
    for offset in range(1, gauge_len):
        running = running + jnp.pad(values, widths + [(offset, gauge_len - 1 - offset)])
    return running


def pad_lateral(values):
    return jnp.pad(values, [(0, 0)] * (values.ndim - 2) + [(1, 1), (1, 1)])


def run_step(velocity, stress, lame_lambda, shear_modulus, buoyancy):
    velocity = velocity_update(velocity, pad_lateral(stress), buoyancy)
    strains = strain_rates(pad_lateral(velocity))
    stress = stress_update(stress, strains, lame_lambda, shear_modulus)
    return velocity, stress, strains


def reference(initial_state, lame_lambda, shear_modulus, buoyancy, source_cells, source_wavelet, segment_start, segment_weight, partial_owner, partial_channel, observed_data):
    span_local = CY - GAUGE + 1
    span_global = NY - GAUGE + 1
    src_device = jnp.arange(SRC_TOTAL, dtype=jnp.int32) // SRC_DEV
    src_depth = source_cells // (CX * CY)
    src_rest = source_cells % (CX * CY)
    src_row = (src_device // N_GY) * CX + src_rest // CY
    src_col = (src_device % N_GY) * CY + src_rest % CY
    src_global = ((src_depth * NX + src_row) * NY + src_col).astype(jnp.int32)
    seg_device = jnp.arange(PART_TOTAL, dtype=jnp.int32) // PART_DEV
    seg_depth = segment_start // (CX * span_local)
    seg_rest = segment_start % (CX * span_local)
    seg_row = (seg_device // N_GY) * CX + seg_rest // span_local
    seg_col = (seg_device % N_GY) * CY + seg_rest % span_local
    seg_global = ((seg_depth * NX + seg_row) * span_global + seg_col).astype(jnp.int32)
    velocity = initial_state[:3]
    stress = initial_state[3:]
    forward_strains = []
    partial_rows = []
    for step_index in range(STEPS):
        normal = stress[:3].reshape(3, -1).at[:, src_global].add(source_wavelet[step_index]).reshape(3, NZ, NX, NY)
        stress = jnp.concatenate([normal, stress[3:]])
        velocity, stress, strains = run_step(velocity, stress, lame_lambda, shear_modulus, buoyancy)
        forward_strains.append(strains)
        windows = window_sums(strains[:2], GAUGE).reshape(2, -1)[:, seg_global]
        partial_rows.append(segment_weight[0] * windows[0] + segment_weight[1] * windows[1])
    partials = jnp.stack(partial_rows)
    channel_index = (partial_owner[:, 0] * CH_DEV + partial_channel).astype(jnp.int32)
    channel_sums = jax.ops.segment_sum(partials.T, channel_index, num_segments=CHANNELS).T
    residuals = channel_sums - observed_data
    adj_velocity = jnp.zeros((3, NZ, NX, NY), jnp.float32)
    adj_stress = jnp.zeros((6, NZ, NX, NY), jnp.float32)
    gradients = jnp.zeros((2, NZ, NX, NY), jnp.float32)
    for turn_index in range(STEPS):
        back_values = residuals[STEPS - 1 - turn_index][channel_index]
        load_map = jnp.zeros((2, NZ * NX * span_global), jnp.float32).at[:, seg_global].add(segment_weight * back_values)
        spread = spread_back(load_map.reshape(2, NZ, NX, span_global), GAUGE)
        adj_stress = jnp.concatenate([adj_stress[:2] + spread, adj_stress[2:]])
        adj_velocity, adj_stress, adj_strains = run_step(adj_velocity, adj_stress, lame_lambda, shear_modulus, buoyancy)
        gradients = gradients + gradient_terms(forward_strains[STEPS - 1 - turn_index], adj_strains)
    return residuals, gradients
```

```python
import functools

import jax
import jax.numpy as jnp
from jax import lax
from jax.experimental import pallas as pl
from jax.experimental.pallas import tpu as pltpu
from jax.sharding import PartitionSpec as P

GAUGE = 8
STEP = 0.25
RIM = 3
LANES = 128
TILE_X = 4
SPAN_X = 16
SPAN_Y = 256
F32, BF16, I32 = jnp.float32, jnp.bfloat16, jnp.int32
NEAR = tuple((dx, dy) for dx in (-1, 0, 1) for dy in (-1, 0, 1))


def call_kernel(body, name, outs, scratch, *args):
    whole = pl.BlockSpec(memory_space=pltpu.VMEM)
    return pl.pallas_call(
        body,
        name=name,
        out_shape=outs,
        in_specs=[whole] * len(args),
        out_specs=[whole] * len(outs),
        scratch_shapes=scratch,
        compiler_params=pltpu.CompilerParams(vmem_limit_bytes=24 * 1024 * 1024),
    )(*args)


def pieces(values):
    high = values.astype(BF16).astype(F32)
    rest = values - high
    middle = rest.astype(BF16).astype(F32)
    return high, middle, rest - middle


def iota(shape, dim):
    return lax.broadcasted_iota(I32, shape, dim)


def times(left, right):
    return lax.dot_general(left, right, (((1,), (0,)), ((), ())), preferred_element_type=F32)


def times_turned(left, right):
    return lax.dot_general(left, right, (((1,), (1,)), ((), ())), preferred_element_type=F32)


def sum_thirds(values):
    third = values.shape[0] // 3
    return values[:third] + values[third : 2 * third] + values[2 * third :]


def neighbour(dx, dy):
    count_x, count_y = lax.axis_size("gx"), lax.axis_size("gy")
    at_x, at_y = lax.axis_index("gx") + dx, lax.axis_index("gy") + dy
    inside = (at_x >= 0) & (at_x < count_x) & (at_y >= 0) & (at_y < count_y)
    return jnp.where(inside, at_x * count_y + at_y, 0), inside


def edge_columns(rows, side_ref):
    groups = rows.shape[0] // LANES
    turned = rows.T
    for side, base in ((0, 0), (1, LANES - RIM)):
        for column in range(RIM):
            for group in range(groups):
                side_ref[side, column * groups + group : column * groups + group + 1, :] = turned[
                    base + column : base + column + 1, group * LANES : (group + 1) * LANES
                ]


def send_sides(side_ref, out_ref, places):
    for dx, dy in places:
        index, inside = neighbour(dx, dy)

        @pl.when(inside)
        def _(index=index, dy=dy):
            out_ref[index] = side_ref[1 if dy > 0 else 0]


def arrived_chunk(recv_ref, dx, dy):
    index, inside = neighbour(dx, dy)
    return jnp.where(inside, recv_ref[index], 0.0)


def rim_rows(recv_ref, dx, groups, turn_ref):
    for dy, base in ((1, 0), (-1, LANES - RIM)):
        chunk = arrived_chunk(recv_ref, dx, dy)
        for column in range(RIM):
            for group in range(groups):
                turn_ref[base + column : base + column + 1, group * LANES : (group + 1) * LANES] = chunk[
                    column * groups + group : column * groups + group + 1, :
                ]
    return turn_ref[...].T


def lay_planes(planes_ref, lane, centre, higher, lower):
    upper_half = iota((8, LANES), 0) < TILE_X
    for pair in range(planes_ref.shape[0] // 2):
        rows = slice(8 * pair, 8 * pair + 8)
        mid, high, low = centre[rows], higher[rows], lower[rows]
        lanes = slice(lane, lane + LANES)
        planes_ref[2 * pair, 0:8, lanes] = jnp.where(upper_half, mid, pltpu.roll(high, 4, 0))
        planes_ref[2 * pair + 1, 0:8, lanes] = jnp.where(upper_half, pltpu.roll(mid, 4, 0), high)
        planes_ref[2 * pair, 8:16, lanes] = jnp.where(upper_half, 0.0, pltpu.roll(low, 4, 0))
        planes_ref[2 * pair + 1, 8:16, lanes] = jnp.where(upper_half, 0.0, low)


def ahead_x(plane):
    return pltpu.roll(plane, SPAN_X - 1, 0) - plane


def behind_x(plane):
    return plane - pltpu.roll(plane, 1, 0)


def ahead_y(plane):
    return pltpu.roll(plane, SPAN_Y - 1, 1) - plane


def behind_y(plane):
    return plane - pltpu.roll(plane, 1, 1)


def advance(field_ref, medium_ref, first, depth, emit, last):
    def field(number, z):
        return field_ref[number * depth + z]

    def ahead_z(number, z):
        here = field(number, z)
        return field(number, z + 1) - here if z + 1 < depth else -here

    def behind_z(number, z):
        here = field(number, z)
        return here - field(number, z - 1) if z else here

    for z in range(depth):
        scale = STEP * medium_ref[first + 2 * depth + z]
        accel = (
            ahead_x(field(3, z)) + behind_y(field(6, z)) + behind_z(7, z),
            behind_x(field(6, z)) + ahead_y(field(4, z)) + behind_z(8, z),
            behind_x(field(7, z)) + behind_y(field(8, z)) + ahead_z(5, z),
        )
        for number in range(3):
            field_ref[number * depth + z] = field(number, z) + scale * accel[number]
    for z in range(depth):
        along_x, along_y, along_z = field(0, z), field(1, z), field(2, z)
        strains = (
            behind_x(along_x),
            behind_y(along_y),
            behind_z(2, z),
            ahead_y(along_x) + ahead_x(along_y),
            ahead_z(0, z) + ahead_x(along_z),
            ahead_z(1, z) + ahead_y(along_z),
        )
        emit(z, strains)
        if not last:
            shear = medium_ref[first + depth + z]
            dilated = medium_ref[first + z] * (strains[0] + strains[1] + strains[2])
            for number in range(3):
                field_ref[(3 + number) * depth + z] = field(3 + number, z) + STEP * (
                    dilated + 2.0 * shear * strains[number]
                )
                field_ref[(6 + number) * depth + z] = (
                    field(6 + number, z) + STEP * shear * strains[3 + number]
                )


def pack_body(fields_ref, cells_ref, wavelet_ref, out_ref, side_ref):
    rows = fields_ref[...]
    spare = 2 * LANES - rows.shape[0]
    edge_columns(jnp.concatenate([rows, jnp.zeros((spare, LANES), F32)], axis=0), side_ref)
    count = cells_ref.shape[1]
    for side in range(2):
        side_ref[side, 6:7, 0:count] = cells_ref[...].astype(F32)
        side_ref[side, 6:7, count : 2 * count] = wavelet_ref[0:1, :]
        side_ref[side, 7:8, 0:count] = wavelet_ref[1:2, :]
        side_ref[side, 7:8, count : 2 * count] = wavelet_ref[2:3, :]
    send_sides(side_ref, out_ref, NEAR)


def slots_body(capacity, devices, cols_y, owner_ref, start_ref, slot_ref, row_ref, cover_ref, place_ref, rank_ref):
    blocks = owner_ref.shape[0]
    group = 32
    before = jnp.where(iota((LANES, 2 * LANES), 0) < iota((LANES, 2 * LANES), 1), 1.0, 0.0).astype(BF16)
    rank_ref[...] = jnp.zeros_like(rank_ref)

    def count_group(number, carry):
        names = iota((group, LANES), 0) + number * group
        hot = [names == owner_ref[b : b + 1, :] for b in range(blocks)]
        marks = jnp.concatenate([jnp.where(h, 1.0, 0.0) for h in hot], axis=0).astype(BF16)
        counts = times(marks, before)
        total = jnp.zeros((group, LANES), F32)
        for b in range(blocks):
            part = counts[b * group : (b + 1) * group]
            rank_ref[b : b + 1, :] = rank_ref[b : b + 1, :] + jnp.sum(
                jnp.where(hot[b], part[:, :LANES] + total, 0.0), axis=0, keepdims=True
            )
            total = total + part[:, LANES:]
        return carry

    if devices == group:
        count_group(0, 0)
    else:
        lax.fori_loop(0, devices // group, count_group, 0)
    slot = owner_ref[...] * capacity + rank_ref[...].astype(I32)
    slot_ref[...] = slot >> 7
    low = slot & (LANES - 1)
    span = cols_y - GAUGE + 1
    start = start_ref[...]
    row = ((start.astype(F32) + 0.5) * (1.0 / span)).astype(I32)
    row_ref[...] = row
    first = start - row * span
    down = iota((LANES, LANES), 0)
    for b in range(blocks):
        lanes = slice(b * LANES, (b + 1) * LANES)
        offset = down - first[b : b + 1, :]
        cover_ref[:, lanes] = jnp.where((offset >= 0) & (offset < GAUGE), 1.0, 0.0).astype(BF16)
        place_ref[:, lanes] = jnp.where(down == low[b : b + 1, :], 1.0, 0.0).astype(BF16)


def source_maps(recv_ref, cols_y, depth, left_ref, right_ref):
    count = LANES // 2
    first_half = iota((1, LANES), 1) < count
    rows_per_step = depth * SPAN_X
    down_rows = iota((rows_per_step, LANES), 0)
    down_lanes = iota((SPAN_Y, LANES), 0)
    halves = []
    for dx, dy in NEAR:
        chunk = arrived_chunk(recv_ref, dx, dy)
        cells = chunk[6:7, :].astype(I32)
        y = cells & (cols_y - 1)
        rest = cells >> (cols_y.bit_length() - 1)
        x = rest & (TILE_X - 1)
        z = rest >> (TILE_X.bit_length() - 1)
        row = z * SPAN_X + x + (TILE_X if dx > 0 else SPAN_X - TILE_X if dx < 0 else 0)
        if dy > 0:
            lane = jnp.where(y < RIM, y + LANES, -1)
        elif dy < 0:
            lane = jnp.where(y >= cols_y - RIM, y + LANES, -1)
        else:
            lane = y
        halves.append((row, lane, chunk[6:7, :], chunk[7:8, :]))
    zero_row = jnp.zeros((1, LANES), F32)
    halves.append((jnp.zeros((1, LANES), I32), jnp.full((1, LANES), -1, I32), zero_row, zero_row))
    for block in range(len(halves) // 2):
        (row_a, lane_a, one_a, two_a), (row_b, lane_b, one_b, two_b) = halves[2 * block : 2 * block + 2]
        row = jnp.where(first_half, row_a, pltpu.roll(row_b, count, 1))
        lane = jnp.where(first_half, lane_a, pltpu.roll(lane_b, count, 1))
        steps = (
            jnp.where(first_half, pltpu.roll(one_a, count, 1), one_b),
            jnp.where(first_half, two_a, pltpu.roll(two_b, count, 1)),
            jnp.where(first_half, pltpu.roll(two_a, count, 1), two_b),
        )
        lanes = slice(block * LANES, (block + 1) * LANES)
        right_ref[:, lanes] = jnp.where(down_lanes == lane, 1.0, 0.0).astype(BF16)
        at_row = down_rows == row
        for step, amplitude in enumerate(steps):
            for third, piece in enumerate(pieces(amplitude)):
                base = (third * 3 + step) * rows_per_step
                left_ref[base : base + rows_per_step, lanes] = jnp.where(at_row, piece, 0.0).astype(BF16)
    return sum_thirds(times_turned(left_ref[...], right_ref[...]))


def forward_body(
    cols_y,
    fields_ref,
    higher_ref,
    lower_ref,
    recv_ref,
    slot_ref,
    row_ref,
    weight_ref,
    channel_ref,
    cover_ref,
    place_ref,
    out_ref,
    strain_ref,
    medium_ref,
    planes_ref,
    turn_ref,
    source_left_ref,
    source_right_ref,
    source_ref,
    spread_ref,
):
    depth = medium_ref.shape[0] // 3
    cells_row = depth * TILE_X
    turn_ref[...] = jnp.zeros_like(turn_ref)
    rims = [rim_rows(recv_ref, dx, 2, turn_ref) for dx in (0, 1, -1)]
    lay_planes(planes_ref, 0, fields_ref, higher_ref, lower_ref)
    lay_planes(planes_ref, LANES, *rims)
    first = 9 * depth
    medium_ref[...] = planes_ref[first:]
    source_ref[...] = source_maps(recv_ref, cols_y, depth, source_left_ref, source_right_ref)
    for step in range(3):
        for z in range(depth):
            base = step * depth * SPAN_X + z * SPAN_X
            load = source_ref[base : base + SPAN_X, :]
            for number in range(3, 6):
                planes_ref[number * depth + z] = planes_ref[number * depth + z] + load

        def emit(z, strains, step=step):
            for number, strain in enumerate(strains):
                base = ((step * 6 + number) * depth + z) * TILE_X
                strain_ref[base : base + TILE_X, :] = strain[0:TILE_X, 0:LANES]

        advance(planes_ref, planes_ref, first, depth, emit, step == 2)
    axial = jnp.concatenate(
        [strain_ref[step * 6 * cells_row : (step * 6 + 2) * cells_row, :] for step in range(3)], axis=0
    )
    axial = jnp.concatenate(pieces(axial), axis=0).astype(BF16)
    rows_down = iota((cells_row, LANES), 0)
    slots_down = iota((LANES, LANES), 0) >> 2
    for block in range(slot_ref.shape[0]):
        lanes = slice(block * LANES, (block + 1) * LANES)
        windows = sum_thirds(times(axial, cover_ref[:, lanes]))
        at_row = rows_down == row_ref[block : block + 1, :]
        weight_x, weight_y = weight_ref[0:1, lanes], weight_ref[1:2, lanes]
        sums = []
        for step in range(3):
            base = 2 * step * cells_row
            both = (
                weight_x * windows[base : base + cells_row]
                + weight_y * windows[base + cells_row : base + 2 * cells_row]
            )
            sums.append(jnp.sum(jnp.where(at_row, both, 0.0), axis=0, keepdims=True))
        sums.append(channel_ref[block : block + 1, :].astype(F32))
        values = jnp.concatenate(sums + sums, axis=0)
        in_slot = slots_down == slot_ref[block : block + 1, :]
        for third, piece in enumerate(pieces(values)):
            spread_ref[third * LANES : (third + 1) * LANES, lanes] = jnp.where(
                in_slot, jnp.concatenate([piece] * (LANES // 8), axis=0), 0.0
            ).astype(BF16)
    out_ref[...] = sum_thirds(times_turned(spread_ref[...], place_ref[...]))


def owner_body(arrived_ref, observed_ref, residual_ref, reply_ref, values_ref, place_ref, held_ref):
    groups = arrived_ref.shape[0] // 4
    parts = observed_ref.shape[1] // LANES
    down = iota((LANES, LANES), 0)
    part_down = iota((parts, LANES), 0)
    nothing = jnp.zeros((parts, LANES), F32)
    numbers = [arrived_ref[4 * s + 3 : 4 * s + 4, :].astype(I32) for s in range(groups)]
    for s in range(groups):
        lanes = slice(s * LANES, (s + 1) * LANES)
        place_ref[:, lanes] = jnp.where(down == (numbers[s] & (LANES - 1)), 1.0, 0.0).astype(BF16)
        at_part = part_down == (numbers[s] >> 7)
        thirds = pieces(arrived_ref[4 * s : 4 * s + 3, :])
        stack = []
        for third in thirds:
            for step in range(3):
                stack.append(jnp.where(at_part, third[step : step + 1, :], 0.0))
            stack.append(nothing)
        values_ref[:, lanes] = jnp.concatenate(stack, axis=0).astype(BF16)
    sums = sum_thirds(times_turned(values_ref[...], place_ref[...]))
    for step in range(3):
        for part in range(parts):
            at = step * parts + part
            held_ref[at : at + 1, :] = observed_ref[step : step + 1, part * LANES : (part + 1) * LANES]
    held_ref[3 * parts :, :] = nothing
    held_ref[...] = sums - held_ref[...]
    for step in range(3):
        for part in range(parts):
            at = step * parts + part
            residual_ref[step : step + 1, part * LANES : (part + 1) * LANES] = held_ref[at : at + 1, :]
    residual = jnp.concatenate(pieces(held_ref[...]), axis=0).astype(BF16)
    for s in range(groups):
        lanes = slice(s * LANES, (s + 1) * LANES)
        found = sum_thirds(times(residual, place_ref[:, lanes]))
        at_part = part_down == (numbers[s] >> 7)
        for step in range(3):
            reply_ref[4 * s + step : 4 * s + step + 1, :] = jnp.sum(
                jnp.where(at_part, found[step * parts : (step + 1) * parts], 0.0), axis=0, keepdims=True
            )
        reply_ref[4 * s + 3 : 4 * s + 4, :] = jnp.zeros((1, LANES), F32)


def load_body(
    arrived_ref,
    slot_ref,
    row_ref,
    weight_ref,
    cover_ref,
    place_ref,
    load_ref,
    out_ref,
    spread_ref,
    side_ref,
):
    cells_row = load_ref.shape[0] // 6
    stack_rows = load_ref.shape[0]
    arrived = jnp.concatenate(pieces(arrived_ref[...]), axis=0).astype(BF16)
    slots_down = iota((LANES, LANES), 0) >> 2
    rows_down = iota((cells_row, LANES), 0)
    for block in range(slot_ref.shape[0]):
        lanes = slice(block * LANES, (block + 1) * LANES)
        found = sum_thirds(times(arrived, place_ref[:, lanes]))
        found = jnp.where(slots_down == slot_ref[block : block + 1, :], found, 0.0)
        folded = found[0:8]
        for part in range(1, LANES // 8):
            folded = folded + found[8 * part : 8 * part + 8]
        folded = folded + pltpu.roll(folded, 4, 0)
        at_row = rows_down == row_ref[block : block + 1, :]
        for turn in range(3):
            back = folded[2 - turn : 3 - turn, :]
            for part in range(2):
                for third, piece in enumerate(pieces(weight_ref[part : part + 1, lanes] * back)):
                    base = third * stack_rows + (2 * turn + part) * cells_row
                    spread_ref[base : base + cells_row, lanes] = jnp.where(at_row, piece, 0.0).astype(BF16)
    load = sum_thirds(times_turned(spread_ref[...], cover_ref[...]))
    load_ref[...] = load
    spare = LANES - stack_rows
    edge_columns(jnp.concatenate([load, jnp.zeros((spare, LANES), F32)], axis=0), side_ref)
    side_ref[:, RIM : RIM + 1, :] = jnp.zeros((2, 1, LANES), F32)
    send_sides(side_ref, out_ref, [(dx, dy) for dx, dy in NEAR if dy])


def adjoint_body(
    load_ref, higher_ref, lower_ref, recv_ref, strain_ref, medium_ref, gradient_ref, load_planes_ref, planes_ref, turn_ref
):
    depth = medium_ref.shape[0] // 3
    turn_ref[...] = jnp.zeros_like(turn_ref)
    rims = [rim_rows(recv_ref, dx, 1, turn_ref) for dx in (0, 1, -1)]
    lay_planes(load_planes_ref, 0, load_ref, higher_ref, lower_ref)
    lay_planes(load_planes_ref, LANES, *rims)
    planes_ref[...] = jnp.zeros_like(planes_ref)
    gradient_ref[...] = jnp.zeros_like(gradient_ref)
    for turn in range(3):
        for part in range(2):
            for z in range(depth):
                at = (3 + part) * depth + z
                planes_ref[at] = planes_ref[at] + load_planes_ref[(2 * turn + part) * depth + z]

        def emit(z, strains, turn=turn):
            forward = []
            for number in range(6):
                base = (((2 - turn) * 6 + number) * depth + z) * TILE_X
                forward.append(strain_ref[base : base + TILE_X, :])
            back = [strain[0:TILE_X, 0:LANES] for strain in strains]
            dilation = (forward[0] + forward[1] + forward[2]) * (back[0] + back[1] + back[2])
            product = [forward[number] * back[number] for number in range(6)]
            shear = 2.0 * (product[0] + product[1] + product[2]) + product[3] + product[4] + product[5]
            for part, term in enumerate((dilation, shear)):
                base = (part * depth + z) * TILE_X
                gradient_ref[base : base + TILE_X, :] = gradient_ref[base : base + TILE_X, :] + term

        advance(planes_ref, medium_ref, 0, depth, emit, turn == 2)


def shards(
    initial_state,
    lame_lambda,
    shear_modulus,
    buoyancy,
    source_cells,
    source_wavelet,
    segment_start,
    segment_weight,
    partial_owner,
    partial_channel,
    observed_data,
):
    depth, rows_x, cols_y = lame_lambda.shape
    part_count = segment_start.shape[0]
    count_x, count_y = lax.axis_size("gx"), lax.axis_size("gy")
    devices = count_x * count_y
    capacity = max(2, 2 * part_count // devices)
    slot_groups = devices * capacity // LANES
    blocks = part_count // LANES
    per_group = LANES // capacity
    cells_row = depth * rows_x
    both = ("gx", "gy")
    up = [(i, i + 1) for i in range(count_x - 1)]
    down = [(j, i) for i, j in up]
    shape = jax.ShapeDtypeStruct

    def exchange(chunks):
        return lax.all_to_all(chunks, both, split_axis=0, concat_axis=0, tiled=True)

    def to_owners(rows):
        chunks = rows.reshape(slot_groups, 4, per_group, capacity).transpose(0, 2, 1, 3)
        back = exchange(chunks.reshape(devices, 4, capacity)).reshape(slot_groups, per_group, 4, capacity)
        return back.transpose(0, 2, 1, 3).reshape(slot_groups * 4, LANES)

    fields = jnp.concatenate(
        [values.reshape(-1, cols_y) for values in (initial_state, lame_lambda, shear_modulus, buoyancy)]
    )
    lower = lax.ppermute(fields, "gx", up)
    higher = lax.ppermute(fields, "gx", down)
    (edges,) = call_kernel(
        pack_body,
        "pack_edges",
        [shape((devices, 8, LANES), F32)],
        [pltpu.VMEM((2, 8, LANES), F32)],
        fields,
        source_cells.reshape(1, -1),
        source_wavelet,
    )
    rims = exchange(edges)
    channels = partial_channel.reshape(blocks, LANES)
    slot, row, cover, place = call_kernel(
        functools.partial(slots_body, capacity, devices, cols_y),
        "segment_slots",
        [
            shape((blocks, LANES), I32),
            shape((blocks, LANES), I32),
            shape((cols_y, part_count), BF16),
            shape((LANES, part_count), BF16),
        ],
        [pltpu.VMEM((blocks, LANES), F32)],
        partial_owner.reshape(blocks, LANES),
        segment_start.reshape(blocks, LANES),
    )
    partials, strains, medium = call_kernel(
        functools.partial(forward_body, cols_y),
        "forward_run",
        [
            shape((slot_groups * 4, LANES), F32),
            shape((18 * cells_row, cols_y), F32),
            shape((3 * depth, SPAN_X, SPAN_Y), F32),
        ],
        [
            pltpu.VMEM((12 * depth, SPAN_X, SPAN_Y), F32),
            pltpu.VMEM((LANES, 2 * LANES), F32),
            pltpu.VMEM((9 * depth * SPAN_X, 5 * LANES), BF16),
            pltpu.VMEM((SPAN_Y, 5 * LANES), BF16),
            pltpu.VMEM((3 * depth * SPAN_X, SPAN_Y), F32),
            pltpu.VMEM((3 * LANES, part_count), BF16),
        ],
        fields,
        higher,
        lower,
        rims,
        slot,
        row,
        segment_weight,
        channels,
        cover,
        place,
    )
    parts = observed_data.shape[1] // LANES
    residuals, reply = call_kernel(
        owner_body,
        "channel_sums",
        [shape(observed_data.shape, F32), shape((slot_groups * 4, LANES), F32)],
        [
            pltpu.VMEM((12 * parts, slot_groups * LANES), BF16),
            pltpu.VMEM((LANES, slot_groups * LANES), BF16),
            pltpu.VMEM((4 * parts, LANES), F32),
        ],
        to_owners(partials),
        observed_data,
    )
    loads, load_edges = call_kernel(
        load_body,
        "segment_loads",
        [shape((6 * cells_row, cols_y), F32), shape((devices, 4, LANES), F32)],
        [pltpu.VMEM((18 * cells_row, part_count), BF16), pltpu.VMEM((2, 4, LANES), F32)],
        to_owners(reply),
        slot,
        row,
        segment_weight,
        cover,
        place,
    )
    load_lower = lax.ppermute(loads, "gx", up)
    load_higher = lax.ppermute(loads, "gx", down)
    load_rims = exchange(load_edges)
    (gradients,) = call_kernel(
        adjoint_body,
        "adjoint_run",
        [shape((2 * cells_row, cols_y), F32)],
        [
            pltpu.VMEM((6 * depth, SPAN_X, SPAN_Y), F32),
            pltpu.VMEM((9 * depth, SPAN_X, SPAN_Y), F32),
            pltpu.VMEM((LANES, LANES), F32),
        ],
        loads,
        load_higher,
        load_lower,
        load_rims,
        strains,
        medium,
    )
    return (residuals, gradients.reshape(2, depth, rows_x, cols_y))


def solution(mesh):
    in_specs = (
        P(None, None, "gx", "gy"),
        P(None, "gx", "gy"),
        P(None, "gx", "gy"),
        P(None, "gx", "gy"),
        P(("gx", "gy")),
        P(None, ("gx", "gy")),
        P(("gx", "gy")),
        P(None, ("gx", "gy")),
        P(("gx", "gy"), None),
        P(("gx", "gy")),
        P(None, ("gx", "gy")),
    )
    out_specs = (P(None, ("gx", "gy")), P(None, None, "gx", "gy"))
    return jax.shard_map(shards, mesh=mesh, in_specs=in_specs, out_specs=out_specs, check_vma=False)
```

```python
import functools

import jax
import jax.numpy as jnp
from jax import lax
from jax.experimental import pallas as pl
from jax.experimental.pallas import tpu as pltpu
from jax.sharding import PartitionSpec as P

GAUGE = 8
STEP = 0.25
RIM = 3
LANES = 128
TILE_X = 4
SPAN_X = 16
SPAN_Y = 256
F32, BF16, I32 = jnp.float32, jnp.bfloat16, jnp.int32
NEAR = tuple((dx, dy) for dx in (-1, 0, 1) for dy in (-1, 0, 1))


def call_kernel(body, name, outs, scratch, *args):
    whole = pl.BlockSpec(memory_space=pltpu.VMEM)
    return pl.pallas_call(
        body,
        name=name,
        out_shape=outs,
        in_specs=[whole] * len(args),
        out_specs=[whole] * len(outs),
        scratch_shapes=scratch,
        compiler_params=pltpu.CompilerParams(vmem_limit_bytes=24 * 1024 * 1024),
    )(*args)


def pieces(values):
    high = values.astype(BF16).astype(F32)
    rest = values - high
    middle = rest.astype(BF16).astype(F32)
    return high, middle, rest - middle


def iota(shape, dim):
    return lax.broadcasted_iota(I32, shape, dim)


def times(left, right):
    return lax.dot_general(left, right, (((1,), (0,)), ((), ())), preferred_element_type=F32)


def times_turned(left, right):
    return lax.dot_general(left, right, (((1,), (1,)), ((), ())), preferred_element_type=F32)


def sum_thirds(values):
    third = values.shape[0] // 3
    return values[:third] + values[third : 2 * third] + values[2 * third :]


def neighbour(dx, dy):
    count_x, count_y = lax.axis_size("gx"), lax.axis_size("gy")
    at_x, at_y = lax.axis_index("gx") + dx, lax.axis_index("gy") + dy
    inside = (at_x >= 0) & (at_x < count_x) & (at_y >= 0) & (at_y < count_y)
    return jnp.where(inside, at_x * count_y + at_y, 0), inside


def edge_columns(rows, side_ref):
    groups = rows.shape[0] // LANES
    turned = rows.T
    for side, base in ((0, 0), (1, LANES - RIM)):
        for column in range(RIM):
            for group in range(groups):
                side_ref[side, column * groups + group : column * groups + group + 1, :] = turned[
                    base + column : base + column + 1, group * LANES : (group + 1) * LANES
                ]


def send_sides(side_ref, out_ref, places):
    for dx, dy in places:
        index, inside = neighbour(dx, dy)

        @pl.when(inside)
        def _(index=index, dy=dy):
            out_ref[index] = side_ref[1 if dy > 0 else 0]


def arrived_chunk(recv_ref, dx, dy):
    index, inside = neighbour(dx, dy)
    return jnp.where(inside, recv_ref[index], 0.0)


def rim_rows(recv_ref, dx, groups, turn_ref):
    for dy, base in ((1, 0), (-1, LANES - RIM)):
        chunk = arrived_chunk(recv_ref, dx, dy)
        for column in range(RIM):
            for group in range(groups):
                turn_ref[base + column : base + column + 1, group * LANES : (group + 1) * LANES] = chunk[
                    column * groups + group : column * groups + group + 1, :
                ]
    return turn_ref[...].T


def lay_planes(planes_ref, lane, centre, higher, lower):
    upper_half = iota((8, LANES), 0) < TILE_X
    for pair in range(planes_ref.shape[0] // 2):
        rows = slice(8 * pair, 8 * pair + 8)
        mid, high, low = centre[rows], higher[rows], lower[rows]
        lanes = slice(lane, lane + LANES)
        planes_ref[2 * pair, 0:8, lanes] = jnp.where(upper_half, mid, pltpu.roll(high, 4, 0))
        planes_ref[2 * pair + 1, 0:8, lanes] = jnp.where(upper_half, pltpu.roll(mid, 4, 0), high)
        planes_ref[2 * pair, 8:16, lanes] = jnp.where(upper_half, 0.0, pltpu.roll(low, 4, 0))
        planes_ref[2 * pair + 1, 8:16, lanes] = jnp.where(upper_half, 0.0, low)


def column_tiles(column_ref):
    count_x, at_x = lax.axis_size("gx"), lax.axis_index("gx")
    tiles = [column_ref[at_x]]
    for move in (1, -1):
        there = at_x + move
        inside = (there >= 0) & (there < count_x)
        tiles.append(jnp.where(inside, column_ref[jnp.where(inside, there, at_x)], 0.0))
    return tiles


def ahead_x(plane):
    return pltpu.roll(plane, SPAN_X - 1, 0) - plane


def behind_x(plane):
    return plane - pltpu.roll(plane, 1, 0)


def ahead_y(plane):
    return pltpu.roll(plane, SPAN_Y - 1, 1) - plane


def behind_y(plane):
    return plane - pltpu.roll(plane, 1, 1)


def advance(field_ref, medium_ref, first, depth, emit, last):
    def field(number, z):
        return field_ref[number * depth + z]

    def ahead_z(number, z):
        here = field(number, z)
        return field(number, z + 1) - here if z + 1 < depth else -here

    def behind_z(number, z):
        here = field(number, z)
        return here - field(number, z - 1) if z else here

    for z in range(depth):
        scale = STEP * medium_ref[first + 2 * depth + z]
        accel = (
            ahead_x(field(3, z)) + behind_y(field(6, z)) + behind_z(7, z),
            behind_x(field(6, z)) + ahead_y(field(4, z)) + behind_z(8, z),
            behind_x(field(7, z)) + behind_y(field(8, z)) + ahead_z(5, z),
        )
        for number in range(3):
            field_ref[number * depth + z] = field(number, z) + scale * accel[number]
    for z in range(depth):
        along_x, along_y, along_z = field(0, z), field(1, z), field(2, z)
        strains = (
            behind_x(along_x),
            behind_y(along_y),
            behind_z(2, z),
            ahead_y(along_x) + ahead_x(along_y),
            ahead_z(0, z) + ahead_x(along_z),
            ahead_z(1, z) + ahead_y(along_z),
        )
        emit(z, strains)
        if not last:
            shear = medium_ref[first + depth + z]
            dilated = medium_ref[first + z] * (strains[0] + strains[1] + strains[2])
            for number in range(3):
                field_ref[(3 + number) * depth + z] = field(3 + number, z) + STEP * (
                    dilated + 2.0 * shear * strains[number]
                )
                field_ref[(6 + number) * depth + z] = (
                    field(6 + number, z) + STEP * shear * strains[3 + number]
                )


def pack_body(fields_ref, cells_ref, wavelet_ref, out_ref, side_ref):
    rows = fields_ref[...]
    spare = 2 * LANES - rows.shape[0]
    edge_columns(jnp.concatenate([rows, jnp.zeros((spare, LANES), F32)], axis=0), side_ref)
    count = cells_ref.shape[1]
    for side in range(2):
        side_ref[side, 6:7, 0:count] = cells_ref[...].astype(F32)
        side_ref[side, 6:7, count : 2 * count] = wavelet_ref[0:1, :]
        side_ref[side, 7:8, 0:count] = wavelet_ref[1:2, :]
        side_ref[side, 7:8, count : 2 * count] = wavelet_ref[2:3, :]
    send_sides(side_ref, out_ref, NEAR)


def slots_body(capacity, devices, cols_y, owner_ref, start_ref, slot_ref, row_ref, cover_ref, place_ref, rank_ref):
    blocks = owner_ref.shape[0]
    group = 32
    before = jnp.where(iota((LANES, 2 * LANES), 0) < iota((LANES, 2 * LANES), 1), 1.0, 0.0).astype(BF16)
    rank_ref[...] = jnp.zeros_like(rank_ref)

    def count_group(number, carry):
        names = iota((group, LANES), 0) + number * group
        hot = [names == owner_ref[b : b + 1, :] for b in range(blocks)]
        marks = jnp.concatenate([jnp.where(h, 1.0, 0.0) for h in hot], axis=0).astype(BF16)
        counts = times(marks, before)
        total = jnp.zeros((group, LANES), F32)
        for b in range(blocks):
            part = counts[b * group : (b + 1) * group]
            rank_ref[b : b + 1, :] = rank_ref[b : b + 1, :] + jnp.sum(
                jnp.where(hot[b], part[:, :LANES] + total, 0.0), axis=0, keepdims=True
            )
            total = total + part[:, LANES:]
        return carry

    if devices == group:
        count_group(0, 0)
    else:
        lax.fori_loop(0, devices // group, count_group, 0)
    slot = owner_ref[...] * capacity + rank_ref[...].astype(I32)
    slot_ref[...] = slot >> 7
    low = slot & (LANES - 1)
    span = cols_y - GAUGE + 1
    start = start_ref[...]
    row = ((start.astype(F32) + 0.5) * (1.0 / span)).astype(I32)
    row_ref[...] = row
    first = start - row * span
    down = iota((LANES, LANES), 0)
    for b in range(blocks):
        lanes = slice(b * LANES, (b + 1) * LANES)
        offset = down - first[b : b + 1, :]
        cover_ref[:, lanes] = jnp.where((offset >= 0) & (offset < GAUGE), 1.0, 0.0).astype(BF16)
        place_ref[:, lanes] = jnp.where(down == low[b : b + 1, :], 1.0, 0.0).astype(BF16)


def source_maps(recv_ref, cols_y, depth, left_ref, right_ref):
    count = LANES // 2
    first_half = iota((1, LANES), 1) < count
    rows_per_step = depth * SPAN_X
    down_rows = iota((rows_per_step, LANES), 0)
    down_lanes = iota((SPAN_Y, LANES), 0)
    halves = []
    for dx, dy in NEAR:
        chunk = arrived_chunk(recv_ref, dx, dy)
        cells = chunk[6:7, :].astype(I32)
        y = cells & (cols_y - 1)
        rest = cells >> (cols_y.bit_length() - 1)
        x = rest & (TILE_X - 1)
        z = rest >> (TILE_X.bit_length() - 1)
        row = z * SPAN_X + x + (TILE_X if dx > 0 else SPAN_X - TILE_X if dx < 0 else 0)
        if dy > 0:
            lane = jnp.where(y < RIM, y + LANES, -1)
        elif dy < 0:
            lane = jnp.where(y >= cols_y - RIM, y + LANES, -1)
        else:
            lane = y
        halves.append((row, lane, chunk[6:7, :], chunk[7:8, :]))
    zero_row = jnp.zeros((1, LANES), F32)
    halves.append((jnp.zeros((1, LANES), I32), jnp.full((1, LANES), -1, I32), zero_row, zero_row))
    for block in range(len(halves) // 2):
        (row_a, lane_a, one_a, two_a), (row_b, lane_b, one_b, two_b) = halves[2 * block : 2 * block + 2]
        row = jnp.where(first_half, row_a, pltpu.roll(row_b, count, 1))
        lane = jnp.where(first_half, lane_a, pltpu.roll(lane_b, count, 1))
        steps = (
            jnp.where(first_half, pltpu.roll(one_a, count, 1), one_b),
            jnp.where(first_half, two_a, pltpu.roll(two_b, count, 1)),
            jnp.where(first_half, pltpu.roll(two_a, count, 1), two_b),
        )
        lanes = slice(block * LANES, (block + 1) * LANES)
        right_ref[:, lanes] = jnp.where(down_lanes == lane, 1.0, 0.0).astype(BF16)
        at_row = down_rows == row
        for step, amplitude in enumerate(steps):
            for third, piece in enumerate(pieces(amplitude)):
                base = (third * 3 + step) * rows_per_step
                left_ref[base : base + rows_per_step, lanes] = jnp.where(at_row, piece, 0.0).astype(BF16)
    return sum_thirds(times_turned(left_ref[...], right_ref[...]))


def forward_body(
    cols_y,
    column_ref,
    recv_ref,
    slot_ref,
    row_ref,
    weight_ref,
    channel_ref,
    cover_ref,
    place_ref,
    out_ref,
    strain_ref,
    medium_ref,
    planes_ref,
    turn_ref,
    source_left_ref,
    source_right_ref,
    source_ref,
    spread_ref,
):
    depth = medium_ref.shape[0] // 3
    cells_row = depth * TILE_X
    turn_ref[...] = jnp.zeros_like(turn_ref)
    rims = [rim_rows(recv_ref, dx, 2, turn_ref) for dx in (0, 1, -1)]
    lay_planes(planes_ref, 0, *column_tiles(column_ref))
    lay_planes(planes_ref, LANES, *rims)
    first = 9 * depth
    medium_ref[...] = planes_ref[first:]
    source_ref[...] = source_maps(recv_ref, cols_y, depth, source_left_ref, source_right_ref)
    for step in range(3):
        for z in range(depth):
            base = step * depth * SPAN_X + z * SPAN_X
            load = source_ref[base : base + SPAN_X, :]
            for number in range(3, 6):
                planes_ref[number * depth + z] = planes_ref[number * depth + z] + load

        def emit(z, strains, step=step):
            for number, strain in enumerate(strains):
                base = ((step * 6 + number) * depth + z) * TILE_X
                strain_ref[base : base + TILE_X, :] = strain[0:TILE_X, 0:LANES]

        advance(planes_ref, planes_ref, first, depth, emit, step == 2)
    axial = jnp.concatenate(
        [strain_ref[step * 6 * cells_row : (step * 6 + 2) * cells_row, :] for step in range(3)], axis=0
    )
    axial = jnp.concatenate(pieces(axial), axis=0).astype(BF16)
    rows_down = iota((cells_row, LANES), 0)
    slots_down = iota((LANES, LANES), 0) >> 2
    for block in range(slot_ref.shape[0]):
        lanes = slice(block * LANES, (block + 1) * LANES)
        windows = sum_thirds(times(axial, cover_ref[:, lanes]))
        at_row = rows_down == row_ref[block : block + 1, :]
        weight_x, weight_y = weight_ref[0:1, lanes], weight_ref[1:2, lanes]
        sums = []
        for step in range(3):
            base = 2 * step * cells_row
            both = (
                weight_x * windows[base : base + cells_row]
                + weight_y * windows[base + cells_row : base + 2 * cells_row]
            )
            sums.append(jnp.sum(jnp.where(at_row, both, 0.0), axis=0, keepdims=True))
        sums.append(channel_ref[block : block + 1, :].astype(F32))
        values = jnp.concatenate(sums + sums, axis=0)
        in_slot = slots_down == slot_ref[block : block + 1, :]
        for third, piece in enumerate(pieces(values)):
            spread_ref[third * LANES : (third + 1) * LANES, lanes] = jnp.where(
                in_slot, jnp.concatenate([piece] * (LANES // 8), axis=0), 0.0
            ).astype(BF16)
    out_ref[...] = sum_thirds(times_turned(spread_ref[...], place_ref[...]))


def owner_body(arrived_ref, observed_ref, residual_ref, reply_ref, values_ref, place_ref, held_ref):
    groups = arrived_ref.shape[0] // 4
    parts = observed_ref.shape[1] // LANES
    down = iota((LANES, LANES), 0)
    part_down = iota((parts, LANES), 0)
    nothing = jnp.zeros((parts, LANES), F32)
    numbers = [arrived_ref[4 * s + 3 : 4 * s + 4, :].astype(I32) for s in range(groups)]
    for s in range(groups):
        lanes = slice(s * LANES, (s + 1) * LANES)
        place_ref[:, lanes] = jnp.where(down == (numbers[s] & (LANES - 1)), 1.0, 0.0).astype(BF16)
        at_part = part_down == (numbers[s] >> 7)
        thirds = pieces(arrived_ref[4 * s : 4 * s + 3, :])
        stack = []
        for third in thirds:
            for step in range(3):
                stack.append(jnp.where(at_part, third[step : step + 1, :], 0.0))
            stack.append(nothing)
        values_ref[:, lanes] = jnp.concatenate(stack, axis=0).astype(BF16)
    sums = sum_thirds(times_turned(values_ref[...], place_ref[...]))
    for step in range(3):
        for part in range(parts):
            at = step * parts + part
            held_ref[at : at + 1, :] = observed_ref[step : step + 1, part * LANES : (part + 1) * LANES]
    held_ref[3 * parts :, :] = nothing
    held_ref[...] = sums - held_ref[...]
    for step in range(3):
        for part in range(parts):
            at = step * parts + part
            residual_ref[step : step + 1, part * LANES : (part + 1) * LANES] = held_ref[at : at + 1, :]
    residual = jnp.concatenate(pieces(held_ref[...]), axis=0).astype(BF16)
    for s in range(groups):
        lanes = slice(s * LANES, (s + 1) * LANES)
        found = sum_thirds(times(residual, place_ref[:, lanes]))
        at_part = part_down == (numbers[s] >> 7)
        for step in range(3):
            reply_ref[4 * s + step : 4 * s + step + 1, :] = jnp.sum(
                jnp.where(at_part, found[step * parts : (step + 1) * parts], 0.0), axis=0, keepdims=True
            )
        reply_ref[4 * s + 3 : 4 * s + 4, :] = jnp.zeros((1, LANES), F32)


def load_body(
    arrived_ref,
    slot_ref,
    row_ref,
    weight_ref,
    cover_ref,
    place_ref,
    load_ref,
    out_ref,
    spread_ref,
    side_ref,
):
    cells_row = load_ref.shape[0] // 6
    stack_rows = load_ref.shape[0]
    arrived = jnp.concatenate(pieces(arrived_ref[...]), axis=0).astype(BF16)
    slots_down = iota((LANES, LANES), 0) >> 2
    rows_down = iota((cells_row, LANES), 0)
    for block in range(slot_ref.shape[0]):
        lanes = slice(block * LANES, (block + 1) * LANES)
        found = sum_thirds(times(arrived, place_ref[:, lanes]))
        found = jnp.where(slots_down == slot_ref[block : block + 1, :], found, 0.0)
        folded = found[0:8]
        for part in range(1, LANES // 8):
            folded = folded + found[8 * part : 8 * part + 8]
        folded = folded + pltpu.roll(folded, 4, 0)
        at_row = rows_down == row_ref[block : block + 1, :]
        for turn in range(3):
            back = folded[2 - turn : 3 - turn, :]
            for part in range(2):
                for third, piece in enumerate(pieces(weight_ref[part : part + 1, lanes] * back)):
                    base = third * stack_rows + (2 * turn + part) * cells_row
                    spread_ref[base : base + cells_row, lanes] = jnp.where(at_row, piece, 0.0).astype(BF16)
    load = sum_thirds(times_turned(spread_ref[...], cover_ref[...]))
    load_ref[...] = load
    spare = LANES - stack_rows
    edge_columns(jnp.concatenate([load, jnp.zeros((spare, LANES), F32)], axis=0), side_ref)
    side_ref[:, RIM : RIM + 1, :] = jnp.zeros((2, 1, LANES), F32)
    send_sides(side_ref, out_ref, [(dx, dy) for dx, dy in NEAR if dy])


def adjoint_body(
    column_ref, recv_ref, strain_ref, medium_ref, gradient_ref, load_planes_ref, planes_ref, turn_ref
):
    depth = medium_ref.shape[0] // 3
    turn_ref[...] = jnp.zeros_like(turn_ref)
    rims = [rim_rows(recv_ref, dx, 1, turn_ref) for dx in (0, 1, -1)]
    lay_planes(load_planes_ref, 0, *column_tiles(column_ref))
    lay_planes(load_planes_ref, LANES, *rims)
    planes_ref[...] = jnp.zeros_like(planes_ref)
    gradient_ref[...] = jnp.zeros_like(gradient_ref)
    for turn in range(3):
        for part in range(2):
            for z in range(depth):
                at = (3 + part) * depth + z
                planes_ref[at] = planes_ref[at] + load_planes_ref[(2 * turn + part) * depth + z]

        def emit(z, strains, turn=turn):
            forward = []
            for number in range(6):
                base = (((2 - turn) * 6 + number) * depth + z) * TILE_X
                forward.append(strain_ref[base : base + TILE_X, :])
            back = [strain[0:TILE_X, 0:LANES] for strain in strains]
            dilation = (forward[0] + forward[1] + forward[2]) * (back[0] + back[1] + back[2])
            product = [forward[number] * back[number] for number in range(6)]
            shear = 2.0 * (product[0] + product[1] + product[2]) + product[3] + product[4] + product[5]
            for part, term in enumerate((dilation, shear)):
                base = (part * depth + z) * TILE_X
                gradient_ref[base : base + TILE_X, :] = gradient_ref[base : base + TILE_X, :] + term

        advance(planes_ref, medium_ref, 0, depth, emit, turn == 2)


def shards(
    initial_state,
    lame_lambda,
    shear_modulus,
    buoyancy,
    source_cells,
    source_wavelet,
    segment_start,
    segment_weight,
    partial_owner,
    partial_channel,
    observed_data,
):
    depth, rows_x, cols_y = lame_lambda.shape
    part_count = segment_start.shape[0]
    count_x, count_y = lax.axis_size("gx"), lax.axis_size("gy")
    devices = count_x * count_y
    capacity = max(2, 2 * part_count // devices)
    slot_groups = devices * capacity // LANES
    blocks = part_count // LANES
    per_group = LANES // capacity
    cells_row = depth * rows_x
    both = ("gx", "gy")
    shape = jax.ShapeDtypeStruct

    def exchange(chunks):
        return lax.all_to_all(chunks, both, split_axis=0, concat_axis=0, tiled=True)

    def to_owners(rows):
        chunks = rows.reshape(slot_groups, 4, per_group, capacity).transpose(0, 2, 1, 3)
        back = exchange(chunks.reshape(devices, 4, capacity)).reshape(slot_groups, per_group, 4, capacity)
        return back.transpose(0, 2, 1, 3).reshape(slot_groups * 4, LANES)

    fields = jnp.concatenate(
        [values.reshape(-1, cols_y) for values in (initial_state, lame_lambda, shear_modulus, buoyancy)]
    )
    column = lax.all_gather(fields, "gx")
    (edges,) = call_kernel(
        pack_body,
        "pack_edges",
        [shape((devices, 8, LANES), F32)],
        [pltpu.VMEM((2, 8, LANES), F32)],
        fields,
        source_cells.reshape(1, -1),
        source_wavelet,
    )
    rims = exchange(edges)
    channels = partial_channel.reshape(blocks, LANES)
    slot, row, cover, place = call_kernel(
        functools.partial(slots_body, capacity, devices, cols_y),
        "segment_slots",
        [
            shape((blocks, LANES), I32),
            shape((blocks, LANES), I32),
            shape((cols_y, part_count), BF16),
            shape((LANES, part_count), BF16),
        ],
        [pltpu.VMEM((blocks, LANES), F32)],
        partial_owner.reshape(blocks, LANES),
        segment_start.reshape(blocks, LANES),
    )
    partials, strains, medium = call_kernel(
        functools.partial(forward_body, cols_y),
        "forward_run",
        [
            shape((slot_groups * 4, LANES), F32),
            shape((18 * cells_row, cols_y), F32),
            shape((3 * depth, SPAN_X, SPAN_Y), F32),
        ],
        [
            pltpu.VMEM((12 * depth, SPAN_X, SPAN_Y), F32),
            pltpu.VMEM((LANES, 2 * LANES), F32),
            pltpu.VMEM((9 * depth * SPAN_X, 5 * LANES), BF16),
            pltpu.VMEM((SPAN_Y, 5 * LANES), BF16),
            pltpu.VMEM((3 * depth * SPAN_X, SPAN_Y), F32),
            pltpu.VMEM((3 * LANES, part_count), BF16),
        ],
        column,
        rims,
        slot,
        row,
        segment_weight,
        channels,
        cover,
        place,
    )
    parts = observed_data.shape[1] // LANES
    residuals, reply = call_kernel(
        owner_body,
        "channel_sums",
        [shape(observed_data.shape, F32), shape((slot_groups * 4, LANES), F32)],
        [
            pltpu.VMEM((12 * parts, slot_groups * LANES), BF16),
            pltpu.VMEM((LANES, slot_groups * LANES), BF16),
            pltpu.VMEM((4 * parts, LANES), F32),
        ],
        to_owners(partials),
        observed_data,
    )
    loads, load_edges = call_kernel(
        load_body,
        "segment_loads",
        [shape((6 * cells_row, cols_y), F32), shape((devices, 4, LANES), F32)],
        [pltpu.VMEM((18 * cells_row, part_count), BF16), pltpu.VMEM((2, 4, LANES), F32)],
        to_owners(reply),
        slot,
        row,
        segment_weight,
        cover,
        place,
    )
    load_column = lax.all_gather(loads, "gx")
    load_rims = exchange(load_edges)
    (gradients,) = call_kernel(
        adjoint_body,
        "adjoint_run",
        [shape((2 * cells_row, cols_y), F32)],
        [
            pltpu.VMEM((6 * depth, SPAN_X, SPAN_Y), F32),
            pltpu.VMEM((9 * depth, SPAN_X, SPAN_Y), F32),
            pltpu.VMEM((LANES, LANES), F32),
        ],
        load_column,
        load_rims,
        strains,
        medium,
    )
    return (residuals, gradients.reshape(2, depth, rows_x, cols_y))


def solution(mesh):
    in_specs = (
        P(None, None, "gx", "gy"),
        P(None, "gx", "gy"),
        P(None, "gx", "gy"),
        P(None, "gx", "gy"),
        P(("gx", "gy")),
        P(None, ("gx", "gy")),
        P(("gx", "gy")),
        P(None, ("gx", "gy")),
        P(("gx", "gy"), None),
        P(("gx", "gy")),
        P(None, ("gx", "gy")),
    )
    out_specs = (P(None, ("gx", "gy")), P(None, None, "gx", "gy"))
    return jax.shard_map(shards, mesh=mesh, in_specs=in_specs, out_specs=out_specs, check_vma=False)
```

```python
import functools

import jax
import jax.numpy as jnp
from jax import lax
from jax.experimental import pallas as pl
from jax.experimental.pallas import tpu as pltpu
from jax.sharding import PartitionSpec as P

GAUGE = 8
STEP = 0.25
RIM = 3
LANES = 128
TILE_X = 4
SPAN_X = 16
SPAN_Y = 256
F32, BF16, I32 = jnp.float32, jnp.bfloat16, jnp.int32
NEAR = tuple((dx, dy) for dx in (-1, 0, 1) for dy in (-1, 0, 1))


def call_kernel(body, name, outs, scratch, *args):
    whole = pl.BlockSpec(memory_space=pltpu.VMEM)
    return pl.pallas_call(
        body,
        name=name,
        out_shape=outs,
        in_specs=[whole] * len(args),
        out_specs=[whole] * len(outs),
        scratch_shapes=scratch,
        compiler_params=pltpu.CompilerParams(vmem_limit_bytes=24 * 1024 * 1024),
    )(*args)


def pieces(values):
    high = values.astype(BF16).astype(F32)
    rest = values - high
    middle = rest.astype(BF16).astype(F32)
    return high, middle, rest - middle


def iota(shape, dim):
    return lax.broadcasted_iota(I32, shape, dim)


def times(left, right):
    return lax.dot_general(left, right, (((1,), (0,)), ((), ())), preferred_element_type=F32)


def times_turned(left, right):
    return lax.dot_general(left, right, (((1,), (1,)), ((), ())), preferred_element_type=F32)


def sum_thirds(values):
    third = values.shape[0] // 3
    return values[:third] + values[third : 2 * third] + values[2 * third :]


def neighbour(dx, dy):
    count_x, count_y = lax.axis_size("gx"), lax.axis_size("gy")
    at_x, at_y = lax.axis_index("gx") + dx, lax.axis_index("gy") + dy
    inside = (at_x >= 0) & (at_x < count_x) & (at_y >= 0) & (at_y < count_y)
    return jnp.where(inside, at_x * count_y + at_y, 0), inside


def neighbour_x(move):
    there = lax.axis_index("gx") + move
    inside = (there >= 0) & (there < lax.axis_size("gx"))
    return jnp.where(inside, there, 0), inside


def column_rows(depth, move):
    at = 0
    for plane in range(6 * depth):
        height = TILE_X if plane < 2 * depth else 2
        yield at, plane * TILE_X + (TILE_X - height if move > 0 else 0), height
        at = at + height


def edge_columns(rows, side_ref):
    groups = rows.shape[0] // LANES
    turned = rows.T
    for side, base in ((0, 0), (1, LANES - RIM)):
        for column in range(RIM):
            for group in range(groups):
                side_ref[side, column * groups + group : column * groups + group + 1, :] = turned[
                    base + column : base + column + 1, group * LANES : (group + 1) * LANES
                ]


def send_sides(side_ref, out_ref, places):
    for dx, dy in places:
        index, inside = neighbour(dx, dy)

        @pl.when(inside)
        def _(index=index, dy=dy):
            out_ref[index] = side_ref[1 if dy > 0 else 0]


def arrived_chunk(recv_ref, dx, dy):
    index, inside = neighbour(dx, dy)
    return jnp.where(inside, recv_ref[index], 0.0)


def rim_rows(recv_ref, dx, groups, turn_ref):
    for dy, base in ((1, 0), (-1, LANES - RIM)):
        chunk = arrived_chunk(recv_ref, dx, dy)
        for column in range(RIM):
            for group in range(groups):
                turn_ref[base + column : base + column + 1, group * LANES : (group + 1) * LANES] = chunk[
                    column * groups + group : column * groups + group + 1, :
                ]
    return turn_ref[...].T


def lay_planes(planes_ref, lane, centre, higher, lower):
    upper_half = iota((8, LANES), 0) < TILE_X
    for pair in range(planes_ref.shape[0] // 2):
        rows = slice(8 * pair, 8 * pair + 8)
        mid, high, low = centre[rows], higher[rows], lower[rows]
        lanes = slice(lane, lane + LANES)
        planes_ref[2 * pair, 0:8, lanes] = jnp.where(upper_half, mid, pltpu.roll(high, 4, 0))
        planes_ref[2 * pair + 1, 0:8, lanes] = jnp.where(upper_half, pltpu.roll(mid, 4, 0), high)
        planes_ref[2 * pair, 8:16, lanes] = jnp.where(upper_half, 0.0, pltpu.roll(low, 4, 0))
        planes_ref[2 * pair + 1, 8:16, lanes] = jnp.where(upper_half, 0.0, low)


def ahead_x(plane):
    return pltpu.roll(plane, SPAN_X - 1, 0) - plane


def behind_x(plane):
    return plane - pltpu.roll(plane, 1, 0)


def ahead_y(plane):
    return pltpu.roll(plane, SPAN_Y - 1, 1) - plane


def behind_y(plane):
    return plane - pltpu.roll(plane, 1, 1)


def advance(field_ref, medium_ref, first, depth, emit, last):
    def field(number, z):
        return field_ref[number * depth + z]

    def ahead_z(number, z):
        here = field(number, z)
        return field(number, z + 1) - here if z + 1 < depth else -here

    def behind_z(number, z):
        here = field(number, z)
        return here - field(number, z - 1) if z else here

    for z in range(depth):
        scale = STEP * medium_ref[first + 2 * depth + z]
        accel = (
            ahead_x(field(3, z)) + behind_y(field(6, z)) + behind_z(7, z),
            behind_x(field(6, z)) + ahead_y(field(4, z)) + behind_z(8, z),
            behind_x(field(7, z)) + behind_y(field(8, z)) + ahead_z(5, z),
        )
        for number in range(3):
            field_ref[number * depth + z] = field(number, z) + scale * accel[number]
    for z in range(depth):
        along_x, along_y, along_z = field(0, z), field(1, z), field(2, z)
        strains = (
            behind_x(along_x),
            behind_y(along_y),
            behind_z(2, z),
            ahead_y(along_x) + ahead_x(along_y),
            ahead_z(0, z) + ahead_x(along_z),
            ahead_z(1, z) + ahead_y(along_z),
        )
        emit(z, strains)
        if not last:
            shear = medium_ref[first + depth + z]
            dilated = medium_ref[first + z] * (strains[0] + strains[1] + strains[2])
            for number in range(3):
                field_ref[(3 + number) * depth + z] = field(3 + number, z) + STEP * (
                    dilated + 2.0 * shear * strains[number]
                )
                field_ref[(6 + number) * depth + z] = (
                    field(6 + number, z) + STEP * shear * strains[3 + number]
                )


def pack_body(state_ref, lambda_ref, shear_ref, buoyancy_ref, cells_ref, wavelet_ref, fields_ref, out_ref, side_ref):
    rows = jnp.concatenate([state_ref[...], lambda_ref[...], shear_ref[...], buoyancy_ref[...]], axis=0)
    fields_ref[...] = rows
    spare = 2 * LANES - rows.shape[0]
    edge_columns(jnp.concatenate([rows, jnp.zeros((spare, LANES), F32)], axis=0), side_ref)
    count = cells_ref.shape[1]
    for side in range(2):
        side_ref[side, 6:7, 0:count] = cells_ref[...].astype(F32)
        side_ref[side, 6:7, count : 2 * count] = wavelet_ref[0:1, :]
        side_ref[side, 7:8, 0:count] = wavelet_ref[1:2, :]
        side_ref[side, 7:8, count : 2 * count] = wavelet_ref[2:3, :]
    send_sides(side_ref, out_ref, NEAR)


def slots_body(capacity, devices, cols_y, owner_ref, start_ref, slot_ref, row_ref, cover_ref, place_ref, rank_ref):
    blocks = owner_ref.shape[0]
    group = 32
    before = jnp.where(iota((LANES, 2 * LANES), 0) < iota((LANES, 2 * LANES), 1), 1.0, 0.0).astype(BF16)
    rank_ref[...] = jnp.zeros_like(rank_ref)

    def count_group(number, carry):
        names = iota((group, LANES), 0) + number * group
        hot = [names == owner_ref[b : b + 1, :] for b in range(blocks)]
        marks = jnp.concatenate([jnp.where(h, 1.0, 0.0) for h in hot], axis=0).astype(BF16)
        counts = times(marks, before)
        total = jnp.zeros((group, LANES), F32)
        for b in range(blocks):
            part = counts[b * group : (b + 1) * group]
            rank_ref[b : b + 1, :] = rank_ref[b : b + 1, :] + jnp.sum(
                jnp.where(hot[b], part[:, :LANES] + total, 0.0), axis=0, keepdims=True
            )
            total = total + part[:, LANES:]
        return carry

    if devices == group:
        count_group(0, 0)
    else:
        lax.fori_loop(0, devices // group, count_group, 0)
    slot = owner_ref[...] * capacity + rank_ref[...].astype(I32)
    slot_ref[...] = slot >> 7
    low = slot & (LANES - 1)
    span = cols_y - GAUGE + 1
    start = start_ref[...]
    row = ((start.astype(F32) + 0.5) * (1.0 / span)).astype(I32)
    row_ref[...] = row
    first = start - row * span
    down = iota((LANES, LANES), 0)
    for b in range(blocks):
        lanes = slice(b * LANES, (b + 1) * LANES)
        offset = down - first[b : b + 1, :]
        cover_ref[:, lanes] = jnp.where((offset >= 0) & (offset < GAUGE), 1.0, 0.0).astype(BF16)
        place_ref[:, lanes] = jnp.where(down == low[b : b + 1, :], 1.0, 0.0).astype(BF16)


def source_maps(recv_ref, cols_y, depth, left_ref, right_ref):
    count = LANES // 2
    first_half = iota((1, LANES), 1) < count
    rows_per_step = depth * SPAN_X
    down_rows = iota((rows_per_step, LANES), 0)
    down_lanes = iota((SPAN_Y, LANES), 0)
    halves = []
    for dx, dy in NEAR:
        chunk = arrived_chunk(recv_ref, dx, dy)
        cells = chunk[6:7, :].astype(I32)
        y = cells & (cols_y - 1)
        rest = cells >> (cols_y.bit_length() - 1)
        x = rest & (TILE_X - 1)
        z = rest >> (TILE_X.bit_length() - 1)
        row = z * SPAN_X + x + (TILE_X if dx > 0 else SPAN_X - TILE_X if dx < 0 else 0)
        if dy > 0:
            lane = jnp.where(y < RIM, y + LANES, -1)
        elif dy < 0:
            lane = jnp.where(y >= cols_y - RIM, y + LANES, -1)
        else:
            lane = y
        halves.append((row, lane, chunk[6:7, :], chunk[7:8, :]))
    zero_row = jnp.zeros((1, LANES), F32)
    halves.append((jnp.zeros((1, LANES), I32), jnp.full((1, LANES), -1, I32), zero_row, zero_row))
    for block in range(len(halves) // 2):
        (row_a, lane_a, one_a, two_a), (row_b, lane_b, one_b, two_b) = halves[2 * block : 2 * block + 2]
        row = jnp.where(first_half, row_a, pltpu.roll(row_b, count, 1))
        lane = jnp.where(first_half, lane_a, pltpu.roll(lane_b, count, 1))
        steps = (
            jnp.where(first_half, pltpu.roll(one_a, count, 1), one_b),
            jnp.where(first_half, two_a, pltpu.roll(two_b, count, 1)),
            jnp.where(first_half, pltpu.roll(two_a, count, 1), two_b),
        )
        lanes = slice(block * LANES, (block + 1) * LANES)
        right_ref[:, lanes] = jnp.where(down_lanes == lane, 1.0, 0.0).astype(BF16)
        at_row = down_rows == row
        for step, amplitude in enumerate(steps):
            for third, piece in enumerate(pieces(amplitude)):
                base = (third * 3 + step) * rows_per_step
                left_ref[base : base + rows_per_step, lanes] = jnp.where(at_row, piece, 0.0).astype(BF16)
    return sum_thirds(times_turned(left_ref[...], right_ref[...]))


def forward_body(
    cols_y,
    fields_ref,
    higher_ref,
    lower_ref,
    recv_ref,
    slot_ref,
    row_ref,
    weight_ref,
    channel_ref,
    cover_ref,
    place_ref,
    out_ref,
    strain_ref,
    medium_ref,
    planes_ref,
    turn_ref,
    source_left_ref,
    source_right_ref,
    source_ref,
    spread_ref,
):
    depth = medium_ref.shape[0] // 3
    cells_row = depth * TILE_X
    turn_ref[...] = jnp.zeros_like(turn_ref)
    rims = [rim_rows(recv_ref, dx, 2, turn_ref) for dx in (0, 1, -1)]
    lay_planes(planes_ref, 0, fields_ref, higher_ref, lower_ref)
    lay_planes(planes_ref, LANES, *rims)
    first = 9 * depth
    medium_ref[...] = planes_ref[first:]
    source_ref[...] = source_maps(recv_ref, cols_y, depth, source_left_ref, source_right_ref)
    for step in range(3):
        for z in range(depth):
            base = step * depth * SPAN_X + z * SPAN_X
            load = source_ref[base : base + SPAN_X, :]
            for number in range(3, 6):
                planes_ref[number * depth + z] = planes_ref[number * depth + z] + load

        def emit(z, strains, step=step):
            for number, strain in enumerate(strains):
                base = ((step * 6 + number) * depth + z) * TILE_X
                strain_ref[base : base + TILE_X, :] = strain[0:TILE_X, 0:LANES]

        advance(planes_ref, planes_ref, first, depth, emit, step == 2)
    axial = jnp.concatenate(
        [strain_ref[step * 6 * cells_row : (step * 6 + 2) * cells_row, :] for step in range(3)], axis=0
    )
    axial = jnp.concatenate(pieces(axial), axis=0).astype(BF16)
    rows_down = iota((cells_row, LANES), 0)
    slots_down = iota((LANES, LANES), 0) >> 2
    for block in range(slot_ref.shape[0]):
        lanes = slice(block * LANES, (block + 1) * LANES)
        windows = sum_thirds(times(axial, cover_ref[:, lanes]))
        at_row = rows_down == row_ref[block : block + 1, :]
        weight_x, weight_y = weight_ref[0:1, lanes], weight_ref[1:2, lanes]
        sums = []
        for step in range(3):
            base = 2 * step * cells_row
            both = (
                weight_x * windows[base : base + cells_row]
                + weight_y * windows[base + cells_row : base + 2 * cells_row]
            )
            sums.append(jnp.sum(jnp.where(at_row, both, 0.0), axis=0, keepdims=True))
        sums.append(channel_ref[block : block + 1, :].astype(F32))
        values = jnp.concatenate(sums + sums, axis=0)
        in_slot = slots_down == slot_ref[block : block + 1, :]
        for third, piece in enumerate(pieces(values)):
            spread_ref[third * LANES : (third + 1) * LANES, lanes] = jnp.where(
                in_slot, jnp.concatenate([piece] * (LANES // 8), axis=0), 0.0
            ).astype(BF16)
    out_ref[...] = sum_thirds(times_turned(spread_ref[...], place_ref[...]))


def owner_body(arrived_ref, observed_ref, residual_ref, reply_ref, values_ref, place_ref, held_ref):
    groups = arrived_ref.shape[0] // 4
    parts = observed_ref.shape[1] // LANES
    down = iota((LANES, LANES), 0)
    part_down = iota((parts, LANES), 0)
    nothing = jnp.zeros((parts, LANES), F32)
    numbers = [arrived_ref[4 * s + 3 : 4 * s + 4, :].astype(I32) for s in range(groups)]
    for s in range(groups):
        lanes = slice(s * LANES, (s + 1) * LANES)
        place_ref[:, lanes] = jnp.where(down == (numbers[s] & (LANES - 1)), 1.0, 0.0).astype(BF16)
        at_part = part_down == (numbers[s] >> 7)
        thirds = pieces(arrived_ref[4 * s : 4 * s + 3, :])
        stack = []
        for third in thirds:
            for step in range(3):
                stack.append(jnp.where(at_part, third[step : step + 1, :], 0.0))
            stack.append(nothing)
        values_ref[:, lanes] = jnp.concatenate(stack, axis=0).astype(BF16)
    sums = sum_thirds(times_turned(values_ref[...], place_ref[...]))
    for step in range(3):
        for part in range(parts):
            at = step * parts + part
            held_ref[at : at + 1, :] = observed_ref[step : step + 1, part * LANES : (part + 1) * LANES]
    held_ref[3 * parts :, :] = nothing
    held_ref[...] = sums - held_ref[...]
    for step in range(3):
        for part in range(parts):
            at = step * parts + part
            residual_ref[step : step + 1, part * LANES : (part + 1) * LANES] = held_ref[at : at + 1, :]
    residual = jnp.concatenate(pieces(held_ref[...]), axis=0).astype(BF16)
    for s in range(groups):
        lanes = slice(s * LANES, (s + 1) * LANES)
        found = sum_thirds(times(residual, place_ref[:, lanes]))
        at_part = part_down == (numbers[s] >> 7)
        for step in range(3):
            reply_ref[4 * s + step : 4 * s + step + 1, :] = jnp.sum(
                jnp.where(at_part, found[step * parts : (step + 1) * parts], 0.0), axis=0, keepdims=True
            )
        reply_ref[4 * s + 3 : 4 * s + 4, :] = jnp.zeros((1, LANES), F32)


def load_body(
    arrived_ref,
    slot_ref,
    row_ref,
    weight_ref,
    cover_ref,
    place_ref,
    load_ref,
    out_ref,
    column_ref,
    spread_ref,
    side_ref,
):
    cells_row = load_ref.shape[0] // 6
    stack_rows = load_ref.shape[0]
    arrived = jnp.concatenate(pieces(arrived_ref[...]), axis=0).astype(BF16)
    slots_down = iota((LANES, LANES), 0) >> 2
    rows_down = iota((cells_row, LANES), 0)
    for block in range(slot_ref.shape[0]):
        lanes = slice(block * LANES, (block + 1) * LANES)
        found = sum_thirds(times(arrived, place_ref[:, lanes]))
        found = jnp.where(slots_down == slot_ref[block : block + 1, :], found, 0.0)
        folded = found[0:8]
        for part in range(1, LANES // 8):
            folded = folded + found[8 * part : 8 * part + 8]
        folded = folded + pltpu.roll(folded, 4, 0)
        at_row = rows_down == row_ref[block : block + 1, :]
        for turn in range(3):
            back = folded[2 - turn : 3 - turn, :]
            for part in range(2):
                for third, piece in enumerate(pieces(weight_ref[part : part + 1, lanes] * back)):
                    base = third * stack_rows + (2 * turn + part) * cells_row
                    spread_ref[base : base + cells_row, lanes] = jnp.where(at_row, piece, 0.0).astype(BF16)
    load = sum_thirds(times_turned(spread_ref[...], cover_ref[...]))
    load_ref[...] = load
    spare = LANES - stack_rows
    edge_columns(jnp.concatenate([load, jnp.zeros((spare, LANES), F32)], axis=0), side_ref)
    side_ref[:, RIM : RIM + 1, :] = jnp.zeros((2, 1, LANES), F32)
    send_sides(side_ref, out_ref, [(dx, dy) for dx, dy in NEAR if dy])
    for move in (1, -1):
        there, inside = neighbour_x(move)

        @pl.when(inside)
        def _(there=there, move=move):
            for at, source, height in column_rows(cells_row // TILE_X, move):
                column_ref[there, at : at + height, :] = load_ref[source : source + height, :]


def adjoint_body(
    load_ref,
    column_ref,
    recv_ref,
    strain_ref,
    medium_ref,
    gradient_ref,
    load_planes_ref,
    planes_ref,
    turn_ref,
    tiles_ref,
):
    depth = medium_ref.shape[0] // 3
    turn_ref[...] = jnp.zeros_like(turn_ref)
    rims = [rim_rows(recv_ref, dx, 1, turn_ref) for dx in (0, 1, -1)]
    tiles_ref[...] = jnp.zeros_like(tiles_ref)
    for side, move in enumerate((1, -1)):
        there, inside = neighbour_x(move)

        @pl.when(inside)
        def _(there=there, side=side, move=move):
            for at, target, height in column_rows(depth, -move):
                tiles_ref[side, target : target + height, :] = column_ref[there, at : at + height, :]

    lay_planes(load_planes_ref, 0, load_ref, tiles_ref[0], tiles_ref[1])
    lay_planes(load_planes_ref, LANES, *rims)
    planes_ref[...] = jnp.zeros_like(planes_ref)
    gradient_ref[...] = jnp.zeros_like(gradient_ref)
    for turn in range(3):
        for part in range(2):
            for z in range(depth):
                at = (3 + part) * depth + z
                planes_ref[at] = planes_ref[at] + load_planes_ref[(2 * turn + part) * depth + z]

        def emit(z, strains, turn=turn):
            forward = []
            for number in range(6):
                base = (((2 - turn) * 6 + number) * depth + z) * TILE_X
                forward.append(strain_ref[base : base + TILE_X, :])
            back = [strain[0:TILE_X, 0:LANES] for strain in strains]
            dilation = (forward[0] + forward[1] + forward[2]) * (back[0] + back[1] + back[2])
            product = [forward[number] * back[number] for number in range(6)]
            shear = 2.0 * (product[0] + product[1] + product[2]) + product[3] + product[4] + product[5]
            for part, term in enumerate((dilation, shear)):
                base = (part * depth + z) * TILE_X
                gradient_ref[base : base + TILE_X, :] = gradient_ref[base : base + TILE_X, :] + term

        advance(planes_ref, medium_ref, 0, depth, emit, turn == 2)


def shards(
    initial_state,
    lame_lambda,
    shear_modulus,
    buoyancy,
    source_cells,
    source_wavelet,
    segment_start,
    segment_weight,
    partial_owner,
    partial_channel,
    observed_data,
):
    depth, rows_x, cols_y = lame_lambda.shape
    part_count = segment_start.shape[0]
    count_x, count_y = lax.axis_size("gx"), lax.axis_size("gy")
    devices = count_x * count_y
    capacity = max(2, 2 * part_count // devices)
    slot_groups = devices * capacity // LANES
    blocks = part_count // LANES
    per_group = LANES // capacity
    cells_row = depth * rows_x
    both = ("gx", "gy")
    up = [(i, i + 1) for i in range(count_x - 1)]
    down = [(j, i) for i, j in up]
    shape = jax.ShapeDtypeStruct

    def exchange(chunks):
        return lax.all_to_all(chunks, both, split_axis=0, concat_axis=0, tiled=True)

    def to_owners(rows):
        chunks = rows.reshape(slot_groups, 4, per_group, capacity).transpose(0, 2, 1, 3)
        back = exchange(chunks.reshape(devices, 4, capacity)).reshape(slot_groups, per_group, 4, capacity)
        return back.transpose(0, 2, 1, 3).reshape(slot_groups * 4, LANES)

    fields, edges = call_kernel(
        pack_body,
        "pack_edges",
        [shape((12 * cells_row, cols_y), F32), shape((devices, 8, LANES), F32)],
        [pltpu.VMEM((2, 8, LANES), F32)],
        *[values.reshape(-1, cols_y) for values in (initial_state, lame_lambda, shear_modulus, buoyancy)],
        source_cells.reshape(1, -1),
        source_wavelet,
    )
    lower = lax.ppermute(fields, "gx", up)
    higher = lax.ppermute(fields, "gx", down)
    rims = exchange(edges)
    channels = partial_channel.reshape(blocks, LANES)
    slot, row, cover, place = call_kernel(
        functools.partial(slots_body, capacity, devices, cols_y),
        "segment_slots",
        [
            shape((blocks, LANES), I32),
            shape((blocks, LANES), I32),
            shape((cols_y, part_count), BF16),
            shape((LANES, part_count), BF16),
        ],
        [pltpu.VMEM((blocks, LANES), F32)],
        partial_owner.reshape(blocks, LANES),
        segment_start.reshape(blocks, LANES),
    )
    partials, strains, medium = call_kernel(
        functools.partial(forward_body, cols_y),
        "forward_run",
        [
            shape((slot_groups * 4, LANES), F32),
            shape((18 * cells_row, cols_y), F32),
            shape((3 * depth, SPAN_X, SPAN_Y), F32),
        ],
        [
            pltpu.VMEM((12 * depth, SPAN_X, SPAN_Y), F32),
            pltpu.VMEM((LANES, 2 * LANES), F32),
            pltpu.VMEM((9 * depth * SPAN_X, 5 * LANES), BF16),
            pltpu.VMEM((SPAN_Y, 5 * LANES), BF16),
            pltpu.VMEM((3 * depth * SPAN_X, SPAN_Y), F32),
            pltpu.VMEM((3 * LANES, part_count), BF16),
        ],
        fields,
        higher,
        lower,
        rims,
        slot,
        row,
        segment_weight,
        channels,
        cover,
        place,
    )
    parts = observed_data.shape[1] // LANES
    residuals, reply = call_kernel(
        owner_body,
        "channel_sums",
        [shape(observed_data.shape, F32), shape((slot_groups * 4, LANES), F32)],
        [
            pltpu.VMEM((12 * parts, slot_groups * LANES), BF16),
            pltpu.VMEM((LANES, slot_groups * LANES), BF16),
            pltpu.VMEM((4 * parts, LANES), F32),
        ],
        to_owners(partials),
        observed_data,
    )
    loads, load_edges, load_rows = call_kernel(
        load_body,
        "segment_loads",
        [
            shape((6 * cells_row, cols_y), F32),
            shape((devices, 4, LANES), F32),
            shape((count_x, 4 * cells_row, cols_y), F32),
        ],
        [pltpu.VMEM((18 * cells_row, part_count), BF16), pltpu.VMEM((2, 4, LANES), F32)],
        to_owners(reply),
        slot,
        row,
        segment_weight,
        cover,
        place,
    )
    load_rims = exchange(load_edges)
    load_column = lax.all_to_all(load_rows, "gx", split_axis=0, concat_axis=0, tiled=True)
    (gradients,) = call_kernel(
        adjoint_body,
        "adjoint_run",
        [shape((2 * cells_row, cols_y), F32)],
        [
            pltpu.VMEM((6 * depth, SPAN_X, SPAN_Y), F32),
            pltpu.VMEM((9 * depth, SPAN_X, SPAN_Y), F32),
            pltpu.VMEM((LANES, LANES), F32),
            pltpu.VMEM((2, 6 * cells_row, cols_y), F32),
        ],
        loads,
        load_column,
        load_rims,
        strains,
        medium,
    )
    return (residuals, gradients.reshape(2, depth, rows_x, cols_y))


def solution(mesh):
    in_specs = (
        P(None, None, "gx", "gy"),
        P(None, "gx", "gy"),
        P(None, "gx", "gy"),
        P(None, "gx", "gy"),
        P(("gx", "gy")),
        P(None, ("gx", "gy")),
        P(("gx", "gy")),
        P(None, ("gx", "gy")),
        P(("gx", "gy"), None),
        P(("gx", "gy")),
        P(None, ("gx", "gy")),
    )
    out_specs = (P(None, ("gx", "gy")), P(None, None, "gx", "gy"))
    return jax.shard_map(shards, mesh=mesh, in_specs=in_specs, out_specs=out_specs, check_vma=False)
```

```python
import functools

import jax
import jax.numpy as jnp
from jax import lax
from jax.experimental import pallas as pl
from jax.experimental.pallas import tpu as pltpu
from jax.sharding import PartitionSpec as P

GAUGE = 8
STEP = 0.25
RIM = 3
LANES = 128
TILE_X = 4
SPAN_X = 16
SPAN_Y = 256
F32, BF16, I32 = jnp.float32, jnp.bfloat16, jnp.int32
NEAR = tuple((dx, dy) for dx in (-1, 0, 1) for dy in (-1, 0, 1))


def call_kernel(body, name, outs, scratch, *args, place=pltpu.VMEM):
    whole = pl.BlockSpec(memory_space=pltpu.VMEM)
    return pl.pallas_call(
        body,
        name=name,
        out_shape=outs,
        in_specs=[pl.BlockSpec(memory_space=place)] * len(args),
        out_specs=[whole] * len(outs),
        scratch_shapes=scratch,
        compiler_params=pltpu.CompilerParams(vmem_limit_bytes=24 * 1024 * 1024),
    )(*args)


def pieces(values):
    high = values.astype(BF16).astype(F32)
    rest = values - high
    middle = rest.astype(BF16).astype(F32)
    return high, middle, rest - middle


def iota(shape, dim):
    return lax.broadcasted_iota(I32, shape, dim)


def times(left, right):
    return lax.dot_general(left, right, (((1,), (0,)), ((), ())), preferred_element_type=F32)


def times_turned(left, right):
    return lax.dot_general(left, right, (((1,), (1,)), ((), ())), preferred_element_type=F32)


def two_pieces(values):
    high = values.astype(BF16).astype(F32)
    return high, values - high


def sum_halves(values):
    half = values.shape[0] // 2
    return values[:half] + values[half:]


def sum_thirds(values):
    third = values.shape[0] // 3
    return values[:third] + values[third : 2 * third] + values[2 * third :]


def neighbour(dx, dy):
    count_x, count_y = lax.axis_size("gx"), lax.axis_size("gy")
    at_x, at_y = lax.axis_index("gx") + dx, lax.axis_index("gy") + dy
    inside = (at_x >= 0) & (at_x < count_x) & (at_y >= 0) & (at_y < count_y)
    return jnp.where(inside, at_x * count_y + at_y, 0), inside


def edge_columns(rows, side_ref):
    width = rows.shape[0]
    turned = rows.T
    for side, base in ((0, 0), (1, LANES - RIM)):
        for column in range(RIM):
            side_ref[side, 0:1, column * width : (column + 1) * width] = turned[base + column : base + column + 1, :]


def send_sides(side_ref, out_ref, places):
    for dx, dy in places:
        index, inside = neighbour(dx, dy)

        @pl.when(inside)
        def _(index=index, dy=dy):
            out_ref[index] = side_ref[1 if dy > 0 else 0]


def arrived_chunk(recv_ref, dx, dy):
    index, inside = neighbour(dx, dy)
    return jnp.where(inside, recv_ref[index], 0.0)


def rim_rows(recv_ref, dx, turn_ref):
    width = turn_ref.shape[1]
    for dy, base in ((1, 0), (-1, LANES - RIM)):
        chunk = arrived_chunk(recv_ref, dx, dy)
        for column in range(RIM):
            turn_ref[base + column : base + column + 1, :] = chunk[:, column * width : (column + 1) * width]
    return turn_ref[...].T


def lay_planes(planes_ref, lane, centre, higher, lower):
    upper_half = iota((8, LANES), 0) < TILE_X
    for pair in range(planes_ref.shape[0] // 2):
        rows = slice(8 * pair, 8 * pair + 8)
        mid, high, low = centre[rows], higher[rows], lower[rows]
        lanes = slice(lane, lane + LANES)
        planes_ref[2 * pair, 0:8, lanes] = jnp.where(upper_half, mid, pltpu.roll(high, 4, 0))
        planes_ref[2 * pair + 1, 0:8, lanes] = jnp.where(upper_half, pltpu.roll(mid, 4, 0), high)
        planes_ref[2 * pair, 8:16, lanes] = jnp.where(upper_half, 0.0, pltpu.roll(low, 4, 0))
        planes_ref[2 * pair + 1, 8:16, lanes] = jnp.where(upper_half, 0.0, low)


def ahead_x(plane):
    return pltpu.roll(plane, SPAN_X - 1, 0) - plane


def behind_x(plane):
    return plane - pltpu.roll(plane, 1, 0)


def ahead_y(plane):
    return pltpu.roll(plane, SPAN_Y - 1, 1) - plane


def behind_y(plane):
    return plane - pltpu.roll(plane, 1, 1)


def advance(field_ref, medium_ref, first, depth, emit, last):
    def field(number, z):
        return field_ref[number * depth + z]

    def ahead_z(number, z):
        here = field(number, z)
        return field(number, z + 1) - here if z + 1 < depth else -here

    def behind_z(number, z):
        here = field(number, z)
        return here - field(number, z - 1) if z else here

    for z in range(depth):
        scale = STEP * medium_ref[first + 2 * depth + z]
        accel = (
            ahead_x(field(3, z)) + behind_y(field(6, z)) + behind_z(7, z),
            behind_x(field(6, z)) + ahead_y(field(4, z)) + behind_z(8, z),
            behind_x(field(7, z)) + behind_y(field(8, z)) + ahead_z(5, z),
        )
        for number in range(3):
            field_ref[number * depth + z] = field(number, z) + scale * accel[number]
    for z in range(depth):
        along_x, along_y, along_z = field(0, z), field(1, z), field(2, z)
        strains = (
            behind_x(along_x),
            behind_y(along_y),
            behind_z(2, z),
            ahead_y(along_x) + ahead_x(along_y),
            ahead_z(0, z) + ahead_x(along_z),
            ahead_z(1, z) + ahead_y(along_z),
        )
        emit(z, strains)
        if not last:
            shear = medium_ref[first + depth + z]
            dilated = medium_ref[first + z] * (strains[0] + strains[1] + strains[2])
            for number in range(3):
                field_ref[(3 + number) * depth + z] = field(3 + number, z) + STEP * (
                    dilated + 2.0 * shear * strains[number]
                )
                field_ref[(6 + number) * depth + z] = (
                    field(6 + number, z) + STEP * shear * strains[3 + number]
                )


def pack_body(*refs):
    inputs, (fields_ref, out_ref, side_ref, cells_ref, wavelet_ref, arrived) = refs[:6], refs[6:]
    targets, at = [], 0
    for source in inputs[:4]:
        targets.append(fields_ref.at[at : at + source.shape[0]])
        at = at + source.shape[0]
    copies = [
        pltpu.make_async_copy(source, target, arrived.at[number])
        for number, (source, target) in enumerate(zip(inputs, targets + [cells_ref, wavelet_ref]))
    ]
    for copy in copies:
        copy.start()
    for copy in copies:
        copy.wait()
    rows = fields_ref[...]
    spare = 2 * LANES - rows.shape[0]
    edge_columns(jnp.concatenate([rows, jnp.zeros((spare, LANES), F32)], axis=0), side_ref)
    count = cells_ref.shape[1]
    first = RIM * 2 * LANES
    for side in range(2):
        side_ref[side, 0:1, first : first + count] = cells_ref[...].astype(F32)
        for step in range(3):
            at = first + (step + 1) * count
            side_ref[side, 0:1, at : at + count] = wavelet_ref[step : step + 1, :]
    send_sides(side_ref, out_ref, NEAR)


def slots_body(capacity, devices, cols_y, owner_ref, start_ref, slot_ref, row_ref, cover_ref, place_ref, rank_ref):
    blocks = owner_ref.shape[0]
    group = 32
    before = jnp.where(iota((LANES, 2 * LANES), 0) < iota((LANES, 2 * LANES), 1), 1.0, 0.0).astype(BF16)
    rank_ref[...] = jnp.zeros_like(rank_ref)

    def count_group(number, carry):
        names = iota((group, LANES), 0) + number * group
        hot = [names == owner_ref[b : b + 1, :] for b in range(blocks)]
        marks = jnp.concatenate([jnp.where(h, 1.0, 0.0) for h in hot], axis=0).astype(BF16)
        counts = times(marks, before)
        total = jnp.zeros((group, LANES), F32)
        for b in range(blocks):
            part = counts[b * group : (b + 1) * group]
            rank_ref[b : b + 1, :] = rank_ref[b : b + 1, :] + jnp.sum(
                jnp.where(hot[b], part[:, :LANES] + total, 0.0), axis=0, keepdims=True
            )
            total = total + part[:, LANES:]
        return carry

    if devices == group:
        count_group(0, 0)
    else:
        lax.fori_loop(0, devices // group, count_group, 0)
    slot = owner_ref[...] * capacity + rank_ref[...].astype(I32)
    slot_ref[...] = slot >> 7
    low = slot & (LANES - 1)
    span = cols_y - GAUGE + 1
    start = start_ref[...]
    row = ((start.astype(F32) + 0.5) * (1.0 / span)).astype(I32)
    row_ref[...] = row
    first = start - row * span
    down = iota((LANES, LANES), 0)
    for b in range(blocks):
        lanes = slice(b * LANES, (b + 1) * LANES)
        offset = down - first[b : b + 1, :]
        cover_ref[:, lanes] = jnp.where((offset >= 0) & (offset < GAUGE), 1.0, 0.0).astype(BF16)
        place_ref[:, lanes] = jnp.where(down == low[b : b + 1, :], 1.0, 0.0).astype(BF16)


def source_maps(recv_ref, cols_y, depth, left_ref, right_ref):
    count = LANES // 2
    first_half = iota((1, LANES), 1) < count
    rows_per_step = depth * SPAN_X
    down_rows = iota((rows_per_step, LANES), 0)
    down_lanes = iota((SPAN_Y, LANES), 0)
    halves = []
    for dx, dy in NEAR:
        chunk = arrived_chunk(recv_ref, dx, dy)
        one, two = chunk[:, 6 * LANES : 7 * LANES], chunk[:, 7 * LANES :]
        cells = one.astype(I32)
        y = cells & (cols_y - 1)
        rest = cells >> (cols_y.bit_length() - 1)
        x = rest & (TILE_X - 1)
        z = rest >> (TILE_X.bit_length() - 1)
        row = z * SPAN_X + x + (TILE_X if dx > 0 else SPAN_X - TILE_X if dx < 0 else 0)
        if dy > 0:
            lane = jnp.where(y < RIM, y + LANES, -1)
        elif dy < 0:
            lane = jnp.where(y >= cols_y - RIM, y + LANES, -1)
        else:
            lane = y
        halves.append((row, lane, one, two))
    zero_row = jnp.zeros((1, LANES), F32)
    halves.append((jnp.zeros((1, LANES), I32), jnp.full((1, LANES), -1, I32), zero_row, zero_row))
    for block in range(len(halves) // 2):
        (row_a, lane_a, one_a, two_a), (row_b, lane_b, one_b, two_b) = halves[2 * block : 2 * block + 2]
        row = jnp.where(first_half, row_a, pltpu.roll(row_b, count, 1))
        lane = jnp.where(first_half, lane_a, pltpu.roll(lane_b, count, 1))
        steps = (
            jnp.where(first_half, pltpu.roll(one_a, count, 1), one_b),
            jnp.where(first_half, two_a, pltpu.roll(two_b, count, 1)),
            jnp.where(first_half, pltpu.roll(two_a, count, 1), two_b),
        )
        lanes = slice(block * LANES, (block + 1) * LANES)
        right_ref[:, lanes] = jnp.where(down_lanes == lane, 1.0, 0.0).astype(BF16)
        at_row = down_rows == row
        for step, amplitude in enumerate(steps):
            for third, piece in enumerate(pieces(amplitude)):
                base = (third * 3 + step) * rows_per_step
                left_ref[base : base + rows_per_step, lanes] = jnp.where(at_row, piece, 0.0).astype(BF16)
    return sum_thirds(times_turned(left_ref[...], right_ref[...]))


def forward_body(
    cols_y,
    fields_ref,
    higher_ref,
    lower_ref,
    recv_ref,
    slot_ref,
    row_ref,
    weight_ref,
    channel_ref,
    cover_ref,
    place_ref,
    out_ref,
    strain_ref,
    medium_ref,
    planes_ref,
    turn_ref,
    source_left_ref,
    source_right_ref,
    source_ref,
    spread_ref,
):
    depth = medium_ref.shape[0] // 3
    cells_row = depth * TILE_X
    turn_ref[...] = jnp.zeros_like(turn_ref)
    rims = [rim_rows(recv_ref, dx, turn_ref) for dx in (0, 1, -1)]
    lay_planes(planes_ref, 0, fields_ref, higher_ref, lower_ref)
    lay_planes(planes_ref, LANES, *rims)
    first = 9 * depth
    medium_ref[...] = planes_ref[first:]
    source_ref[...] = source_maps(recv_ref, cols_y, depth, source_left_ref, source_right_ref)
    for step in range(3):
        for z in range(depth):
            base = step * depth * SPAN_X + z * SPAN_X
            load = source_ref[base : base + SPAN_X, :]
            for number in range(3, 6):
                planes_ref[number * depth + z] = planes_ref[number * depth + z] + load

        def emit(z, strains, step=step):
            for number, strain in enumerate(strains):
                base = ((step * 6 + number) * depth + z) * TILE_X
                strain_ref[base : base + TILE_X, :] = strain[0:TILE_X, 0:LANES]

        advance(planes_ref, planes_ref, first, depth, emit, step == 2)
    axial = jnp.concatenate(
        [strain_ref[step * 6 * cells_row : (step * 6 + 2) * cells_row, :] for step in range(3)], axis=0
    )
    axial = jnp.concatenate(pieces(axial), axis=0).astype(BF16)
    rows_down = iota((cells_row, LANES), 0)
    slots_down = iota((LANES, LANES), 0) >> 2
    for block in range(slot_ref.shape[0]):
        lanes = slice(block * LANES, (block + 1) * LANES)
        windows = sum_thirds(times(axial, cover_ref[:, lanes]))
        at_row = rows_down == row_ref[block : block + 1, :]
        weight_x, weight_y = weight_ref[0:1, lanes], weight_ref[1:2, lanes]
        sums = []
        for step in range(3):
            base = 2 * step * cells_row
            both = (
                weight_x * windows[base : base + cells_row]
                + weight_y * windows[base + cells_row : base + 2 * cells_row]
            )
            sums.append(jnp.sum(jnp.where(at_row, both, 0.0), axis=0, keepdims=True))
        sums.append(channel_ref[block : block + 1, :].astype(F32))
        values = jnp.concatenate(sums + sums, axis=0)
        in_slot = slots_down == slot_ref[block : block + 1, :]
        for third, piece in enumerate(pieces(values)):
            spread_ref[third * LANES : (third + 1) * LANES, lanes] = jnp.where(
                in_slot, jnp.concatenate([piece] * (LANES // 8), axis=0), 0.0
            ).astype(BF16)
    out_ref[...] = sum_thirds(times_turned(spread_ref[...], place_ref[...]))


def owner_body(arrived_ref, observed_ref, residual_ref, reply_ref, values_ref, place_ref, held_ref):
    groups = arrived_ref.shape[0] // 4
    parts = observed_ref.shape[1] // LANES
    down = iota((LANES, LANES), 0)
    part_down = iota((parts, LANES), 0)
    nothing = jnp.zeros((parts, LANES), F32)
    numbers = [arrived_ref[4 * s + 3 : 4 * s + 4, :].astype(I32) for s in range(groups)]
    for s in range(groups):
        lanes = slice(s * LANES, (s + 1) * LANES)
        place_ref[:, lanes] = jnp.where(down == (numbers[s] & (LANES - 1)), 1.0, 0.0).astype(BF16)
        at_part = part_down == (numbers[s] >> 7)
        thirds = pieces(arrived_ref[4 * s : 4 * s + 3, :])
        stack = []
        for third in thirds:
            for step in range(3):
                stack.append(jnp.where(at_part, third[step : step + 1, :], 0.0))
            stack.append(nothing)
        values_ref[:, lanes] = jnp.concatenate(stack, axis=0).astype(BF16)
    sums = sum_thirds(times_turned(values_ref[...], place_ref[...]))
    for step in range(3):
        for part in range(parts):
            at = step * parts + part
            held_ref[at : at + 1, :] = observed_ref[step : step + 1, part * LANES : (part + 1) * LANES]
    held_ref[3 * parts :, :] = nothing
    held_ref[...] = sums - held_ref[...]
    for step in range(3):
        for part in range(parts):
            at = step * parts + part
            residual_ref[step : step + 1, part * LANES : (part + 1) * LANES] = held_ref[at : at + 1, :]
    residual = jnp.concatenate(two_pieces(held_ref[...]), axis=0).astype(BF16)
    for s in range(groups):
        lanes = slice(s * LANES, (s + 1) * LANES)
        found = sum_halves(times(residual, place_ref[:, lanes]))
        at_part = part_down == (numbers[s] >> 7)
        for step in range(3):
            reply_ref[s, 0:1, step * LANES : (step + 1) * LANES] = jnp.sum(
                jnp.where(at_part, found[step * parts : (step + 1) * parts], 0.0), axis=0, keepdims=True
            )


def load_body(
    arrived_ref,
    slot_ref,
    row_ref,
    weight_ref,
    cover_ref,
    place_ref,
    load_ref,
    out_ref,
    spread_ref,
    side_ref,
    rows_ref,
):
    cells_row = load_ref.shape[0] // 6
    stack_rows = load_ref.shape[0]
    groups = arrived_ref.shape[0]
    for step in range(3):
        for s in range(groups):
            at = step * groups + s
            rows_ref[at : at + 1, :] = arrived_ref[s, 0:1, step * LANES : (step + 1) * LANES]
    arrived = jnp.concatenate(two_pieces(rows_ref[...]), axis=0).astype(BF16)
    slots_down = iota((groups, LANES), 0)
    rows_down = iota((cells_row, LANES), 0)
    for block in range(slot_ref.shape[0]):
        lanes = slice(block * LANES, (block + 1) * LANES)
        found = sum_halves(times(arrived, place_ref[:, lanes]))
        in_slot = slots_down == slot_ref[block : block + 1, :]
        at_row = rows_down == row_ref[block : block + 1, :]
        for turn in range(3):
            base = (2 - turn) * groups
            back = jnp.sum(jnp.where(in_slot, found[base : base + groups], 0.0), axis=0, keepdims=True)
            for part in range(2):
                for half, piece in enumerate(two_pieces(weight_ref[part : part + 1, lanes] * back)):
                    base = half * stack_rows + (2 * turn + part) * cells_row
                    spread_ref[base : base + cells_row, lanes] = jnp.where(at_row, piece, 0.0).astype(BF16)
    load = sum_halves(times_turned(spread_ref[...], cover_ref[...]))
    load_ref[...] = load
    spare = LANES - stack_rows
    edge_columns(jnp.concatenate([load, jnp.zeros((spare, LANES), F32)], axis=0), side_ref)
    send_sides(side_ref, out_ref, [(dx, dy) for dx, dy in NEAR if dy])


def adjoint_body(
    load_ref, higher_ref, lower_ref, recv_ref, strain_ref, medium_ref, gradient_ref, load_planes_ref, planes_ref, turn_ref
):
    depth = medium_ref.shape[0] // 3
    turn_ref[...] = jnp.zeros_like(turn_ref)
    rims = [rim_rows(recv_ref, dx, turn_ref) for dx in (0, 1, -1)]
    lay_planes(load_planes_ref, 0, load_ref, higher_ref, lower_ref)
    lay_planes(load_planes_ref, LANES, *rims)
    planes_ref[...] = jnp.zeros_like(planes_ref)
    gradient_ref[...] = jnp.zeros_like(gradient_ref)
    for turn in range(3):
        for part in range(2):
            for z in range(depth):
                at = (3 + part) * depth + z
                planes_ref[at] = planes_ref[at] + load_planes_ref[(2 * turn + part) * depth + z]

        def emit(z, strains, turn=turn):
            forward = []
            for number in range(6):
                base = (((2 - turn) * 6 + number) * depth + z) * TILE_X
                forward.append(strain_ref[base : base + TILE_X, :])
            back = [strain[0:TILE_X, 0:LANES] for strain in strains]
            dilation = (forward[0] + forward[1] + forward[2]) * (back[0] + back[1] + back[2])
            product = [forward[number] * back[number] for number in range(6)]
            shear = 2.0 * (product[0] + product[1] + product[2]) + product[3] + product[4] + product[5]
            for part, term in enumerate((dilation, shear)):
                base = (part * depth + z) * TILE_X
                gradient_ref[base : base + TILE_X, :] = gradient_ref[base : base + TILE_X, :] + term

        advance(planes_ref, medium_ref, 0, depth, emit, turn == 2)


def shards(
    initial_state,
    lame_lambda,
    shear_modulus,
    buoyancy,
    source_cells,
    source_wavelet,
    segment_start,
    segment_weight,
    partial_owner,
    partial_channel,
    observed_data,
):
    depth, rows_x, cols_y = lame_lambda.shape
    part_count = segment_start.shape[0]
    count_x, count_y = lax.axis_size("gx"), lax.axis_size("gy")
    devices = count_x * count_y
    capacity = max(2, 2 * part_count // devices)
    slot_groups = devices * capacity // LANES
    blocks = part_count // LANES
    per_group = LANES // capacity
    cells_row = depth * rows_x
    both = ("gx", "gy")
    up = [(i, i + 1) for i in range(count_x - 1)]
    down = [(j, i) for i, j in up]
    shape = jax.ShapeDtypeStruct

    def exchange(chunks):
        return lax.all_to_all(chunks, both, split_axis=0, concat_axis=0, tiled=True)

    def route(rows, chunk):
        parts = rows.reshape(slot_groups, -1, per_group, capacity).transpose(0, 2, 1, 3)
        back = exchange(parts.reshape((devices,) + chunk)).reshape(slot_groups, per_group, -1, capacity)
        return back.transpose(0, 2, 1, 3).reshape(rows.shape)

    sources = source_cells.shape[0]
    fields, edges = call_kernel(
        pack_body,
        "pack_edges",
        [shape((12 * cells_row, cols_y), F32), shape((devices, 1, 8 * LANES), F32)],
        [
            pltpu.VMEM((2, 1, 8 * LANES), F32),
            pltpu.VMEM((1, sources), I32),
            pltpu.VMEM(source_wavelet.shape, F32),
            pltpu.SemaphoreType.DMA((6,)),
        ],
        *[values.reshape(-1, cols_y) for values in (initial_state, lame_lambda, shear_modulus, buoyancy)],
        source_cells.reshape(1, -1),
        source_wavelet,
        place=pl.ANY,
    )
    lower = lax.ppermute(fields, "gx", up)
    higher = lax.ppermute(fields, "gx", down)
    rims = exchange(edges)
    channels = partial_channel.reshape(blocks, LANES)
    slot, row, cover, place = call_kernel(
        functools.partial(slots_body, capacity, devices, cols_y),
        "segment_slots",
        [
            shape((blocks, LANES), I32),
            shape((blocks, LANES), I32),
            shape((cols_y, part_count), BF16),
            shape((LANES, part_count), BF16),
        ],
        [pltpu.VMEM((blocks, LANES), F32)],
        partial_owner.reshape(blocks, LANES),
        segment_start.reshape(blocks, LANES),
    )
    partials, strains, medium = call_kernel(
        functools.partial(forward_body, cols_y),
        "forward_run",
        [
            shape((slot_groups * 4, LANES), F32),
            shape((18 * cells_row, cols_y), F32),
            shape((3 * depth, SPAN_X, SPAN_Y), F32),
        ],
        [
            pltpu.VMEM((12 * depth, SPAN_X, SPAN_Y), F32),
            pltpu.VMEM((LANES, 2 * LANES), F32),
            pltpu.VMEM((9 * depth * SPAN_X, 5 * LANES), BF16),
            pltpu.VMEM((SPAN_Y, 5 * LANES), BF16),
            pltpu.VMEM((3 * depth * SPAN_X, SPAN_Y), F32),
            pltpu.VMEM((3 * LANES, part_count), BF16),
        ],
        fields,
        higher,
        lower,
        rims,
        slot,
        row,
        segment_weight,
        channels,
        cover,
        place,
    )
    parts = observed_data.shape[1] // LANES
    residuals, reply = call_kernel(
        owner_body,
        "channel_sums",
        [shape(observed_data.shape, F32), shape((slot_groups, 1, 3 * LANES), F32)],
        [
            pltpu.VMEM((12 * parts, slot_groups * LANES), BF16),
            pltpu.VMEM((LANES, slot_groups * LANES), BF16),
            pltpu.VMEM((4 * parts, LANES), F32),
        ],
        route(partials, (4, capacity)),
        observed_data,
    )
    loads, load_edges = call_kernel(
        load_body,
        "segment_loads",
        [shape((6 * cells_row, cols_y), F32), shape((devices, 1, RIM * LANES), F32)],
        [
            pltpu.VMEM((12 * cells_row, part_count), BF16),
            pltpu.VMEM((2, 1, RIM * LANES), F32),
            pltpu.VMEM((3 * slot_groups, LANES), F32),
        ],
        route(reply, (1, 3 * capacity)),
        slot,
        row,
        segment_weight,
        cover,
        place,
    )
    load_lower = lax.ppermute(loads, "gx", up)
    load_higher = lax.ppermute(loads, "gx", down)
    load_rims = exchange(load_edges)
    (gradients,) = call_kernel(
        adjoint_body,
        "adjoint_run",
        [shape((2 * cells_row, cols_y), F32)],
        [
            pltpu.VMEM((6 * depth, SPAN_X, SPAN_Y), F32),
            pltpu.VMEM((9 * depth, SPAN_X, SPAN_Y), F32),
            pltpu.VMEM((LANES, LANES), F32),
        ],
        loads,
        load_higher,
        load_lower,
        load_rims,
        strains,
        medium,
    )
    return (residuals, gradients.reshape(2, depth, rows_x, cols_y))


def solution(mesh):
    in_specs = (
        P(None, None, "gx", "gy"),
        P(None, "gx", "gy"),
        P(None, "gx", "gy"),
        P(None, "gx", "gy"),
        P(("gx", "gy")),
        P(None, ("gx", "gy")),
        P(("gx", "gy")),
        P(None, ("gx", "gy")),
        P(("gx", "gy"), None),
        P(("gx", "gy")),
        P(None, ("gx", "gy")),
    )
    out_specs = (P(None, ("gx", "gy")), P(None, None, "gx", "gy"))
    return jax.shard_map(shards, mesh=mesh, in_specs=in_specs, out_specs=out_specs, check_vma=False)
```

```python
import functools

import jax
import jax.numpy as jnp
from jax import lax
from jax.experimental import pallas as pl
from jax.experimental.pallas import tpu as pltpu
from jax.sharding import PartitionSpec as P

GAUGE = 8
STEP = 0.25
RIM = 3
LANES = 128
TILE_X = 4
SPAN_X = 16
SPAN_Y = 256
F32, BF16, I32 = jnp.float32, jnp.bfloat16, jnp.int32
NEAR = tuple((dx, dy) for dx in (-1, 0, 1) for dy in (-1, 0, 1))


def call_kernel(body, name, outs, scratch, *args, place=pltpu.VMEM, room=24 * 1024 * 1024):
    whole = pl.BlockSpec(memory_space=pltpu.VMEM)
    return pl.pallas_call(
        body,
        name=name,
        out_shape=outs,
        in_specs=[pl.BlockSpec(memory_space=place)] * len(args),
        out_specs=[whole] * len(outs),
        scratch_shapes=scratch,
        compiler_params=pltpu.CompilerParams(vmem_limit_bytes=room),
    )(*args)


def pieces(values):
    high = values.astype(BF16).astype(F32)
    rest = values - high
    middle = rest.astype(BF16).astype(F32)
    return high, middle, rest - middle


def iota(shape, dim):
    return lax.broadcasted_iota(I32, shape, dim)


def times(left, right):
    return lax.dot_general(left, right, (((1,), (0,)), ((), ())), preferred_element_type=F32)


def times_turned(left, right):
    return lax.dot_general(left, right, (((1,), (1,)), ((), ())), preferred_element_type=F32)


def two_pieces(values):
    high = values.astype(BF16).astype(F32)
    return high, values - high


def sum_halves(values):
    half = values.shape[0] // 2
    return values[:half] + values[half:]


def sum_thirds(values):
    third = values.shape[0] // 3
    return values[:third] + values[third : 2 * third] + values[2 * third :]


def neighbour(dx, dy):
    count_x, count_y = lax.axis_size("gx"), lax.axis_size("gy")
    at_x, at_y = lax.axis_index("gx") + dx, lax.axis_index("gy") + dy
    inside = (at_x >= 0) & (at_x < count_x) & (at_y >= 0) & (at_y < count_y)
    return jnp.where(inside, at_x * count_y + at_y, 0), inside


def edge_columns(rows, side_ref):
    width = rows.shape[0]
    turned = rows.T
    for side, base in ((0, 0), (1, LANES - RIM)):
        for column in range(RIM):
            side_ref[side, 0:1, column * width : (column + 1) * width] = turned[base + column : base + column + 1, :]


def send_sides(side_ref, out_ref, places):
    for dx, dy in places:
        index, inside = neighbour(dx, dy)

        @pl.when(inside)
        def _(index=index, dy=dy):
            out_ref[index] = side_ref[1 if dy > 0 else 0]


def arrived_chunk(recv_ref, dx, dy):
    index, inside = neighbour(dx, dy)
    return jnp.where(inside, recv_ref[index], 0.0)


def rim_rows(recv_ref, dx, turn_ref):
    width = turn_ref.shape[1]
    for dy, base in ((1, 0), (-1, LANES - RIM)):
        chunk = arrived_chunk(recv_ref, dx, dy)
        for column in range(RIM):
            turn_ref[base + column : base + column + 1, :] = chunk[:, column * width : (column + 1) * width]
    return turn_ref[...].T


def lay_planes(planes_ref, lane, centre, higher, lower):
    upper_half = iota((8, LANES), 0) < TILE_X
    for pair in range(planes_ref.shape[0] // 2):
        rows = slice(8 * pair, 8 * pair + 8)
        mid, high, low = centre[rows], higher[rows], lower[rows]
        lanes = slice(lane, lane + LANES)
        planes_ref[2 * pair, 0:8, lanes] = jnp.where(upper_half, mid, pltpu.roll(high, 4, 0))
        planes_ref[2 * pair + 1, 0:8, lanes] = jnp.where(upper_half, pltpu.roll(mid, 4, 0), high)
        planes_ref[2 * pair, 8:16, lanes] = jnp.where(upper_half, 0.0, pltpu.roll(low, 4, 0))
        planes_ref[2 * pair + 1, 8:16, lanes] = jnp.where(upper_half, 0.0, low)


def ahead_x(plane):
    return pltpu.roll(plane, SPAN_X - 1, 0) - plane


def behind_x(plane):
    return plane - pltpu.roll(plane, 1, 0)


def ahead_y(plane):
    return pltpu.roll(plane, SPAN_Y - 1, 1) - plane


def behind_y(plane):
    return plane - pltpu.roll(plane, 1, 1)


def scaled_medium(medium_ref, first, depth, z):
    shear = STEP * medium_ref[first + depth + z]
    return STEP * medium_ref[first + 2 * depth + z], STEP * medium_ref[first + z], shear, 2.0 * shear


def advance(field_ref, medium, depth, emit, last):
    def field(number, z):
        return field_ref[number * depth + z]

    def ahead_z(number, z):
        here = field(number, z)
        return field(number, z + 1) - here if z + 1 < depth else -here

    def behind_z(number, z):
        here = field(number, z)
        return here - field(number, z - 1) if z else here

    for z in range(depth):
        scale = medium(z)[0]
        accel = (
            ahead_x(field(3, z)) + behind_y(field(6, z)) + behind_z(7, z),
            behind_x(field(6, z)) + ahead_y(field(4, z)) + behind_z(8, z),
            behind_x(field(7, z)) + behind_y(field(8, z)) + ahead_z(5, z),
        )
        for number in range(3):
            field_ref[number * depth + z] = field(number, z) + scale * accel[number]
    for z in range(depth):
        along_x, along_y, along_z = field(0, z), field(1, z), field(2, z)
        strains = (
            behind_x(along_x),
            behind_y(along_y),
            behind_z(2, z),
            ahead_y(along_x) + ahead_x(along_y),
            ahead_z(0, z) + ahead_x(along_z),
            ahead_z(1, z) + ahead_y(along_z),
        )
        emit(z, strains)
        if not last:
            _, dilate, shear, twice = medium(z)
            dilated = dilate * (strains[0] + strains[1] + strains[2])
            for number in range(3):
                field_ref[(3 + number) * depth + z] = field(3 + number, z) + (dilated + twice * strains[number])
                field_ref[(6 + number) * depth + z] = field(6 + number, z) + shear * strains[3 + number]


def pack_body(*refs):
    inputs, (fields_ref, out_ref, side_ref, cells_ref, wavelet_ref, arrived) = refs[:6], refs[6:]
    targets, at = [], 0
    for source in inputs[:4]:
        targets.append(fields_ref.at[at : at + source.shape[0]])
        at = at + source.shape[0]
    copies = [
        pltpu.make_async_copy(source, target, arrived.at[number])
        for number, (source, target) in enumerate(zip(inputs, targets + [cells_ref, wavelet_ref]))
    ]
    for copy in copies:
        copy.start()
    for copy in copies:
        copy.wait()
    rows = fields_ref[...]
    spare = 2 * LANES - rows.shape[0]
    edge_columns(jnp.concatenate([rows, jnp.zeros((spare, LANES), F32)], axis=0), side_ref)
    count = cells_ref.shape[1]
    first = RIM * 2 * LANES
    for side in range(2):
        side_ref[side, 0:1, first : first + count] = cells_ref[...].astype(F32)
        for step in range(3):
            at = first + (step + 1) * count
            side_ref[side, 0:1, at : at + count] = wavelet_ref[step : step + 1, :]
    send_sides(side_ref, out_ref, NEAR)


def slots_body(capacity, devices, cols_y, owner_ref, start_ref, slot_ref, row_ref, cover_ref, place_ref, rank_ref):
    blocks = owner_ref.shape[0]
    group = 32
    before = jnp.where(iota((LANES, 2 * LANES), 0) < iota((LANES, 2 * LANES), 1), 1.0, 0.0).astype(BF16)
    rank_ref[...] = jnp.zeros_like(rank_ref)

    def count_group(number, carry):
        names = iota((group, LANES), 0) + number * group
        hot = [names == owner_ref[b : b + 1, :] for b in range(blocks)]
        marks = jnp.concatenate([jnp.where(h, 1.0, 0.0) for h in hot], axis=0).astype(BF16)
        counts = times(marks, before)
        total = jnp.zeros((group, LANES), F32)
        for b in range(blocks):
            part = counts[b * group : (b + 1) * group]
            rank_ref[b : b + 1, :] = rank_ref[b : b + 1, :] + jnp.sum(
                jnp.where(hot[b], part[:, :LANES] + total, 0.0), axis=0, keepdims=True
            )
            total = total + part[:, LANES:]
        return carry

    if devices == group:
        count_group(0, 0)
    else:
        lax.fori_loop(0, devices // group, count_group, 0)
    slot = owner_ref[...] * capacity + rank_ref[...].astype(I32)
    slot_ref[...] = slot >> 7
    low = slot & (LANES - 1)
    span = cols_y - GAUGE + 1
    start = start_ref[...]
    row = ((start.astype(F32) + 0.5) * (1.0 / span)).astype(I32)
    row_ref[...] = row
    first = start - row * span
    down = iota((LANES, LANES), 0)
    for b in range(blocks):
        lanes = slice(b * LANES, (b + 1) * LANES)
        offset = down - first[b : b + 1, :]
        cover_ref[:, lanes] = jnp.where((offset >= 0) & (offset < GAUGE), 1.0, 0.0).astype(BF16)
        place_ref[:, lanes] = jnp.where(down == low[b : b + 1, :], 1.0, 0.0).astype(BF16)


def source_maps(recv_ref, cols_y, depth, left_ref, right_ref):
    count = LANES // 2
    first_half = iota((1, LANES), 1) < count
    rows_per_step = depth * SPAN_X
    down_rows = iota((rows_per_step, LANES), 0)
    down_lanes = iota((SPAN_Y, LANES), 0)
    halves = []
    for dx, dy in NEAR:
        chunk = arrived_chunk(recv_ref, dx, dy)
        one, two = chunk[:, 6 * LANES : 7 * LANES], chunk[:, 7 * LANES :]
        cells = one.astype(I32)
        y = cells & (cols_y - 1)
        rest = cells >> (cols_y.bit_length() - 1)
        x = rest & (TILE_X - 1)
        z = rest >> (TILE_X.bit_length() - 1)
        row = z * SPAN_X + x + (TILE_X if dx > 0 else SPAN_X - TILE_X if dx < 0 else 0)
        if dy > 0:
            lane = jnp.where(y < RIM, y + LANES, -1)
        elif dy < 0:
            lane = jnp.where(y >= cols_y - RIM, y + LANES, -1)
        else:
            lane = y
        halves.append((row, lane, one, two))
    zero_row = jnp.zeros((1, LANES), F32)
    halves.append((jnp.zeros((1, LANES), I32), jnp.full((1, LANES), -1, I32), zero_row, zero_row))
    for block in range(len(halves) // 2):
        (row_a, lane_a, one_a, two_a), (row_b, lane_b, one_b, two_b) = halves[2 * block : 2 * block + 2]
        row = jnp.where(first_half, row_a, pltpu.roll(row_b, count, 1))
        lane = jnp.where(first_half, lane_a, pltpu.roll(lane_b, count, 1))
        steps = (
            jnp.where(first_half, pltpu.roll(one_a, count, 1), one_b),
            jnp.where(first_half, two_a, pltpu.roll(two_b, count, 1)),
            jnp.where(first_half, pltpu.roll(two_a, count, 1), two_b),
        )
        lanes = slice(block * LANES, (block + 1) * LANES)
        right_ref[:, lanes] = jnp.where(down_lanes == lane, 1.0, 0.0).astype(BF16)
        at_row = down_rows == row
        for step, amplitude in enumerate(steps):
            for third, piece in enumerate(pieces(amplitude)):
                base = (third * 3 + step) * rows_per_step
                left_ref[base : base + rows_per_step, lanes] = jnp.where(at_row, piece, 0.0).astype(BF16)
    return sum_thirds(times_turned(left_ref[...], right_ref[...]))


def forward_body(
    cols_y,
    fields_ref,
    higher_ref,
    lower_ref,
    recv_ref,
    slot_ref,
    row_ref,
    weight_ref,
    channel_ref,
    cover_ref,
    place_ref,
    out_ref,
    strain_ref,
    medium_ref,
    planes_ref,
    turn_ref,
    source_left_ref,
    source_right_ref,
    source_ref,
    spread_ref,
):
    depth = medium_ref.shape[0] // 3
    cells_row = depth * TILE_X
    turn_ref[...] = jnp.zeros_like(turn_ref)
    rims = [rim_rows(recv_ref, dx, turn_ref) for dx in (0, 1, -1)]
    lay_planes(planes_ref, 0, fields_ref, higher_ref, lower_ref)
    lay_planes(planes_ref, LANES, *rims)
    first = 9 * depth
    medium_ref[...] = planes_ref[first:]
    medium = functools.partial(scaled_medium, planes_ref, first, depth)
    source_ref[...] = source_maps(recv_ref, cols_y, depth, source_left_ref, source_right_ref)
    for step in range(3):
        for z in range(depth):
            base = step * depth * SPAN_X + z * SPAN_X
            load = source_ref[base : base + SPAN_X, :]
            for number in range(3, 6):
                planes_ref[number * depth + z] = planes_ref[number * depth + z] + load

        def emit(z, strains, step=step):
            for number, strain in enumerate(strains):
                base = ((step * 6 + number) * depth + z) * TILE_X
                strain_ref[base : base + TILE_X, :] = strain[0:TILE_X, 0:LANES]

        advance(planes_ref, medium, depth, emit, step == 2)
    axial = jnp.concatenate(
        [strain_ref[step * 6 * cells_row : (step * 6 + 2) * cells_row, :] for step in range(3)], axis=0
    )
    axial = jnp.concatenate(pieces(axial), axis=0).astype(BF16)
    rows_down = iota((cells_row, LANES), 0)
    slots_down = iota((LANES, LANES), 0) >> 2
    for block in range(slot_ref.shape[0]):
        lanes = slice(block * LANES, (block + 1) * LANES)
        windows = sum_thirds(times(axial, cover_ref[:, lanes]))
        at_row = rows_down == row_ref[block : block + 1, :]
        weight_x, weight_y = weight_ref[0:1, lanes], weight_ref[1:2, lanes]
        sums = []
        for step in range(3):
            base = 2 * step * cells_row
            both = (
                weight_x * windows[base : base + cells_row]
                + weight_y * windows[base + cells_row : base + 2 * cells_row]
            )
            sums.append(jnp.sum(jnp.where(at_row, both, 0.0), axis=0, keepdims=True))
        sums.append(channel_ref[block : block + 1, :].astype(F32))
        values = jnp.concatenate(sums + sums, axis=0)
        in_slot = slots_down == slot_ref[block : block + 1, :]
        for third, piece in enumerate(pieces(values)):
            spread_ref[third * LANES : (third + 1) * LANES, lanes] = jnp.where(
                in_slot, jnp.concatenate([piece] * (LANES // 8), axis=0), 0.0
            ).astype(BF16)
    out_ref[...] = sum_thirds(times_turned(spread_ref[...], place_ref[...]))


def owner_body(arrived_ref, observed_ref, residual_ref, reply_ref, values_ref, place_ref, held_ref):
    groups = arrived_ref.shape[0] // 4
    parts = observed_ref.shape[1] // LANES
    down = iota((LANES, LANES), 0)
    part_down = iota((parts, LANES), 0)
    nothing = jnp.zeros((parts, LANES), F32)
    numbers = [arrived_ref[4 * s + 3 : 4 * s + 4, :].astype(I32) for s in range(groups)]
    for s in range(groups):
        lanes = slice(s * LANES, (s + 1) * LANES)
        place_ref[:, lanes] = jnp.where(down == (numbers[s] & (LANES - 1)), 1.0, 0.0).astype(BF16)
        at_part = part_down == (numbers[s] >> 7)
        thirds = pieces(arrived_ref[4 * s : 4 * s + 3, :])
        stack = []
        for third in thirds:
            for step in range(3):
                stack.append(jnp.where(at_part, third[step : step + 1, :], 0.0))
            stack.append(nothing)
        values_ref[:, lanes] = jnp.concatenate(stack, axis=0).astype(BF16)
    sums = sum_thirds(times_turned(values_ref[...], place_ref[...]))
    for step in range(3):
        for part in range(parts):
            at = step * parts + part
            held_ref[at : at + 1, :] = observed_ref[step : step + 1, part * LANES : (part + 1) * LANES]
    held_ref[3 * parts :, :] = nothing
    held_ref[...] = sums - held_ref[...]
    for step in range(3):
        for part in range(parts):
            at = step * parts + part
            residual_ref[step : step + 1, part * LANES : (part + 1) * LANES] = held_ref[at : at + 1, :]
    residual = jnp.concatenate(two_pieces(held_ref[...]), axis=0).astype(BF16)
    for s in range(groups):
        lanes = slice(s * LANES, (s + 1) * LANES)
        found = sum_halves(times(residual, place_ref[:, lanes]))
        at_part = part_down == (numbers[s] >> 7)
        for step in range(3):
            reply_ref[s, 0:1, step * LANES : (step + 1) * LANES] = jnp.sum(
                jnp.where(at_part, found[step * parts : (step + 1) * parts], 0.0), axis=0, keepdims=True
            )


def load_body(
    arrived_ref,
    slot_ref,
    row_ref,
    weight_ref,
    cover_ref,
    place_ref,
    load_ref,
    out_ref,
    spread_ref,
    side_ref,
    rows_ref,
):
    cells_row = load_ref.shape[0] // 6
    stack_rows = load_ref.shape[0]
    groups = arrived_ref.shape[0]
    for step in range(3):
        for s in range(groups):
            at = step * groups + s
            rows_ref[at : at + 1, :] = arrived_ref[s, 0:1, step * LANES : (step + 1) * LANES]
    arrived = jnp.concatenate(two_pieces(rows_ref[...]), axis=0).astype(BF16)
    slots_down = iota((groups, LANES), 0)
    rows_down = iota((cells_row, LANES), 0)
    for block in range(slot_ref.shape[0]):
        lanes = slice(block * LANES, (block + 1) * LANES)
        found = sum_halves(times(arrived, place_ref[:, lanes]))
        in_slot = slots_down == slot_ref[block : block + 1, :]
        at_row = rows_down == row_ref[block : block + 1, :]
        for turn in range(3):
            base = (2 - turn) * groups
            back = jnp.sum(jnp.where(in_slot, found[base : base + groups], 0.0), axis=0, keepdims=True)
            for part in range(2):
                for half, piece in enumerate(two_pieces(weight_ref[part : part + 1, lanes] * back)):
                    base = half * stack_rows + (2 * turn + part) * cells_row
                    spread_ref[base : base + cells_row, lanes] = jnp.where(at_row, piece, 0.0).astype(BF16)
    load = sum_halves(times_turned(spread_ref[...], cover_ref[...]))
    load_ref[...] = load
    spare = LANES - stack_rows
    edge_columns(jnp.concatenate([load, jnp.zeros((spare, LANES), F32)], axis=0), side_ref)
    send_sides(side_ref, out_ref, [(dx, dy) for dx, dy in NEAR if dy])


def factors_body(strain_ref, factor_ref):
    rows = strain_ref.shape[0] // 18
    for step in range(3):
        strains = [strain_ref[(step * 6 + n) * rows : (step * 6 + n + 1) * rows, :] for n in range(6)]
        factors = [2.0 * s for s in strains[:3]] + strains[3:] + [strains[0] + strains[1] + strains[2]]
        for number, factor in enumerate(factors):
            base = (step * 7 + number) * rows
            factor_ref[base : base + rows, :] = factor


def medium_body(medium_ref, scaled_ref):
    depth = medium_ref.shape[0] // 3
    for z in range(depth):
        for number, plane in enumerate(scaled_medium(medium_ref, 0, depth, z)):
            scaled_ref[number * depth + z] = plane


def adjoint_body(
    load_ref, higher_ref, lower_ref, recv_ref, strain_ref, medium_ref, gradient_ref, load_planes_ref, planes_ref, turn_ref
):
    depth = medium_ref.shape[0] // 4

    def medium(z):
        return [medium_ref[number * depth + z] for number in range(4)]

    turn_ref[...] = jnp.zeros_like(turn_ref)
    rims = [rim_rows(recv_ref, dx, turn_ref) for dx in (0, 1, -1)]
    lay_planes(load_planes_ref, 0, load_ref, higher_ref, lower_ref)
    lay_planes(load_planes_ref, LANES, *rims)
    planes_ref[...] = jnp.zeros_like(planes_ref)
    gradient_ref[...] = jnp.zeros_like(gradient_ref)
    for turn in range(3):
        for part in range(2):
            for z in range(depth):
                at = (3 + part) * depth + z
                planes_ref[at] = planes_ref[at] + load_planes_ref[(2 * turn + part) * depth + z]

        def emit(z, strains, turn=turn):
            forward = []
            for number in range(7):
                base = (((2 - turn) * 7 + number) * depth + z) * TILE_X
                forward.append(strain_ref[base : base + TILE_X, :])
            back = [strain[0:TILE_X, 0:LANES] for strain in strains]
            dilation = forward[6] * (back[0] + back[1] + back[2])
            product = [forward[number] * back[number] for number in range(6)]
            shear = (product[0] + product[1] + product[2]) + product[3] + product[4] + product[5]
            for part, term in enumerate((dilation, shear)):
                base = (part * depth + z) * TILE_X
                gradient_ref[base : base + TILE_X, :] = gradient_ref[base : base + TILE_X, :] + term

        advance(planes_ref, medium, depth, emit, turn == 2)


def shards(
    initial_state,
    lame_lambda,
    shear_modulus,
    buoyancy,
    source_cells,
    source_wavelet,
    segment_start,
    segment_weight,
    partial_owner,
    partial_channel,
    observed_data,
):
    depth, rows_x, cols_y = lame_lambda.shape
    part_count = segment_start.shape[0]
    count_x, count_y = lax.axis_size("gx"), lax.axis_size("gy")
    devices = count_x * count_y
    capacity = max(2, 2 * part_count // devices)
    slot_groups = devices * capacity // LANES
    blocks = part_count // LANES
    per_group = LANES // capacity
    cells_row = depth * rows_x
    both = ("gx", "gy")
    up = [(i, i + 1) for i in range(count_x - 1)]
    down = [(j, i) for i, j in up]
    shape = jax.ShapeDtypeStruct

    def exchange(chunks):
        return lax.all_to_all(chunks, both, split_axis=0, concat_axis=0, tiled=True)

    def route(rows, chunk):
        parts = rows.reshape(slot_groups, -1, per_group, capacity).transpose(0, 2, 1, 3)
        back = exchange(parts.reshape((devices,) + chunk)).reshape(slot_groups, per_group, -1, capacity)
        return back.transpose(0, 2, 1, 3).reshape(rows.shape)

    sources = source_cells.shape[0]
    fields, edges = call_kernel(
        pack_body,
        "pack_edges",
        [shape((12 * cells_row, cols_y), F32), shape((devices, 1, 8 * LANES), F32)],
        [
            pltpu.VMEM((2, 1, 8 * LANES), F32),
            pltpu.VMEM((1, sources), I32),
            pltpu.VMEM(source_wavelet.shape, F32),
            pltpu.SemaphoreType.DMA((6,)),
        ],
        *[values.reshape(-1, cols_y) for values in (initial_state, lame_lambda, shear_modulus, buoyancy)],
        source_cells.reshape(1, -1),
        source_wavelet,
        place=pl.ANY,
        room=60 * 1024 * 1024,
    )
    lower = lax.ppermute(fields, "gx", up)
    higher = lax.ppermute(fields, "gx", down)
    rims = exchange(edges)
    channels = partial_channel.reshape(blocks, LANES)
    slot, row, cover, place = call_kernel(
        functools.partial(slots_body, capacity, devices, cols_y),
        "segment_slots",
        [
            shape((blocks, LANES), I32),
            shape((blocks, LANES), I32),
            shape((cols_y, part_count), BF16),
            shape((LANES, part_count), BF16),
        ],
        [pltpu.VMEM((blocks, LANES), F32)],
        partial_owner.reshape(blocks, LANES),
        segment_start.reshape(blocks, LANES),
    )
    partials, strains, medium = call_kernel(
        functools.partial(forward_body, cols_y),
        "forward_run",
        [
            shape((slot_groups * 4, LANES), F32),
            shape((18 * cells_row, cols_y), F32),
            shape((3 * depth, SPAN_X, SPAN_Y), F32),
        ],
        [
            pltpu.VMEM((12 * depth, SPAN_X, SPAN_Y), F32),
            pltpu.VMEM((LANES, 2 * LANES), F32),
            pltpu.VMEM((9 * depth * SPAN_X, 5 * LANES), BF16),
            pltpu.VMEM((SPAN_Y, 5 * LANES), BF16),
            pltpu.VMEM((3 * depth * SPAN_X, SPAN_Y), F32),
            pltpu.VMEM((3 * LANES, part_count), BF16),
        ],
        fields,
        higher,
        lower,
        rims,
        slot,
        row,
        segment_weight,
        channels,
        cover,
        place,
    )
    (factors,) = call_kernel(
        factors_body, "forward_factors", [shape((21 * cells_row, cols_y), F32)], [], strains
    )
    arrived, factors = lax.optimization_barrier((route(partials, (4, capacity)), factors))
    parts = observed_data.shape[1] // LANES
    residuals, reply = call_kernel(
        owner_body,
        "channel_sums",
        [shape(observed_data.shape, F32), shape((slot_groups, 1, 3 * LANES), F32)],
        [
            pltpu.VMEM((12 * parts, slot_groups * LANES), BF16),
            pltpu.VMEM((LANES, slot_groups * LANES), BF16),
            pltpu.VMEM((4 * parts, LANES), F32),
        ],
        arrived,
        observed_data,
    )
    medium, reply = lax.optimization_barrier((medium, reply))
    (scaled,) = call_kernel(
        medium_body, "scaled_medium", [shape((4 * depth, SPAN_X, SPAN_Y), F32)], [], medium
    )
    returned, scaled = lax.optimization_barrier((route(reply, (1, 3 * capacity)), scaled))
    loads, load_edges = call_kernel(
        load_body,
        "segment_loads",
        [shape((6 * cells_row, cols_y), F32), shape((devices, 1, RIM * LANES), F32)],
        [
            pltpu.VMEM((12 * cells_row, part_count), BF16),
            pltpu.VMEM((2, 1, RIM * LANES), F32),
            pltpu.VMEM((3 * slot_groups, LANES), F32),
        ],
        returned,
        slot,
        row,
        segment_weight,
        cover,
        place,
    )
    load_lower = lax.ppermute(loads, "gx", up)
    load_higher = lax.ppermute(loads, "gx", down)
    load_rims = exchange(load_edges)
    (gradients,) = call_kernel(
        adjoint_body,
        "adjoint_run",
        [shape((2 * cells_row, cols_y), F32)],
        [
            pltpu.VMEM((6 * depth, SPAN_X, SPAN_Y), F32),
            pltpu.VMEM((9 * depth, SPAN_X, SPAN_Y), F32),
            pltpu.VMEM((LANES, LANES), F32),
        ],
        loads,
        load_higher,
        load_lower,
        load_rims,
        factors,
        scaled,
    )
    return (residuals, gradients.reshape(2, depth, rows_x, cols_y))


def solution(mesh):
    in_specs = (
        P(None, None, "gx", "gy"),
        P(None, "gx", "gy"),
        P(None, "gx", "gy"),
        P(None, "gx", "gy"),
        P(("gx", "gy")),
        P(None, ("gx", "gy")),
        P(("gx", "gy")),
        P(None, ("gx", "gy")),
        P(("gx", "gy"), None),
        P(("gx", "gy")),
        P(None, ("gx", "gy")),
    )
    out_specs = (P(None, ("gx", "gy")), P(None, None, "gx", "gy"))
    return jax.shard_map(shards, mesh=mesh, in_specs=in_specs, out_specs=out_specs, check_vma=False)
```

```python
import functools

import jax
import jax.numpy as jnp
from jax import lax
from jax.experimental import pallas as pl
from jax.experimental.pallas import tpu as pltpu
from jax.sharding import PartitionSpec as P

GAUGE = 8
STEP = 0.25
RIM = 3
LANES = 128
TILE_X = 4
SPAN_X = 16
SPAN_NEAR = 8
SPAN_Y = 256
F32, BF16, I32 = jnp.float32, jnp.bfloat16, jnp.int32
NEAR = tuple((dx, dy) for dx in (-1, 0, 1) for dy in (-1, 0, 1))


def call_kernel(body, name, outs, scratch, *args, place=pltpu.VMEM, room=24 * 1024 * 1024):
    whole = pl.BlockSpec(memory_space=pltpu.VMEM)
    return pl.pallas_call(
        body,
        name=name,
        out_shape=outs,
        in_specs=[pl.BlockSpec(memory_space=place)] * len(args),
        out_specs=[whole] * len(outs),
        scratch_shapes=scratch,
        compiler_params=pltpu.CompilerParams(vmem_limit_bytes=room),
    )(*args)


def pieces(values):
    high = values.astype(BF16).astype(F32)
    rest = values - high
    middle = rest.astype(BF16).astype(F32)
    return high, middle, rest - middle


def iota(shape, dim):
    return lax.broadcasted_iota(I32, shape, dim)


def times(left, right):
    return lax.dot_general(left, right, (((1,), (0,)), ((), ())), preferred_element_type=F32)


def times_turned(left, right):
    return lax.dot_general(left, right, (((1,), (1,)), ((), ())), preferred_element_type=F32)


def two_pieces(values):
    high = values.astype(BF16).astype(F32)
    return high, values - high


def sum_halves(values):
    half = values.shape[0] // 2
    return values[:half] + values[half:]


def sum_thirds(values):
    third = values.shape[0] // 3
    return values[:third] + values[third : 2 * third] + values[2 * third :]


def neighbour(dx, dy):
    count_x, count_y = lax.axis_size("gx"), lax.axis_size("gy")
    at_x, at_y = lax.axis_index("gx") + dx, lax.axis_index("gy") + dy
    inside = (at_x >= 0) & (at_x < count_x) & (at_y >= 0) & (at_y < count_y)
    return jnp.where(inside, at_x * count_y + at_y, 0), inside


def edge_columns(rows, side_ref):
    width = rows.shape[0]
    turned = rows.T
    for side, base in ((0, 0), (1, LANES - RIM)):
        for column in range(RIM):
            side_ref[side, 0:1, column * width : (column + 1) * width] = turned[base + column : base + column + 1, :]


def send_sides(side_ref, out_ref, places):
    for dx, dy in places:
        index, inside = neighbour(dx, dy)

        @pl.when(inside)
        def _(index=index, dy=dy):
            out_ref[index] = side_ref[1 if dy > 0 else 0]


def arrived_chunk(recv_ref, dx, dy):
    index, inside = neighbour(dx, dy)
    return jnp.where(inside, recv_ref[index], 0.0)


def rim_rows(recv_ref, dx, turn_ref):
    width = turn_ref.shape[1]
    for dy, base in ((1, 0), (-1, LANES - RIM)):
        chunk = arrived_chunk(recv_ref, dx, dy)
        for column in range(RIM):
            turn_ref[base + column : base + column + 1, :] = chunk[:, column * width : (column + 1) * width]
    return turn_ref[...].T


def lay_planes(wide_ref, narrow_ref, lane, centre, higher, lower):
    row = iota((8, LANES), 0)
    wide = wide_ref.shape[0]
    lanes = slice(lane, lane + LANES)
    for plane in range(wide + narrow_ref.shape[0]):
        rows = slice(8 * (plane // 2), 8 * (plane // 2) + 8)
        mid, high, low = centre[rows], higher[rows], lower[rows]
        if plane % 2:
            mid = pltpu.roll(mid, TILE_X, 0)
        else:
            high, low = pltpu.roll(high, TILE_X, 0), pltpu.roll(low, TILE_X, 0)
        near = jnp.where(row < TILE_X, mid, high)
        if plane < wide:
            wide_ref[plane, 0:8, lanes] = near
            wide_ref[plane, 8:16, lanes] = jnp.where(row < TILE_X, 0.0, low)
        else:
            narrow_ref[plane - wide, :, lanes] = jnp.where(row < SPAN_NEAR - 2, near, low)


def narrowed(plane):
    row = iota((SPAN_NEAR, plane.shape[1]), 0)
    return jnp.where(row < SPAN_NEAR - 2, plane[:SPAN_NEAR], plane[SPAN_NEAR:])


def ahead_x(plane):
    return pltpu.roll(plane, plane.shape[0] - 1, 0) - plane


def behind_x(plane):
    return plane - pltpu.roll(plane, 1, 0)


def ahead_y(plane):
    return pltpu.roll(plane, SPAN_Y - 1, 1) - plane


def behind_y(plane):
    return plane - pltpu.roll(plane, 1, 1)


def ahead_z(planes, z):
    return planes[z + 1] - planes[z] if z + 1 < len(planes) else -planes[z]


def behind_z(planes, z):
    return planes[z] - planes[z - 1] if z else planes[z]


class Planes:
    def __init__(self, ref, first, depth):
        self.ref, self.first, self.depth = ref, first, depth

    def __len__(self):
        return self.depth

    def __getitem__(self, z):
        return self.ref[self.first + z]

    def __setitem__(self, z, plane):
        self.ref[self.first + z] = plane


def fields_of(ref, count, depth, first=0):
    return [Planes(ref, (first + number) * depth, depth) for number in range(count)]


def strain_rates(velocity, z):
    along_x, along_y, along_z = [field[z] for field in velocity]
    return (
        behind_x(along_x),
        behind_y(along_y),
        behind_z(velocity[2], z),
        ahead_y(along_x) + ahead_x(along_y),
        ahead_z(velocity[0], z) + ahead_x(along_z),
        ahead_z(velocity[1], z) + ahead_y(along_z),
    )


def new_stress(stress, strains, lame_lambda, shear_modulus, z):
    dilated = lame_lambda[z] * (strains[0] + strains[1] + strains[2])
    shear = shear_modulus[z]
    normal = [stress[n][z] + STEP * (dilated + 2.0 * shear * strains[n]) for n in range(3)]
    return normal + [stress[n][z] + STEP * shear * strains[n] for n in range(3, 6)]


def advance(state, medium, emit, target):
    velocity, stress = state[:3], state[3:]
    lame_lambda, shear_modulus, buoyancy = medium
    depth = len(buoyancy)
    wide = target is not None and target is not state
    for z in range(depth):
        scale = STEP * buoyancy[z]
        accel = (
            ahead_x(stress[0][z]) + behind_y(stress[3][z]) + behind_z(stress[4], z),
            behind_x(stress[3][z]) + ahead_y(stress[1][z]) + behind_z(stress[5], z),
            behind_x(stress[4][z]) + behind_y(stress[5][z]) + ahead_z(stress[2], z),
        )
        for number in range(3):
            moved = velocity[number][z] + scale * accel[number]
            velocity[number][z] = moved
            if wide:
                target[number][z] = narrowed(moved)
    for z in range(depth):
        strains = strain_rates(velocity, z)
        emit(z, strains)
        if target is not None:
            for number, plane in enumerate(new_stress(stress, strains, lame_lambda, shear_modulus, z)):
                target[3 + number][z] = narrowed(plane) if wide else plane


def pack_body(*refs):
    inputs, (fields_ref, out_ref, side_ref, cells_ref, wavelet_ref, arrived) = refs[:6], refs[6:]
    targets, at = [], 0
    for source in inputs[:4]:
        targets.append(fields_ref.at[at : at + source.shape[0]])
        at = at + source.shape[0]
    copies = [
        pltpu.make_async_copy(source, target, arrived.at[number])
        for number, (source, target) in enumerate(zip(inputs, targets + [cells_ref, wavelet_ref]))
    ]
    for copy in copies:
        copy.start()
    copies[4].wait()
    copies[5].wait()
    cells_row = inputs[1].shape[0]
    cells = cells_ref[...]
    count = cells.shape[1]
    at_lane = iota((LANES, count), 0) == (cells & (LANES - 1))
    at_row = iota((cells_row, count), 0) == (cells >> (LANES.bit_length() - 1))
    stack = [
        jnp.where(at_row, third[step : step + 1, :], 0.0) for third in pieces(wavelet_ref[...]) for step in range(3)
    ]
    maps = sum_thirds(
        times_turned(jnp.concatenate(stack, axis=0).astype(BF16), jnp.where(at_lane, 1.0, 0.0).astype(BF16))
    )
    for copy in copies[:4]:
        copy.wait()
    fields_ref[at:, :] = maps[cells_row:]
    for number in range(3, 6):
        rows = slice(number * cells_row, (number + 1) * cells_row)
        fields_ref[rows, :] = fields_ref[rows, :] + maps[:cells_row]
    rows = fields_ref[...]
    spare = 2 * LANES - rows.shape[0]
    edge_columns(jnp.concatenate([rows, jnp.zeros((spare, LANES), F32)], axis=0), side_ref)
    send_sides(side_ref, out_ref, [(dx, dy) for dx, dy in NEAR if dy])


def slots_body(capacity, devices, cols_y, owner_ref, start_ref, slot_ref, row_ref, cover_ref, place_ref, rank_ref):
    blocks = owner_ref.shape[0]
    group = 32
    before = jnp.where(iota((LANES, 2 * LANES), 0) < iota((LANES, 2 * LANES), 1), 1.0, 0.0).astype(BF16)
    rank_ref[...] = jnp.zeros_like(rank_ref)

    def count_group(number, carry):
        names = iota((group, LANES), 0) + number * group
        hot = [names == owner_ref[b : b + 1, :] for b in range(blocks)]
        marks = jnp.concatenate([jnp.where(h, 1.0, 0.0) for h in hot], axis=0).astype(BF16)
        counts = times(marks, before)
        total = jnp.zeros((group, LANES), F32)
        for b in range(blocks):
            part = counts[b * group : (b + 1) * group]
            rank_ref[b : b + 1, :] = rank_ref[b : b + 1, :] + jnp.sum(
                jnp.where(hot[b], part[:, :LANES] + total, 0.0), axis=0, keepdims=True
            )
            total = total + part[:, LANES:]
        return carry

    if devices == group:
        count_group(0, 0)
    else:
        lax.fori_loop(0, devices // group, count_group, 0)
    slot = owner_ref[...] * capacity + rank_ref[...].astype(I32)
    slot_ref[...] = slot >> 7
    low = slot & (LANES - 1)
    span = cols_y - GAUGE + 1
    start = start_ref[...]
    row = ((start.astype(F32) + 0.5) * (1.0 / span)).astype(I32)
    row_ref[...] = row
    first = start - row * span
    down = iota((LANES, LANES), 0)
    for b in range(blocks):
        lanes = slice(b * LANES, (b + 1) * LANES)
        offset = down - first[b : b + 1, :]
        cover_ref[:, lanes] = jnp.where((offset >= 0) & (offset < GAUGE), 1.0, 0.0).astype(BF16)
        place_ref[:, lanes] = jnp.where(down == low[b : b + 1, :], 1.0, 0.0).astype(BF16)


def forward_body(
    fields_ref,
    higher_ref,
    lower_ref,
    recv_ref,
    slot_ref,
    row_ref,
    weight_ref,
    channel_ref,
    cover_ref,
    place_ref,
    out_ref,
    strain_ref,
    medium_ref,
    wide_ref,
    source_ref,
    state_ref,
    near_ref,
    turn_ref,
    spread_ref,
):
    depth = medium_ref.shape[0] // 3
    cells_row = depth * TILE_X
    turn_ref[...] = jnp.zeros_like(turn_ref)
    rims = [rim_rows(recv_ref, dx, turn_ref) for dx in (0, 1, -1)]
    lay_planes(wide_ref, source_ref, 0, fields_ref, higher_ref, lower_ref)
    lay_planes(wide_ref, source_ref, LANES, *rims)
    first = 9 * depth
    medium_ref[...] = wide_ref[first:]
    for plane in range(3 * depth):
        near_ref[plane] = narrowed(wide_ref[first + plane])
    state, near = fields_of(state_ref, 9, depth), fields_of(near_ref, 3, depth)
    for step in range(3):

        def emit(z, strains, step=step):
            for number, strain in enumerate(strains):
                base = ((step * 6 + number) * depth + z) * TILE_X
                strain_ref[base : base + TILE_X, :] = strain[0:TILE_X, 0:LANES]

        if step == 0:
            advance(fields_of(wide_ref, 9, depth), fields_of(wide_ref, 3, depth, 9), emit, state)
            continue
        for z in range(depth):
            load = source_ref[(step - 1) * depth + z]
            for number in range(3, 6):
                state[number][z] = state[number][z] + load
        advance(state, near, emit, state if step == 1 else None)
    axial = jnp.concatenate(
        [strain_ref[step * 6 * cells_row : (step * 6 + 2) * cells_row, :] for step in range(3)], axis=0
    )
    axial = jnp.concatenate(pieces(axial), axis=0).astype(BF16)
    rows_down = iota((cells_row, LANES), 0)
    slots_down = iota((LANES, LANES), 0) >> 2
    for block in range(slot_ref.shape[0]):
        lanes = slice(block * LANES, (block + 1) * LANES)
        if block % 2 == 0:
            both = sum_thirds(times(axial, cover_ref[:, block * LANES : (block + 2) * LANES]))
        windows = both[:, :LANES] if block % 2 == 0 else both[:, LANES:]
        at_row = rows_down == row_ref[block : block + 1, :]
        weight_x, weight_y = weight_ref[0:1, lanes], weight_ref[1:2, lanes]
        sums = []
        for step in range(3):
            base = 2 * step * cells_row
            axial_sum = (
                weight_x * windows[base : base + cells_row]
                + weight_y * windows[base + cells_row : base + 2 * cells_row]
            )
            sums.append(jnp.sum(jnp.where(at_row, axial_sum, 0.0), axis=0, keepdims=True))
        sums.append(channel_ref[block : block + 1, :].astype(F32))
        values = jnp.concatenate(sums + sums, axis=0)
        in_slot = slots_down == slot_ref[block : block + 1, :]
        for third, piece in enumerate(pieces(values)):
            spread_ref[third * LANES : (third + 1) * LANES, lanes] = jnp.where(
                in_slot, jnp.concatenate([piece] * (LANES // 8), axis=0), 0.0
            ).astype(BF16)
    out_ref[...] = sum_thirds(times_turned(spread_ref[...], place_ref[...]))


def owner_body(arrived_ref, observed_ref, residual_ref, reply_ref, values_ref, place_ref, held_ref):
    groups = arrived_ref.shape[0] // 4
    parts = observed_ref.shape[1] // LANES
    down = iota((LANES, LANES), 0)
    part_down = iota((parts, LANES), 0)
    nothing = jnp.zeros((parts, LANES), F32)
    numbers = [arrived_ref[4 * s + 3 : 4 * s + 4, :].astype(I32) for s in range(groups)]
    for s in range(groups):
        lanes = slice(s * LANES, (s + 1) * LANES)
        place_ref[:, lanes] = jnp.where(down == (numbers[s] & (LANES - 1)), 1.0, 0.0).astype(BF16)
        at_part = part_down == (numbers[s] >> 7)
        thirds = pieces(arrived_ref[4 * s : 4 * s + 3, :])
        stack = []
        for third in thirds:
            for step in range(3):
                stack.append(jnp.where(at_part, third[step : step + 1, :], 0.0))
            stack.append(nothing)
        values_ref[:, lanes] = jnp.concatenate(stack, axis=0).astype(BF16)
    sums = sum_thirds(times_turned(values_ref[...], place_ref[...]))
    for step in range(3):
        for part in range(parts):
            at = step * parts + part
            held_ref[at : at + 1, :] = observed_ref[step : step + 1, part * LANES : (part + 1) * LANES]
    held_ref[3 * parts :, :] = nothing
    held_ref[...] = sums - held_ref[...]
    for step in range(3):
        for part in range(parts):
            at = step * parts + part
            residual_ref[step : step + 1, part * LANES : (part + 1) * LANES] = held_ref[at : at + 1, :]
    residual = jnp.concatenate(two_pieces(held_ref[...]), axis=0).astype(BF16)
    for s in range(groups):
        if s % 2 == 0:
            both = sum_halves(times(residual, place_ref[:, s * LANES : (s + 2) * LANES]))
        found = both[:, :LANES] if s % 2 == 0 else both[:, LANES:]
        at_part = part_down == (numbers[s] >> 7)
        for step in range(3):
            reply_ref[4 * s + step : 4 * s + step + 1, :] = jnp.sum(
                jnp.where(at_part, found[step * parts : (step + 1) * parts], 0.0), axis=0, keepdims=True
            )
        reply_ref[4 * s + 3 : 4 * s + 4, :] = jnp.zeros((1, LANES), F32)


def load_body(
    arrived_ref,
    slot_ref,
    row_ref,
    weight_ref,
    cover_ref,
    place_ref,
    load_ref,
    out_ref,
    spread_ref,
    side_ref,
):
    cells_row = load_ref.shape[0] // 6
    stack_rows = load_ref.shape[0]
    arrived = jnp.concatenate(two_pieces(arrived_ref[...]), axis=0).astype(BF16)
    slots_down = iota((LANES, LANES), 0) >> 2
    rows_down = iota((cells_row, LANES), 0)
    for block in range(slot_ref.shape[0]):
        lanes = slice(block * LANES, (block + 1) * LANES)
        if block % 2 == 0:
            both = sum_halves(times(arrived, place_ref[:, block * LANES : (block + 2) * LANES]))
        found = both[:, :LANES] if block % 2 == 0 else both[:, LANES:]
        found = jnp.where(slots_down == slot_ref[block : block + 1, :], found, 0.0)
        folded = found[0:8]
        for part in range(1, LANES // 8):
            folded = folded + found[8 * part : 8 * part + 8]
        folded = folded + pltpu.roll(folded, 4, 0)
        at_row = rows_down == row_ref[block : block + 1, :]
        for turn in range(3):
            back = folded[2 - turn : 3 - turn, :]
            for part in range(2):
                for half, piece in enumerate(two_pieces(weight_ref[part : part + 1, lanes] * back)):
                    base = half * stack_rows + (2 * turn + part) * cells_row
                    spread_ref[base : base + cells_row, lanes] = jnp.where(at_row, piece, 0.0).astype(BF16)
    load = sum_halves(times_turned(spread_ref[...], cover_ref[...]))
    load_ref[...] = load
    spare = LANES - stack_rows
    edge_columns(jnp.concatenate([load, jnp.zeros((spare, LANES), F32)], axis=0), side_ref)
    send_sides(side_ref, out_ref, [(dx, dy) for dx, dy in NEAR if dy])


def adjoint_body(
    load_ref,
    higher_ref,
    lower_ref,
    recv_ref,
    strain_ref,
    medium_ref,
    gradient_ref,
    first_ref,
    later_ref,
    velocity_ref,
    state_ref,
    near_ref,
    turn_ref,
):
    depth = medium_ref.shape[0] // 3
    turn_ref[...] = jnp.zeros_like(turn_ref)
    rims = [rim_rows(recv_ref, dx, turn_ref) for dx in (0, 1, -1)]
    lay_planes(first_ref, later_ref, 0, load_ref, higher_ref, lower_ref)
    lay_planes(first_ref, later_ref, LANES, *rims)
    for plane in range(3 * depth):
        near_ref[plane] = narrowed(medium_ref[plane])
    gradient_ref[...] = jnp.zeros_like(gradient_ref)
    state, near, medium = (
        fields_of(state_ref, 9, depth),
        fields_of(near_ref, 3, depth),
        fields_of(medium_ref, 3, depth),
    )

    def add_terms(turn, z, strains):
        dilation, dilation_back, doubled, product = None, None, None, None
        for number, strain in enumerate(strains):
            base = (((2 - turn) * 6 + number) * depth + z) * TILE_X
            forward = strain_ref[base : base + TILE_X, :]
            if number < 3:
                dilation = forward if dilation is None else dilation + forward
            if strain is None:
                continue
            back = strain[0:TILE_X, 0:LANES]
            term = forward * back
            if number < 3:
                dilation_back = back if dilation_back is None else dilation_back + back
                doubled = term if doubled is None else doubled + term
            else:
                product = term if product is None else product + term
        for part, term in enumerate((dilation * dilation_back, 2.0 * doubled + product)):
            base = (part * depth + z) * TILE_X
            gradient_ref[base : base + TILE_X, :] = gradient_ref[base : base + TILE_X, :] + term

    loads, velocity = fields_of(first_ref, 2, depth), fields_of(velocity_ref, 2, depth)
    for z in range(depth):
        scale = STEP * medium[2][z]
        velocity[0][z] = scale * ahead_x(loads[0][z])
        velocity[1][z] = scale * ahead_y(loads[1][z])
        state[0][z] = narrowed(velocity[0][z])
        state[1][z] = narrowed(velocity[1][z])
        state[2][z] = jnp.zeros((SPAN_NEAR, SPAN_Y), F32)
    for z in range(depth):
        along_x, along_y = velocity[0][z], velocity[1][z]
        strain_x, strain_y = behind_x(along_x), behind_y(along_y)
        sheared = (
            ahead_y(along_x) + ahead_x(along_y),
            ahead_z(velocity[0], z),
            ahead_z(velocity[1], z),
        )
        add_terms(0, z, (strain_x, strain_y, None) + sheared)
        dilated = medium[0][z] * (strain_x + strain_y)
        shear = medium[1][z]
        state[3][z] = narrowed(loads[0][z] + STEP * (dilated + 2.0 * shear * strain_x))
        state[4][z] = narrowed(loads[1][z] + STEP * (dilated + 2.0 * shear * strain_y))
        state[5][z] = narrowed(STEP * dilated)
        for number, strain in enumerate(sheared):
            state[6 + number][z] = narrowed(STEP * shear * strain)
    for turn in (1, 2):
        for part in range(2):
            for z in range(depth):
                load = later_ref[(2 * (turn - 1) + part) * depth + z]
                state[3 + part][z] = state[3 + part][z] + load
        advance(state, near, functools.partial(add_terms, turn), state if turn == 1 else None)


def shards(
    initial_state,
    lame_lambda,
    shear_modulus,
    buoyancy,
    source_cells,
    source_wavelet,
    segment_start,
    segment_weight,
    partial_owner,
    partial_channel,
    observed_data,
):
    depth, rows_x, cols_y = lame_lambda.shape
    part_count = segment_start.shape[0]
    count_x, count_y = lax.axis_size("gx"), lax.axis_size("gy")
    devices = count_x * count_y
    capacity = max(2, 2 * part_count // devices)
    slot_groups = devices * capacity // LANES
    blocks = part_count // LANES
    per_group = LANES // capacity
    cells_row = depth * rows_x
    both = ("gx", "gy")
    up = [(i, i + 1) for i in range(count_x - 1)]
    down = [(j, i) for i, j in up]
    shape = jax.ShapeDtypeStruct

    def exchange(chunks):
        return lax.all_to_all(chunks, both, split_axis=0, concat_axis=0, tiled=True)

    def to_owners(rows):
        chunks = rows.reshape(slot_groups, 4, per_group, capacity).transpose(0, 2, 1, 3)
        back = exchange(chunks.reshape(devices, 4, capacity)).reshape(slot_groups, per_group, 4, capacity)
        return back.transpose(0, 2, 1, 3).reshape(slot_groups * 4, LANES)

    fields, edges = call_kernel(
        pack_body,
        "pack_edges",
        [shape((14 * cells_row, cols_y), F32), shape((devices, 1, 2 * RIM * LANES), F32)],
        [
            pltpu.VMEM((2, 1, 2 * RIM * LANES), F32),
            pltpu.VMEM((1, source_cells.shape[0]), I32),
            pltpu.VMEM(source_wavelet.shape, F32),
            pltpu.SemaphoreType.DMA((6,)),
        ],
        *[values.reshape(-1, cols_y) for values in (initial_state, lame_lambda, shear_modulus, buoyancy)],
        source_cells.reshape(1, -1),
        source_wavelet,
        place=pl.ANY,
        room=60 * 1024 * 1024,
    )
    lower = lax.ppermute(fields, "gx", up)
    higher = lax.ppermute(fields, "gx", down)
    rims = exchange(edges)
    channels = partial_channel.reshape(blocks, LANES)
    slot, row, cover, place = call_kernel(
        functools.partial(slots_body, capacity, devices, cols_y),
        "segment_slots",
        [
            shape((blocks, LANES), I32),
            shape((blocks, LANES), I32),
            shape((cols_y, part_count), BF16),
            shape((LANES, part_count), BF16),
        ],
        [pltpu.VMEM((blocks, LANES), F32)],
        partial_owner.reshape(blocks, LANES),
        segment_start.reshape(blocks, LANES),
    )
    partials, strains, medium = call_kernel(
        forward_body,
        "forward_run",
        [
            shape((slot_groups * 4, LANES), F32),
            shape((18 * cells_row, cols_y), F32),
            shape((3 * depth, SPAN_X, SPAN_Y), F32),
        ],
        [
            pltpu.VMEM((12 * depth, SPAN_X, SPAN_Y), F32),
            pltpu.VMEM((2 * depth, SPAN_NEAR, SPAN_Y), F32),
            pltpu.VMEM((9 * depth, SPAN_NEAR, SPAN_Y), F32),
            pltpu.VMEM((3 * depth, SPAN_NEAR, SPAN_Y), F32),
            pltpu.VMEM((LANES, 2 * LANES), F32),
            pltpu.VMEM((3 * LANES, part_count), BF16),
        ],
        fields,
        higher,
        lower,
        rims,
        slot,
        row,
        segment_weight,
        channels,
        cover,
        place,
    )
    parts = observed_data.shape[1] // LANES
    residuals, reply = call_kernel(
        owner_body,
        "channel_sums",
        [shape(observed_data.shape, F32), shape((slot_groups * 4, LANES), F32)],
        [
            pltpu.VMEM((12 * parts, slot_groups * LANES), BF16),
            pltpu.VMEM((LANES, slot_groups * LANES), BF16),
            pltpu.VMEM((4 * parts, LANES), F32),
        ],
        to_owners(partials),
        observed_data,
    )
    loads, load_edges = call_kernel(
        load_body,
        "segment_loads",
        [shape((6 * cells_row, cols_y), F32), shape((devices, 1, RIM * LANES), F32)],
        [pltpu.VMEM((12 * cells_row, part_count), BF16), pltpu.VMEM((2, 1, RIM * LANES), F32)],
        to_owners(reply),
        slot,
        row,
        segment_weight,
        cover,
        place,
    )
    load_lower = lax.ppermute(loads, "gx", up)
    load_higher = lax.ppermute(loads, "gx", down)
    load_rims = exchange(load_edges)
    (gradients,) = call_kernel(
        adjoint_body,
        "adjoint_run",
        [shape((2 * cells_row, cols_y), F32)],
        [
            pltpu.VMEM((2 * depth, SPAN_X, SPAN_Y), F32),
            pltpu.VMEM((4 * depth, SPAN_NEAR, SPAN_Y), F32),
            pltpu.VMEM((2 * depth, SPAN_X, SPAN_Y), F32),
            pltpu.VMEM((9 * depth, SPAN_NEAR, SPAN_Y), F32),
            pltpu.VMEM((3 * depth, SPAN_NEAR, SPAN_Y), F32),
            pltpu.VMEM((LANES, LANES), F32),
        ],
        loads,
        load_higher,
        load_lower,
        load_rims,
        strains,
        medium,
    )
    return (residuals, gradients.reshape(2, depth, rows_x, cols_y))


def solution(mesh):
    in_specs = (
        P(None, None, "gx", "gy"),
        P(None, "gx", "gy"),
        P(None, "gx", "gy"),
        P(None, "gx", "gy"),
        P(("gx", "gy")),
        P(None, ("gx", "gy")),
        P(("gx", "gy")),
        P(None, ("gx", "gy")),
        P(("gx", "gy"), None),
        P(("gx", "gy")),
        P(None, ("gx", "gy")),
    )
    out_specs = (P(None, ("gx", "gy")), P(None, None, "gx", "gy"))
    return jax.shard_map(shards, mesh=mesh, in_specs=in_specs, out_specs=out_specs, check_vma=False)
```

```python
import functools

import jax
import jax.numpy as jnp
from jax import lax
from jax.experimental import pallas as pl
from jax.experimental.pallas import tpu as pltpu
from jax.sharding import PartitionSpec as P

GAUGE = 8
STEP = 0.25
RIM = 3
LANES = 128
TILE_X = 4
SPAN_X = 16
SPAN_NEAR = 8
SPAN_Y = 256
F32, BF16, I32 = jnp.float32, jnp.bfloat16, jnp.int32
NEAR = tuple((dx, dy) for dx in (-1, 0, 1) for dy in (-1, 0, 1))


def call_kernel(
    body, name, outs, scratch, *args, place=pltpu.VMEM, place_out=pltpu.VMEM, room=24 * 1024 * 1024
):
    return pl.pallas_call(
        body,
        name=name,
        out_shape=outs,
        in_specs=[pl.BlockSpec(memory_space=place)] * len(args),
        out_specs=[pl.BlockSpec(memory_space=place_out)] * len(outs),
        scratch_shapes=scratch,
        compiler_params=pltpu.CompilerParams(vmem_limit_bytes=room),
    )(*args)


def pieces(values):
    high = values.astype(BF16).astype(F32)
    rest = values - high
    middle = rest.astype(BF16).astype(F32)
    return high, middle, rest - middle


def iota(shape, dim):
    return lax.broadcasted_iota(I32, shape, dim)


def times(left, right):
    return lax.dot_general(left, right, (((1,), (0,)), ((), ())), preferred_element_type=F32)


def times_turned(left, right):
    return lax.dot_general(left, right, (((1,), (1,)), ((), ())), preferred_element_type=F32)


def packed_rows(row, height):
    tile = jnp.broadcast_to(row.astype(F32), (16, row.shape[1])).astype(BF16)
    return jnp.concatenate([tile] * (height // 16), axis=0) if height > 16 else tile


def packed_iota(height, shift=0):
    return (iota((height, LANES), 0) >> shift).astype(F32).astype(BF16)


def two_pieces(values):
    high = values.astype(BF16).astype(F32)
    return high, values - high


def sum_halves(values):
    half = values.shape[0] // 2
    return values[:half] + values[half:]


def sum_thirds(values):
    third = values.shape[0] // 3
    return values[:third] + values[third : 2 * third] + values[2 * third :]


def neighbour(dx, dy):
    count_x, count_y = lax.axis_size("gx"), lax.axis_size("gy")
    at_x, at_y = lax.axis_index("gx") + dx, lax.axis_index("gy") + dy
    inside = (at_x >= 0) & (at_x < count_x) & (at_y >= 0) & (at_y < count_y)
    return jnp.where(inside, at_x * count_y + at_y, 0), inside


def edge_columns(rows, side_ref):
    width = rows.shape[0]
    turned = rows.T
    for side, base in ((0, 0), (1, LANES - RIM)):
        for column in range(RIM):
            side_ref[side, 0:1, column * width : (column + 1) * width] = turned[base + column : base + column + 1, :]


def send_sides(side_ref, out_ref, places):
    for dx, dy in places:
        index, inside = neighbour(dx, dy)

        @pl.when(inside)
        def _(index=index, dy=dy):
            out_ref[index] = side_ref[1 if dy > 0 else 0]


def arrived_chunk(recv_ref, dx, dy):
    index, inside = neighbour(dx, dy)
    return jnp.where(inside, recv_ref[index], 0.0)


def rim_rows(recv_ref, dx, turn_ref):
    width = turn_ref.shape[1]
    for dy, base in ((1, 0), (-1, LANES - RIM)):
        chunk = arrived_chunk(recv_ref, dx, dy)
        for column in range(RIM):
            turn_ref[base + column : base + column + 1, :] = chunk[:, column * width : (column + 1) * width]
    return turn_ref[...].T


def lay_planes(wide_ref, narrow_ref, lane, centre, higher, lower):
    row = iota((8, LANES), 0)
    wide = wide_ref.shape[0]
    lanes = slice(lane, lane + LANES)
    for plane in range(wide + narrow_ref.shape[0]):
        rows = slice(8 * (plane // 2), 8 * (plane // 2) + 8)
        mid, high, low = centre[rows], higher[rows], lower[rows]
        if plane % 2:
            mid = pltpu.roll(mid, TILE_X, 0)
        else:
            high, low = pltpu.roll(high, TILE_X, 0), pltpu.roll(low, TILE_X, 0)
        near = jnp.where(row < TILE_X, mid, high)
        if plane < wide:
            wide_ref[plane, 0:8, lanes] = near
            wide_ref[plane, 8:16, lanes] = jnp.where(row < TILE_X, 0.0, low)
        else:
            narrow_ref[plane - wide, :, lanes] = jnp.where(row < SPAN_NEAR - 2, near, low)


def narrowed(plane):
    row = iota((SPAN_NEAR, plane.shape[1]), 0)
    return jnp.where(row < SPAN_NEAR - 2, plane[:SPAN_NEAR], plane[SPAN_NEAR:])


def ahead_x(plane):
    return pltpu.roll(plane, plane.shape[0] - 1, 0) - plane


def behind_x(plane):
    return plane - pltpu.roll(plane, 1, 0)


def ahead_y(plane):
    return pltpu.roll(plane, SPAN_Y - 1, 1) - plane


def behind_y(plane):
    return plane - pltpu.roll(plane, 1, 1)


def ahead_z(planes, z):
    return planes[z + 1] - planes[z] if z + 1 < len(planes) else -planes[z]


def behind_z(planes, z):
    return planes[z] - planes[z - 1] if z else planes[z]


class Planes:
    def __init__(self, ref, first, depth):
        self.ref, self.first, self.depth = ref, first, depth

    def __len__(self):
        return self.depth

    def __getitem__(self, z):
        return self.ref[self.first + z]

    def __setitem__(self, z, plane):
        self.ref[self.first + z] = plane


def fields_of(ref, count, depth, first=0):
    return [Planes(ref, (first + number) * depth, depth) for number in range(count)]


def strain_rates(velocity, z):
    along_x, along_y, along_z = [field[z] for field in velocity]
    return (
        behind_x(along_x),
        behind_y(along_y),
        behind_z(velocity[2], z),
        ahead_y(along_x) + ahead_x(along_y),
        ahead_z(velocity[0], z) + ahead_x(along_z),
        ahead_z(velocity[1], z) + ahead_y(along_z),
    )


def new_stress(stress, strains, lame_lambda, shear_modulus, z):
    dilated = lame_lambda[z] * (strains[0] + strains[1] + strains[2])
    shear = shear_modulus[z]
    normal = [stress[n][z] + STEP * (dilated + 2.0 * shear * strains[n]) for n in range(3)]
    return normal + [stress[n][z] + STEP * shear * strains[n] for n in range(3, 6)]


def advance(state, medium, emit, target):
    velocity, stress = state[:3], state[3:]
    lame_lambda, shear_modulus, buoyancy = medium
    depth = len(buoyancy)
    wide = target is not None and target is not state
    for z in range(depth):
        scale = STEP * buoyancy[z]
        accel = (
            ahead_x(stress[0][z]) + behind_y(stress[3][z]) + behind_z(stress[4], z),
            behind_x(stress[3][z]) + ahead_y(stress[1][z]) + behind_z(stress[5], z),
            behind_x(stress[4][z]) + behind_y(stress[5][z]) + ahead_z(stress[2], z),
        )
        for number in range(3):
            moved = velocity[number][z] + scale * accel[number]
            velocity[number][z] = moved
            if wide:
                target[number][z] = narrowed(moved)
    for z in range(depth):
        strains = strain_rates(velocity, z)
        emit(z, strains)
        if target is not None:
            for number, plane in enumerate(new_stress(stress, strains, lame_lambda, shear_modulus, z)):
                target[3 + number][z] = narrowed(plane) if wide else plane


def pack_body(*refs):
    inputs, outputs, scratch = refs[:6], refs[6:10], refs[10:]
    fields_ref, low_ref, high_ref, side_ref, cells_ref, wavelet_ref, arrived, sent, sent_sides = scratch
    targets, at = [], 0
    for source in inputs[:4]:
        targets.append(fields_ref.at[at : at + source.shape[0]])
        at = at + source.shape[0]
    copies = [
        pltpu.make_async_copy(source, target, arrived.at[number])
        for number, (source, target) in enumerate(zip(inputs, targets + [cells_ref, wavelet_ref]))
    ]
    for copy in copies:
        copy.start()
    copies[4].wait()
    copies[5].wait()
    cells_row = inputs[1].shape[0]
    cells = cells_ref[...]
    count = cells.shape[1]
    at_lane = iota((LANES, count), 0) == (cells & (LANES - 1))
    at_row = iota((cells_row, count), 0) == (cells >> (LANES.bit_length() - 1))
    stack = [
        jnp.where(at_row, third[step : step + 1, :], 0.0) for third in pieces(wavelet_ref[...]) for step in range(3)
    ]
    maps = sum_thirds(
        times_turned(jnp.concatenate(stack, axis=0).astype(BF16), jnp.where(at_lane, 1.0, 0.0).astype(BF16))
    )
    for copy in copies[:4]:
        copy.wait()
    fields_ref[at:, :] = maps[cells_row:]
    for number in range(3, 6):
        rows = slice(number * cells_row, (number + 1) * cells_row)
        fields_ref[rows, :] = fields_ref[rows, :] + maps[:cells_row]
    height = fields_ref.shape[0] // TILE_X
    for x in range(TILE_X):
        slab = fields_ref[pl.ds(x, height, stride=TILE_X), :]
        if x < RIM:
            low_ref[x * height : (x + 1) * height, :] = slab
        if x >= TILE_X - RIM:
            at = x - TILE_X + RIM
            high_ref[at * height : (at + 1) * height, :] = slab
    writes = [
        pltpu.make_async_copy(source, target, sent.at[number])
        for number, (source, target) in enumerate(zip((fields_ref, low_ref, high_ref), outputs))
    ]
    for copy in writes:
        copy.start()
    rows = fields_ref[...]
    spare = 2 * LANES - rows.shape[0]
    edge_columns(jnp.concatenate([rows, jnp.zeros((spare, LANES), F32)], axis=0), side_ref)
    sides = []
    for number, (dx, dy) in enumerate((dx, dy) for dx, dy in NEAR if dy):
        index, inside = neighbour(dx, dy)
        source, target = side_ref.at[1 if dy > 0 else 0], outputs[3].at[index]
        sides.append((inside, pltpu.make_async_copy(source, target, sent_sides.at[number])))
    for inside, copy in sides:
        pl.when(inside)(copy.start)
    for copy in writes:
        copy.wait()
    for inside, copy in sides:
        pl.when(inside)(copy.wait)


def slots_body(capacity, devices, cols_y, owner_ref, start_ref, slot_ref, row_ref, cover_ref, place_ref, rank_ref):
    blocks = owner_ref.shape[0]
    group = 32
    before = jnp.where(iota((LANES, 2 * LANES), 0) < iota((LANES, 2 * LANES), 1), 1.0, 0.0).astype(BF16)
    rank_ref[...] = jnp.zeros_like(rank_ref)

    def count_group(number, carry):
        names = iota((group, LANES), 0) + number * group
        hot = [names == owner_ref[b : b + 1, :] for b in range(blocks)]
        marks = jnp.concatenate([jnp.where(h, 1.0, 0.0) for h in hot], axis=0).astype(BF16)
        counts = times(marks, before)
        total = jnp.zeros((group, LANES), F32)
        for b in range(blocks):
            part = counts[b * group : (b + 1) * group]
            rank_ref[b : b + 1, :] = rank_ref[b : b + 1, :] + jnp.sum(
                jnp.where(hot[b], part[:, :LANES] + total, 0.0), axis=0, keepdims=True
            )
            total = total + part[:, LANES:]
        return carry

    if devices == group:
        count_group(0, 0)
    else:
        lax.fori_loop(0, devices // group, count_group, 0)
    slot = owner_ref[...] * capacity + rank_ref[...].astype(I32)
    slot_ref[...] = slot >> 7
    low = slot & (LANES - 1)
    span = cols_y - GAUGE + 1
    start = start_ref[...]
    row = ((start.astype(F32) + 0.5) * (1.0 / span)).astype(I32)
    row_ref[...] = row
    first = start - row * span
    down = iota((LANES, LANES), 0)
    for b in range(blocks):
        lanes = slice(b * LANES, (b + 1) * LANES)
        offset = down - first[b : b + 1, :]
        cover_ref[:, lanes] = jnp.where((offset >= 0) & (offset < GAUGE), 1.0, 0.0).astype(BF16)
        place_ref[:, lanes] = jnp.where(down == low[b : b + 1, :], 1.0, 0.0).astype(BF16)


def forward_body(
    fields_ref,
    higher_ref,
    lower_ref,
    recv_ref,
    slot_ref,
    row_ref,
    weight_ref,
    channel_ref,
    cover_ref,
    place_ref,
    out_ref,
    strain_ref,
    medium_ref,
    wide_ref,
    source_ref,
    state_ref,
    near_ref,
    turn_ref,
    sides_ref,
    spread_ref,
):
    depth = medium_ref.shape[0] // 3
    cells_row = depth * TILE_X
    turn_ref[...] = jnp.zeros_like(turn_ref)
    rims = [rim_rows(recv_ref, dx, turn_ref) for dx in (0, 1, -1)]
    height = fields_ref.shape[0] // TILE_X
    sides_ref[...] = jnp.zeros_like(sides_ref)
    for x in range(RIM):
        slab = slice(x * height, (x + 1) * height)
        sides_ref[0, pl.ds(x, height, stride=TILE_X), :] = higher_ref[slab, :]
        sides_ref[1, pl.ds(x + TILE_X - RIM, height, stride=TILE_X), :] = lower_ref[slab, :]
    lay_planes(wide_ref, source_ref, 0, fields_ref, sides_ref.at[0], sides_ref.at[1])
    lay_planes(wide_ref, source_ref, LANES, *rims)
    first = 9 * depth
    medium_ref[...] = wide_ref[first:]
    for plane in range(3 * depth):
        near_ref[plane] = narrowed(wide_ref[first + plane])
    state, near = fields_of(state_ref, 9, depth), fields_of(near_ref, 3, depth)
    for step in range(3):

        def emit(z, strains, step=step):
            for number, strain in enumerate(strains):
                base = ((step * 6 + number) * depth + z) * TILE_X
                strain_ref[base : base + TILE_X, :] = strain[0:TILE_X, 0:LANES]

        if step == 0:
            advance(fields_of(wide_ref, 9, depth), fields_of(wide_ref, 3, depth, 9), emit, state)
            continue
        for z in range(depth):
            load = source_ref[(step - 1) * depth + z]
            for number in range(3, 6):
                state[number][z] = state[number][z] + load
        advance(state, near, emit, state if step == 1 else None)
    axial = jnp.concatenate(
        [strain_ref[step * 6 * cells_row : (step * 6 + 2) * cells_row, :] for step in range(3)], axis=0
    )
    axial = jnp.concatenate(pieces(axial), axis=0).astype(BF16)
    rows_down = iota((cells_row, LANES), 0)
    slots_down = packed_iota(LANES, 2)
    for block in range(slot_ref.shape[0]):
        lanes = slice(block * LANES, (block + 1) * LANES)
        if block % 2 == 0:
            both = sum_thirds(times(axial, cover_ref[:, block * LANES : (block + 2) * LANES]))
        windows = both[:, :LANES] if block % 2 == 0 else both[:, LANES:]
        at_row = rows_down == row_ref[block : block + 1, :]
        weight_x, weight_y = weight_ref[0:1, lanes], weight_ref[1:2, lanes]
        sums = []
        for step in range(3):
            base = 2 * step * cells_row
            axial_sum = (
                weight_x * windows[base : base + cells_row]
                + weight_y * windows[base + cells_row : base + 2 * cells_row]
            )
            sums.append(jnp.sum(jnp.where(at_row, axial_sum, 0.0), axis=0, keepdims=True))
        sums.append(channel_ref[block : block + 1, :].astype(F32))
        values = jnp.concatenate(sums + sums, axis=0)
        in_slot = slots_down == packed_rows(slot_ref[block : block + 1, :], LANES)
        for third, piece in enumerate(pieces(values)):
            tile = jnp.concatenate([piece, piece], axis=0).astype(BF16)
            spread_ref[third * LANES : (third + 1) * LANES, lanes] = jnp.where(
                in_slot, jnp.concatenate([tile] * (LANES // 16), axis=0), jnp.zeros((), BF16)
            )
    out_ref[...] = sum_thirds(times_turned(spread_ref[...], place_ref[...]))


def owner_body(arrived_ref, observed_ref, residual_ref, reply_ref, values_ref, place_ref, held_ref):
    groups = arrived_ref.shape[0] // 4
    parts = observed_ref.shape[1] // LANES
    down = packed_iota(LANES)
    part_down = iota((parts, LANES), 0)
    nothing = jnp.zeros((parts, LANES), F32)
    numbers = [arrived_ref[4 * s + 3 : 4 * s + 4, :].astype(I32) for s in range(groups)]
    for s in range(groups):
        lanes = slice(s * LANES, (s + 1) * LANES)
        place_ref[:, lanes] = jnp.where(
            down == packed_rows(numbers[s] & (LANES - 1), LANES), jnp.ones((), BF16), jnp.zeros((), BF16)
        )
        at_part = part_down == (numbers[s] >> 7)
        thirds = pieces(arrived_ref[4 * s : 4 * s + 3, :])
        stack = []
        for third in thirds:
            for step in range(3):
                stack.append(jnp.where(at_part, third[step : step + 1, :], 0.0))
            stack.append(nothing)
        values_ref[:, lanes] = jnp.concatenate(stack, axis=0).astype(BF16)
    sums = sum_thirds(times_turned(values_ref[...], place_ref[...]))
    for step in range(3):
        for part in range(parts):
            at = step * parts + part
            held_ref[at : at + 1, :] = observed_ref[step : step + 1, part * LANES : (part + 1) * LANES]
    held_ref[3 * parts :, :] = nothing
    held_ref[...] = sums - held_ref[...]
    for step in range(3):
        for part in range(parts):
            at = step * parts + part
            residual_ref[step : step + 1, part * LANES : (part + 1) * LANES] = held_ref[at : at + 1, :]
    residual = jnp.concatenate(two_pieces(held_ref[...]), axis=0).astype(BF16)
    for s in range(groups):
        if s % 2 == 0:
            both = sum_halves(times(residual, place_ref[:, s * LANES : (s + 2) * LANES]))
        found = both[:, :LANES] if s % 2 == 0 else both[:, LANES:]
        at_part = part_down == (numbers[s] >> 7)
        for step in range(3):
            reply_ref[4 * s + step : 4 * s + step + 1, :] = jnp.sum(
                jnp.where(at_part, found[step * parts : (step + 1) * parts], 0.0), axis=0, keepdims=True
            )
        reply_ref[4 * s + 3 : 4 * s + 4, :] = jnp.zeros((1, LANES), F32)


def load_body(
    arrived_ref,
    slot_ref,
    row_ref,
    weight_ref,
    cover_ref,
    place_ref,
    load_ref,
    out_ref,
    spread_ref,
    side_ref,
):
    cells_row = load_ref.shape[0] // 6
    stack_rows = load_ref.shape[0]
    arrived = jnp.concatenate(two_pieces(arrived_ref[...]), axis=0).astype(BF16)
    slots_down = iota((LANES, LANES), 0) >> 2
    rows_down = packed_iota(cells_row)
    for block in range(slot_ref.shape[0]):
        lanes = slice(block * LANES, (block + 1) * LANES)
        if block % 2 == 0:
            both = sum_halves(times(arrived, place_ref[:, block * LANES : (block + 2) * LANES]))
        found = both[:, :LANES] if block % 2 == 0 else both[:, LANES:]
        found = jnp.where(slots_down == slot_ref[block : block + 1, :], found, 0.0)
        folded = found[0:8]
        for part in range(1, LANES // 8):
            folded = folded + found[8 * part : 8 * part + 8]
        folded = folded + pltpu.roll(folded, 4, 0)
        at_row = rows_down == packed_rows(row_ref[block : block + 1, :], cells_row)
        for turn in range(3):
            back = folded[2 - turn : 3 - turn, :]
            for part in range(2):
                for half, piece in enumerate(two_pieces(weight_ref[part : part + 1, lanes] * back)):
                    base = half * stack_rows + (2 * turn + part) * cells_row
                    spread_ref[base : base + cells_row, lanes] = jnp.where(
                        at_row, packed_rows(piece, cells_row), jnp.zeros((), BF16)
                    )
    load = sum_halves(times_turned(spread_ref[...], cover_ref[...]))
    load_ref[...] = load
    spare = LANES - stack_rows
    edge_columns(jnp.concatenate([load, jnp.zeros((spare, LANES), F32)], axis=0), side_ref)
    send_sides(side_ref, out_ref, [(dx, dy) for dx, dy in NEAR if dy])


def adjoint_body(
    load_ref,
    higher_ref,
    lower_ref,
    recv_ref,
    strain_ref,
    medium_ref,
    gradient_ref,
    first_ref,
    later_ref,
    velocity_ref,
    state_ref,
    near_ref,
    turn_ref,
):
    depth = medium_ref.shape[0] // 3
    turn_ref[...] = jnp.zeros_like(turn_ref)
    rims = [rim_rows(recv_ref, dx, turn_ref) for dx in (0, 1, -1)]
    lay_planes(first_ref, later_ref, 0, load_ref, higher_ref, lower_ref)
    lay_planes(first_ref, later_ref, LANES, *rims)
    for plane in range(3 * depth):
        near_ref[plane] = narrowed(medium_ref[plane])
    gradient_ref[...] = jnp.zeros_like(gradient_ref)
    state, near, medium = (
        fields_of(state_ref, 9, depth),
        fields_of(near_ref, 3, depth),
        fields_of(medium_ref, 3, depth),
    )

    def add_terms(turn, z, strains):
        dilation, dilation_back, doubled, product = None, None, None, None
        for number, strain in enumerate(strains):
            base = (((2 - turn) * 6 + number) * depth + z) * TILE_X
            forward = strain_ref[base : base + TILE_X, :]
            if number < 3:
                dilation = forward if dilation is None else dilation + forward
            if strain is None:
                continue
            back = strain[0:TILE_X, 0:LANES]
            term = forward * back
            if number < 3:
                dilation_back = back if dilation_back is None else dilation_back + back
                doubled = term if doubled is None else doubled + term
            else:
                product = term if product is None else product + term
        for part, term in enumerate((dilation * dilation_back, 2.0 * doubled + product)):
            base = (part * depth + z) * TILE_X
            gradient_ref[base : base + TILE_X, :] = gradient_ref[base : base + TILE_X, :] + term

    loads, velocity = fields_of(first_ref, 2, depth), fields_of(velocity_ref, 2, depth)
    for z in range(depth):
        scale = STEP * medium[2][z]
        velocity[0][z] = scale * ahead_x(loads[0][z])
        velocity[1][z] = scale * ahead_y(loads[1][z])
        state[0][z] = narrowed(velocity[0][z])
        state[1][z] = narrowed(velocity[1][z])
        state[2][z] = jnp.zeros((SPAN_NEAR, SPAN_Y), F32)
    for z in range(depth):
        along_x, along_y = velocity[0][z], velocity[1][z]
        strain_x, strain_y = behind_x(along_x), behind_y(along_y)
        sheared = (
            ahead_y(along_x) + ahead_x(along_y),
            ahead_z(velocity[0], z),
            ahead_z(velocity[1], z),
        )
        add_terms(0, z, (strain_x, strain_y, None) + sheared)
        dilated = medium[0][z] * (strain_x + strain_y)
        shear = medium[1][z]
        state[3][z] = narrowed(loads[0][z] + STEP * (dilated + 2.0 * shear * strain_x))
        state[4][z] = narrowed(loads[1][z] + STEP * (dilated + 2.0 * shear * strain_y))
        state[5][z] = narrowed(STEP * dilated)
        for number, strain in enumerate(sheared):
            state[6 + number][z] = narrowed(STEP * shear * strain)
    for turn in (1, 2):
        for part in range(2):
            for z in range(depth):
                load = later_ref[(2 * (turn - 1) + part) * depth + z]
                state[3 + part][z] = state[3 + part][z] + load
        advance(state, near, functools.partial(add_terms, turn), state if turn == 1 else None)


def shards(
    initial_state,
    lame_lambda,
    shear_modulus,
    buoyancy,
    source_cells,
    source_wavelet,
    segment_start,
    segment_weight,
    partial_owner,
    partial_channel,
    observed_data,
):
    depth, rows_x, cols_y = lame_lambda.shape
    part_count = segment_start.shape[0]
    count_x, count_y = lax.axis_size("gx"), lax.axis_size("gy")
    devices = count_x * count_y
    capacity = max(2, 2 * part_count // devices)
    slot_groups = devices * capacity // LANES
    blocks = part_count // LANES
    per_group = LANES // capacity
    cells_row = depth * rows_x
    both = ("gx", "gy")
    up = [(i, i + 1) for i in range(count_x - 1)]
    down = [(j, i) for i, j in up]
    shape = jax.ShapeDtypeStruct

    def exchange(chunks):
        return lax.all_to_all(chunks, both, split_axis=0, concat_axis=0, tiled=True)

    def to_owners(rows):
        chunks = rows.reshape(slot_groups, 4, per_group, capacity).transpose(0, 2, 1, 3)
        back = exchange(chunks.reshape(devices, 4, capacity)).reshape(slot_groups, per_group, 4, capacity)
        return back.transpose(0, 2, 1, 3).reshape(slot_groups * 4, LANES)

    trimmed = shape((14 * depth * RIM, cols_y), F32)
    fields, low, high, edges = call_kernel(
        pack_body,
        "pack_edges",
        [shape((14 * cells_row, cols_y), F32), trimmed, trimmed, shape((devices, 1, 2 * RIM * LANES), F32)],
        [
            pltpu.VMEM((14 * cells_row, cols_y), F32),
            pltpu.VMEM(trimmed.shape, F32),
            pltpu.VMEM(trimmed.shape, F32),
            pltpu.VMEM((2, 1, 2 * RIM * LANES), F32),
            pltpu.VMEM((1, source_cells.shape[0]), I32),
            pltpu.VMEM(source_wavelet.shape, F32),
            pltpu.SemaphoreType.DMA((6,)),
            pltpu.SemaphoreType.DMA((3,)),
            pltpu.SemaphoreType.DMA((6,)),
        ],
        *[values.reshape(-1, cols_y) for values in (initial_state, lame_lambda, shear_modulus, buoyancy)],
        source_cells.reshape(1, -1),
        source_wavelet,
        place=pl.ANY,
        place_out=pl.ANY,
        room=60 * 1024 * 1024,
    )
    lower = lax.ppermute(high, "gx", up)
    higher = lax.ppermute(low, "gx", down)
    rims = exchange(edges)
    channels = partial_channel.reshape(blocks, LANES)
    slot, row, cover, place = call_kernel(
        functools.partial(slots_body, capacity, devices, cols_y),
        "segment_slots",
        [
            shape((blocks, LANES), I32),
            shape((blocks, LANES), I32),
            shape((cols_y, part_count), BF16),
            shape((LANES, part_count), BF16),
        ],
        [pltpu.VMEM((blocks, LANES), F32)],
        partial_owner.reshape(blocks, LANES),
        segment_start.reshape(blocks, LANES),
    )
    partials, strains, medium = call_kernel(
        forward_body,
        "forward_run",
        [
            shape((slot_groups * 4, LANES), F32),
            shape((18 * cells_row, cols_y), F32),
            shape((3 * depth, SPAN_X, SPAN_Y), F32),
        ],
        [
            pltpu.VMEM((12 * depth, SPAN_X, SPAN_Y), F32),
            pltpu.VMEM((2 * depth, SPAN_NEAR, SPAN_Y), F32),
            pltpu.VMEM((9 * depth, SPAN_NEAR, SPAN_Y), F32),
            pltpu.VMEM((3 * depth, SPAN_NEAR, SPAN_Y), F32),
            pltpu.VMEM((LANES, 2 * LANES), F32),
            pltpu.VMEM((2, 14 * cells_row, cols_y), F32),
            pltpu.VMEM((3 * LANES, part_count), BF16),
        ],
        fields,
        higher,
        lower,
        rims,
        slot,
        row,
        segment_weight,
        channels,
        cover,
        place,
    )
    parts = observed_data.shape[1] // LANES
    residuals, reply = call_kernel(
        owner_body,
        "channel_sums",
        [shape(observed_data.shape, F32), shape((slot_groups * 4, LANES), F32)],
        [
            pltpu.VMEM((12 * parts, slot_groups * LANES), BF16),
            pltpu.VMEM((LANES, slot_groups * LANES), BF16),
            pltpu.VMEM((4 * parts, LANES), F32),
        ],
        to_owners(partials),
        observed_data,
    )
    loads, load_edges = call_kernel(
        load_body,
        "segment_loads",
        [shape((6 * cells_row, cols_y), F32), shape((devices, 1, RIM * LANES), F32)],
        [pltpu.VMEM((12 * cells_row, part_count), BF16), pltpu.VMEM((2, 1, RIM * LANES), F32)],
        to_owners(reply),
        slot,
        row,
        segment_weight,
        cover,
        place,
    )
    load_lower = lax.ppermute(loads, "gx", up)
    load_higher = lax.ppermute(loads, "gx", down)
    load_rims = exchange(load_edges)
    (gradients,) = call_kernel(
        adjoint_body,
        "adjoint_run",
        [shape((2 * cells_row, cols_y), F32)],
        [
            pltpu.VMEM((2 * depth, SPAN_X, SPAN_Y), F32),
            pltpu.VMEM((4 * depth, SPAN_NEAR, SPAN_Y), F32),
            pltpu.VMEM((2 * depth, SPAN_X, SPAN_Y), F32),
            pltpu.VMEM((9 * depth, SPAN_NEAR, SPAN_Y), F32),
            pltpu.VMEM((3 * depth, SPAN_NEAR, SPAN_Y), F32),
            pltpu.VMEM((LANES, LANES), F32),
        ],
        loads,
        load_higher,
        load_lower,
        load_rims,
        strains,
        medium,
    )
    return (residuals, gradients.reshape(2, depth, rows_x, cols_y))


def solution(mesh):
    in_specs = (
        P(None, None, "gx", "gy"),
        P(None, "gx", "gy"),
        P(None, "gx", "gy"),
        P(None, "gx", "gy"),
        P(("gx", "gy")),
        P(None, ("gx", "gy")),
        P(("gx", "gy")),
        P(None, ("gx", "gy")),
        P(("gx", "gy"), None),
        P(("gx", "gy")),
        P(None, ("gx", "gy")),
    )
    out_specs = (P(None, ("gx", "gy")), P(None, None, "gx", "gy"))
    return jax.shard_map(shards, mesh=mesh, in_specs=in_specs, out_specs=out_specs, check_vma=False)
```

```python
import functools

import jax
import jax.numpy as jnp
from jax import lax
from jax.experimental import pallas as pl
from jax.experimental.pallas import tpu as pltpu
from jax.sharding import PartitionSpec as P

GAUGE = 8
STEP = 0.25
RIM = 3
LANES = 128
TILE_X = 4
SPAN_X = 16
SPAN_NEAR = 8
SPAN_Y = 256
F32, BF16, I32 = jnp.float32, jnp.bfloat16, jnp.int32
NEAR = tuple((dx, dy) for dx in (-1, 0, 1) for dy in (-1, 0, 1))


def call_kernel(
    body, name, outs, scratch, *args, place=pltpu.VMEM, place_out=pltpu.VMEM, room=24 * 1024 * 1024
):
    spaces = place_out if isinstance(place_out, tuple) else (place_out,) * len(outs)
    return pl.pallas_call(
        body,
        name=name,
        out_shape=outs,
        in_specs=[pl.BlockSpec(memory_space=place)] * len(args),
        out_specs=[pl.BlockSpec(memory_space=space) for space in spaces],
        scratch_shapes=scratch,
        compiler_params=pltpu.CompilerParams(vmem_limit_bytes=room),
    )(*args)


def pieces(values):
    high = values.astype(BF16).astype(F32)
    rest = values - high
    middle = rest.astype(BF16).astype(F32)
    return high, middle, rest - middle


def iota(shape, dim):
    return lax.broadcasted_iota(I32, shape, dim)


def times(left, right):
    return lax.dot_general(left, right, (((1,), (0,)), ((), ())), preferred_element_type=F32)


def times_turned(left, right):
    return lax.dot_general(left, right, (((1,), (1,)), ((), ())), preferred_element_type=F32)


def packed_rows(row, height):
    tile = jnp.broadcast_to(row.astype(F32), (16, row.shape[1])).astype(BF16)
    return jnp.concatenate([tile] * (height // 16), axis=0) if height > 16 else tile


def packed_iota(height, shift=0):
    return (iota((height, LANES), 0) >> shift).astype(F32).astype(BF16)


def two_pieces(values):
    high = values.astype(BF16).astype(F32)
    return high, values - high


def sum_halves(values):
    half = values.shape[0] // 2
    return values[:half] + values[half:]


def sum_thirds(values):
    third = values.shape[0] // 3
    return values[:third] + values[third : 2 * third] + values[2 * third :]


def neighbour(dx, dy):
    count_x, count_y = lax.axis_size("gx"), lax.axis_size("gy")
    at_x, at_y = lax.axis_index("gx") + dx, lax.axis_index("gy") + dy
    inside = (at_x >= 0) & (at_x < count_x) & (at_y >= 0) & (at_y < count_y)
    return jnp.where(inside, at_x * count_y + at_y, 0), inside


def edge_columns(rows, side_ref):
    width = rows.shape[0]
    turned = rows.T
    for side, base in ((0, 0), (1, LANES - RIM)):
        for column in range(RIM):
            side_ref[side, 0:1, column * width : (column + 1) * width] = turned[base + column : base + column + 1, :]


def start_sides(side_ref, out_ref, sent):
    sides = []
    for number, (dx, dy) in enumerate((dx, dy) for dx, dy in NEAR if dy):
        index, inside = neighbour(dx, dy)
        source, target = side_ref.at[1 if dy > 0 else 0], out_ref.at[index]
        sides.append((inside, pltpu.make_async_copy(source, target, sent.at[number])))
    for inside, copy in sides:
        pl.when(inside)(copy.start)
    return sides


def wait_sides(sides):
    for inside, copy in sides:
        pl.when(inside)(copy.wait)


def arrived_chunk(recv_ref, dx, dy):
    index, inside = neighbour(dx, dy)
    return jnp.where(inside, recv_ref[index], 0.0)


def rim_rows(recv_ref, dx, turn_ref):
    width = turn_ref.shape[1]
    for dy, base in ((1, 0), (-1, LANES - RIM)):
        chunk = arrived_chunk(recv_ref, dx, dy)
        for column in range(RIM):
            turn_ref[base + column : base + column + 1, :] = chunk[:, column * width : (column + 1) * width]
    return turn_ref[...].T


def lay_planes(wide_ref, narrow_ref, lane, centre, higher, lower):
    row = iota((8, LANES), 0)
    wide = wide_ref.shape[0]
    lanes = slice(lane, lane + LANES)
    for plane in range(wide + narrow_ref.shape[0]):
        rows = slice(8 * (plane // 2), 8 * (plane // 2) + 8)
        mid, high, low = centre[rows], higher[rows], lower[rows]
        if plane % 2:
            mid = pltpu.roll(mid, TILE_X, 0)
        else:
            high, low = pltpu.roll(high, TILE_X, 0), pltpu.roll(low, TILE_X, 0)
        near = jnp.where(row < TILE_X, mid, high)
        if plane < wide:
            wide_ref[plane, 0:8, lanes] = near
            wide_ref[plane, 8:16, lanes] = jnp.where(row < TILE_X, 0.0, low)
        else:
            narrow_ref[plane - wide, :, lanes] = jnp.where(row < SPAN_NEAR - 2, near, low)


def narrowed(plane):
    row = iota((SPAN_NEAR, plane.shape[1]), 0)
    return jnp.where(row < SPAN_NEAR - 2, plane[:SPAN_NEAR], plane[SPAN_NEAR:])


def ahead_x(plane):
    return pltpu.roll(plane, plane.shape[0] - 1, 0) - plane


def behind_x(plane):
    return plane - pltpu.roll(plane, 1, 0)


def ahead_y(plane):
    return pltpu.roll(plane, SPAN_Y - 1, 1) - plane


def behind_y(plane):
    return plane - pltpu.roll(plane, 1, 1)


def ahead_z(planes, z):
    return planes[z + 1] - planes[z] if z + 1 < len(planes) else -planes[z]


def behind_z(planes, z):
    return planes[z] - planes[z - 1] if z else planes[z]


class Planes:
    def __init__(self, ref, first, depth):
        self.ref, self.first, self.depth = ref, first, depth

    def __len__(self):
        return self.depth

    def __getitem__(self, z):
        return self.ref[self.first + z]

    def __setitem__(self, z, plane):
        self.ref[self.first + z] = plane


def fields_of(ref, count, depth, first=0):
    return [Planes(ref, (first + number) * depth, depth) for number in range(count)]


def strain_rates(velocity, z):
    along_x, along_y, along_z = [field[z] for field in velocity]
    return (
        behind_x(along_x),
        behind_y(along_y),
        behind_z(velocity[2], z),
        ahead_y(along_x) + ahead_x(along_y),
        ahead_z(velocity[0], z) + ahead_x(along_z),
        ahead_z(velocity[1], z) + ahead_y(along_z),
    )


def new_stress(stress, strains, lame_lambda, shear_modulus, z):
    dilated = lame_lambda[z] * (strains[0] + strains[1] + strains[2])
    shear = shear_modulus[z]
    normal = [stress[n][z] + STEP * (dilated + 2.0 * shear * strains[n]) for n in range(3)]
    return normal + [stress[n][z] + STEP * shear * strains[n] for n in range(3, 6)]


def advance(state, medium, emit, target):
    velocity, stress = state[:3], state[3:]
    lame_lambda, shear_modulus, buoyancy = medium
    depth = len(buoyancy)
    wide = target is not None and target is not state
    for z in range(depth):
        scale = STEP * buoyancy[z]
        accel = (
            ahead_x(stress[0][z]) + behind_y(stress[3][z]) + behind_z(stress[4], z),
            behind_x(stress[3][z]) + ahead_y(stress[1][z]) + behind_z(stress[5], z),
            behind_x(stress[4][z]) + behind_y(stress[5][z]) + ahead_z(stress[2], z),
        )
        for number in range(3):
            moved = velocity[number][z] + scale * accel[number]
            velocity[number][z] = moved
            if wide:
                target[number][z] = narrowed(moved)
    for z in range(depth):
        strains = strain_rates(velocity, z)
        emit(z, strains)
        if target is not None:
            for number, plane in enumerate(new_stress(stress, strains, lame_lambda, shear_modulus, z)):
                target[3 + number][z] = narrowed(plane) if wide else plane


def pack_body(*refs):
    inputs, outputs, scratch = refs[:6], refs[6:10], refs[10:]
    fields_ref, high_ref, low_ref, side_ref, cells_ref, wavelet_ref, arrived, sent, sent_sides = scratch
    targets, at = [], 0
    for source in inputs[:4]:
        targets.append(fields_ref.at[at : at + source.shape[0]])
        at = at + source.shape[0]
    copies = [
        pltpu.make_async_copy(source, target, arrived.at[number])
        for number, (source, target) in enumerate(zip(inputs, targets + [cells_ref, wavelet_ref]))
    ]
    for copy in copies:
        copy.start()
    copies[4].wait()
    copies[5].wait()
    cells_row = inputs[1].shape[0]
    cells = cells_ref[...]
    count = cells.shape[1]
    at_lane = iota((LANES, count), 0) == (cells & (LANES - 1))
    at_row = iota((cells_row, count), 0) == (cells >> (LANES.bit_length() - 1))
    stack = [
        jnp.where(at_row, third[step : step + 1, :], 0.0) for third in pieces(wavelet_ref[...]) for step in range(3)
    ]
    maps = sum_thirds(
        times_turned(jnp.concatenate(stack, axis=0).astype(BF16), jnp.where(at_lane, 1.0, 0.0).astype(BF16))
    )
    for copy in copies[:4]:
        copy.wait()
    fields_ref[at:, :] = maps[cells_row:]
    for number in range(3, 6):
        rows = slice(number * cells_row, (number + 1) * cells_row)
        fields_ref[rows, :] = fields_ref[rows, :] + maps[:cells_row]
    height = fields_ref.shape[0] // TILE_X
    for x in range(TILE_X):
        slab = fields_ref[pl.ds(x, height, stride=TILE_X), :]
        if x < RIM:
            low_ref[x * height : (x + 1) * height, :] = slab
        if x >= TILE_X - RIM:
            at = x - TILE_X + RIM
            high_ref[at * height : (at + 1) * height, :] = slab
    writes = [
        pltpu.make_async_copy(source, target, sent.at[number])
        for number, (source, target) in enumerate(zip((fields_ref, high_ref, low_ref), outputs))
    ]
    for copy in writes:
        copy.start()
    rows = fields_ref[...]
    spare = 2 * LANES - rows.shape[0]
    edge_columns(jnp.concatenate([rows, jnp.zeros((spare, LANES), F32)], axis=0), side_ref)
    sides = start_sides(side_ref, outputs[3], sent_sides)
    for copy in writes:
        copy.wait()
    wait_sides(sides)


def slots_body(capacity, devices, cols_y, owner_ref, start_ref, slot_ref, row_ref, cover_ref, place_ref, rank_ref):
    blocks = owner_ref.shape[0]
    group = 32
    before = jnp.where(iota((LANES, 2 * LANES), 0) < iota((LANES, 2 * LANES), 1), 1.0, 0.0).astype(BF16)
    rank_ref[...] = jnp.zeros_like(rank_ref)

    def count_group(number, carry):
        names = iota((group, LANES), 0) + number * group
        hot = [names == owner_ref[b : b + 1, :] for b in range(blocks)]
        marks = jnp.concatenate([jnp.where(h, 1.0, 0.0) for h in hot], axis=0).astype(BF16)
        counts = times(marks, before)
        total = jnp.zeros((group, LANES), F32)
        for b in range(blocks):
            part = counts[b * group : (b + 1) * group]
            rank_ref[b : b + 1, :] = rank_ref[b : b + 1, :] + jnp.sum(
                jnp.where(hot[b], part[:, :LANES] + total, 0.0), axis=0, keepdims=True
            )
            total = total + part[:, LANES:]
        return carry

    if devices == group:
        count_group(0, 0)
    else:
        lax.fori_loop(0, devices // group, count_group, 0)
    slot = owner_ref[...] * capacity + rank_ref[...].astype(I32)
    slot_ref[...] = slot >> 7
    low = slot & (LANES - 1)
    span = cols_y - GAUGE + 1
    start = start_ref[...]
    row = ((start.astype(F32) + 0.5) * (1.0 / span)).astype(I32)
    row_ref[...] = row
    first = start - row * span
    down = iota((LANES, LANES), 0)
    for b in range(blocks):
        lanes = slice(b * LANES, (b + 1) * LANES)
        offset = down - first[b : b + 1, :]
        cover_ref[:, lanes] = jnp.where((offset >= 0) & (offset < GAUGE), 1.0, 0.0).astype(BF16)
        place_ref[:, lanes] = jnp.where(down == low[b : b + 1, :], 1.0, 0.0).astype(BF16)


def forward_body(
    fields_ref,
    lower_ref,
    higher_ref,
    recv_ref,
    slot_ref,
    row_ref,
    weight_ref,
    channel_ref,
    cover_ref,
    place_ref,
    out_ref,
    strain_ref,
    medium_ref,
    wide_ref,
    source_ref,
    state_ref,
    near_ref,
    turn_ref,
    sides_ref,
    spread_ref,
):
    depth = medium_ref.shape[0] // 3
    cells_row = depth * TILE_X
    turn_ref[...] = jnp.zeros_like(turn_ref)
    rims = [rim_rows(recv_ref, dx, turn_ref) for dx in (0, 1, -1)]
    height = fields_ref.shape[0] // TILE_X
    sides_ref[...] = jnp.zeros_like(sides_ref)
    for x in range(RIM):
        slab = slice(x * height, (x + 1) * height)
        sides_ref[0, pl.ds(x, height, stride=TILE_X), :] = higher_ref[slab, :]
        sides_ref[1, pl.ds(x + TILE_X - RIM, height, stride=TILE_X), :] = lower_ref[slab, :]
    lay_planes(wide_ref, source_ref, 0, fields_ref, sides_ref.at[0], sides_ref.at[1])
    lay_planes(wide_ref, source_ref, LANES, *rims)
    first = 9 * depth
    medium_ref[...] = wide_ref[first:]
    for plane in range(3 * depth):
        near_ref[plane] = narrowed(wide_ref[first + plane])
    state, near = fields_of(state_ref, 9, depth), fields_of(near_ref, 3, depth)
    for step in range(3):

        def emit(z, strains, step=step):
            for number, strain in enumerate(strains):
                base = ((step * 6 + number) * depth + z) * TILE_X
                strain_ref[base : base + TILE_X, :] = strain[0:TILE_X, 0:LANES]

        if step == 0:
            advance(fields_of(wide_ref, 9, depth), fields_of(wide_ref, 3, depth, 9), emit, state)
            continue
        for z in range(depth):
            load = source_ref[(step - 1) * depth + z]
            for number in range(3, 6):
                state[number][z] = state[number][z] + load
        advance(state, near, emit, state if step == 1 else None)
    axial = jnp.concatenate(
        [strain_ref[step * 6 * cells_row : (step * 6 + 2) * cells_row, :] for step in range(3)], axis=0
    )
    axial = jnp.concatenate(pieces(axial), axis=0).astype(BF16)
    rows_down = iota((cells_row, LANES), 0)
    slots_down = packed_iota(LANES, 2)
    for block in range(slot_ref.shape[0]):
        lanes = slice(block * LANES, (block + 1) * LANES)
        if block % 2 == 0:
            both = sum_thirds(times(axial, cover_ref[:, block * LANES : (block + 2) * LANES]))
        windows = both[:, :LANES] if block % 2 == 0 else both[:, LANES:]
        at_row = rows_down == row_ref[block : block + 1, :]
        weight_x, weight_y = weight_ref[0:1, lanes], weight_ref[1:2, lanes]
        sums = []
        for step in range(3):
            base = 2 * step * cells_row
            axial_sum = (
                weight_x * windows[base : base + cells_row]
                + weight_y * windows[base + cells_row : base + 2 * cells_row]
            )
            sums.append(jnp.sum(jnp.where(at_row, axial_sum, 0.0), axis=0, keepdims=True))
        sums.append(channel_ref[block : block + 1, :].astype(F32))
        values = jnp.concatenate(sums + sums, axis=0)
        in_slot = slots_down == packed_rows(slot_ref[block : block + 1, :], LANES)
        for third, piece in enumerate(pieces(values)):
            tile = jnp.concatenate([piece, piece], axis=0).astype(BF16)
            spread_ref[third * LANES : (third + 1) * LANES, lanes] = jnp.where(
                in_slot, jnp.concatenate([tile] * (LANES // 16), axis=0), jnp.zeros((), BF16)
            )
    out_ref[...] = sum_thirds(times_turned(spread_ref[...], place_ref[...]))


def owner_body(arrived_ref, observed_ref, residual_ref, reply_ref, values_ref, place_ref, held_ref):
    groups = arrived_ref.shape[0] // 4
    parts = observed_ref.shape[1] // LANES
    down = packed_iota(LANES)
    part_down = iota((parts, LANES), 0)
    nothing = jnp.zeros((parts, LANES), F32)
    numbers = [arrived_ref[4 * s + 3 : 4 * s + 4, :].astype(I32) for s in range(groups)]
    for s in range(groups):
        lanes = slice(s * LANES, (s + 1) * LANES)
        place_ref[:, lanes] = jnp.where(
            down == packed_rows(numbers[s] & (LANES - 1), LANES), jnp.ones((), BF16), jnp.zeros((), BF16)
        )
        at_part = part_down == (numbers[s] >> 7)
        thirds = pieces(arrived_ref[4 * s : 4 * s + 3, :])
        stack = []
        for third in thirds:
            for step in range(3):
                stack.append(jnp.where(at_part, third[step : step + 1, :], 0.0))
            stack.append(nothing)
        values_ref[:, lanes] = jnp.concatenate(stack, axis=0).astype(BF16)
    sums = sum_thirds(times_turned(values_ref[...], place_ref[...]))
    for step in range(3):
        for part in range(parts):
            at = step * parts + part
            held_ref[at : at + 1, :] = observed_ref[step : step + 1, part * LANES : (part + 1) * LANES]
    held_ref[3 * parts :, :] = nothing
    held_ref[...] = sums - held_ref[...]
    for step in range(3):
        for part in range(parts):
            at = step * parts + part
            residual_ref[step : step + 1, part * LANES : (part + 1) * LANES] = held_ref[at : at + 1, :]
    residual = jnp.concatenate(two_pieces(held_ref[...]), axis=0).astype(BF16)
    for s in range(groups):
        if s % 2 == 0:
            both = sum_halves(times(residual, place_ref[:, s * LANES : (s + 2) * LANES]))
        found = both[:, :LANES] if s % 2 == 0 else both[:, LANES:]
        at_part = part_down == (numbers[s] >> 7)
        for step in range(3):
            reply_ref[4 * s + step : 4 * s + step + 1, :] = jnp.sum(
                jnp.where(at_part, found[step * parts : (step + 1) * parts], 0.0), axis=0, keepdims=True
            )
        reply_ref[4 * s + 3 : 4 * s + 4, :] = jnp.zeros((1, LANES), F32)


def load_body(
    arrived_ref,
    slot_ref,
    row_ref,
    weight_ref,
    cover_ref,
    place_ref,
    load_ref,
    out_ref,
    spread_ref,
    side_ref,
    sent_sides,
):
    cells_row = load_ref.shape[0] // 6
    stack_rows = load_ref.shape[0]
    arrived = jnp.concatenate(two_pieces(arrived_ref[...]), axis=0).astype(BF16)
    slots_down = iota((LANES, LANES), 0) >> 2
    rows_down = packed_iota(cells_row)
    for block in range(slot_ref.shape[0]):
        lanes = slice(block * LANES, (block + 1) * LANES)
        if block % 2 == 0:
            both = sum_halves(times(arrived, place_ref[:, block * LANES : (block + 2) * LANES]))
        found = both[:, :LANES] if block % 2 == 0 else both[:, LANES:]
        found = jnp.where(slots_down == slot_ref[block : block + 1, :], found, 0.0)
        folded = found[0:8]
        for part in range(1, LANES // 8):
            folded = folded + found[8 * part : 8 * part + 8]
        folded = folded + pltpu.roll(folded, 4, 0)
        at_row = rows_down == packed_rows(row_ref[block : block + 1, :], cells_row)
        for turn in range(3):
            back = folded[2 - turn : 3 - turn, :]
            for part in range(2):
                for half, piece in enumerate(two_pieces(weight_ref[part : part + 1, lanes] * back)):
                    base = half * stack_rows + (2 * turn + part) * cells_row
                    spread_ref[base : base + cells_row, lanes] = jnp.where(
                        at_row, packed_rows(piece, cells_row), jnp.zeros((), BF16)
                    )
    cover = jnp.concatenate([cover_ref[0:16, :], cover_ref[LANES - 16 :, :]], axis=0)
    edges = times_turned(cover, spread_ref[0:stack_rows, :]) + times_turned(cover, spread_ref[stack_rows:, :])
    side_ref[...] = jnp.zeros_like(side_ref)
    for side, base in ((0, 0), (1, 32 - RIM)):
        for column in range(RIM):
            lanes = slice(column * LANES, column * LANES + stack_rows)
            side_ref[side, 0:1, lanes] = edges[base + column : base + column + 1, :]
    sides = start_sides(side_ref, out_ref, sent_sides)
    load_ref[...] = sum_halves(times_turned(spread_ref[...], cover_ref[...]))
    wait_sides(sides)


def adjoint_body(
    load_ref,
    higher_ref,
    lower_ref,
    recv_ref,
    strain_ref,
    medium_ref,
    gradient_ref,
    first_ref,
    later_ref,
    velocity_ref,
    state_ref,
    near_ref,
    turn_ref,
):
    depth = medium_ref.shape[0] // 3
    turn_ref[...] = jnp.zeros_like(turn_ref)
    rims = [rim_rows(recv_ref, dx, turn_ref) for dx in (0, 1, -1)]
    lay_planes(first_ref, later_ref, 0, load_ref, higher_ref, lower_ref)
    lay_planes(first_ref, later_ref, LANES, *rims)
    for plane in range(3 * depth):
        near_ref[plane] = narrowed(medium_ref[plane])
    gradient_ref[...] = jnp.zeros_like(gradient_ref)
    state, near, medium = (
        fields_of(state_ref, 9, depth),
        fields_of(near_ref, 3, depth),
        fields_of(medium_ref, 3, depth),
    )

    def add_terms(turn, z, strains):
        dilation, dilation_back, doubled, product = None, None, None, None
        for number, strain in enumerate(strains):
            base = (((2 - turn) * 6 + number) * depth + z) * TILE_X
            forward = strain_ref[base : base + TILE_X, :]
            if number < 3:
                dilation = forward if dilation is None else dilation + forward
            if strain is None:
                continue
            back = strain[0:TILE_X, 0:LANES]
            term = forward * back
            if number < 3:
                dilation_back = back if dilation_back is None else dilation_back + back
                doubled = term if doubled is None else doubled + term
            else:
                product = term if product is None else product + term
        for part, term in enumerate((dilation * dilation_back, 2.0 * doubled + product)):
            base = (part * depth + z) * TILE_X
            gradient_ref[base : base + TILE_X, :] = gradient_ref[base : base + TILE_X, :] + term

    loads, velocity = fields_of(first_ref, 2, depth), fields_of(velocity_ref, 2, depth)
    for z in range(depth):
        scale = STEP * medium[2][z]
        velocity[0][z] = scale * ahead_x(loads[0][z])
        velocity[1][z] = scale * ahead_y(loads[1][z])
        state[0][z] = narrowed(velocity[0][z])
        state[1][z] = narrowed(velocity[1][z])
        state[2][z] = jnp.zeros((SPAN_NEAR, SPAN_Y), F32)
    for z in range(depth):
        along_x, along_y = velocity[0][z], velocity[1][z]
        strain_x, strain_y = behind_x(along_x), behind_y(along_y)
        sheared = (
            ahead_y(along_x) + ahead_x(along_y),
            ahead_z(velocity[0], z),
            ahead_z(velocity[1], z),
        )
        add_terms(0, z, (strain_x, strain_y, None) + sheared)
        dilated = medium[0][z] * (strain_x + strain_y)
        shear = medium[1][z]
        state[3][z] = narrowed(loads[0][z] + STEP * (dilated + 2.0 * shear * strain_x))
        state[4][z] = narrowed(loads[1][z] + STEP * (dilated + 2.0 * shear * strain_y))
        state[5][z] = narrowed(STEP * dilated)
        for number, strain in enumerate(sheared):
            state[6 + number][z] = narrowed(STEP * shear * strain)
    for turn in (1, 2):
        for part in range(2):
            for z in range(depth):
                load = later_ref[(2 * (turn - 1) + part) * depth + z]
                state[3 + part][z] = state[3 + part][z] + load
        advance(state, near, functools.partial(add_terms, turn), state if turn == 1 else None)


def shards(
    initial_state,
    lame_lambda,
    shear_modulus,
    buoyancy,
    source_cells,
    source_wavelet,
    segment_start,
    segment_weight,
    partial_owner,
    partial_channel,
    observed_data,
):
    depth, rows_x, cols_y = lame_lambda.shape
    part_count = segment_start.shape[0]
    count_x, count_y = lax.axis_size("gx"), lax.axis_size("gy")
    devices = count_x * count_y
    capacity = max(2, 2 * part_count // devices)
    slot_groups = devices * capacity // LANES
    blocks = part_count // LANES
    per_group = LANES // capacity
    cells_row = depth * rows_x
    both = ("gx", "gy")
    up = [(i, i + 1) for i in range(count_x - 1)]
    down = [(j, i) for i, j in up]
    shape = jax.ShapeDtypeStruct

    def exchange(chunks):
        return lax.all_to_all(chunks, both, split_axis=0, concat_axis=0, tiled=True)

    def to_owners(rows):
        chunks = rows.reshape(slot_groups, 4, per_group, capacity).transpose(0, 2, 1, 3)
        back = exchange(chunks.reshape(devices, 4, capacity)).reshape(slot_groups, per_group, 4, capacity)
        return back.transpose(0, 2, 1, 3).reshape(slot_groups * 4, LANES)

    trimmed = shape((14 * depth * RIM, cols_y), F32)
    fields, high, low, edges = call_kernel(
        pack_body,
        "pack_edges",
        [shape((14 * cells_row, cols_y), F32), trimmed, trimmed, shape((devices, 1, 2 * RIM * LANES), F32)],
        [
            pltpu.VMEM((14 * cells_row, cols_y), F32),
            pltpu.VMEM(trimmed.shape, F32),
            pltpu.VMEM(trimmed.shape, F32),
            pltpu.VMEM((2, 1, 2 * RIM * LANES), F32),
            pltpu.VMEM((1, source_cells.shape[0]), I32),
            pltpu.VMEM(source_wavelet.shape, F32),
            pltpu.SemaphoreType.DMA((6,)),
            pltpu.SemaphoreType.DMA((3,)),
            pltpu.SemaphoreType.DMA((6,)),
        ],
        *[values.reshape(-1, cols_y) for values in (initial_state, lame_lambda, shear_modulus, buoyancy)],
        source_cells.reshape(1, -1),
        source_wavelet,
        place=pl.ANY,
        place_out=pl.ANY,
        room=60 * 1024 * 1024,
    )
    lower = lax.ppermute(high, "gx", up)
    higher = lax.ppermute(low, "gx", down)
    rims = exchange(edges)
    channels = partial_channel.reshape(blocks, LANES)
    slot, row, cover, place = call_kernel(
        functools.partial(slots_body, capacity, devices, cols_y),
        "segment_slots",
        [
            shape((blocks, LANES), I32),
            shape((blocks, LANES), I32),
            shape((cols_y, part_count), BF16),
            shape((LANES, part_count), BF16),
        ],
        [pltpu.VMEM((blocks, LANES), F32)],
        partial_owner.reshape(blocks, LANES),
        segment_start.reshape(blocks, LANES),
    )
    partials, strains, medium = call_kernel(
        forward_body,
        "forward_run",
        [
            shape((slot_groups * 4, LANES), F32),
            shape((18 * cells_row, cols_y), F32),
            shape((3 * depth, SPAN_X, SPAN_Y), F32),
        ],
        [
            pltpu.VMEM((12 * depth, SPAN_X, SPAN_Y), F32),
            pltpu.VMEM((2 * depth, SPAN_NEAR, SPAN_Y), F32),
            pltpu.VMEM((9 * depth, SPAN_NEAR, SPAN_Y), F32),
            pltpu.VMEM((3 * depth, SPAN_NEAR, SPAN_Y), F32),
            pltpu.VMEM((LANES, 2 * LANES), F32),
            pltpu.VMEM((2, 14 * cells_row, cols_y), F32),
            pltpu.VMEM((3 * LANES, part_count), BF16),
        ],
        fields,
        lower,
        higher,
        rims,
        slot,
        row,
        segment_weight,
        channels,
        cover,
        place,
    )
    parts = observed_data.shape[1] // LANES
    residuals, reply = call_kernel(
        owner_body,
        "channel_sums",
        [shape(observed_data.shape, F32), shape((slot_groups * 4, LANES), F32)],
        [
            pltpu.VMEM((12 * parts, slot_groups * LANES), BF16),
            pltpu.VMEM((LANES, slot_groups * LANES), BF16),
            pltpu.VMEM((4 * parts, LANES), F32),
        ],
        to_owners(partials),
        observed_data,
    )
    loads, load_edges = call_kernel(
        load_body,
        "segment_loads",
        [shape((6 * cells_row, cols_y), F32), shape((devices, 1, RIM * LANES), F32)],
        [
            pltpu.VMEM((12 * cells_row, part_count), BF16),
            pltpu.VMEM((2, 1, RIM * LANES), F32),
            pltpu.SemaphoreType.DMA((6,)),
        ],
        to_owners(reply),
        slot,
        row,
        segment_weight,
        cover,
        place,
        place_out=(pltpu.VMEM, pl.ANY),
    )
    load_lower = lax.ppermute(loads, "gx", up)
    load_higher = lax.ppermute(loads, "gx", down)
    load_rims = exchange(load_edges)
    (gradients,) = call_kernel(
        adjoint_body,
        "adjoint_run",
        [shape((2 * cells_row, cols_y), F32)],
        [
            pltpu.VMEM((2 * depth, SPAN_X, SPAN_Y), F32),
            pltpu.VMEM((4 * depth, SPAN_NEAR, SPAN_Y), F32),
            pltpu.VMEM((2 * depth, SPAN_X, SPAN_Y), F32),
            pltpu.VMEM((9 * depth, SPAN_NEAR, SPAN_Y), F32),
            pltpu.VMEM((3 * depth, SPAN_NEAR, SPAN_Y), F32),
            pltpu.VMEM((LANES, LANES), F32),
        ],
        loads,
        load_higher,
        load_lower,
        load_rims,
        strains,
        medium,
    )
    return (residuals, gradients.reshape(2, depth, rows_x, cols_y))


def solution(mesh):
    in_specs = (
        P(None, None, "gx", "gy"),
        P(None, "gx", "gy"),
        P(None, "gx", "gy"),
        P(None, "gx", "gy"),
        P(("gx", "gy")),
        P(None, ("gx", "gy")),
        P(("gx", "gy")),
        P(None, ("gx", "gy")),
        P(("gx", "gy"), None),
        P(("gx", "gy")),
        P(None, ("gx", "gy")),
    )
    out_specs = (P(None, ("gx", "gy")), P(None, None, "gx", "gy"))
    return jax.shard_map(shards, mesh=mesh, in_specs=in_specs, out_specs=out_specs, check_vma=False)
```

```python
import functools

import jax
import jax.numpy as jnp
from jax import lax
from jax.experimental import pallas as pl
from jax.experimental.pallas import tpu as pltpu
from jax.sharding import PartitionSpec as P

GAUGE = 8
STEP = 0.25
RIM = 3
LANES = 128
TILE_X = 4
SPAN_X = 16
SPAN_NEAR = 8
SPAN_Y = 256
F32, BF16, I32 = jnp.float32, jnp.bfloat16, jnp.int32
NEAR = tuple((dx, dy) for dx in (-1, 0, 1) for dy in (-1, 0, 1))


def call_kernel(
    body, name, outs, scratch, *args, place=pltpu.VMEM, place_out=pltpu.VMEM, room=24 * 1024 * 1024
):
    spaces = place_out if isinstance(place_out, tuple) else (place_out,) * len(outs)
    return pl.pallas_call(
        body,
        name=name,
        out_shape=outs,
        in_specs=[pl.BlockSpec(memory_space=place)] * len(args),
        out_specs=[pl.BlockSpec(memory_space=space) for space in spaces],
        scratch_shapes=scratch,
        compiler_params=pltpu.CompilerParams(vmem_limit_bytes=room),
    )(*args)


def pieces(values):
    high = values.astype(BF16).astype(F32)
    rest = values - high
    middle = rest.astype(BF16).astype(F32)
    return high, middle, rest - middle


def iota(shape, dim):
    return lax.broadcasted_iota(I32, shape, dim)


def times(left, right):
    return lax.dot_general(left, right, (((1,), (0,)), ((), ())), preferred_element_type=F32)


def times_turned(left, right):
    return lax.dot_general(left, right, (((1,), (1,)), ((), ())), preferred_element_type=F32)


def packed_rows(row, height):
    tile = jnp.broadcast_to(row.astype(F32), (16, row.shape[1])).astype(BF16)
    return jnp.concatenate([tile] * (height // 16), axis=0) if height > 16 else tile


def packed_iota(height, shift=0):
    return (iota((height, LANES), 0) >> shift).astype(F32).astype(BF16)


def two_pieces(values):
    high = values.astype(BF16).astype(F32)
    return high, values - high


def sum_halves(values):
    half = values.shape[0] // 2
    return values[:half] + values[half:]


def sum_thirds(values):
    third = values.shape[0] // 3
    return values[:third] + values[third : 2 * third] + values[2 * third :]


def neighbour(dx, dy):
    count_x, count_y = lax.axis_size("gx"), lax.axis_size("gy")
    at_x, at_y = lax.axis_index("gx") + dx, lax.axis_index("gy") + dy
    inside = (at_x >= 0) & (at_x < count_x) & (at_y >= 0) & (at_y < count_y)
    return jnp.where(inside, at_x * count_y + at_y, 0), inside


def edge_columns(rows, side_ref):
    width = rows.shape[0]
    turned = rows.T
    for side, base in ((0, 0), (1, LANES - RIM)):
        for column in range(RIM):
            side_ref[side, 0:1, column * width : (column + 1) * width] = turned[base + column : base + column + 1, :]


def start_sides(side_ref, out_ref, sent):
    sides = []
    for number, (dx, dy) in enumerate((dx, dy) for dx, dy in NEAR if dy):
        index, inside = neighbour(dx, dy)
        source, target = side_ref.at[1 if dy > 0 else 0], out_ref.at[index]
        sides.append((inside, pltpu.make_async_copy(source, target, sent.at[number])))
    for inside, copy in sides:
        pl.when(inside)(copy.start)
    return sides


def wait_sides(sides):
    for inside, copy in sides:
        pl.when(inside)(copy.wait)


def arrived_chunk(recv_ref, dx, dy):
    index, inside = neighbour(dx, dy)
    return jnp.where(inside, recv_ref[index], 0.0)


def rim_rows(recv_ref, dx, turn_ref):
    width = turn_ref.shape[1]
    for dy, base in ((1, 0), (-1, LANES - RIM)):
        chunk = arrived_chunk(recv_ref, dx, dy)
        for column in range(RIM):
            turn_ref[base + column : base + column + 1, :] = chunk[:, column * width : (column + 1) * width]
    return turn_ref[...].T


def lay_planes(wide_ref, narrow_ref, lane, centre, higher, lower):
    row = iota((8, LANES), 0)
    wide = wide_ref.shape[0]
    lanes = slice(lane, lane + LANES)
    for plane in range(wide + narrow_ref.shape[0]):
        rows = slice(8 * (plane // 2), 8 * (plane // 2) + 8)
        mid, high, low = centre[rows], higher[rows], lower[rows]
        if plane % 2:
            mid = pltpu.roll(mid, TILE_X, 0)
        else:
            high, low = pltpu.roll(high, TILE_X, 0), pltpu.roll(low, TILE_X, 0)
        near = jnp.where(row < TILE_X, mid, high)
        if plane < wide:
            wide_ref[plane, 0:8, lanes] = near
            wide_ref[plane, 8:16, lanes] = jnp.where(row < TILE_X, 0.0, low)
        else:
            narrow_ref[plane - wide, :, lanes] = jnp.where(row < SPAN_NEAR - 2, near, low)


def narrowed(plane):
    row = iota((SPAN_NEAR, plane.shape[1]), 0)
    return jnp.where(row < SPAN_NEAR - 2, plane[:SPAN_NEAR], plane[SPAN_NEAR:])


def ahead_x(plane):
    return pltpu.roll(plane, plane.shape[0] - 1, 0) - plane


def behind_x(plane):
    return plane - pltpu.roll(plane, 1, 0)


def ahead_y(plane):
    return pltpu.roll(plane, SPAN_Y - 1, 1) - plane


def behind_y(plane):
    return plane - pltpu.roll(plane, 1, 1)


def ahead_z(planes, z):
    return planes[z + 1] - planes[z] if z + 1 < len(planes) else -planes[z]


def behind_z(planes, z):
    return planes[z] - planes[z - 1] if z else planes[z]


class Planes:
    def __init__(self, ref, first, depth):
        self.ref, self.first, self.depth = ref, first, depth

    def __len__(self):
        return self.depth

    def __getitem__(self, z):
        return self.ref[self.first + z]

    def __setitem__(self, z, plane):
        self.ref[self.first + z] = plane


def fields_of(ref, count, depth, first=0):
    return [Planes(ref, (first + number) * depth, depth) for number in range(count)]


def strain_rates(velocity, z):
    along_x, along_y, along_z = [field[z] for field in velocity]
    return (
        behind_x(along_x),
        behind_y(along_y),
        behind_z(velocity[2], z),
        ahead_y(along_x) + ahead_x(along_y),
        ahead_z(velocity[0], z) + ahead_x(along_z),
        ahead_z(velocity[1], z) + ahead_y(along_z),
    )


def new_stress(stress, strains, lame_lambda, shear_modulus, z):
    dilated = lame_lambda[z] * (strains[0] + strains[1] + strains[2])
    shear = shear_modulus[z]
    normal = [stress[n][z] + STEP * (dilated + 2.0 * shear * strains[n]) for n in range(3)]
    return normal + [stress[n][z] + STEP * shear * strains[n] for n in range(3, 6)]


def advance(state, medium, emit, target):
    velocity, stress = state[:3], state[3:]
    lame_lambda, shear_modulus, buoyancy = medium
    depth = len(buoyancy)
    wide = target is not None and target is not state
    for z in range(depth):
        scale = STEP * buoyancy[z]
        accel = (
            ahead_x(stress[0][z]) + behind_y(stress[3][z]) + behind_z(stress[4], z),
            behind_x(stress[3][z]) + ahead_y(stress[1][z]) + behind_z(stress[5], z),
            behind_x(stress[4][z]) + behind_y(stress[5][z]) + ahead_z(stress[2], z),
        )
        for number in range(3):
            moved = velocity[number][z] + scale * accel[number]
            velocity[number][z] = moved
            if wide:
                target[number][z] = narrowed(moved)
    for z in range(depth):
        strains = strain_rates(velocity, z)
        emit(z, strains)
        if target is not None:
            for number, plane in enumerate(new_stress(stress, strains, lame_lambda, shear_modulus, z)):
                target[3 + number][z] = narrowed(plane) if wide else plane


def pack_body(*refs):
    inputs, outputs, scratch = refs[:6], refs[6:10], refs[10:]
    fields_ref, high_ref, low_ref, side_ref, cells_ref, wavelet_ref, arrived, sent, sent_sides = scratch
    targets, at = [], 0
    for source in inputs[:4]:
        targets.append(fields_ref.at[at : at + source.shape[0]])
        at = at + source.shape[0]
    copies = [
        pltpu.make_async_copy(source, target, arrived.at[number])
        for number, (source, target) in enumerate(zip(inputs, targets + [cells_ref, wavelet_ref]))
    ]
    for copy in copies:
        copy.start()
    copies[4].wait()
    copies[5].wait()
    cells_row = inputs[1].shape[0]
    cells = cells_ref[...]
    count = cells.shape[1]
    at_lane = iota((LANES, count), 0) == (cells & (LANES - 1))
    at_row = iota((cells_row, count), 0) == (cells >> (LANES.bit_length() - 1))
    stack = [
        jnp.where(at_row, third[step : step + 1, :], 0.0) for third in pieces(wavelet_ref[...]) for step in range(3)
    ]
    maps = sum_thirds(
        times_turned(jnp.concatenate(stack, axis=0).astype(BF16), jnp.where(at_lane, 1.0, 0.0).astype(BF16))
    )
    for copy in copies[:4]:
        copy.wait()
    fields_ref[at:, :] = maps[cells_row:]
    for number in range(3, 6):
        rows = slice(number * cells_row, (number + 1) * cells_row)
        fields_ref[rows, :] = fields_ref[rows, :] + maps[:cells_row]
    height = fields_ref.shape[0] // TILE_X
    for x in range(TILE_X):
        slab = fields_ref[pl.ds(x, height, stride=TILE_X), :]
        if x < RIM:
            low_ref[x * height : (x + 1) * height, :] = slab
        if x >= TILE_X - RIM:
            at = x - TILE_X + RIM
            high_ref[at * height : (at + 1) * height, :] = slab
    writes = [
        pltpu.make_async_copy(source, target, sent.at[number])
        for number, (source, target) in enumerate(zip((fields_ref, high_ref, low_ref), outputs))
    ]
    for copy in writes:
        copy.start()
    rows = fields_ref[...]
    spare = 2 * LANES - rows.shape[0]
    edge_columns(jnp.concatenate([rows, jnp.zeros((spare, LANES), F32)], axis=0), side_ref)
    sides = start_sides(side_ref, outputs[3], sent_sides)
    for copy in writes:
        copy.wait()
    wait_sides(sides)


def slots_body(capacity, devices, cols_y, owner_ref, start_ref, slot_ref, row_ref, cover_ref, place_ref, rank_ref):
    blocks = owner_ref.shape[0]
    group = 32
    before = jnp.where(iota((LANES, 2 * LANES), 0) < iota((LANES, 2 * LANES), 1), 1.0, 0.0).astype(BF16)
    rank_ref[...] = jnp.zeros_like(rank_ref)

    def count_group(number, carry):
        names = iota((group, LANES), 0) + number * group
        hot = [names == owner_ref[b : b + 1, :] for b in range(blocks)]
        marks = jnp.concatenate([jnp.where(h, 1.0, 0.0) for h in hot], axis=0).astype(BF16)
        counts = times(marks, before)
        total = jnp.zeros((group, LANES), F32)
        for b in range(blocks):
            part = counts[b * group : (b + 1) * group]
            rank_ref[b : b + 1, :] = rank_ref[b : b + 1, :] + jnp.sum(
                jnp.where(hot[b], part[:, :LANES] + total, 0.0), axis=0, keepdims=True
            )
            total = total + part[:, LANES:]
        return carry

    if devices == group:
        count_group(0, 0)
    else:
        lax.fori_loop(0, devices // group, count_group, 0)
    slot = owner_ref[...] * capacity + rank_ref[...].astype(I32)
    slot_ref[...] = slot >> 7
    low = slot & (LANES - 1)
    span = cols_y - GAUGE + 1
    start = start_ref[...]
    row = ((start.astype(F32) + 0.5) * (1.0 / span)).astype(I32)
    row_ref[...] = row
    first = start - row * span
    down = iota((LANES, LANES), 0)
    for b in range(blocks):
        lanes = slice(b * LANES, (b + 1) * LANES)
        offset = down - first[b : b + 1, :]
        cover_ref[:, lanes] = jnp.where((offset >= 0) & (offset < GAUGE), 1.0, 0.0).astype(BF16)
        place_ref[:, lanes] = jnp.where(down == low[b : b + 1, :], 1.0, 0.0).astype(BF16)


def forward_body(
    fields_ref,
    lower_ref,
    higher_ref,
    recv_ref,
    slot_ref,
    row_ref,
    weight_ref,
    channel_ref,
    cover_ref,
    place_ref,
    out_ref,
    strain_ref,
    medium_ref,
    wide_ref,
    source_ref,
    state_ref,
    near_ref,
    turn_ref,
    sides_ref,
    spread_ref,
):
    depth = medium_ref.shape[0] // 3
    cells_row = depth * TILE_X
    turn_ref[...] = jnp.zeros_like(turn_ref)
    rims = [rim_rows(recv_ref, dx, turn_ref) for dx in (0, 1, -1)]
    height = fields_ref.shape[0] // TILE_X
    sides_ref[...] = jnp.zeros_like(sides_ref)
    for x in range(RIM):
        slab = slice(x * height, (x + 1) * height)
        sides_ref[0, pl.ds(x, height, stride=TILE_X), :] = higher_ref[slab, :]
        sides_ref[1, pl.ds(x + TILE_X - RIM, height, stride=TILE_X), :] = lower_ref[slab, :]
    lay_planes(wide_ref, source_ref, 0, fields_ref, sides_ref.at[0], sides_ref.at[1])
    lay_planes(wide_ref, source_ref, LANES, *rims)
    first = 9 * depth
    medium_ref[...] = wide_ref[first:]
    for plane in range(3 * depth):
        near_ref[plane] = narrowed(wide_ref[first + plane])
    state, near = fields_of(state_ref, 9, depth), fields_of(near_ref, 3, depth)
    for step in range(3):

        def emit(z, strains, step=step):
            for number, strain in enumerate(strains):
                base = ((step * 6 + number) * depth + z) * TILE_X
                strain_ref[base : base + TILE_X, :] = strain[0:TILE_X, 0:LANES]

        if step == 0:
            advance(fields_of(wide_ref, 9, depth), fields_of(wide_ref, 3, depth, 9), emit, state)
            continue
        for z in range(depth):
            load = source_ref[(step - 1) * depth + z]
            for number in range(3, 6):
                state[number][z] = state[number][z] + load
        advance(state, near, emit, state if step == 1 else None)
    axial = jnp.concatenate(
        [strain_ref[step * 6 * cells_row : (step * 6 + 2) * cells_row, :] for step in range(3)], axis=0
    )
    axial = jnp.concatenate(pieces(axial), axis=0).astype(BF16)
    rows_down = iota((cells_row, LANES), 0)
    slots_down = packed_iota(LANES, 2)
    for block in range(slot_ref.shape[0]):
        lanes = slice(block * LANES, (block + 1) * LANES)
        if block % 2 == 0:
            both = sum_thirds(times(axial, cover_ref[:, block * LANES : (block + 2) * LANES]))
        windows = both[:, :LANES] if block % 2 == 0 else both[:, LANES:]
        at_row = rows_down == row_ref[block : block + 1, :]
        weight_x, weight_y = weight_ref[0:1, lanes], weight_ref[1:2, lanes]
        sums = []
        for step in range(3):
            base = 2 * step * cells_row
            axial_sum = (
                weight_x * windows[base : base + cells_row]
                + weight_y * windows[base + cells_row : base + 2 * cells_row]
            )
            sums.append(jnp.sum(jnp.where(at_row, axial_sum, 0.0), axis=0, keepdims=True))
        sums.append(channel_ref[block : block + 1, :].astype(F32))
        values = jnp.concatenate(sums + sums, axis=0)
        in_slot = slots_down == packed_rows(slot_ref[block : block + 1, :], LANES)
        for third, piece in enumerate(pieces(values)):
            tile = jnp.concatenate([piece, piece], axis=0).astype(BF16)
            spread_ref[third * LANES : (third + 1) * LANES, lanes] = jnp.where(
                in_slot, jnp.concatenate([tile] * (LANES // 16), axis=0), jnp.zeros((), BF16)
            )
    out_ref[...] = sum_thirds(times_turned(spread_ref[...], place_ref[...]))


def owner_body(arrived_ref, observed_ref, residual_ref, reply_ref, values_ref, place_ref, held_ref):
    groups = arrived_ref.shape[0] // 4
    parts = observed_ref.shape[1] // LANES
    down = packed_iota(LANES)
    part_down = iota((parts, LANES), 0)
    nothing = jnp.zeros((parts, LANES), F32)
    numbers = [arrived_ref[4 * s + 3 : 4 * s + 4, :].astype(I32) for s in range(groups)]
    for s in range(groups):
        lanes = slice(s * LANES, (s + 1) * LANES)
        place_ref[:, lanes] = jnp.where(
            down == packed_rows(numbers[s] & (LANES - 1), LANES), jnp.ones((), BF16), jnp.zeros((), BF16)
        )
        at_part = part_down == (numbers[s] >> 7)
        thirds = pieces(arrived_ref[4 * s : 4 * s + 3, :])
        stack = []
        for third in thirds:
            for step in range(3):
                stack.append(jnp.where(at_part, third[step : step + 1, :], 0.0))
            stack.append(nothing)
        values_ref[:, lanes] = jnp.concatenate(stack, axis=0).astype(BF16)
    sums = sum_thirds(times_turned(values_ref[...], place_ref[...]))
    for step in range(3):
        for part in range(parts):
            at = step * parts + part
            held_ref[at : at + 1, :] = observed_ref[step : step + 1, part * LANES : (part + 1) * LANES]
    held_ref[3 * parts :, :] = nothing
    held_ref[...] = sums - held_ref[...]
    for step in range(3):
        for part in range(parts):
            at = step * parts + part
            residual_ref[step : step + 1, part * LANES : (part + 1) * LANES] = held_ref[at : at + 1, :]
    residual = jnp.concatenate(two_pieces(held_ref[...]), axis=0).astype(BF16)
    for s in range(groups):
        if s % 2 == 0:
            both = sum_halves(times(residual, place_ref[:, s * LANES : (s + 2) * LANES]))
        found = both[:, :LANES] if s % 2 == 0 else both[:, LANES:]
        at_part = part_down == (numbers[s] >> 7)
        for step in range(3):
            reply_ref[4 * s + step : 4 * s + step + 1, :] = jnp.sum(
                jnp.where(at_part, found[step * parts : (step + 1) * parts], 0.0), axis=0, keepdims=True
            )
        reply_ref[4 * s + 3 : 4 * s + 4, :] = jnp.zeros((1, LANES), F32)


def load_body(
    arrived_ref,
    slot_ref,
    row_ref,
    weight_ref,
    cover_ref,
    place_ref,
    load_ref,
    side_ref,
    spread_ref,
):
    cells_row = load_ref.shape[0] // 6
    stack_rows = load_ref.shape[0]
    arrived = jnp.concatenate(two_pieces(arrived_ref[...]), axis=0).astype(BF16)
    slots_down = iota((LANES, LANES), 0) >> 2
    rows_down = packed_iota(cells_row)
    for block in range(slot_ref.shape[0]):
        lanes = slice(block * LANES, (block + 1) * LANES)
        if block % 2 == 0:
            both = sum_halves(times(arrived, place_ref[:, block * LANES : (block + 2) * LANES]))
        found = both[:, :LANES] if block % 2 == 0 else both[:, LANES:]
        found = jnp.where(slots_down == slot_ref[block : block + 1, :], found, 0.0)
        folded = found[0:8]
        for part in range(1, LANES // 8):
            folded = folded + found[8 * part : 8 * part + 8]
        folded = folded + pltpu.roll(folded, 4, 0)
        at_row = rows_down == packed_rows(row_ref[block : block + 1, :], cells_row)
        for turn in range(3):
            back = folded[2 - turn : 3 - turn, :]
            for part in range(2):
                for half, piece in enumerate(two_pieces(weight_ref[part : part + 1, lanes] * back)):
                    base = half * stack_rows + (2 * turn + part) * cells_row
                    spread_ref[base : base + cells_row, lanes] = jnp.where(
                        at_row, packed_rows(piece, cells_row), jnp.zeros((), BF16)
                    )
    cover = jnp.concatenate([cover_ref[0:16, :], cover_ref[LANES - 16 :, :]], axis=0)
    edges = times_turned(cover, spread_ref[0:stack_rows, :]) + times_turned(cover, spread_ref[stack_rows:, :])
    side_ref[...] = jnp.zeros_like(side_ref)
    for side, base in ((0, 0), (1, 32 - RIM)):
        for column in range(RIM):
            lanes = slice(column * LANES, column * LANES + stack_rows)
            side_ref[side, 0:1, lanes] = edges[base + column : base + column + 1, :]
    load_ref[...] = sum_halves(times_turned(spread_ref[...], cover_ref[...]))


def rims_body(load_ref, side_ref, copy_ref, out_ref, sent_sides):
    sides = start_sides(side_ref, out_ref, sent_sides)
    copy_ref[...] = load_ref[...]
    wait_sides(sides)


def adjoint_body(
    load_ref,
    higher_ref,
    lower_ref,
    recv_ref,
    strain_ref,
    medium_ref,
    gradient_ref,
    first_ref,
    later_ref,
    velocity_ref,
    state_ref,
    near_ref,
    turn_ref,
):
    depth = medium_ref.shape[0] // 3
    turn_ref[...] = jnp.zeros_like(turn_ref)
    rims = [rim_rows(recv_ref, dx, turn_ref) for dx in (0, 1, -1)]
    lay_planes(first_ref, later_ref, 0, load_ref, higher_ref, lower_ref)
    lay_planes(first_ref, later_ref, LANES, *rims)
    for plane in range(3 * depth):
        near_ref[plane] = narrowed(medium_ref[plane])
    gradient_ref[...] = jnp.zeros_like(gradient_ref)
    state, near, medium = (
        fields_of(state_ref, 9, depth),
        fields_of(near_ref, 3, depth),
        fields_of(medium_ref, 3, depth),
    )

    def add_terms(turn, z, strains):
        dilation, dilation_back, doubled, product = None, None, None, None
        for number, strain in enumerate(strains):
            base = (((2 - turn) * 6 + number) * depth + z) * TILE_X
            forward = strain_ref[base : base + TILE_X, :]
            if number < 3:
                dilation = forward if dilation is None else dilation + forward
            if strain is None:
                continue
            back = strain[0:TILE_X, 0:LANES]
            term = forward * back
            if number < 3:
                dilation_back = back if dilation_back is None else dilation_back + back
                doubled = term if doubled is None else doubled + term
            else:
                product = term if product is None else product + term
        for part, term in enumerate((dilation * dilation_back, 2.0 * doubled + product)):
            base = (part * depth + z) * TILE_X
            gradient_ref[base : base + TILE_X, :] = gradient_ref[base : base + TILE_X, :] + term

    loads, velocity = fields_of(first_ref, 2, depth), fields_of(velocity_ref, 2, depth)
    for z in range(depth):
        scale = STEP * medium[2][z]
        velocity[0][z] = scale * ahead_x(loads[0][z])
        velocity[1][z] = scale * ahead_y(loads[1][z])
        state[0][z] = narrowed(velocity[0][z])
        state[1][z] = narrowed(velocity[1][z])
        state[2][z] = jnp.zeros((SPAN_NEAR, SPAN_Y), F32)
    for z in range(depth):
        along_x, along_y = velocity[0][z], velocity[1][z]
        strain_x, strain_y = behind_x(along_x), behind_y(along_y)
        sheared = (
            ahead_y(along_x) + ahead_x(along_y),
            ahead_z(velocity[0], z),
            ahead_z(velocity[1], z),
        )
        add_terms(0, z, (strain_x, strain_y, None) + sheared)
        dilated = medium[0][z] * (strain_x + strain_y)
        shear = medium[1][z]
        state[3][z] = narrowed(loads[0][z] + STEP * (dilated + 2.0 * shear * strain_x))
        state[4][z] = narrowed(loads[1][z] + STEP * (dilated + 2.0 * shear * strain_y))
        state[5][z] = narrowed(STEP * dilated)
        for number, strain in enumerate(sheared):
            state[6 + number][z] = narrowed(STEP * shear * strain)
    for turn in (1, 2):
        for part in range(2):
            for z in range(depth):
                load = later_ref[(2 * (turn - 1) + part) * depth + z]
                state[3 + part][z] = state[3 + part][z] + load
        advance(state, near, functools.partial(add_terms, turn), state if turn == 1 else None)


def shards(
    initial_state,
    lame_lambda,
    shear_modulus,
    buoyancy,
    source_cells,
    source_wavelet,
    segment_start,
    segment_weight,
    partial_owner,
    partial_channel,
    observed_data,
):
    depth, rows_x, cols_y = lame_lambda.shape
    part_count = segment_start.shape[0]
    count_x, count_y = lax.axis_size("gx"), lax.axis_size("gy")
    devices = count_x * count_y
    capacity = max(2, 2 * part_count // devices)
    slot_groups = devices * capacity // LANES
    blocks = part_count // LANES
    per_group = LANES // capacity
    cells_row = depth * rows_x
    both = ("gx", "gy")
    up = [(i, i + 1) for i in range(count_x - 1)]
    down = [(j, i) for i, j in up]
    shape = jax.ShapeDtypeStruct

    def exchange(chunks):
        return lax.all_to_all(chunks, both, split_axis=0, concat_axis=0, tiled=True)

    def to_owners(rows):
        chunks = rows.reshape(slot_groups, 4, per_group, capacity).transpose(0, 2, 1, 3)
        back = exchange(chunks.reshape(devices, 4, capacity)).reshape(slot_groups, per_group, 4, capacity)
        return back.transpose(0, 2, 1, 3).reshape(slot_groups * 4, LANES)

    trimmed = shape((14 * depth * RIM, cols_y), F32)
    fields, high, low, edges = call_kernel(
        pack_body,
        "pack_edges",
        [shape((14 * cells_row, cols_y), F32), trimmed, trimmed, shape((devices, 1, 2 * RIM * LANES), F32)],
        [
            pltpu.VMEM((14 * cells_row, cols_y), F32),
            pltpu.VMEM(trimmed.shape, F32),
            pltpu.VMEM(trimmed.shape, F32),
            pltpu.VMEM((2, 1, 2 * RIM * LANES), F32),
            pltpu.VMEM((1, source_cells.shape[0]), I32),
            pltpu.VMEM(source_wavelet.shape, F32),
            pltpu.SemaphoreType.DMA((6,)),
            pltpu.SemaphoreType.DMA((3,)),
            pltpu.SemaphoreType.DMA((6,)),
        ],
        *[values.reshape(-1, cols_y) for values in (initial_state, lame_lambda, shear_modulus, buoyancy)],
        source_cells.reshape(1, -1),
        source_wavelet,
        place=pl.ANY,
        place_out=pl.ANY,
        room=60 * 1024 * 1024,
    )
    lower = lax.ppermute(high, "gx", up)
    higher = lax.ppermute(low, "gx", down)
    rims = exchange(edges)
    channels = partial_channel.reshape(blocks, LANES)
    slot, row, cover, place = call_kernel(
        functools.partial(slots_body, capacity, devices, cols_y),
        "segment_slots",
        [
            shape((blocks, LANES), I32),
            shape((blocks, LANES), I32),
            shape((cols_y, part_count), BF16),
            shape((LANES, part_count), BF16),
        ],
        [pltpu.VMEM((blocks, LANES), F32)],
        partial_owner.reshape(blocks, LANES),
        segment_start.reshape(blocks, LANES),
    )
    partials, strains, medium = call_kernel(
        forward_body,
        "forward_run",
        [
            shape((slot_groups * 4, LANES), F32),
            shape((18 * cells_row, cols_y), F32),
            shape((3 * depth, SPAN_X, SPAN_Y), F32),
        ],
        [
            pltpu.VMEM((12 * depth, SPAN_X, SPAN_Y), F32),
            pltpu.VMEM((2 * depth, SPAN_NEAR, SPAN_Y), F32),
            pltpu.VMEM((9 * depth, SPAN_NEAR, SPAN_Y), F32),
            pltpu.VMEM((3 * depth, SPAN_NEAR, SPAN_Y), F32),
            pltpu.VMEM((LANES, 2 * LANES), F32),
            pltpu.VMEM((2, 14 * cells_row, cols_y), F32),
            pltpu.VMEM((3 * LANES, part_count), BF16),
        ],
        fields,
        lower,
        higher,
        rims,
        slot,
        row,
        segment_weight,
        channels,
        cover,
        place,
    )
    parts = observed_data.shape[1] // LANES
    residuals, reply = call_kernel(
        owner_body,
        "channel_sums",
        [shape(observed_data.shape, F32), shape((slot_groups * 4, LANES), F32)],
        [
            pltpu.VMEM((12 * parts, slot_groups * LANES), BF16),
            pltpu.VMEM((LANES, slot_groups * LANES), BF16),
            pltpu.VMEM((4 * parts, LANES), F32),
        ],
        to_owners(partials),
        observed_data,
    )
    load_rows, load_sides = shape((6 * cells_row, cols_y), F32), shape((2, 1, RIM * LANES), F32)
    loads, sides = call_kernel(
        load_body,
        "segment_loads",
        [load_rows, load_sides],
        [pltpu.VMEM((12 * cells_row, part_count), BF16)],
        to_owners(reply),
        slot,
        row,
        segment_weight,
        cover,
        place,
    )
    load_lower = lax.ppermute(loads, "gx", up)
    loads_again, load_edges = call_kernel(
        rims_body,
        "load_rims",
        [load_rows, shape((devices, 1, RIM * LANES), F32)],
        [pltpu.SemaphoreType.DMA((6,))],
        loads,
        sides,
        place_out=(pltpu.VMEM, pl.ANY),
    )
    load_higher = lax.ppermute(loads_again, "gx", down)
    load_rims = exchange(load_edges)
    (gradients,) = call_kernel(
        adjoint_body,
        "adjoint_run",
        [shape((2 * cells_row, cols_y), F32)],
        [
            pltpu.VMEM((2 * depth, SPAN_X, SPAN_Y), F32),
            pltpu.VMEM((4 * depth, SPAN_NEAR, SPAN_Y), F32),
            pltpu.VMEM((2 * depth, SPAN_X, SPAN_Y), F32),
            pltpu.VMEM((9 * depth, SPAN_NEAR, SPAN_Y), F32),
            pltpu.VMEM((3 * depth, SPAN_NEAR, SPAN_Y), F32),
            pltpu.VMEM((LANES, LANES), F32),
        ],
        loads,
        load_higher,
        load_lower,
        load_rims,
        strains,
        medium,
    )
    return (residuals, gradients.reshape(2, depth, rows_x, cols_y))


def solution(mesh):
    in_specs = (
        P(None, None, "gx", "gy"),
        P(None, "gx", "gy"),
        P(None, "gx", "gy"),
        P(None, "gx", "gy"),
        P(("gx", "gy")),
        P(None, ("gx", "gy")),
        P(("gx", "gy")),
        P(None, ("gx", "gy")),
        P(("gx", "gy"), None),
        P(("gx", "gy")),
        P(None, ("gx", "gy")),
    )
    out_specs = (P(None, ("gx", "gy")), P(None, None, "gx", "gy"))
    return jax.shard_map(shards, mesh=mesh, in_specs=in_specs, out_specs=out_specs, check_vma=False)
```

```python
import functools

import jax
import jax.numpy as jnp
from jax import lax
from jax.experimental import pallas as pl
from jax.experimental.pallas import tpu as pltpu
from jax.sharding import PartitionSpec as P

GAUGE = 8
STEP = 0.25
RIM = 3
LANES = 128
TILE_X = 4
SPAN_X = 16
SPAN_NEAR = 8
SPAN_Y = 256
F32, BF16, I32 = jnp.float32, jnp.bfloat16, jnp.int32
NEAR = tuple((dx, dy) for dx in (-1, 0, 1) for dy in (-1, 0, 1))


def call_kernel(
    body, name, outs, scratch, *args, place=pltpu.VMEM, place_out=pltpu.VMEM, room=24 * 1024 * 1024
):
    spaces = place_out if isinstance(place_out, tuple) else (place_out,) * len(outs)
    return pl.pallas_call(
        body,
        name=name,
        out_shape=outs,
        in_specs=[pl.BlockSpec(memory_space=place)] * len(args),
        out_specs=[pl.BlockSpec(memory_space=space) for space in spaces],
        scratch_shapes=scratch,
        compiler_params=pltpu.CompilerParams(vmem_limit_bytes=room),
    )(*args)


def pieces(values):
    high = values.astype(BF16).astype(F32)
    rest = values - high
    middle = rest.astype(BF16).astype(F32)
    return high, middle, rest - middle


def iota(shape, dim):
    return lax.broadcasted_iota(I32, shape, dim)


def times(left, right):
    return lax.dot_general(left, right, (((1,), (0,)), ((), ())), preferred_element_type=F32)


def times_turned(left, right):
    return lax.dot_general(left, right, (((1,), (1,)), ((), ())), preferred_element_type=F32)


def packed_rows(row, height):
    tile = jnp.broadcast_to(row.astype(F32), (16, row.shape[1])).astype(BF16)
    return jnp.concatenate([tile] * (height // 16), axis=0) if height > 16 else tile


def packed_iota(height, shift=0):
    return (iota((height, LANES), 0) >> shift).astype(F32).astype(BF16)


def two_pieces(values):
    high = values.astype(BF16).astype(F32)
    return high, values - high


def sum_halves(values):
    half = values.shape[0] // 2
    return values[:half] + values[half:]


def sum_thirds(values):
    third = values.shape[0] // 3
    return values[:third] + values[third : 2 * third] + values[2 * third :]


def neighbour(dx, dy):
    count_x, count_y = lax.axis_size("gx"), lax.axis_size("gy")
    at_x, at_y = lax.axis_index("gx") + dx, lax.axis_index("gy") + dy
    inside = (at_x >= 0) & (at_x < count_x) & (at_y >= 0) & (at_y < count_y)
    return jnp.where(inside, at_x * count_y + at_y, 0), inside


def edge_columns(rows, side_ref):
    width = rows.shape[0]
    turned = rows.T
    for side, base in ((0, 0), (1, LANES - RIM)):
        for column in range(RIM):
            side_ref[side, 0:1, column * width : (column + 1) * width] = turned[base + column : base + column + 1, :]


def start_sides(side_ref, out_ref, sent):
    sides = []
    for number, (dx, dy) in enumerate((dx, dy) for dx, dy in NEAR if dy):
        index, inside = neighbour(dx, dy)
        source, target = side_ref.at[1 if dy > 0 else 0], out_ref.at[index]
        sides.append((inside, pltpu.make_async_copy(source, target, sent.at[number])))
    for inside, copy in sides:
        pl.when(inside)(copy.start)
    return sides


def wait_sides(sides):
    for inside, copy in sides:
        pl.when(inside)(copy.wait)


def arrived_chunk(recv_ref, dx, dy):
    index, inside = neighbour(dx, dy)
    return jnp.where(inside, recv_ref[index], 0.0)


def rim_rows(recv_ref, dx, turn_ref):
    width = turn_ref.shape[1]
    for dy, base in ((1, 0), (-1, LANES - RIM)):
        chunk = arrived_chunk(recv_ref, dx, dy)
        for column in range(RIM):
            turn_ref[base + column : base + column + 1, :] = chunk[:, column * width : (column + 1) * width]
    return turn_ref[...].T


def lay_planes(wide_ref, narrow_ref, lane, centre, higher, lower):
    row = iota((8, LANES), 0)
    wide = wide_ref.shape[0]
    lanes = slice(lane, lane + LANES)
    for plane in range(wide + narrow_ref.shape[0]):
        rows = slice(8 * (plane // 2), 8 * (plane // 2) + 8)
        mid, high, low = centre[rows], higher[rows], lower[rows]
        if plane % 2:
            mid = pltpu.roll(mid, TILE_X, 0)
        else:
            high, low = pltpu.roll(high, TILE_X, 0), pltpu.roll(low, TILE_X, 0)
        near = jnp.where(row < TILE_X, mid, high)
        if plane < wide:
            wide_ref[plane, 0:8, lanes] = near
            wide_ref[plane, 8:16, lanes] = jnp.where(row < TILE_X, 0.0, low)
        else:
            narrow_ref[plane - wide, :, lanes] = jnp.where(row < SPAN_NEAR - 2, near, low)


def narrowed(plane):
    row = iota((SPAN_NEAR, plane.shape[1]), 0)
    return jnp.where(row < SPAN_NEAR - 2, plane[:SPAN_NEAR], plane[SPAN_NEAR:])


def ahead_x(plane):
    return pltpu.roll(plane, plane.shape[0] - 1, 0) - plane


def behind_x(plane):
    return plane - pltpu.roll(plane, 1, 0)


def ahead_y(plane):
    return pltpu.roll(plane, SPAN_Y - 1, 1) - plane


def behind_y(plane):
    return plane - pltpu.roll(plane, 1, 1)


def ahead_z(planes, z):
    return planes[z + 1] - planes[z] if z + 1 < len(planes) else -planes[z]


def behind_z(planes, z):
    return planes[z] - planes[z - 1] if z else planes[z]


class Planes:
    def __init__(self, ref, first, depth):
        self.ref, self.first, self.depth = ref, first, depth

    def __len__(self):
        return self.depth

    def __getitem__(self, z):
        return self.ref[self.first + z]

    def __setitem__(self, z, plane):
        self.ref[self.first + z] = plane


def fields_of(ref, count, depth, first=0):
    return [Planes(ref, (first + number) * depth, depth) for number in range(count)]


def strain_rates(velocity, z):
    along_x, along_y, along_z = [field[z] for field in velocity]
    return (
        behind_x(along_x),
        behind_y(along_y),
        behind_z(velocity[2], z),
        ahead_y(along_x) + ahead_x(along_y),
        ahead_z(velocity[0], z) + ahead_x(along_z),
        ahead_z(velocity[1], z) + ahead_y(along_z),
    )


def new_stress(stress, strains, lame_lambda, shear_modulus, z):
    dilated = lame_lambda[z] * (strains[0] + strains[1] + strains[2])
    shear = shear_modulus[z]
    normal = [stress[n][z] + STEP * (dilated + 2.0 * shear * strains[n]) for n in range(3)]
    return normal + [stress[n][z] + STEP * shear * strains[n] for n in range(3, 6)]


def advance(state, medium, emit, target):
    velocity, stress = state[:3], state[3:]
    lame_lambda, shear_modulus, buoyancy = medium
    depth = len(buoyancy)
    wide = target is not None and target is not state
    for z in range(depth):
        scale = STEP * buoyancy[z]
        accel = (
            ahead_x(stress[0][z]) + behind_y(stress[3][z]) + behind_z(stress[4], z),
            behind_x(stress[3][z]) + ahead_y(stress[1][z]) + behind_z(stress[5], z),
            behind_x(stress[4][z]) + behind_y(stress[5][z]) + ahead_z(stress[2], z),
        )
        for number in range(3):
            moved = velocity[number][z] + scale * accel[number]
            velocity[number][z] = moved
            if wide:
                target[number][z] = narrowed(moved)
    for z in range(depth):
        strains = strain_rates(velocity, z)
        emit(z, strains)
        if target is not None:
            for number, plane in enumerate(new_stress(stress, strains, lame_lambda, shear_modulus, z)):
                target[3 + number][z] = narrowed(plane) if wide else plane


def pack_body(*refs):
    inputs, outputs, scratch = refs[:6], refs[6:10], refs[10:]
    fields_ref, high_ref, low_ref, side_ref, cells_ref, wavelet_ref, arrived, sent, sent_sides = scratch
    targets, at = [], 0
    for source in inputs[:4]:
        targets.append(fields_ref.at[at : at + source.shape[0]])
        at = at + source.shape[0]
    copies = [
        pltpu.make_async_copy(source, target, arrived.at[number])
        for number, (source, target) in enumerate(zip(inputs, targets + [cells_ref, wavelet_ref]))
    ]
    for copy in copies:
        copy.start()
    copies[4].wait()
    copies[5].wait()
    cells_row = inputs[1].shape[0]
    cells = cells_ref[...]
    count = cells.shape[1]
    at_lane = iota((LANES, count), 0) == (cells & (LANES - 1))
    at_row = iota((cells_row, count), 0) == (cells >> (LANES.bit_length() - 1))
    stack = [
        jnp.where(at_row, third[step : step + 1, :], 0.0) for third in pieces(wavelet_ref[...]) for step in range(3)
    ]
    maps = sum_thirds(
        times_turned(jnp.concatenate(stack, axis=0).astype(BF16), jnp.where(at_lane, 1.0, 0.0).astype(BF16))
    )
    for copy in copies[:4]:
        copy.wait()
    fields_ref[at:, :] = maps[cells_row:]
    for number in range(3, 6):
        rows = slice(number * cells_row, (number + 1) * cells_row)
        fields_ref[rows, :] = fields_ref[rows, :] + maps[:cells_row]
    height = fields_ref.shape[0] // TILE_X
    for x in range(TILE_X):
        slab = fields_ref[pl.ds(x, height, stride=TILE_X), :]
        if x < RIM:
            low_ref[x * height : (x + 1) * height, :] = slab
        if x >= TILE_X - RIM:
            at = x - TILE_X + RIM
            high_ref[at * height : (at + 1) * height, :] = slab
    writes = [
        pltpu.make_async_copy(source, target, sent.at[number])
        for number, (source, target) in enumerate(zip((fields_ref, high_ref, low_ref), outputs))
    ]
    for copy in writes:
        copy.start()
    rows = fields_ref[...]
    spare = 2 * LANES - rows.shape[0]
    edge_columns(jnp.concatenate([rows, jnp.zeros((spare, LANES), F32)], axis=0), side_ref)
    sides = start_sides(side_ref, outputs[3], sent_sides)
    for copy in writes:
        copy.wait()
    wait_sides(sides)


def slots_body(capacity, devices, cols_y, owner_ref, start_ref, slot_ref, row_ref, cover_ref, place_ref, rank_ref):
    blocks = owner_ref.shape[0]
    group = 32
    before = jnp.where(iota((LANES, 2 * LANES), 0) < iota((LANES, 2 * LANES), 1), 1.0, 0.0).astype(BF16)
    rank_ref[...] = jnp.zeros_like(rank_ref)

    def count_group(number, carry):
        names = iota((group, LANES), 0) + number * group
        hot = [names == owner_ref[b : b + 1, :] for b in range(blocks)]
        marks = jnp.concatenate([jnp.where(h, 1.0, 0.0) for h in hot], axis=0).astype(BF16)
        counts = times(marks, before)
        total = jnp.zeros((group, LANES), F32)
        for b in range(blocks):
            part = counts[b * group : (b + 1) * group]
            rank_ref[b : b + 1, :] = rank_ref[b : b + 1, :] + jnp.sum(
                jnp.where(hot[b], part[:, :LANES] + total, 0.0), axis=0, keepdims=True
            )
            total = total + part[:, LANES:]
        return carry

    if devices == group:
        count_group(0, 0)
    else:
        lax.fori_loop(0, devices // group, count_group, 0)
    slot = owner_ref[...] * capacity + rank_ref[...].astype(I32)
    slot_ref[...] = slot >> 7
    low = slot & (LANES - 1)
    span = cols_y - GAUGE + 1
    start = start_ref[...]
    row = ((start.astype(F32) + 0.5) * (1.0 / span)).astype(I32)
    row_ref[...] = row
    first = start - row * span
    down = iota((LANES, LANES), 0)
    for b in range(blocks):
        lanes = slice(b * LANES, (b + 1) * LANES)
        offset = down - first[b : b + 1, :]
        cover_ref[:, lanes] = jnp.where((offset >= 0) & (offset < GAUGE), 1.0, 0.0).astype(BF16)
        place_ref[:, lanes] = jnp.where(down == low[b : b + 1, :], 1.0, 0.0).astype(BF16)


def forward_body(
    fields_ref,
    lower_ref,
    higher_ref,
    recv_ref,
    slot_ref,
    row_ref,
    weight_ref,
    channel_ref,
    cover_ref,
    place_ref,
    out_ref,
    strain_ref,
    medium_ref,
    wide_ref,
    source_ref,
    state_ref,
    near_ref,
    turn_ref,
    sides_ref,
    spread_ref,
):
    depth = medium_ref.shape[0] // 3
    cells_row = depth * TILE_X
    turn_ref[...] = jnp.zeros_like(turn_ref)
    rims = [rim_rows(recv_ref, dx, turn_ref) for dx in (0, 1, -1)]
    height = fields_ref.shape[0] // TILE_X
    sides_ref[...] = jnp.zeros_like(sides_ref)
    for x in range(RIM):
        slab = slice(x * height, (x + 1) * height)
        sides_ref[0, pl.ds(x, height, stride=TILE_X), :] = higher_ref[slab, :]
        sides_ref[1, pl.ds(x + TILE_X - RIM, height, stride=TILE_X), :] = lower_ref[slab, :]
    lay_planes(wide_ref, source_ref, 0, fields_ref, sides_ref.at[0], sides_ref.at[1])
    lay_planes(wide_ref, source_ref, LANES, *rims)
    first = 9 * depth
    medium_ref[...] = wide_ref[first:]
    for plane in range(3 * depth):
        near_ref[plane] = narrowed(wide_ref[first + plane])
    state, near = fields_of(state_ref, 9, depth), fields_of(near_ref, 3, depth)
    for step in range(3):

        def emit(z, strains, step=step):
            for number, strain in enumerate(strains):
                base = ((step * 6 + number) * depth + z) * TILE_X
                strain_ref[base : base + TILE_X, :] = strain[0:TILE_X, 0:LANES]

        if step == 0:
            advance(fields_of(wide_ref, 9, depth), fields_of(wide_ref, 3, depth, 9), emit, state)
            continue
        for z in range(depth):
            load = source_ref[(step - 1) * depth + z]
            for number in range(3, 6):
                state[number][z] = state[number][z] + load
        advance(state, near, emit, state if step == 1 else None)
    axial = jnp.concatenate(
        [strain_ref[step * 6 * cells_row : (step * 6 + 2) * cells_row, :] for step in range(3)], axis=0
    )
    axial = jnp.concatenate(pieces(axial), axis=0).astype(BF16)
    rows_down = iota((cells_row, LANES), 0)
    slots_down = packed_iota(LANES, 2)
    for block in range(slot_ref.shape[0]):
        lanes = slice(block * LANES, (block + 1) * LANES)
        if block % 2 == 0:
            both = sum_thirds(times(axial, cover_ref[:, block * LANES : (block + 2) * LANES]))
        windows = both[:, :LANES] if block % 2 == 0 else both[:, LANES:]
        at_row = rows_down == row_ref[block : block + 1, :]
        weight_x, weight_y = weight_ref[0:1, lanes], weight_ref[1:2, lanes]
        sums = []
        for step in range(3):
            base = 2 * step * cells_row
            axial_sum = (
                weight_x * windows[base : base + cells_row]
                + weight_y * windows[base + cells_row : base + 2 * cells_row]
            )
            sums.append(jnp.sum(jnp.where(at_row, axial_sum, 0.0), axis=0, keepdims=True))
        sums.append(channel_ref[block : block + 1, :].astype(F32))
        values = jnp.concatenate(sums + sums, axis=0)
        in_slot = slots_down == packed_rows(slot_ref[block : block + 1, :], LANES)
        for third, piece in enumerate(pieces(values)):
            tile = jnp.concatenate([piece, piece], axis=0).astype(BF16)
            spread_ref[third * LANES : (third + 1) * LANES, lanes] = jnp.where(
                in_slot, jnp.concatenate([tile] * (LANES // 16), axis=0), jnp.zeros((), BF16)
            )
    out_ref[...] = sum_thirds(times_turned(spread_ref[...], place_ref[...]))


def owner_body(arrived_ref, observed_ref, residual_ref, reply_ref, values_ref, place_ref, held_ref):
    groups = arrived_ref.shape[0] // 4
    parts = observed_ref.shape[1] // LANES
    down = packed_iota(LANES)
    part_down = iota((parts, LANES), 0)
    nothing = jnp.zeros((parts, LANES), F32)
    numbers = [arrived_ref[4 * s + 3 : 4 * s + 4, :].astype(I32) for s in range(groups)]
    for s in range(groups):
        lanes = slice(s * LANES, (s + 1) * LANES)
        place_ref[:, lanes] = jnp.where(
            down == packed_rows(numbers[s] & (LANES - 1), LANES), jnp.ones((), BF16), jnp.zeros((), BF16)
        )
        at_part = part_down == (numbers[s] >> 7)
        thirds = pieces(arrived_ref[4 * s : 4 * s + 3, :])
        stack = []
        for third in thirds:
            for step in range(3):
                stack.append(jnp.where(at_part, third[step : step + 1, :], 0.0))
            stack.append(nothing)
        values_ref[:, lanes] = jnp.concatenate(stack, axis=0).astype(BF16)
    sums = sum_thirds(times_turned(values_ref[...], place_ref[...]))
    for step in range(3):
        for part in range(parts):
            at = step * parts + part
            held_ref[at : at + 1, :] = observed_ref[step : step + 1, part * LANES : (part + 1) * LANES]
    held_ref[3 * parts :, :] = nothing
    held_ref[...] = sums - held_ref[...]
    for step in range(3):
        for part in range(parts):
            at = step * parts + part
            residual_ref[step : step + 1, part * LANES : (part + 1) * LANES] = held_ref[at : at + 1, :]
    residual = jnp.concatenate(two_pieces(held_ref[...]), axis=0).astype(BF16)
    for s in range(groups):
        if s % 2 == 0:
            both = sum_halves(times(residual, place_ref[:, s * LANES : (s + 2) * LANES]))
        found = both[:, :LANES] if s % 2 == 0 else both[:, LANES:]
        at_part = part_down == (numbers[s] >> 7)
        for step in range(3):
            reply_ref[4 * s + step : 4 * s + step + 1, :] = jnp.sum(
                jnp.where(at_part, found[step * parts : (step + 1) * parts], 0.0), axis=0, keepdims=True
            )
        reply_ref[4 * s + 3 : 4 * s + 4, :] = jnp.zeros((1, LANES), F32)


def load_body(
    arrived_ref,
    slot_ref,
    row_ref,
    weight_ref,
    cover_ref,
    place_ref,
    load_ref,
    side_ref,
    spread_ref,
):
    cells_row = load_ref.shape[0] // 6
    stack_rows = load_ref.shape[0]
    arrived = jnp.concatenate(two_pieces(arrived_ref[...]), axis=0).astype(BF16)
    slots_down = iota((LANES, LANES), 0) >> 2
    rows_down = packed_iota(cells_row)
    for block in range(slot_ref.shape[0]):
        lanes = slice(block * LANES, (block + 1) * LANES)
        if block % 2 == 0:
            both = sum_halves(times(arrived, place_ref[:, block * LANES : (block + 2) * LANES]))
        found = both[:, :LANES] if block % 2 == 0 else both[:, LANES:]
        found = jnp.where(slots_down == slot_ref[block : block + 1, :], found, 0.0)
        folded = found[0:8]
        for part in range(1, LANES // 8):
            folded = folded + found[8 * part : 8 * part + 8]
        folded = folded + pltpu.roll(folded, 4, 0)
        at_row = rows_down == packed_rows(row_ref[block : block + 1, :], cells_row)
        for turn in range(3):
            back = folded[2 - turn : 3 - turn, :]
            for part in range(2):
                for half, piece in enumerate(two_pieces(weight_ref[part : part + 1, lanes] * back)):
                    base = half * stack_rows + (2 * turn + part) * cells_row
                    spread_ref[base : base + cells_row, lanes] = jnp.where(
                        at_row, packed_rows(piece, cells_row), jnp.zeros((), BF16)
                    )
    cover = jnp.concatenate([cover_ref[0:16, :], cover_ref[LANES - 16 :, :]], axis=0)
    edges = times_turned(cover, spread_ref[0:stack_rows, :]) + times_turned(cover, spread_ref[stack_rows:, :])
    side_ref[...] = jnp.zeros_like(side_ref)
    for side, base in ((0, 0), (1, 32 - RIM)):
        for column in range(RIM):
            lanes = slice(column * LANES, column * LANES + stack_rows)
            side_ref[side, 0:1, lanes] = edges[base + column : base + column + 1, :]
    load_ref[...] = sum_halves(times_turned(spread_ref[...], cover_ref[...]))


def rims_body(load_ref, side_ref, copy_ref, out_ref, sent_sides):
    sides = start_sides(side_ref, out_ref, sent_sides)
    copy_ref[...] = load_ref[...]
    wait_sides(sides)


def adjoint_planes_body(load_ref, lower_ref, medium_ref, first_ref, later_ref, near_ref):
    lay_planes(first_ref, later_ref, 0, load_ref, jnp.zeros_like(load_ref), lower_ref)
    for plane in range(medium_ref.shape[0]):
        near_ref[plane] = narrowed(medium_ref[plane])


def adjoint_body(
    first_laid_ref,
    later_laid_ref,
    higher_ref,
    recv_ref,
    strain_ref,
    medium_ref,
    near_ref,
    gradient_ref,
    first_ref,
    later_ref,
    velocity_ref,
    state_ref,
    turn_ref,
):
    depth = medium_ref.shape[0] // 3
    turn_ref[...] = jnp.zeros_like(turn_ref)
    rims = [rim_rows(recv_ref, dx, turn_ref) for dx in (0, 1, -1)]
    lay_planes(first_ref, later_ref, LANES, *rims)
    row = iota((8, LANES), 0)
    wide = first_ref.shape[0]
    for plane in range(wide + later_ref.shape[0]):
        high = higher_ref[8 * (plane // 2) : 8 * (plane // 2) + 8, :]
        if plane % 2 == 0:
            high = pltpu.roll(high, TILE_X, 0)
        if plane < wide:
            first_ref[plane, 0:8, 0:LANES] = jnp.where(row < TILE_X, first_laid_ref[plane, 0:8, 0:LANES], high)
            first_ref[plane, 8:16, 0:LANES] = first_laid_ref[plane, 8:16, 0:LANES]
        else:
            laid = later_laid_ref[plane - wide, :, 0:LANES]
            later_ref[plane - wide, :, 0:LANES] = jnp.where(
                (row >= TILE_X) & (row < SPAN_NEAR - 2), high, laid
            )
    gradient_ref[...] = jnp.zeros_like(gradient_ref)
    state, near, medium = (
        fields_of(state_ref, 9, depth),
        fields_of(near_ref, 3, depth),
        fields_of(medium_ref, 3, depth),
    )

    def add_terms(turn, z, strains):
        dilation, dilation_back, doubled, product = None, None, None, None
        for number, strain in enumerate(strains):
            base = (((2 - turn) * 6 + number) * depth + z) * TILE_X
            forward = strain_ref[base : base + TILE_X, :]
            if number < 3:
                dilation = forward if dilation is None else dilation + forward
            if strain is None:
                continue
            back = strain[0:TILE_X, 0:LANES]
            term = forward * back
            if number < 3:
                dilation_back = back if dilation_back is None else dilation_back + back
                doubled = term if doubled is None else doubled + term
            else:
                product = term if product is None else product + term
        for part, term in enumerate((dilation * dilation_back, 2.0 * doubled + product)):
            base = (part * depth + z) * TILE_X
            gradient_ref[base : base + TILE_X, :] = gradient_ref[base : base + TILE_X, :] + term

    loads, velocity = fields_of(first_ref, 2, depth), fields_of(velocity_ref, 2, depth)
    for z in range(depth):
        scale = STEP * medium[2][z]
        velocity[0][z] = scale * ahead_x(loads[0][z])
        velocity[1][z] = scale * ahead_y(loads[1][z])
        state[0][z] = narrowed(velocity[0][z])
        state[1][z] = narrowed(velocity[1][z])
        state[2][z] = jnp.zeros((SPAN_NEAR, SPAN_Y), F32)
    for z in range(depth):
        along_x, along_y = velocity[0][z], velocity[1][z]
        strain_x, strain_y = behind_x(along_x), behind_y(along_y)
        sheared = (
            ahead_y(along_x) + ahead_x(along_y),
            ahead_z(velocity[0], z),
            ahead_z(velocity[1], z),
        )
        add_terms(0, z, (strain_x, strain_y, None) + sheared)
        dilated = medium[0][z] * (strain_x + strain_y)
        shear = medium[1][z]
        state[3][z] = narrowed(loads[0][z] + STEP * (dilated + 2.0 * shear * strain_x))
        state[4][z] = narrowed(loads[1][z] + STEP * (dilated + 2.0 * shear * strain_y))
        state[5][z] = narrowed(STEP * dilated)
        for number, strain in enumerate(sheared):
            state[6 + number][z] = narrowed(STEP * shear * strain)
    for turn in (1, 2):
        for part in range(2):
            for z in range(depth):
                load = later_ref[(2 * (turn - 1) + part) * depth + z]
                state[3 + part][z] = state[3 + part][z] + load
        advance(state, near, functools.partial(add_terms, turn), state if turn == 1 else None)


def shards(
    initial_state,
    lame_lambda,
    shear_modulus,
    buoyancy,
    source_cells,
    source_wavelet,
    segment_start,
    segment_weight,
    partial_owner,
    partial_channel,
    observed_data,
):
    depth, rows_x, cols_y = lame_lambda.shape
    part_count = segment_start.shape[0]
    count_x, count_y = lax.axis_size("gx"), lax.axis_size("gy")
    devices = count_x * count_y
    capacity = max(2, 2 * part_count // devices)
    slot_groups = devices * capacity // LANES
    blocks = part_count // LANES
    per_group = LANES // capacity
    cells_row = depth * rows_x
    both = ("gx", "gy")
    up = [(i, i + 1) for i in range(count_x - 1)]
    down = [(j, i) for i, j in up]
    shape = jax.ShapeDtypeStruct

    def exchange(chunks):
        return lax.all_to_all(chunks, both, split_axis=0, concat_axis=0, tiled=True)

    def to_owners(rows):
        chunks = rows.reshape(slot_groups, 4, per_group, capacity).transpose(0, 2, 1, 3)
        back = exchange(chunks.reshape(devices, 4, capacity)).reshape(slot_groups, per_group, 4, capacity)
        return back.transpose(0, 2, 1, 3).reshape(slot_groups * 4, LANES)

    trimmed = shape((14 * depth * RIM, cols_y), F32)
    fields, high, low, edges = call_kernel(
        pack_body,
        "pack_edges",
        [shape((14 * cells_row, cols_y), F32), trimmed, trimmed, shape((devices, 1, 2 * RIM * LANES), F32)],
        [
            pltpu.VMEM((14 * cells_row, cols_y), F32),
            pltpu.VMEM(trimmed.shape, F32),
            pltpu.VMEM(trimmed.shape, F32),
            pltpu.VMEM((2, 1, 2 * RIM * LANES), F32),
            pltpu.VMEM((1, source_cells.shape[0]), I32),
            pltpu.VMEM(source_wavelet.shape, F32),
            pltpu.SemaphoreType.DMA((6,)),
            pltpu.SemaphoreType.DMA((3,)),
            pltpu.SemaphoreType.DMA((6,)),
        ],
        *[values.reshape(-1, cols_y) for values in (initial_state, lame_lambda, shear_modulus, buoyancy)],
        source_cells.reshape(1, -1),
        source_wavelet,
        place=pl.ANY,
        place_out=pl.ANY,
        room=60 * 1024 * 1024,
    )
    lower = lax.ppermute(high, "gx", up)
    higher = lax.ppermute(low, "gx", down)
    rims = exchange(edges)
    channels = partial_channel.reshape(blocks, LANES)
    slot, row, cover, place = call_kernel(
        functools.partial(slots_body, capacity, devices, cols_y),
        "segment_slots",
        [
            shape((blocks, LANES), I32),
            shape((blocks, LANES), I32),
            shape((cols_y, part_count), BF16),
            shape((LANES, part_count), BF16),
        ],
        [pltpu.VMEM((blocks, LANES), F32)],
        partial_owner.reshape(blocks, LANES),
        segment_start.reshape(blocks, LANES),
    )
    partials, strains, medium = call_kernel(
        forward_body,
        "forward_run",
        [
            shape((slot_groups * 4, LANES), F32),
            shape((18 * cells_row, cols_y), F32),
            shape((3 * depth, SPAN_X, SPAN_Y), F32),
        ],
        [
            pltpu.VMEM((12 * depth, SPAN_X, SPAN_Y), F32),
            pltpu.VMEM((2 * depth, SPAN_NEAR, SPAN_Y), F32),
            pltpu.VMEM((9 * depth, SPAN_NEAR, SPAN_Y), F32),
            pltpu.VMEM((3 * depth, SPAN_NEAR, SPAN_Y), F32),
            pltpu.VMEM((LANES, 2 * LANES), F32),
            pltpu.VMEM((2, 14 * cells_row, cols_y), F32),
            pltpu.VMEM((3 * LANES, part_count), BF16),
        ],
        fields,
        lower,
        higher,
        rims,
        slot,
        row,
        segment_weight,
        channels,
        cover,
        place,
    )
    parts = observed_data.shape[1] // LANES
    residuals, reply = call_kernel(
        owner_body,
        "channel_sums",
        [shape(observed_data.shape, F32), shape((slot_groups * 4, LANES), F32)],
        [
            pltpu.VMEM((12 * parts, slot_groups * LANES), BF16),
            pltpu.VMEM((LANES, slot_groups * LANES), BF16),
            pltpu.VMEM((4 * parts, LANES), F32),
        ],
        to_owners(partials),
        observed_data,
    )
    load_rows, load_sides = shape((6 * cells_row, cols_y), F32), shape((2, 1, RIM * LANES), F32)
    loads, sides = call_kernel(
        load_body,
        "segment_loads",
        [load_rows, load_sides],
        [pltpu.VMEM((12 * cells_row, part_count), BF16)],
        to_owners(reply),
        slot,
        row,
        segment_weight,
        cover,
        place,
    )
    load_lower = lax.ppermute(loads, "gx", up)
    loads_again, load_edges = call_kernel(
        rims_body,
        "load_rims",
        [load_rows, shape((devices, 1, RIM * LANES), F32)],
        [pltpu.SemaphoreType.DMA((6,))],
        loads,
        sides,
        place_out=(pltpu.VMEM, pl.ANY),
    )
    load_higher = lax.ppermute(loads_again, "gx", down)
    load_rims = exchange(load_edges)
    first_laid, later_laid, near = call_kernel(
        adjoint_planes_body,
        "adjoint_planes",
        [
            shape((2 * depth, SPAN_X, LANES), F32),
            shape((4 * depth, SPAN_NEAR, LANES), F32),
            shape((3 * depth, SPAN_NEAR, SPAN_Y), F32),
        ],
        [],
        loads,
        load_lower,
        medium,
    )
    (gradients,) = call_kernel(
        adjoint_body,
        "adjoint_run",
        [shape((2 * cells_row, cols_y), F32)],
        [
            pltpu.VMEM((2 * depth, SPAN_X, SPAN_Y), F32),
            pltpu.VMEM((4 * depth, SPAN_NEAR, SPAN_Y), F32),
            pltpu.VMEM((2 * depth, SPAN_X, SPAN_Y), F32),
            pltpu.VMEM((9 * depth, SPAN_NEAR, SPAN_Y), F32),
            pltpu.VMEM((LANES, LANES), F32),
        ],
        first_laid,
        later_laid,
        load_higher,
        load_rims,
        strains,
        medium,
        near,
    )
    return (residuals, gradients.reshape(2, depth, rows_x, cols_y))


def solution(mesh):
    in_specs = (
        P(None, None, "gx", "gy"),
        P(None, "gx", "gy"),
        P(None, "gx", "gy"),
        P(None, "gx", "gy"),
        P(("gx", "gy")),
        P(None, ("gx", "gy")),
        P(("gx", "gy")),
        P(None, ("gx", "gy")),
        P(("gx", "gy"), None),
        P(("gx", "gy")),
        P(None, ("gx", "gy")),
    )
    out_specs = (P(None, ("gx", "gy")), P(None, None, "gx", "gy"))
    return jax.shard_map(shards, mesh=mesh, in_specs=in_specs, out_specs=out_specs, check_vma=False)
```

```python
import functools

import jax
import jax.numpy as jnp
from jax import lax
from jax.experimental import pallas as pl
from jax.experimental.pallas import tpu as pltpu
from jax.sharding import PartitionSpec as P

GAUGE = 8
STEP = 0.25
RIM = 3
LANES = 128
TILE_X = 4
SPAN_X = 16
SPAN_NEAR = 8
SPAN_Y = 256
F32, BF16, I32 = jnp.float32, jnp.bfloat16, jnp.int32
NEAR = tuple((dx, dy) for dx in (-1, 0, 1) for dy in (-1, 0, 1))


def call_kernel(
    body, name, outs, scratch, *args, place=pltpu.VMEM, place_out=pltpu.VMEM, room=24 * 1024 * 1024
):
    spaces = place_out if isinstance(place_out, tuple) else (place_out,) * len(outs)
    return pl.pallas_call(
        body,
        name=name,
        out_shape=outs,
        in_specs=[pl.BlockSpec(memory_space=place)] * len(args),
        out_specs=[pl.BlockSpec(memory_space=space) for space in spaces],
        scratch_shapes=scratch,
        compiler_params=pltpu.CompilerParams(vmem_limit_bytes=room),
    )(*args)


def pieces(values):
    high = values.astype(BF16).astype(F32)
    rest = values - high
    middle = rest.astype(BF16).astype(F32)
    return high, middle, rest - middle


def iota(shape, dim):
    return lax.broadcasted_iota(I32, shape, dim)


def times(left, right):
    return lax.dot_general(left, right, (((1,), (0,)), ((), ())), preferred_element_type=F32)


def times_turned(left, right):
    return lax.dot_general(left, right, (((1,), (1,)), ((), ())), preferred_element_type=F32)


def packed_rows(row, height):
    tile = jnp.broadcast_to(row.astype(F32), (16, row.shape[1])).astype(BF16)
    return jnp.concatenate([tile] * (height // 16), axis=0) if height > 16 else tile


def packed_iota(height, shift=0):
    return (iota((height, LANES), 0) >> shift).astype(F32).astype(BF16)


def two_pieces(values):
    high = values.astype(BF16).astype(F32)
    return high, values - high


def sum_halves(values):
    half = values.shape[0] // 2
    return values[:half] + values[half:]


def sum_thirds(values):
    third = values.shape[0] // 3
    return values[:third] + values[third : 2 * third] + values[2 * third :]


def neighbour(dx, dy):
    count_x, count_y = lax.axis_size("gx"), lax.axis_size("gy")
    at_x, at_y = lax.axis_index("gx") + dx, lax.axis_index("gy") + dy
    inside = (at_x >= 0) & (at_x < count_x) & (at_y >= 0) & (at_y < count_y)
    return jnp.where(inside, at_x * count_y + at_y, 0), inside


def edge_columns(rows, side_ref):
    width = rows.shape[0]
    turned = rows.T
    for side, base in ((0, 0), (1, LANES - RIM)):
        for column in range(RIM):
            side_ref[side, 0:1, column * width : (column + 1) * width] = turned[base + column : base + column + 1, :]


def start_sides(side_ref, out_ref, sent):
    sides = []
    for number, (dx, dy) in enumerate((dx, dy) for dx, dy in NEAR if dy):
        index, inside = neighbour(dx, dy)
        source, target = side_ref.at[1 if dy > 0 else 0], out_ref.at[index]
        sides.append((inside, pltpu.make_async_copy(source, target, sent.at[number])))
    for inside, copy in sides:
        pl.when(inside)(copy.start)
    return sides


def wait_sides(sides):
    for inside, copy in sides:
        pl.when(inside)(copy.wait)


def arrived_chunk(recv_ref, dx, dy):
    index, inside = neighbour(dx, dy)
    return jnp.where(inside, recv_ref[index], 0.0)


def rim_rows(recv_ref, turn_ref):
    width = turn_ref.shape[1]
    turn_ref[...] = jnp.zeros_like(turn_ref)
    blocks = ((0, 0), (1, 40), (-1, 80))
    for dx, base in blocks:
        for dy, first in ((1, base), (-1, (base - RIM) % LANES)):
            chunk = arrived_chunk(recv_ref, dx, dy)
            for column in range(RIM):
                turn_ref[first + column : first + column + 1, :] = chunk[:, column * width : (column + 1) * width]
    turned = turn_ref[...].T
    return [pltpu.roll(turned, LANES - base, 1) if base else turned for _, base in blocks]


def lay_planes(wide_ref, narrow_ref, lane, centre, higher, lower):
    row = iota((8, LANES), 0)
    wide = wide_ref.shape[0]
    lanes = slice(lane, lane + LANES)
    for plane in range(wide + narrow_ref.shape[0]):
        rows = slice(8 * (plane // 2), 8 * (plane // 2) + 8)
        mid, high, low = centre[rows], higher[rows], lower[rows]
        if plane % 2:
            mid = pltpu.roll(mid, TILE_X, 0)
        else:
            high, low = pltpu.roll(high, TILE_X, 0), pltpu.roll(low, TILE_X, 0)
        near = jnp.where(row < TILE_X, mid, high)
        if plane < wide:
            wide_ref[plane, 0:8, lanes] = near
            wide_ref[plane, 8:16, lanes] = jnp.where(row < TILE_X, 0.0, low)
        else:
            narrow_ref[plane - wide, :, lanes] = jnp.where(row < SPAN_NEAR - 2, near, low)


def narrowed(plane):
    row = iota((SPAN_NEAR, plane.shape[1]), 0)
    return jnp.where(row < SPAN_NEAR - 2, plane[:SPAN_NEAR], plane[SPAN_NEAR:])


def ahead_x(plane):
    return pltpu.roll(plane, plane.shape[0] - 1, 0) - plane


def behind_x(plane):
    return plane - pltpu.roll(plane, 1, 0)


def ahead_y(plane):
    return pltpu.roll(plane, SPAN_Y - 1, 1) - plane


def behind_y(plane):
    return plane - pltpu.roll(plane, 1, 1)


def ahead_z(planes, z):
    return planes[z + 1] - planes[z] if z + 1 < len(planes) else -planes[z]


def behind_z(planes, z):
    return planes[z] - planes[z - 1] if z else planes[z]


class Planes:
    def __init__(self, ref, first, depth):
        self.ref, self.first, self.depth = ref, first, depth

    def __len__(self):
        return self.depth

    def __getitem__(self, z):
        return self.ref[self.first + z]

    def __setitem__(self, z, plane):
        self.ref[self.first + z] = plane


def fields_of(ref, count, depth, first=0):
    return [Planes(ref, (first + number) * depth, depth) for number in range(count)]


def strain_rates(velocity, z):
    along_x, along_y, along_z = [field[z] for field in velocity]
    return (
        behind_x(along_x),
        behind_y(along_y),
        behind_z(velocity[2], z),
        ahead_y(along_x) + ahead_x(along_y),
        ahead_z(velocity[0], z) + ahead_x(along_z),
        ahead_z(velocity[1], z) + ahead_y(along_z),
    )


def new_stress(stress, strains, lame_lambda, shear_modulus, z):
    dilated = lame_lambda[z] * (strains[0] + strains[1] + strains[2])
    shear = shear_modulus[z]
    normal = [stress[n][z] + STEP * (dilated + 2.0 * shear * strains[n]) for n in range(3)]
    return normal + [stress[n][z] + STEP * shear * strains[n] for n in range(3, 6)]


def advance(state, medium, emit, target):
    velocity, stress = state[:3], state[3:]
    lame_lambda, shear_modulus, buoyancy = medium
    depth = len(buoyancy)
    wide = target is not None and target is not state
    for z in range(depth):
        scale = STEP * buoyancy[z]
        accel = (
            ahead_x(stress[0][z]) + behind_y(stress[3][z]) + behind_z(stress[4], z),
            behind_x(stress[3][z]) + ahead_y(stress[1][z]) + behind_z(stress[5], z),
            behind_x(stress[4][z]) + behind_y(stress[5][z]) + ahead_z(stress[2], z),
        )
        for number in range(3):
            moved = velocity[number][z] + scale * accel[number]
            velocity[number][z] = moved
            if wide:
                target[number][z] = narrowed(moved)
    for z in range(depth):
        strains = strain_rates(velocity, z)
        emit(z, strains)
        if target is not None:
            for number, plane in enumerate(new_stress(stress, strains, lame_lambda, shear_modulus, z)):
                target[3 + number][z] = narrowed(plane) if wide else plane


def pack_body(*refs):
    inputs, outputs, scratch = refs[:6], refs[6:10], refs[10:]
    fields_ref, high_ref, low_ref, side_ref, cells_ref, wavelet_ref, arrived, sent, sent_sides = scratch
    targets, at = [], 0
    for source in inputs[:4]:
        targets.append(fields_ref.at[at : at + source.shape[0]])
        at = at + source.shape[0]
    copies = [
        pltpu.make_async_copy(source, target, arrived.at[number])
        for number, (source, target) in enumerate(zip(inputs, targets + [cells_ref, wavelet_ref]))
    ]
    for copy in copies:
        copy.start()
    copies[4].wait()
    copies[5].wait()
    cells_row = inputs[1].shape[0]
    cells = cells_ref[...]
    count = cells.shape[1]
    at_lane = iota((LANES, count), 0) == (cells & (LANES - 1))
    at_row = iota((cells_row, count), 0) == (cells >> (LANES.bit_length() - 1))
    stack = [
        jnp.where(at_row, third[step : step + 1, :], 0.0) for third in pieces(wavelet_ref[...]) for step in range(3)
    ]
    maps = sum_thirds(
        times_turned(jnp.concatenate(stack, axis=0).astype(BF16), jnp.where(at_lane, 1.0, 0.0).astype(BF16))
    )
    for copy in copies[:4]:
        copy.wait()
    fields_ref[at:, :] = maps[cells_row:]
    for number in range(3, 6):
        rows = slice(number * cells_row, (number + 1) * cells_row)
        fields_ref[rows, :] = fields_ref[rows, :] + maps[:cells_row]
    height = fields_ref.shape[0] // TILE_X
    for x in range(TILE_X):
        slab = fields_ref[pl.ds(x, height, stride=TILE_X), :]
        if x < RIM:
            low_ref[x * height : (x + 1) * height, :] = slab
        if x >= TILE_X - RIM:
            at = x - TILE_X + RIM
            high_ref[at * height : (at + 1) * height, :] = slab
    writes = [
        pltpu.make_async_copy(source, target, sent.at[number])
        for number, (source, target) in enumerate(zip((fields_ref, high_ref, low_ref), outputs))
    ]
    for copy in writes:
        copy.start()
    rows = fields_ref[...]
    spare = 2 * LANES - rows.shape[0]
    edge_columns(jnp.concatenate([rows, jnp.zeros((spare, LANES), F32)], axis=0), side_ref)
    sides = start_sides(side_ref, outputs[3], sent_sides)
    for copy in writes:
        copy.wait()
    wait_sides(sides)


def slots_body(capacity, devices, cols_y, owner_ref, start_ref, slot_ref, row_ref, cover_ref, place_ref, rank_ref):
    blocks = owner_ref.shape[0]
    group = 32
    before = jnp.where(iota((LANES, 2 * LANES), 0) < iota((LANES, 2 * LANES), 1), 1.0, 0.0).astype(BF16)
    rank_ref[...] = jnp.zeros_like(rank_ref)

    def count_group(number, carry):
        names = iota((group, LANES), 0) + number * group
        hot = [names == owner_ref[b : b + 1, :] for b in range(blocks)]
        marks = jnp.concatenate([jnp.where(h, 1.0, 0.0) for h in hot], axis=0).astype(BF16)
        counts = times(marks, before)
        total = jnp.zeros((group, LANES), F32)
        for b in range(blocks):
            part = counts[b * group : (b + 1) * group]
            rank_ref[b : b + 1, :] = rank_ref[b : b + 1, :] + jnp.sum(
                jnp.where(hot[b], part[:, :LANES] + total, 0.0), axis=0, keepdims=True
            )
            total = total + part[:, LANES:]
        return carry

    if devices == group:
        count_group(0, 0)
    else:
        lax.fori_loop(0, devices // group, count_group, 0)
    slot = owner_ref[...] * capacity + rank_ref[...].astype(I32)
    slot_ref[...] = slot >> 7
    low = slot & (LANES - 1)
    span = cols_y - GAUGE + 1
    start = start_ref[...]
    row = ((start.astype(F32) + 0.5) * (1.0 / span)).astype(I32)
    row_ref[...] = row
    first = start - row * span
    down = iota((LANES, LANES), 0)
    for b in range(blocks):
        lanes = slice(b * LANES, (b + 1) * LANES)
        offset = down - first[b : b + 1, :]
        cover_ref[:, lanes] = jnp.where((offset >= 0) & (offset < GAUGE), 1.0, 0.0).astype(BF16)
        place_ref[:, lanes] = jnp.where(down == low[b : b + 1, :], 1.0, 0.0).astype(BF16)


def forward_body(
    fields_ref,
    lower_ref,
    higher_ref,
    recv_ref,
    slot_ref,
    row_ref,
    weight_ref,
    channel_ref,
    cover_ref,
    place_ref,
    out_ref,
    strain_ref,
    medium_ref,
    wide_ref,
    source_ref,
    state_ref,
    near_ref,
    turn_ref,
    sides_ref,
    spread_ref,
):
    depth = medium_ref.shape[0] // 3
    cells_row = depth * TILE_X
    rims = rim_rows(recv_ref, turn_ref)
    height = fields_ref.shape[0] // TILE_X
    sides_ref[...] = jnp.zeros_like(sides_ref)
    for x in range(RIM):
        slab = slice(x * height, (x + 1) * height)
        sides_ref[0, pl.ds(x, height, stride=TILE_X), :] = higher_ref[slab, :]
        sides_ref[1, pl.ds(x + TILE_X - RIM, height, stride=TILE_X), :] = lower_ref[slab, :]
    lay_planes(wide_ref, source_ref, 0, fields_ref, sides_ref.at[0], sides_ref.at[1])
    lay_planes(wide_ref, source_ref, LANES, *rims)
    first = 9 * depth
    medium_ref[...] = wide_ref[first:]
    for plane in range(3 * depth):
        near_ref[plane] = narrowed(wide_ref[first + plane])
    state, near = fields_of(state_ref, 9, depth), fields_of(near_ref, 3, depth)
    for step in range(3):

        def emit(z, strains, step=step):
            for number, strain in enumerate(strains):
                base = ((step * 6 + number) * depth + z) * TILE_X
                strain_ref[base : base + TILE_X, :] = strain[0:TILE_X, 0:LANES]

        if step == 0:
            advance(fields_of(wide_ref, 9, depth), fields_of(wide_ref, 3, depth, 9), emit, state)
            continue
        for z in range(depth):
            load = source_ref[(step - 1) * depth + z]
            for number in range(3, 6):
                state[number][z] = state[number][z] + load
        advance(state, near, emit, state if step == 1 else None)
    axial = jnp.concatenate(
        [strain_ref[step * 6 * cells_row : (step * 6 + 2) * cells_row, :] for step in range(3)], axis=0
    )
    axial = jnp.concatenate(pieces(axial), axis=0).astype(BF16)
    rows_down = iota((cells_row, LANES), 0)
    slots_down = packed_iota(LANES, 2)
    for block in range(slot_ref.shape[0]):
        lanes = slice(block * LANES, (block + 1) * LANES)
        if block % 2 == 0:
            both = sum_thirds(times(axial, cover_ref[:, block * LANES : (block + 2) * LANES]))
        windows = both[:, :LANES] if block % 2 == 0 else both[:, LANES:]
        at_row = rows_down == row_ref[block : block + 1, :]
        weight_x, weight_y = weight_ref[0:1, lanes], weight_ref[1:2, lanes]
        sums = []
        for step in range(3):
            base = 2 * step * cells_row
            axial_sum = (
                weight_x * windows[base : base + cells_row]
                + weight_y * windows[base + cells_row : base + 2 * cells_row]
            )
            sums.append(jnp.sum(jnp.where(at_row, axial_sum, 0.0), axis=0, keepdims=True))
        sums.append(channel_ref[block : block + 1, :].astype(F32))
        values = jnp.concatenate(sums + sums, axis=0)
        in_slot = slots_down == packed_rows(slot_ref[block : block + 1, :], LANES)
        for third, piece in enumerate(pieces(values)):
            tile = jnp.concatenate([piece, piece], axis=0).astype(BF16)
            spread_ref[third * LANES : (third + 1) * LANES, lanes] = jnp.where(
                in_slot, jnp.concatenate([tile] * (LANES // 16), axis=0), jnp.zeros((), BF16)
            )
    out_ref[...] = sum_thirds(times_turned(spread_ref[...], place_ref[...]))


def owner_body(arrived_ref, observed_ref, residual_ref, reply_ref, values_ref, place_ref, held_ref):
    groups = arrived_ref.shape[0] // 4
    parts = observed_ref.shape[1] // LANES
    down = packed_iota(LANES)
    part_down = iota((parts, LANES), 0)
    nothing = jnp.zeros((parts, LANES), F32)
    numbers = [arrived_ref[4 * s + 3 : 4 * s + 4, :].astype(I32) for s in range(groups)]
    for s in range(groups):
        lanes = slice(s * LANES, (s + 1) * LANES)
        place_ref[:, lanes] = jnp.where(
            down == packed_rows(numbers[s] & (LANES - 1), LANES), jnp.ones((), BF16), jnp.zeros((), BF16)
        )
        at_part = part_down == (numbers[s] >> 7)
        thirds = pieces(arrived_ref[4 * s : 4 * s + 3, :])
        stack = []
        for third in thirds:
            for step in range(3):
                stack.append(jnp.where(at_part, third[step : step + 1, :], 0.0))
            stack.append(nothing)
        values_ref[:, lanes] = jnp.concatenate(stack, axis=0).astype(BF16)
    sums = sum_thirds(times_turned(values_ref[...], place_ref[...]))
    for step in range(3):
        for part in range(parts):
            at = step * parts + part
            held_ref[at : at + 1, :] = observed_ref[step : step + 1, part * LANES : (part + 1) * LANES]
    held_ref[3 * parts :, :] = nothing
    held_ref[...] = sums - held_ref[...]
    for step in range(3):
        for part in range(parts):
            at = step * parts + part
            residual_ref[step : step + 1, part * LANES : (part + 1) * LANES] = held_ref[at : at + 1, :]
    residual = jnp.concatenate(two_pieces(held_ref[...]), axis=0).astype(BF16)
    for s in range(groups):
        if s % 2 == 0:
            both = sum_halves(times(residual, place_ref[:, s * LANES : (s + 2) * LANES]))
        found = both[:, :LANES] if s % 2 == 0 else both[:, LANES:]
        at_part = part_down == (numbers[s] >> 7)
        for step in range(3):
            reply_ref[4 * s + step : 4 * s + step + 1, :] = jnp.sum(
                jnp.where(at_part, found[step * parts : (step + 1) * parts], 0.0), axis=0, keepdims=True
            )
        reply_ref[4 * s + 3 : 4 * s + 4, :] = jnp.zeros((1, LANES), F32)


def load_body(
    arrived_ref,
    slot_ref,
    row_ref,
    weight_ref,
    cover_ref,
    place_ref,
    load_ref,
    out_ref,
    spread_ref,
    side_ref,
    sent_sides,
):
    cells_row = load_ref.shape[0] // 6
    stack_rows = load_ref.shape[0]
    arrived = jnp.concatenate(two_pieces(arrived_ref[...]), axis=0).astype(BF16)
    slots_down = iota((LANES, LANES), 0) >> 2
    rows_down = packed_iota(cells_row)
    for block in range(slot_ref.shape[0]):
        lanes = slice(block * LANES, (block + 1) * LANES)
        if block % 2 == 0:
            both = sum_halves(times(arrived, place_ref[:, block * LANES : (block + 2) * LANES]))
        found = both[:, :LANES] if block % 2 == 0 else both[:, LANES:]
        found = jnp.where(slots_down == slot_ref[block : block + 1, :], found, 0.0)
        folded = found[0:8]
        for part in range(1, LANES // 8):
            folded = folded + found[8 * part : 8 * part + 8]
        folded = folded + pltpu.roll(folded, 4, 0)
        at_row = rows_down == packed_rows(row_ref[block : block + 1, :], cells_row)
        for turn in range(3):
            back = folded[2 - turn : 3 - turn, :]
            for part in range(2):
                for half, piece in enumerate(two_pieces(weight_ref[part : part + 1, lanes] * back)):
                    base = half * stack_rows + (2 * turn + part) * cells_row
                    spread_ref[base : base + cells_row, lanes] = jnp.where(
                        at_row, packed_rows(piece, cells_row), jnp.zeros((), BF16)
                    )
    cover = jnp.concatenate([cover_ref[0:16, :], cover_ref[LANES - 16 :, :]], axis=0)
    edges = times_turned(cover, spread_ref[0:stack_rows, :]) + times_turned(cover, spread_ref[stack_rows:, :])
    side_ref[...] = jnp.zeros_like(side_ref)
    for side, base in ((0, 0), (1, 32 - RIM)):
        for column in range(RIM):
            lanes = slice(column * LANES, column * LANES + stack_rows)
            side_ref[side, 0:1, lanes] = edges[base + column : base + column + 1, :]
    sides = start_sides(side_ref, out_ref, sent_sides)
    load_ref[...] = sum_halves(times_turned(spread_ref[...], cover_ref[...]))
    wait_sides(sides)


def adjoint_body(
    load_ref,
    higher_ref,
    lower_ref,
    recv_ref,
    strain_ref,
    medium_ref,
    residual_ref,
    gradient_ref,
    residual_out_ref,
    first_ref,
    later_ref,
    velocity_ref,
    state_ref,
    near_ref,
    turn_ref,
):
    depth = medium_ref.shape[0] // 3
    rims = rim_rows(recv_ref, turn_ref)
    lay_planes(first_ref, later_ref, 0, load_ref, higher_ref, lower_ref)
    lay_planes(first_ref, later_ref, LANES, *rims)
    for plane in range(3 * depth):
        near_ref[plane] = narrowed(medium_ref[plane])
    gradient_ref[...] = jnp.zeros_like(gradient_ref)
    residual_out_ref[...] = residual_ref[...]
    state, near, medium = (
        fields_of(state_ref, 9, depth),
        fields_of(near_ref, 3, depth),
        fields_of(medium_ref, 3, depth),
    )

    def add_terms(turn, z, strains):
        dilation, dilation_back, doubled, product = None, None, None, None
        for number, strain in enumerate(strains):
            base = (((2 - turn) * 6 + number) * depth + z) * TILE_X
            forward = strain_ref[base : base + TILE_X, :]
            if number < 3:
                dilation = forward if dilation is None else dilation + forward
            if strain is None:
                continue
            back = strain[0:TILE_X, 0:LANES]
            term = forward * back
            if number < 3:
                dilation_back = back if dilation_back is None else dilation_back + back
                doubled = term if doubled is None else doubled + term
            else:
                product = term if product is None else product + term
        for part, term in enumerate((dilation * dilation_back, 2.0 * doubled + product)):
            base = (part * depth + z) * TILE_X
            gradient_ref[base : base + TILE_X, :] = gradient_ref[base : base + TILE_X, :] + term

    loads, velocity = fields_of(first_ref, 2, depth), fields_of(velocity_ref, 2, depth)
    for z in range(depth):
        scale = STEP * medium[2][z]
        velocity[0][z] = scale * ahead_x(loads[0][z])
        velocity[1][z] = scale * ahead_y(loads[1][z])
        state[0][z] = narrowed(velocity[0][z])
        state[1][z] = narrowed(velocity[1][z])
        state[2][z] = jnp.zeros((SPAN_NEAR, SPAN_Y), F32)
    for z in range(depth):
        along_x, along_y = velocity[0][z], velocity[1][z]
        strain_x, strain_y = behind_x(along_x), behind_y(along_y)
        sheared = (
            ahead_y(along_x) + ahead_x(along_y),
            ahead_z(velocity[0], z),
            ahead_z(velocity[1], z),
        )
        add_terms(0, z, (strain_x, strain_y, None) + sheared)
        dilated = medium[0][z] * (strain_x + strain_y)
        shear = medium[1][z]
        state[3][z] = narrowed(loads[0][z] + STEP * (dilated + 2.0 * shear * strain_x))
        state[4][z] = narrowed(loads[1][z] + STEP * (dilated + 2.0 * shear * strain_y))
        state[5][z] = narrowed(STEP * dilated)
        for number, strain in enumerate(sheared):
            state[6 + number][z] = narrowed(STEP * shear * strain)
    for turn in (1, 2):
        for part in range(2):
            for z in range(depth):
                load = later_ref[(2 * (turn - 1) + part) * depth + z]
                state[3 + part][z] = state[3 + part][z] + load
        advance(state, near, functools.partial(add_terms, turn), state if turn == 1 else None)


def shards(
    initial_state,
    lame_lambda,
    shear_modulus,
    buoyancy,
    source_cells,
    source_wavelet,
    segment_start,
    segment_weight,
    partial_owner,
    partial_channel,
    observed_data,
):
    depth, rows_x, cols_y = lame_lambda.shape
    part_count = segment_start.shape[0]
    count_x, count_y = lax.axis_size("gx"), lax.axis_size("gy")
    devices = count_x * count_y
    capacity = max(2, 2 * part_count // devices)
    slot_groups = devices * capacity // LANES
    blocks = part_count // LANES
    per_group = LANES // capacity
    cells_row = depth * rows_x
    both = ("gx", "gy")
    up = [(i, i + 1) for i in range(count_x - 1)]
    down = [(j, i) for i, j in up]
    shape = jax.ShapeDtypeStruct

    def exchange(chunks):
        return lax.all_to_all(chunks, both, split_axis=0, concat_axis=0, tiled=True)

    def to_owners(rows):
        chunks = rows.reshape(slot_groups, 4, per_group, capacity).transpose(0, 2, 1, 3)
        back = exchange(chunks.reshape(devices, 4, capacity)).reshape(slot_groups, per_group, 4, capacity)
        return back.transpose(0, 2, 1, 3).reshape(slot_groups * 4, LANES)

    trimmed = shape((14 * depth * RIM, cols_y), F32)
    fields, high, low, edges = call_kernel(
        pack_body,
        "pack_edges",
        [shape((14 * cells_row, cols_y), F32), trimmed, trimmed, shape((devices, 1, 2 * RIM * LANES), F32)],
        [
            pltpu.VMEM((14 * cells_row, cols_y), F32),
            pltpu.VMEM(trimmed.shape, F32),
            pltpu.VMEM(trimmed.shape, F32),
            pltpu.VMEM((2, 1, 2 * RIM * LANES), F32),
            pltpu.VMEM((1, source_cells.shape[0]), I32),
            pltpu.VMEM(source_wavelet.shape, F32),
            pltpu.SemaphoreType.DMA((6,)),
            pltpu.SemaphoreType.DMA((3,)),
            pltpu.SemaphoreType.DMA((6,)),
        ],
        *[values.reshape(-1, cols_y) for values in (initial_state, lame_lambda, shear_modulus, buoyancy)],
        source_cells.reshape(1, -1),
        source_wavelet,
        place=pl.ANY,
        place_out=pl.ANY,
        room=60 * 1024 * 1024,
    )
    lower = lax.ppermute(high, "gx", up)
    higher = lax.ppermute(low, "gx", down)
    rims = exchange(edges)
    channels = partial_channel.reshape(blocks, LANES)
    slot, row, cover, place = call_kernel(
        functools.partial(slots_body, capacity, devices, cols_y),
        "segment_slots",
        [
            shape((blocks, LANES), I32),
            shape((blocks, LANES), I32),
            shape((cols_y, part_count), BF16),
            shape((LANES, part_count), BF16),
        ],
        [pltpu.VMEM((blocks, LANES), F32)],
        partial_owner.reshape(blocks, LANES),
        segment_start.reshape(blocks, LANES),
    )
    partials, strains, medium = call_kernel(
        forward_body,
        "forward_run",
        [
            shape((slot_groups * 4, LANES), F32),
            shape((18 * cells_row, cols_y), F32),
            shape((3 * depth, SPAN_X, SPAN_Y), F32),
        ],
        [
            pltpu.VMEM((12 * depth, SPAN_X, SPAN_Y), F32),
            pltpu.VMEM((2 * depth, SPAN_NEAR, SPAN_Y), F32),
            pltpu.VMEM((9 * depth, SPAN_NEAR, SPAN_Y), F32),
            pltpu.VMEM((3 * depth, SPAN_NEAR, SPAN_Y), F32),
            pltpu.VMEM((LANES, 2 * LANES), F32),
            pltpu.VMEM((2, 14 * cells_row, cols_y), F32),
            pltpu.VMEM((3 * LANES, part_count), BF16),
        ],
        fields,
        lower,
        higher,
        rims,
        slot,
        row,
        segment_weight,
        channels,
        cover,
        place,
    )
    parts = observed_data.shape[1] // LANES
    residuals, reply = call_kernel(
        owner_body,
        "channel_sums",
        [shape(observed_data.shape, F32), shape((slot_groups * 4, LANES), F32)],
        [
            pltpu.VMEM((12 * parts, slot_groups * LANES), BF16),
            pltpu.VMEM((LANES, slot_groups * LANES), BF16),
            pltpu.VMEM((4 * parts, LANES), F32),
        ],
        to_owners(partials),
        observed_data,
    )
    loads, load_edges = call_kernel(
        load_body,
        "segment_loads",
        [shape((6 * cells_row, cols_y), F32), shape((devices, 1, RIM * LANES), F32)],
        [
            pltpu.VMEM((12 * cells_row, part_count), BF16),
            pltpu.VMEM((2, 1, RIM * LANES), F32),
            pltpu.SemaphoreType.DMA((6,)),
        ],
        to_owners(reply),
        slot,
        row,
        segment_weight,
        cover,
        place,
        place_out=(pltpu.VMEM, pl.ANY),
    )
    load_lower = lax.ppermute(loads, "gx", up)
    load_higher = lax.ppermute(loads, "gx", down)
    load_rims = exchange(load_edges)
    gradients, residuals = call_kernel(
        adjoint_body,
        "adjoint_run",
        [shape((2 * cells_row, cols_y), F32), shape(observed_data.shape, F32)],
        [
            pltpu.VMEM((2 * depth, SPAN_X, SPAN_Y), F32),
            pltpu.VMEM((4 * depth, SPAN_NEAR, SPAN_Y), F32),
            pltpu.VMEM((2 * depth, SPAN_X, SPAN_Y), F32),
            pltpu.VMEM((9 * depth, SPAN_NEAR, SPAN_Y), F32),
            pltpu.VMEM((3 * depth, SPAN_NEAR, SPAN_Y), F32),
            pltpu.VMEM((LANES, LANES), F32),
        ],
        loads,
        load_higher,
        load_lower,
        load_rims,
        strains,
        medium,
        residuals,
    )
    return (residuals, gradients.reshape(2, depth, rows_x, cols_y))


def solution(mesh):
    in_specs = (
        P(None, None, "gx", "gy"),
        P(None, "gx", "gy"),
        P(None, "gx", "gy"),
        P(None, "gx", "gy"),
        P(("gx", "gy")),
        P(None, ("gx", "gy")),
        P(("gx", "gy")),
        P(None, ("gx", "gy")),
        P(("gx", "gy"), None),
        P(("gx", "gy")),
        P(None, ("gx", "gy")),
    )
    out_specs = (P(None, ("gx", "gy")), P(None, None, "gx", "gy"))
    return jax.shard_map(shards, mesh=mesh, in_specs=in_specs, out_specs=out_specs, check_vma=False)
```

```python
import functools

import jax
import jax.numpy as jnp
from jax import lax
from jax.experimental import pallas as pl
from jax.experimental.pallas import tpu as pltpu
from jax.sharding import PartitionSpec as P

GAUGE = 8
STEP = 0.25
RIM = 3
LANES = 128
TILE_X = 4
SPAN_X = 16
SPAN_NEAR = 8
SPAN_Y = 256
F32, BF16, I32 = jnp.float32, jnp.bfloat16, jnp.int32
NEAR = tuple((dx, dy) for dx in (-1, 0, 1) for dy in (-1, 0, 1))


def call_kernel(
    body, name, outs, scratch, *args, place=pltpu.VMEM, place_out=pltpu.VMEM, room=24 * 1024 * 1024
):
    spaces = place_out if isinstance(place_out, tuple) else (place_out,) * len(outs)
    return pl.pallas_call(
        body,
        name=name,
        out_shape=outs,
        in_specs=[pl.BlockSpec(memory_space=place)] * len(args),
        out_specs=[pl.BlockSpec(memory_space=space) for space in spaces],
        scratch_shapes=scratch,
        compiler_params=pltpu.CompilerParams(vmem_limit_bytes=room),
    )(*args)


def pieces(values):
    high = values.astype(BF16).astype(F32)
    rest = values - high
    middle = rest.astype(BF16).astype(F32)
    return high, middle, rest - middle


def iota(shape, dim):
    return lax.broadcasted_iota(I32, shape, dim)


def times(left, right):
    return lax.dot_general(left, right, (((1,), (0,)), ((), ())), preferred_element_type=F32)


def times_turned(left, right):
    return lax.dot_general(left, right, (((1,), (1,)), ((), ())), preferred_element_type=F32)


def packed_rows(row, height):
    tile = jnp.broadcast_to(row.astype(F32), (16, row.shape[1])).astype(BF16)
    return jnp.concatenate([tile] * (height // 16), axis=0) if height > 16 else tile


def packed_iota(height, shift=0):
    return (iota((height, LANES), 0) >> shift).astype(F32).astype(BF16)


def two_pieces(values):
    high = values.astype(BF16).astype(F32)
    return high, values - high


def sum_halves(values):
    half = values.shape[0] // 2
    return values[:half] + values[half:]


def sum_thirds(values):
    third = values.shape[0] // 3
    return values[:third] + values[third : 2 * third] + values[2 * third :]


def neighbour(dx, dy):
    count_x, count_y = lax.axis_size("gx"), lax.axis_size("gy")
    at_x, at_y = lax.axis_index("gx") + dx, lax.axis_index("gy") + dy
    inside = (at_x >= 0) & (at_x < count_x) & (at_y >= 0) & (at_y < count_y)
    return jnp.where(inside, at_x * count_y + at_y, 0), inside


def edge_columns(rows, side_ref):
    width = rows.shape[0]
    turned = rows.T
    for side, base in ((0, 0), (1, LANES - RIM)):
        for column in range(RIM):
            side_ref[side, 0:1, column * width : (column + 1) * width] = turned[base + column : base + column + 1, :]


def start_sides(side_ref, out_ref, sent):
    sides = []
    for number, (dx, dy) in enumerate((dx, dy) for dx, dy in NEAR if dy):
        index, inside = neighbour(dx, dy)
        source, target = side_ref.at[1 if dy > 0 else 0], out_ref.at[index]
        sides.append((inside, pltpu.make_async_copy(source, target, sent.at[number])))
    for inside, copy in sides:
        pl.when(inside)(copy.start)
    return sides


def wait_sides(sides):
    for inside, copy in sides:
        pl.when(inside)(copy.wait)


def arrived_chunk(recv_ref, dx, dy):
    index, inside = neighbour(dx, dy)
    return jnp.where(inside, recv_ref[index], 0.0)


def rim_rows(recv_ref, dx, turn_ref):
    width = turn_ref.shape[1]
    for dy, base in ((1, 0), (-1, LANES - RIM)):
        chunk = arrived_chunk(recv_ref, dx, dy)
        for column in range(RIM):
            turn_ref[base + column : base + column + 1, :] = chunk[:, column * width : (column + 1) * width]
    return turn_ref[...].T


def lay_planes(wide_ref, narrow_ref, lane, centre, higher, lower):
    row = iota((8, LANES), 0)
    wide = wide_ref.shape[0]
    lanes = slice(lane, lane + LANES)
    for plane in range(wide + narrow_ref.shape[0]):
        rows = slice(8 * (plane // 2), 8 * (plane // 2) + 8)
        mid, high, low = centre[rows], higher[rows], lower[rows]
        if plane % 2:
            mid = pltpu.roll(mid, TILE_X, 0)
        else:
            high, low = pltpu.roll(high, TILE_X, 0), pltpu.roll(low, TILE_X, 0)
        near = jnp.where(row < TILE_X, mid, high)
        if plane < wide:
            wide_ref[plane, 0:8, lanes] = near
            wide_ref[plane, 8:16, lanes] = jnp.where(row < TILE_X, 0.0, low)
        else:
            narrow_ref[plane - wide, :, lanes] = jnp.where(row < SPAN_NEAR - 2, near, low)


def narrowed(plane):
    row = iota((SPAN_NEAR, plane.shape[1]), 0)
    return jnp.where(row < SPAN_NEAR - 2, plane[:SPAN_NEAR], plane[SPAN_NEAR:])


def ahead_x(plane):
    return pltpu.roll(plane, plane.shape[0] - 1, 0) - plane


def behind_x(plane):
    return plane - pltpu.roll(plane, 1, 0)


def ahead_y(plane):
    return pltpu.roll(plane, SPAN_Y - 1, 1) - plane


def behind_y(plane):
    return plane - pltpu.roll(plane, 1, 1)


def ahead_z(planes, z):
    return planes[z + 1] - planes[z] if z + 1 < len(planes) else -planes[z]


def behind_z(planes, z):
    return planes[z] - planes[z - 1] if z else planes[z]


class Planes:
    def __init__(self, ref, first, depth):
        self.ref, self.first, self.depth = ref, first, depth

    def __len__(self):
        return self.depth

    def __getitem__(self, z):
        return self.ref[self.first + z]

    def __setitem__(self, z, plane):
        self.ref[self.first + z] = plane


def fields_of(ref, count, depth, first=0):
    return [Planes(ref, (first + number) * depth, depth) for number in range(count)]


def strain_rates(velocity, z):
    along_x, along_y, along_z = [field[z] for field in velocity]
    return (
        behind_x(along_x),
        behind_y(along_y),
        behind_z(velocity[2], z),
        ahead_y(along_x) + ahead_x(along_y),
        ahead_z(velocity[0], z) + ahead_x(along_z),
        ahead_z(velocity[1], z) + ahead_y(along_z),
    )


def new_stress(stress, strains, lame_lambda, shear_modulus, z):
    dilated = lame_lambda[z] * (strains[0] + strains[1] + strains[2])
    shear = shear_modulus[z]
    normal = [stress[n][z] + STEP * (dilated + 2.0 * shear * strains[n]) for n in range(3)]
    return normal + [stress[n][z] + STEP * shear * strains[n] for n in range(3, 6)]


def advance(state, medium, emit, target):
    velocity, stress = state[:3], state[3:]
    lame_lambda, shear_modulus, buoyancy = medium
    depth = len(buoyancy)
    wide = target is not None and target is not state
    for z in range(depth):
        scale = STEP * buoyancy[z]
        accel = (
            ahead_x(stress[0][z]) + behind_y(stress[3][z]) + behind_z(stress[4], z),
            behind_x(stress[3][z]) + ahead_y(stress[1][z]) + behind_z(stress[5], z),
            behind_x(stress[4][z]) + behind_y(stress[5][z]) + ahead_z(stress[2], z),
        )
        for number in range(3):
            moved = velocity[number][z] + scale * accel[number]
            velocity[number][z] = moved
            if wide:
                target[number][z] = narrowed(moved)
    for z in range(depth):
        strains = strain_rates(velocity, z)
        emit(z, strains)
        if target is not None:
            for number, plane in enumerate(new_stress(stress, strains, lame_lambda, shear_modulus, z)):
                target[3 + number][z] = narrowed(plane) if wide else plane


def pack_body(*refs):
    inputs, outputs, scratch = refs[:6], refs[6:10], refs[10:]
    fields_ref, high_ref, low_ref, side_ref, cells_ref, wavelet_ref, arrived, sent, sent_sides = scratch
    targets, at = [], 0
    for source in inputs[:4]:
        targets.append(fields_ref.at[at : at + source.shape[0]])
        at = at + source.shape[0]
    copies = [
        pltpu.make_async_copy(source, target, arrived.at[number])
        for number, (source, target) in enumerate(zip(inputs, targets + [cells_ref, wavelet_ref]))
    ]
    for copy in copies:
        copy.start()
    copies[4].wait()
    copies[5].wait()
    cells_row = inputs[1].shape[0]
    cells = cells_ref[...]
    count = cells.shape[1]
    at_lane = iota((LANES, count), 0) == (cells & (LANES - 1))
    at_row = iota((cells_row, count), 0) == (cells >> (LANES.bit_length() - 1))
    stack = [
        jnp.where(at_row, third[step : step + 1, :], 0.0) for third in pieces(wavelet_ref[...]) for step in range(3)
    ]
    maps = sum_thirds(
        times_turned(jnp.concatenate(stack, axis=0).astype(BF16), jnp.where(at_lane, 1.0, 0.0).astype(BF16))
    )
    for copy in copies[:4]:
        copy.wait()
    fields_ref[at:, :] = maps[cells_row:]
    for number in range(3, 6):
        rows = slice(number * cells_row, (number + 1) * cells_row)
        fields_ref[rows, :] = fields_ref[rows, :] + maps[:cells_row]
    height = fields_ref.shape[0] // TILE_X
    for x in range(TILE_X):
        slab = fields_ref[pl.ds(x, height, stride=TILE_X), :]
        if x < RIM:
            low_ref[x * height : (x + 1) * height, :] = slab
        if x >= TILE_X - RIM:
            at = x - TILE_X + RIM
            high_ref[at * height : (at + 1) * height, :] = slab
    writes = [
        pltpu.make_async_copy(source, target, sent.at[number])
        for number, (source, target) in enumerate(zip((fields_ref, high_ref, low_ref), outputs))
    ]
    for copy in writes:
        copy.start()
    rows = fields_ref[...]
    spare = 2 * LANES - rows.shape[0]
    edge_columns(jnp.concatenate([rows, jnp.zeros((spare, LANES), F32)], axis=0), side_ref)
    sides = start_sides(side_ref, outputs[3], sent_sides)
    for copy in writes:
        copy.wait()
    wait_sides(sides)


def slots_body(capacity, devices, cols_y, owner_ref, start_ref, slot_ref, row_ref, cover_ref, place_ref, rank_ref):
    blocks = owner_ref.shape[0]
    group = 32
    before = jnp.where(iota((LANES, 2 * LANES), 0) < iota((LANES, 2 * LANES), 1), 1.0, 0.0).astype(BF16)
    rank_ref[...] = jnp.zeros_like(rank_ref)

    def count_group(number, carry):
        names = iota((group, LANES), 0) + number * group
        hot = [names == owner_ref[b : b + 1, :] for b in range(blocks)]
        marks = jnp.concatenate([jnp.where(h, 1.0, 0.0) for h in hot], axis=0).astype(BF16)
        counts = times(marks, before)
        total = jnp.zeros((group, LANES), F32)
        for b in range(blocks):
            part = counts[b * group : (b + 1) * group]
            rank_ref[b : b + 1, :] = rank_ref[b : b + 1, :] + jnp.sum(
                jnp.where(hot[b], part[:, :LANES] + total, 0.0), axis=0, keepdims=True
            )
            total = total + part[:, LANES:]
        return carry

    if devices == group:
        count_group(0, 0)
    else:
        lax.fori_loop(0, devices // group, count_group, 0)
    slot = owner_ref[...] * capacity + rank_ref[...].astype(I32)
    slot_ref[...] = slot >> 7
    low = slot & (LANES - 1)
    span = cols_y - GAUGE + 1
    start = start_ref[...]
    row = ((start.astype(F32) + 0.5) * (1.0 / span)).astype(I32)
    row_ref[...] = row
    first = start - row * span
    down = iota((LANES, LANES), 0)
    for b in range(blocks):
        lanes = slice(b * LANES, (b + 1) * LANES)
        offset = down - first[b : b + 1, :]
        cover_ref[:, lanes] = jnp.where((offset >= 0) & (offset < GAUGE), 1.0, 0.0).astype(BF16)
        place_ref[:, lanes] = jnp.where(down == low[b : b + 1, :], 1.0, 0.0).astype(BF16)


def forward_body(
    fields_ref,
    lower_ref,
    higher_ref,
    recv_ref,
    slot_ref,
    row_ref,
    weight_ref,
    channel_ref,
    cover_ref,
    place_ref,
    out_ref,
    strain_ref,
    medium_ref,
    wide_ref,
    source_ref,
    state_ref,
    near_ref,
    turn_ref,
    sides_ref,
    spread_ref,
):
    depth = medium_ref.shape[0] // 3
    cells_row = depth * TILE_X
    turn_ref[...] = jnp.zeros_like(turn_ref)
    rims = [rim_rows(recv_ref, dx, turn_ref) for dx in (0, 1, -1)]
    height = fields_ref.shape[0] // TILE_X
    sides_ref[...] = jnp.zeros_like(sides_ref)
    for x in range(RIM):
        slab = slice(x * height, (x + 1) * height)
        sides_ref[0, pl.ds(x, height, stride=TILE_X), :] = higher_ref[slab, :]
        sides_ref[1, pl.ds(x + TILE_X - RIM, height, stride=TILE_X), :] = lower_ref[slab, :]
    lay_planes(wide_ref, source_ref, 0, fields_ref, sides_ref.at[0], sides_ref.at[1])
    lay_planes(wide_ref, source_ref, LANES, *rims)
    first = 9 * depth
    medium_ref[...] = wide_ref[first:]
    for plane in range(3 * depth):
        near_ref[plane] = narrowed(wide_ref[first + plane])
    state, near = fields_of(state_ref, 9, depth), fields_of(near_ref, 3, depth)
    for step in range(3):

        def emit(z, strains, step=step):
            for number, strain in enumerate(strains):
                base = ((step * 6 + number) * depth + z) * TILE_X
                strain_ref[base : base + TILE_X, :] = strain[0:TILE_X, 0:LANES]

        if step == 0:
            advance(fields_of(wide_ref, 9, depth), fields_of(wide_ref, 3, depth, 9), emit, state)
            continue
        for z in range(depth):
            load = source_ref[(step - 1) * depth + z]
            for number in range(3, 6):
                state[number][z] = state[number][z] + load
        advance(state, near, emit, state if step == 1 else None)
    axial = jnp.concatenate(
        [strain_ref[step * 6 * cells_row : (step * 6 + 2) * cells_row, :] for step in range(3)], axis=0
    )
    axial = jnp.concatenate(pieces(axial), axis=0).astype(BF16)
    rows_down = iota((cells_row, LANES), 0)
    slots_down = packed_iota(LANES, 2)
    for block in range(slot_ref.shape[0]):
        lanes = slice(block * LANES, (block + 1) * LANES)
        if block % 2 == 0:
            both = sum_thirds(times(axial, cover_ref[:, block * LANES : (block + 2) * LANES]))
        windows = both[:, :LANES] if block % 2 == 0 else both[:, LANES:]
        at_row = rows_down == row_ref[block : block + 1, :]
        weight_x, weight_y = weight_ref[0:1, lanes], weight_ref[1:2, lanes]
        sums = []
        for step in range(3):
            base = 2 * step * cells_row
            axial_sum = (
                weight_x * windows[base : base + cells_row]
                + weight_y * windows[base + cells_row : base + 2 * cells_row]
            )
            sums.append(jnp.sum(jnp.where(at_row, axial_sum, 0.0), axis=0, keepdims=True))
        sums.append(channel_ref[block : block + 1, :].astype(F32))
        values = jnp.concatenate(sums + sums, axis=0)
        in_slot = slots_down == packed_rows(slot_ref[block : block + 1, :], LANES)
        for third, piece in enumerate(pieces(values)):
            tile = jnp.concatenate([piece, piece], axis=0).astype(BF16)
            spread_ref[third * LANES : (third + 1) * LANES, lanes] = jnp.where(
                in_slot, jnp.concatenate([tile] * (LANES // 16), axis=0), jnp.zeros((), BF16)
            )
    out_ref[...] = sum_thirds(times_turned(spread_ref[...], place_ref[...]))


def owner_body(arrived_ref, observed_ref, residual_ref, reply_ref, values_ref, place_ref, held_ref):
    groups = arrived_ref.shape[0] // 4
    parts = observed_ref.shape[1] // LANES
    down = packed_iota(LANES)
    part_down = iota((parts, LANES), 0)
    nothing = jnp.zeros((parts, LANES), F32)
    numbers = [arrived_ref[4 * s + 3 : 4 * s + 4, :].astype(I32) for s in range(groups)]
    for s in range(groups):
        lanes = slice(s * LANES, (s + 1) * LANES)
        place_ref[:, lanes] = jnp.where(
            down == packed_rows(numbers[s] & (LANES - 1), LANES), jnp.ones((), BF16), jnp.zeros((), BF16)
        )
        at_part = part_down == (numbers[s] >> 7)
        thirds = pieces(arrived_ref[4 * s : 4 * s + 3, :])
        stack = []
        for third in thirds:
            for step in range(3):
                stack.append(jnp.where(at_part, third[step : step + 1, :], 0.0))
            stack.append(nothing)
        values_ref[:, lanes] = jnp.concatenate(stack, axis=0).astype(BF16)
    sums = sum_thirds(times_turned(values_ref[...], place_ref[...]))
    for step in range(3):
        for part in range(parts):
            at = step * parts + part
            held_ref[at : at + 1, :] = observed_ref[step : step + 1, part * LANES : (part + 1) * LANES]
    held_ref[3 * parts :, :] = nothing
    held_ref[...] = sums - held_ref[...]
    for step in range(3):
        for part in range(parts):
            at = step * parts + part
            residual_ref[step : step + 1, part * LANES : (part + 1) * LANES] = held_ref[at : at + 1, :]
    residual = jnp.concatenate(two_pieces(held_ref[...]), axis=0).astype(BF16)
    for s in range(groups):
        if s % 2 == 0:
            both = sum_halves(times(residual, place_ref[:, s * LANES : (s + 2) * LANES]))
        found = both[:, :LANES] if s % 2 == 0 else both[:, LANES:]
        at_part = part_down == (numbers[s] >> 7)
        for step in range(3):
            reply_ref[4 * s + step : 4 * s + step + 1, :] = jnp.sum(
                jnp.where(at_part, found[step * parts : (step + 1) * parts], 0.0), axis=0, keepdims=True
            )
        reply_ref[4 * s + 3 : 4 * s + 4, :] = jnp.zeros((1, LANES), F32)


def load_body(
    arrived_ref,
    slot_ref,
    row_ref,
    weight_ref,
    cover_ref,
    place_ref,
    strain_ref,
    load_ref,
    side_ref,
    spread_ref,
):
    stack_rows = load_ref.shape[0] - strain_ref.shape[0]
    cells_row = stack_rows // 6
    load_ref[stack_rows:, :] = strain_ref[...]
    arrived = jnp.concatenate(two_pieces(arrived_ref[...]), axis=0).astype(BF16)
    slots_down = iota((LANES, LANES), 0) >> 2
    rows_down = packed_iota(cells_row)
    for block in range(slot_ref.shape[0]):
        lanes = slice(block * LANES, (block + 1) * LANES)
        if block % 2 == 0:
            both = sum_halves(times(arrived, place_ref[:, block * LANES : (block + 2) * LANES]))
        found = both[:, :LANES] if block % 2 == 0 else both[:, LANES:]
        found = jnp.where(slots_down == slot_ref[block : block + 1, :], found, 0.0)
        folded = found[0:8]
        for part in range(1, LANES // 8):
            folded = folded + found[8 * part : 8 * part + 8]
        folded = folded + pltpu.roll(folded, 4, 0)
        at_row = rows_down == packed_rows(row_ref[block : block + 1, :], cells_row)
        for turn in range(3):
            back = folded[2 - turn : 3 - turn, :]
            for part in range(2):
                for half, piece in enumerate(two_pieces(weight_ref[part : part + 1, lanes] * back)):
                    base = half * stack_rows + (2 * turn + part) * cells_row
                    spread_ref[base : base + cells_row, lanes] = jnp.where(
                        at_row, packed_rows(piece, cells_row), jnp.zeros((), BF16)
                    )
    cover = jnp.concatenate([cover_ref[0:16, :], cover_ref[LANES - 16 :, :]], axis=0)
    edges = times_turned(cover, spread_ref[0:stack_rows, :]) + times_turned(cover, spread_ref[stack_rows:, :])
    side_ref[...] = jnp.zeros_like(side_ref)
    for side, base in ((0, 0), (1, 32 - RIM)):
        for column in range(RIM):
            lanes = slice(column * LANES, column * LANES + stack_rows)
            side_ref[side, 0:1, lanes] = edges[base + column : base + column + 1, :]
    load_ref[0:stack_rows, :] = sum_halves(times_turned(spread_ref[...], cover_ref[...]))


def rims_body(load_ref, side_ref, copy_ref, out_ref, sent_sides):
    sides = start_sides(side_ref, out_ref, sent_sides)
    copy_ref[...] = load_ref[0 : copy_ref.shape[0], :]
    wait_sides(sides)


def adjoint_body(
    load_ref,
    higher_ref,
    lower_ref,
    recv_ref,
    strain_ref,
    medium_ref,
    residual_ref,
    gradient_ref,
    residual_out_ref,
    first_ref,
    later_ref,
    velocity_ref,
    state_ref,
    near_ref,
    turn_ref,
):
    depth = medium_ref.shape[0] // 3
    turn_ref[...] = jnp.zeros_like(turn_ref)
    rims = [rim_rows(recv_ref, dx, turn_ref) for dx in (0, 1, -1)]
    lay_planes(first_ref, later_ref, 0, load_ref, higher_ref, lower_ref)
    lay_planes(first_ref, later_ref, LANES, *rims)
    for plane in range(3 * depth):
        near_ref[plane] = narrowed(medium_ref[plane])
    gradient_ref[...] = jnp.zeros_like(gradient_ref)
    residual_out_ref[...] = residual_ref[...]
    state, near, medium = (
        fields_of(state_ref, 9, depth),
        fields_of(near_ref, 3, depth),
        fields_of(medium_ref, 3, depth),
    )

    def add_terms(turn, z, strains):
        dilation, dilation_back, doubled, product = None, None, None, None
        for number, strain in enumerate(strains):
            base = (((2 - turn) * 6 + number) * depth + z) * TILE_X
            forward = strain_ref[base : base + TILE_X, :]
            if number < 3:
                dilation = forward if dilation is None else dilation + forward
            if strain is None:
                continue
            back = strain[0:TILE_X, 0:LANES]
            term = forward * back
            if number < 3:
                dilation_back = back if dilation_back is None else dilation_back + back
                doubled = term if doubled is None else doubled + term
            else:
                product = term if product is None else product + term
        for part, term in enumerate((dilation * dilation_back, 2.0 * doubled + product)):
            base = (part * depth + z) * TILE_X
            gradient_ref[base : base + TILE_X, :] = gradient_ref[base : base + TILE_X, :] + term

    loads, velocity = fields_of(first_ref, 2, depth), fields_of(velocity_ref, 2, depth)
    for z in range(depth):
        scale = STEP * medium[2][z]
        velocity[0][z] = scale * ahead_x(loads[0][z])
        velocity[1][z] = scale * ahead_y(loads[1][z])
        state[0][z] = narrowed(velocity[0][z])
        state[1][z] = narrowed(velocity[1][z])
        state[2][z] = jnp.zeros((SPAN_NEAR, SPAN_Y), F32)
    for z in range(depth):
        along_x, along_y = velocity[0][z], velocity[1][z]
        strain_x, strain_y = behind_x(along_x), behind_y(along_y)
        sheared = (
            ahead_y(along_x) + ahead_x(along_y),
            ahead_z(velocity[0], z),
            ahead_z(velocity[1], z),
        )
        add_terms(0, z, (strain_x, strain_y, None) + sheared)
        dilated = medium[0][z] * (strain_x + strain_y)
        shear = medium[1][z]
        state[3][z] = narrowed(loads[0][z] + STEP * (dilated + 2.0 * shear * strain_x))
        state[4][z] = narrowed(loads[1][z] + STEP * (dilated + 2.0 * shear * strain_y))
        state[5][z] = narrowed(STEP * dilated)
        for number, strain in enumerate(sheared):
            state[6 + number][z] = narrowed(STEP * shear * strain)
    for turn in (1, 2):
        for part in range(2):
            for z in range(depth):
                load = later_ref[(2 * (turn - 1) + part) * depth + z]
                state[3 + part][z] = state[3 + part][z] + load
        advance(state, near, functools.partial(add_terms, turn), state if turn == 1 else None)


def shards(
    initial_state,
    lame_lambda,
    shear_modulus,
    buoyancy,
    source_cells,
    source_wavelet,
    segment_start,
    segment_weight,
    partial_owner,
    partial_channel,
    observed_data,
):
    depth, rows_x, cols_y = lame_lambda.shape
    part_count = segment_start.shape[0]
    count_x, count_y = lax.axis_size("gx"), lax.axis_size("gy")
    devices = count_x * count_y
    capacity = max(2, 2 * part_count // devices)
    slot_groups = devices * capacity // LANES
    blocks = part_count // LANES
    per_group = LANES // capacity
    cells_row = depth * rows_x
    both = ("gx", "gy")
    up = [(i, i + 1) for i in range(count_x - 1)]
    down = [(j, i) for i, j in up]
    shape = jax.ShapeDtypeStruct

    def exchange(chunks):
        return lax.all_to_all(chunks, both, split_axis=0, concat_axis=0, tiled=True)

    def to_owners(rows):
        chunks = rows.reshape(slot_groups, 4, per_group, capacity).transpose(0, 2, 1, 3)
        back = exchange(chunks.reshape(devices, 4, capacity)).reshape(slot_groups, per_group, 4, capacity)
        return back.transpose(0, 2, 1, 3).reshape(slot_groups * 4, LANES)

    trimmed = shape((14 * depth * RIM, cols_y), F32)
    fields, high, low, edges = call_kernel(
        pack_body,
        "pack_edges",
        [shape((14 * cells_row, cols_y), F32), trimmed, trimmed, shape((devices, 1, 2 * RIM * LANES), F32)],
        [
            pltpu.VMEM((14 * cells_row, cols_y), F32),
            pltpu.VMEM(trimmed.shape, F32),
            pltpu.VMEM(trimmed.shape, F32),
            pltpu.VMEM((2, 1, 2 * RIM * LANES), F32),
            pltpu.VMEM((1, source_cells.shape[0]), I32),
            pltpu.VMEM(source_wavelet.shape, F32),
            pltpu.SemaphoreType.DMA((6,)),
            pltpu.SemaphoreType.DMA((3,)),
            pltpu.SemaphoreType.DMA((6,)),
        ],
        *[values.reshape(-1, cols_y) for values in (initial_state, lame_lambda, shear_modulus, buoyancy)],
        source_cells.reshape(1, -1),
        source_wavelet,
        place=pl.ANY,
        place_out=pl.ANY,
        room=60 * 1024 * 1024,
    )
    lower = lax.ppermute(high, "gx", up)
    higher = lax.ppermute(low, "gx", down)
    rims = exchange(edges)
    channels = partial_channel.reshape(blocks, LANES)
    slot, row, cover, place = call_kernel(
        functools.partial(slots_body, capacity, devices, cols_y),
        "segment_slots",
        [
            shape((blocks, LANES), I32),
            shape((blocks, LANES), I32),
            shape((cols_y, part_count), BF16),
            shape((LANES, part_count), BF16),
        ],
        [pltpu.VMEM((blocks, LANES), F32)],
        partial_owner.reshape(blocks, LANES),
        segment_start.reshape(blocks, LANES),
    )
    partials, strains, medium = call_kernel(
        forward_body,
        "forward_run",
        [
            shape((slot_groups * 4, LANES), F32),
            shape((18 * cells_row, cols_y), F32),
            shape((3 * depth, SPAN_X, SPAN_Y), F32),
        ],
        [
            pltpu.VMEM((12 * depth, SPAN_X, SPAN_Y), F32),
            pltpu.VMEM((2 * depth, SPAN_NEAR, SPAN_Y), F32),
            pltpu.VMEM((9 * depth, SPAN_NEAR, SPAN_Y), F32),
            pltpu.VMEM((3 * depth, SPAN_NEAR, SPAN_Y), F32),
            pltpu.VMEM((LANES, 2 * LANES), F32),
            pltpu.VMEM((2, 14 * cells_row, cols_y), F32),
            pltpu.VMEM((3 * LANES, part_count), BF16),
        ],
        fields,
        lower,
        higher,
        rims,
        slot,
        row,
        segment_weight,
        channels,
        cover,
        place,
    )
    parts = observed_data.shape[1] // LANES
    residuals, reply = call_kernel(
        owner_body,
        "channel_sums",
        [shape(observed_data.shape, F32), shape((slot_groups * 4, LANES), F32)],
        [
            pltpu.VMEM((12 * parts, slot_groups * LANES), BF16),
            pltpu.VMEM((LANES, slot_groups * LANES), BF16),
            pltpu.VMEM((4 * parts, LANES), F32),
        ],
        to_owners(partials),
        observed_data,
    )
    load_rows, load_sides = shape((6 * cells_row, cols_y), F32), shape((2, 1, RIM * LANES), F32)
    loads, sides = call_kernel(
        load_body,
        "segment_loads",
        [shape((24 * cells_row, cols_y), F32), load_sides],
        [pltpu.VMEM((12 * cells_row, part_count), BF16)],
        to_owners(reply),
        slot,
        row,
        segment_weight,
        cover,
        place,
        strains,
    )
    load_lower = lax.ppermute(loads, "gx", up)
    loads_again, load_edges = call_kernel(
        rims_body,
        "load_rims",
        [load_rows, shape((devices, 1, RIM * LANES), F32)],
        [pltpu.SemaphoreType.DMA((6,))],
        loads,
        sides,
        place_out=(pltpu.VMEM, pl.ANY),
    )
    load_higher = lax.ppermute(loads_again, "gx", down)
    load_rims = exchange(load_edges)
    gradients, residuals = call_kernel(
        adjoint_body,
        "adjoint_run",
        [shape((2 * cells_row, cols_y), F32), shape(observed_data.shape, F32)],
        [
            pltpu.VMEM((2 * depth, SPAN_X, SPAN_Y), F32),
            pltpu.VMEM((4 * depth, SPAN_NEAR, SPAN_Y), F32),
            pltpu.VMEM((2 * depth, SPAN_X, SPAN_Y), F32),
            pltpu.VMEM((9 * depth, SPAN_NEAR, SPAN_Y), F32),
            pltpu.VMEM((3 * depth, SPAN_NEAR, SPAN_Y), F32),
            pltpu.VMEM((LANES, LANES), F32),
        ],
        loads,
        load_higher,
        load_lower,
        load_rims,
        strains,
        medium,
        residuals,
    )
    return (residuals, gradients.reshape(2, depth, rows_x, cols_y))


def solution(mesh):
    in_specs = (
        P(None, None, "gx", "gy"),
        P(None, "gx", "gy"),
        P(None, "gx", "gy"),
        P(None, "gx", "gy"),
        P(("gx", "gy")),
        P(None, ("gx", "gy")),
        P(("gx", "gy")),
        P(None, ("gx", "gy")),
        P(("gx", "gy"), None),
        P(("gx", "gy")),
        P(None, ("gx", "gy")),
    )
    out_specs = (P(None, ("gx", "gy")), P(None, None, "gx", "gy"))
    return jax.shard_map(shards, mesh=mesh, in_specs=in_specs, out_specs=out_specs, check_vma=False)
```

```python
import functools

import jax
import jax.numpy as jnp
from jax import lax
from jax.experimental import pallas as pl
from jax.experimental.pallas import tpu as pltpu
from jax.sharding import PartitionSpec as P

GAUGE = 8
STEP = 0.25
RIM = 3
LANES = 128
TILE_X = 4
SPAN_X = 16
SPAN_NEAR = 8
SPAN_Y = 256
F32, BF16, I32 = jnp.float32, jnp.bfloat16, jnp.int32
NEAR = tuple((dx, dy) for dx in (-1, 0, 1) for dy in (-1, 0, 1))


def call_kernel(
    body, name, outs, scratch, *args, place=pltpu.VMEM, place_out=pltpu.VMEM, room=24 * 1024 * 1024
):
    spaces = place_out if isinstance(place_out, tuple) else (place_out,) * len(outs)
    return pl.pallas_call(
        body,
        name=name,
        out_shape=outs,
        in_specs=[pl.BlockSpec(memory_space=place)] * len(args),
        out_specs=[pl.BlockSpec(memory_space=space) for space in spaces],
        scratch_shapes=scratch,
        compiler_params=pltpu.CompilerParams(vmem_limit_bytes=room),
    )(*args)


def pieces(values):
    high = values.astype(BF16).astype(F32)
    rest = values - high
    middle = rest.astype(BF16).astype(F32)
    return high, middle, rest - middle


def iota(shape, dim):
    return lax.broadcasted_iota(I32, shape, dim)


def times(left, right):
    return lax.dot_general(left, right, (((1,), (0,)), ((), ())), preferred_element_type=F32)


def times_turned(left, right):
    return lax.dot_general(left, right, (((1,), (1,)), ((), ())), preferred_element_type=F32)


def packed_rows(row, height):
    tile = jnp.broadcast_to(row.astype(F32), (16, row.shape[1])).astype(BF16)
    return jnp.concatenate([tile] * (height // 16), axis=0) if height > 16 else tile


def packed_iota(height, shift=0):
    return (iota((height, LANES), 0) >> shift).astype(F32).astype(BF16)


def two_pieces(values):
    high = values.astype(BF16).astype(F32)
    return high, values - high


def sum_halves(values):
    half = values.shape[0] // 2
    return values[:half] + values[half:]


def sum_thirds(values):
    third = values.shape[0] // 3
    return values[:third] + values[third : 2 * third] + values[2 * third :]


def neighbour(dx, dy):
    count_x, count_y = lax.axis_size("gx"), lax.axis_size("gy")
    at_x, at_y = lax.axis_index("gx") + dx, lax.axis_index("gy") + dy
    inside = (at_x >= 0) & (at_x < count_x) & (at_y >= 0) & (at_y < count_y)
    return jnp.where(inside, at_x * count_y + at_y, 0), inside


def edge_columns(rows, side_ref):
    width = rows.shape[0]
    turned = rows.T
    for side, base in ((0, 0), (1, LANES - RIM)):
        for column in range(RIM):
            side_ref[side, 0:1, column * width : (column + 1) * width] = turned[base + column : base + column + 1, :]


def start_sides(side_ref, out_ref, sent):
    sides = []
    for number, (dx, dy) in enumerate((dx, dy) for dx, dy in NEAR if dy):
        index, inside = neighbour(dx, dy)
        source, target = side_ref.at[1 if dy > 0 else 0], out_ref.at[index]
        sides.append((inside, pltpu.make_async_copy(source, target, sent.at[number])))
    for inside, copy in sides:
        pl.when(inside)(copy.start)
    return sides


def wait_sides(sides):
    for inside, copy in sides:
        pl.when(inside)(copy.wait)


def arrived_chunk(recv_ref, dx, dy):
    index, inside = neighbour(dx, dy)
    return jnp.where(inside, recv_ref[index], 0.0)


def rim_rows(recv_ref, turn_ref):
    width = turn_ref.shape[2]
    turn_ref[...] = jnp.zeros_like(turn_ref)
    for block, dx in enumerate((0, 1, -1)):
        for dy, first in ((1, 0), (-1, LANES - RIM)):
            chunk = arrived_chunk(recv_ref, dx, dy)
            for column in range(RIM):
                turn_ref[block, first + column : first + column + 1, :] = chunk[
                    :, column * width : (column + 1) * width
                ]
    return [turn_ref[block].T for block in range(3)]


def lay_planes(wide_ref, narrow_ref, lane, centre, higher, lower):
    row = iota((8, LANES), 0)
    wide = wide_ref.shape[0]
    lanes = slice(lane, lane + LANES)
    for plane in range(wide + narrow_ref.shape[0]):
        rows = slice(8 * (plane // 2), 8 * (plane // 2) + 8)
        mid, high, low = centre[rows], higher[rows], lower[rows]
        if plane % 2:
            mid = pltpu.roll(mid, TILE_X, 0)
        else:
            high, low = pltpu.roll(high, TILE_X, 0), pltpu.roll(low, TILE_X, 0)
        near = jnp.where(row < TILE_X, mid, high)
        if plane < wide:
            wide_ref[plane, 0:8, lanes] = near
            wide_ref[plane, 8:16, lanes] = jnp.where(row < TILE_X, 0.0, low)
        else:
            narrow_ref[plane - wide, :, lanes] = jnp.where(row < SPAN_NEAR - 2, near, low)


def narrowed(plane):
    row = iota((SPAN_NEAR, plane.shape[1]), 0)
    return jnp.where(row < SPAN_NEAR - 2, plane[:SPAN_NEAR], plane[SPAN_NEAR:])


def ahead_x(plane):
    return pltpu.roll(plane, plane.shape[0] - 1, 0) - plane


def behind_x(plane):
    return plane - pltpu.roll(plane, 1, 0)


def ahead_y(plane):
    return pltpu.roll(plane, SPAN_Y - 1, 1) - plane


def behind_y(plane):
    return plane - pltpu.roll(plane, 1, 1)


def ahead_z(planes, z):
    return planes[z + 1] - planes[z] if z + 1 < len(planes) else -planes[z]


def behind_z(planes, z):
    return planes[z] - planes[z - 1] if z else planes[z]


class Planes:
    def __init__(self, ref, first, depth):
        self.ref, self.first, self.depth = ref, first, depth

    def __len__(self):
        return self.depth

    def __getitem__(self, z):
        return self.ref[self.first + z]

    def __setitem__(self, z, plane):
        self.ref[self.first + z] = plane


def fields_of(ref, count, depth, first=0):
    return [Planes(ref, (first + number) * depth, depth) for number in range(count)]


def strain_rates(velocity, z):
    along_x, along_y, along_z = [field[z] for field in velocity]
    return (
        behind_x(along_x),
        behind_y(along_y),
        behind_z(velocity[2], z),
        ahead_y(along_x) + ahead_x(along_y),
        ahead_z(velocity[0], z) + ahead_x(along_z),
        ahead_z(velocity[1], z) + ahead_y(along_z),
    )


def new_stress(stress, strains, lame_lambda, shear_modulus, z):
    dilated = lame_lambda[z] * (strains[0] + strains[1] + strains[2])
    shear = shear_modulus[z]
    normal = [stress[n][z] + STEP * (dilated + 2.0 * shear * strains[n]) for n in range(3)]
    return normal + [stress[n][z] + STEP * shear * strains[n] for n in range(3, 6)]


def advance(state, medium, emit, target):
    velocity, stress = state[:3], state[3:]
    lame_lambda, shear_modulus, buoyancy = medium
    depth = len(buoyancy)
    wide = target is not None and target is not state
    for z in range(depth):
        scale = STEP * buoyancy[z]
        accel = (
            ahead_x(stress[0][z]) + behind_y(stress[3][z]) + behind_z(stress[4], z),
            behind_x(stress[3][z]) + ahead_y(stress[1][z]) + behind_z(stress[5], z),
            behind_x(stress[4][z]) + behind_y(stress[5][z]) + ahead_z(stress[2], z),
        )
        for number in range(3):
            moved = velocity[number][z] + scale * accel[number]
            velocity[number][z] = moved
            if wide:
                target[number][z] = narrowed(moved)
    for z in range(depth):
        strains = strain_rates(velocity, z)
        emit(z, strains)
        if target is not None:
            for number, plane in enumerate(new_stress(stress, strains, lame_lambda, shear_modulus, z)):
                target[3 + number][z] = narrowed(plane) if wide else plane


def pack_body(*refs):
    inputs, outputs, scratch = refs[:6], refs[6:10], refs[10:]
    fields_ref, high_ref, low_ref, side_ref, cells_ref, wavelet_ref, arrived, sent, sent_sides = scratch
    targets, at = [], 0
    for source in inputs[:4]:
        targets.append(fields_ref.at[at : at + source.shape[0]])
        at = at + source.shape[0]
    copies = [
        pltpu.make_async_copy(source, target, arrived.at[number])
        for number, (source, target) in enumerate(zip(inputs, targets + [cells_ref, wavelet_ref]))
    ]
    for copy in copies[4:] + copies[:4]:
        copy.start()
    copies[4].wait()
    copies[5].wait()
    cells_row = inputs[1].shape[0]
    cells = cells_ref[...]
    count = cells.shape[1]
    at_lane = iota((LANES, count), 0) == (cells & (LANES - 1))
    at_row = iota((cells_row, count), 0) == (cells >> (LANES.bit_length() - 1))
    stack = [
        jnp.where(at_row, third[step : step + 1, :], 0.0) for third in pieces(wavelet_ref[...]) for step in range(3)
    ]
    maps = sum_thirds(
        times_turned(jnp.concatenate(stack, axis=0).astype(BF16), jnp.where(at_lane, 1.0, 0.0).astype(BF16))
    )
    for copy in copies[:4]:
        copy.wait()
    fields_ref[at:, :] = maps[cells_row:]
    for number in range(3, 6):
        rows = slice(number * cells_row, (number + 1) * cells_row)
        fields_ref[rows, :] = fields_ref[rows, :] + maps[:cells_row]
    rows = fields_ref[...]
    spare = 2 * LANES - rows.shape[0]
    edge_columns(jnp.concatenate([rows, jnp.zeros((spare, LANES), F32)], axis=0), side_ref)
    sides = start_sides(side_ref, outputs[3], sent_sides)
    height = fields_ref.shape[0] // TILE_X
    for x in range(TILE_X):
        slab = fields_ref[pl.ds(x, height, stride=TILE_X), :]
        if x < RIM:
            low_ref[x * height : (x + 1) * height, :] = slab
        if x >= TILE_X - RIM:
            at = x - TILE_X + RIM
            high_ref[at * height : (at + 1) * height, :] = slab
    writes = [
        pltpu.make_async_copy(source, target, sent.at[number])
        for number, (source, target) in enumerate(zip((fields_ref, high_ref, low_ref), outputs))
    ]
    for copy in writes:
        copy.start()
    for copy in writes:
        copy.wait()
    wait_sides(sides)


def slots_body(capacity, devices, cols_y, owner_ref, start_ref, slot_ref, row_ref, cover_ref, place_ref, rank_ref):
    blocks = owner_ref.shape[0]
    group = 32
    before = jnp.where(iota((LANES, 2 * LANES), 0) < iota((LANES, 2 * LANES), 1), 1.0, 0.0).astype(BF16)
    rank_ref[...] = jnp.zeros_like(rank_ref)

    def count_group(number, carry):
        names = iota((group, LANES), 0) + number * group
        hot = [names == owner_ref[b : b + 1, :] for b in range(blocks)]
        marks = jnp.concatenate([jnp.where(h, 1.0, 0.0) for h in hot], axis=0).astype(BF16)
        counts = times(marks, before)
        total = jnp.zeros((group, LANES), F32)
        for b in range(blocks):
            part = counts[b * group : (b + 1) * group]
            rank_ref[b : b + 1, :] = rank_ref[b : b + 1, :] + jnp.sum(
                jnp.where(hot[b], part[:, :LANES] + total, 0.0), axis=0, keepdims=True
            )
            total = total + part[:, LANES:]
        return carry

    if devices == group:
        count_group(0, 0)
    else:
        lax.fori_loop(0, devices // group, count_group, 0)
    slot = owner_ref[...] * capacity + rank_ref[...].astype(I32)
    slot_ref[...] = slot >> 7
    low = slot & (LANES - 1)
    span = cols_y - GAUGE + 1
    start = start_ref[...]
    row = ((start.astype(F32) + 0.5) * (1.0 / span)).astype(I32)
    row_ref[...] = row
    first = start - row * span
    down = iota((LANES, LANES), 0)
    for b in range(blocks):
        lanes = slice(b * LANES, (b + 1) * LANES)
        offset = down - first[b : b + 1, :]
        cover_ref[:, lanes] = jnp.where((offset >= 0) & (offset < GAUGE), 1.0, 0.0).astype(BF16)
        place_ref[:, lanes] = jnp.where(down == low[b : b + 1, :], 1.0, 0.0).astype(BF16)


def forward_body(
    fields_ref,
    lower_ref,
    higher_ref,
    recv_ref,
    slot_ref,
    row_ref,
    weight_ref,
    channel_ref,
    cover_ref,
    place_ref,
    out_ref,
    strain_ref,
    medium_ref,
    wide_ref,
    source_ref,
    state_ref,
    near_ref,
    turn_ref,
    sides_ref,
    spread_ref,
):
    depth = medium_ref.shape[0] // 3
    cells_row = depth * TILE_X
    rims = rim_rows(recv_ref, turn_ref)
    height = fields_ref.shape[0] // TILE_X
    sides_ref[...] = jnp.zeros_like(sides_ref)
    for x in range(RIM):
        slab = slice(x * height, (x + 1) * height)
        sides_ref[0, pl.ds(x, height, stride=TILE_X), :] = higher_ref[slab, :]
        sides_ref[1, pl.ds(x + TILE_X - RIM, height, stride=TILE_X), :] = lower_ref[slab, :]
    lay_planes(wide_ref, source_ref, 0, fields_ref, sides_ref.at[0], sides_ref.at[1])
    lay_planes(wide_ref, source_ref, LANES, *rims)
    first = 9 * depth
    medium_ref[...] = wide_ref[first:]
    for plane in range(3 * depth):
        near_ref[plane] = narrowed(wide_ref[first + plane])
    state, near = fields_of(state_ref, 9, depth), fields_of(near_ref, 3, depth)
    for step in range(3):

        def emit(z, strains, step=step):
            for number, strain in enumerate(strains):
                base = ((step * 6 + number) * depth + z) * TILE_X
                strain_ref[base : base + TILE_X, :] = strain[0:TILE_X, 0:LANES]

        if step == 0:
            advance(fields_of(wide_ref, 9, depth), fields_of(wide_ref, 3, depth, 9), emit, state)
            continue
        for z in range(depth):
            load = source_ref[(step - 1) * depth + z]
            for number in range(3, 6):
                state[number][z] = state[number][z] + load
        advance(state, near, emit, state if step == 1 else None)
    axial = jnp.concatenate(
        [strain_ref[step * 6 * cells_row : (step * 6 + 2) * cells_row, :] for step in range(3)], axis=0
    )
    axial = jnp.concatenate(pieces(axial), axis=0).astype(BF16)
    rows_down = iota((cells_row, LANES), 0)
    slots_down = packed_iota(LANES, 2)
    for block in range(slot_ref.shape[0]):
        lanes = slice(block * LANES, (block + 1) * LANES)
        if block % 2 == 0:
            both = sum_thirds(times(axial, cover_ref[:, block * LANES : (block + 2) * LANES]))
        windows = both[:, :LANES] if block % 2 == 0 else both[:, LANES:]
        at_row = rows_down == row_ref[block : block + 1, :]
        weight_x, weight_y = weight_ref[0:1, lanes], weight_ref[1:2, lanes]
        sums = []
        for step in range(3):
            base = 2 * step * cells_row
            axial_sum = (
                weight_x * windows[base : base + cells_row]
                + weight_y * windows[base + cells_row : base + 2 * cells_row]
            )
            sums.append(jnp.sum(jnp.where(at_row, axial_sum, 0.0), axis=0, keepdims=True))
        sums.append(channel_ref[block : block + 1, :].astype(F32))
        values = jnp.concatenate(sums + sums, axis=0)
        in_slot = slots_down == packed_rows(slot_ref[block : block + 1, :], LANES)
        for third, piece in enumerate(pieces(values)):
            tile = jnp.concatenate([piece, piece], axis=0).astype(BF16)
            spread_ref[third * LANES : (third + 1) * LANES, lanes] = jnp.where(
                in_slot, jnp.concatenate([tile] * (LANES // 16), axis=0), jnp.zeros((), BF16)
            )
    out_ref[...] = sum_thirds(times_turned(spread_ref[...], place_ref[...]))


def owner_body(arrived_ref, observed_ref, residual_ref, reply_ref, values_ref, place_ref, held_ref):
    groups = arrived_ref.shape[0] // 4
    parts = observed_ref.shape[1] // LANES
    down = packed_iota(LANES)
    part_down = iota((parts, LANES), 0)
    nothing = jnp.zeros((parts, LANES), F32)
    numbers = [arrived_ref[4 * s + 3 : 4 * s + 4, :].astype(I32) for s in range(groups)]
    for s in range(groups):
        lanes = slice(s * LANES, (s + 1) * LANES)
        place_ref[:, lanes] = jnp.where(
            down == packed_rows(numbers[s] & (LANES - 1), LANES), jnp.ones((), BF16), jnp.zeros((), BF16)
        )
        at_part = part_down == (numbers[s] >> 7)
        thirds = pieces(arrived_ref[4 * s : 4 * s + 3, :])
        stack = []
        for third in thirds:
            for step in range(3):
                stack.append(jnp.where(at_part, third[step : step + 1, :], 0.0))
        stack.append(nothing)
        values_ref[:, lanes] = jnp.concatenate(stack, axis=0).astype(BF16)
    rows = 3 * parts
    sums = sum_thirds(times_turned(values_ref[...], place_ref[...])[: 3 * rows])
    for step in range(3):
        for part in range(parts):
            at = step * parts + part
            held_ref[at : at + 1, :] = observed_ref[step : step + 1, part * LANES : (part + 1) * LANES]
    held_ref[rows:, :] = nothing
    held_ref[0:rows, :] = sums - held_ref[0:rows, :]
    for step in range(3):
        for part in range(parts):
            at = step * parts + part
            residual_ref[step : step + 1, part * LANES : (part + 1) * LANES] = held_ref[at : at + 1, :]
    residual = jnp.concatenate(two_pieces(held_ref[...]), axis=0).astype(BF16)
    for s in range(groups):
        if s % 2 == 0:
            both = sum_halves(times(residual, place_ref[:, s * LANES : (s + 2) * LANES]))
        found = both[:, :LANES] if s % 2 == 0 else both[:, LANES:]
        at_part = part_down == (numbers[s] >> 7)
        for step in range(3):
            reply_ref[4 * s + step : 4 * s + step + 1, :] = jnp.sum(
                jnp.where(at_part, found[step * parts : (step + 1) * parts], 0.0), axis=0, keepdims=True
            )
        reply_ref[4 * s + 3 : 4 * s + 4, :] = jnp.zeros((1, LANES), F32)


def load_body(
    arrived_ref,
    slot_ref,
    row_ref,
    weight_ref,
    cover_ref,
    place_ref,
    load_ref,
    out_ref,
    spread_ref,
    side_ref,
    sent_sides,
):
    cells_row = load_ref.shape[0] // 6
    stack_rows = load_ref.shape[0]
    arrived = jnp.concatenate(two_pieces(arrived_ref[...]), axis=0).astype(BF16)
    slots_down = iota((LANES, LANES), 0) >> 2
    rows_down = packed_iota(cells_row)
    for block in range(slot_ref.shape[0]):
        lanes = slice(block * LANES, (block + 1) * LANES)
        if block % 2 == 0:
            both = sum_halves(times(arrived, place_ref[:, block * LANES : (block + 2) * LANES]))
        found = both[:, :LANES] if block % 2 == 0 else both[:, LANES:]
        found = jnp.where(slots_down == slot_ref[block : block + 1, :], found, 0.0)
        folded = found[0:8]
        for part in range(1, LANES // 8):
            folded = folded + found[8 * part : 8 * part + 8]
        folded = folded + pltpu.roll(folded, 4, 0)
        at_row = rows_down == packed_rows(row_ref[block : block + 1, :], cells_row)
        for turn in range(3):
            back = folded[2 - turn : 3 - turn, :]
            for part in range(2):
                for half, piece in enumerate(two_pieces(weight_ref[part : part + 1, lanes] * back)):
                    base = half * stack_rows + (2 * turn + part) * cells_row
                    spread_ref[base : base + cells_row, lanes] = jnp.where(
                        at_row, packed_rows(piece, cells_row), jnp.zeros((), BF16)
                    )
    cover = jnp.concatenate([cover_ref[0:16, :], cover_ref[LANES - 16 :, :]], axis=0)
    edges = times_turned(cover, spread_ref[0:stack_rows, :]) + times_turned(cover, spread_ref[stack_rows:, :])
    side_ref[...] = jnp.zeros_like(side_ref)
    for side, base in ((0, 0), (1, 32 - RIM)):
        for column in range(RIM):
            lanes = slice(column * LANES, column * LANES + stack_rows)
            side_ref[side, 0:1, lanes] = edges[base + column : base + column + 1, :]
    sides = start_sides(side_ref, out_ref, sent_sides)
    load_ref[...] = sum_halves(times_turned(spread_ref[...], cover_ref[...]))
    wait_sides(sides)


def adjoint_body(
    load_ref,
    higher_ref,
    lower_ref,
    recv_ref,
    strain_ref,
    medium_ref,
    residual_ref,
    gradient_ref,
    residual_out_ref,
    first_ref,
    later_ref,
    velocity_ref,
    state_ref,
    near_ref,
    turn_ref,
):
    depth = medium_ref.shape[0] // 3
    rims = rim_rows(recv_ref, turn_ref)
    lay_planes(first_ref, later_ref, 0, load_ref, higher_ref, lower_ref)
    lay_planes(first_ref, later_ref, LANES, *rims)
    for plane in range(3 * depth):
        near_ref[plane] = narrowed(medium_ref[plane])
    gradient_ref[...] = jnp.zeros_like(gradient_ref)
    residual_out_ref[...] = residual_ref[...]
    state, near, medium = (
        fields_of(state_ref, 9, depth),
        fields_of(near_ref, 3, depth),
        fields_of(medium_ref, 3, depth),
    )

    def add_terms(turn, z, strains):
        dilation, dilation_back, doubled, product = None, None, None, None
        for number, strain in enumerate(strains):
            base = (((2 - turn) * 6 + number) * depth + z) * TILE_X
            forward = strain_ref[base : base + TILE_X, :]
            if number < 3:
                dilation = forward if dilation is None else dilation + forward
            if strain is None:
                continue
            back = strain[0:TILE_X, 0:LANES]
            term = forward * back
            if number < 3:
                dilation_back = back if dilation_back is None else dilation_back + back
                doubled = term if doubled is None else doubled + term
            else:
                product = term if product is None else product + term
        for part, term in enumerate((dilation * dilation_back, 2.0 * doubled + product)):
            base = (part * depth + z) * TILE_X
            gradient_ref[base : base + TILE_X, :] = gradient_ref[base : base + TILE_X, :] + term

    loads, velocity = fields_of(first_ref, 2, depth), fields_of(velocity_ref, 2, depth)
    for z in range(depth):
        scale = STEP * medium[2][z]
        velocity[0][z] = scale * ahead_x(loads[0][z])
        velocity[1][z] = scale * ahead_y(loads[1][z])
        state[0][z] = narrowed(velocity[0][z])
        state[1][z] = narrowed(velocity[1][z])
        state[2][z] = jnp.zeros((SPAN_NEAR, SPAN_Y), F32)
    for z in range(depth):
        along_x, along_y = velocity[0][z], velocity[1][z]
        strain_x, strain_y = behind_x(along_x), behind_y(along_y)
        sheared = (
            ahead_y(along_x) + ahead_x(along_y),
            ahead_z(velocity[0], z),
            ahead_z(velocity[1], z),
        )
        add_terms(0, z, (strain_x, strain_y, None) + sheared)
        dilated = medium[0][z] * (strain_x + strain_y)
        shear = medium[1][z]
        state[3][z] = narrowed(loads[0][z] + STEP * (dilated + 2.0 * shear * strain_x))
        state[4][z] = narrowed(loads[1][z] + STEP * (dilated + 2.0 * shear * strain_y))
        state[5][z] = narrowed(STEP * dilated)
        for number, strain in enumerate(sheared):
            state[6 + number][z] = narrowed(STEP * shear * strain)
    for turn in (1, 2):
        for part in range(2):
            for z in range(depth):
                load = later_ref[(2 * (turn - 1) + part) * depth + z]
                state[3 + part][z] = state[3 + part][z] + load
        advance(state, near, functools.partial(add_terms, turn), state if turn == 1 else None)


def shards(
    initial_state,
    lame_lambda,
    shear_modulus,
    buoyancy,
    source_cells,
    source_wavelet,
    segment_start,
    segment_weight,
    partial_owner,
    partial_channel,
    observed_data,
):
    depth, rows_x, cols_y = lame_lambda.shape
    part_count = segment_start.shape[0]
    count_x, count_y = lax.axis_size("gx"), lax.axis_size("gy")
    devices = count_x * count_y
    capacity = max(2, 2 * part_count // devices)
    slot_groups = devices * capacity // LANES
    blocks = part_count // LANES
    per_group = LANES // capacity
    cells_row = depth * rows_x
    both = ("gx", "gy")
    up = [(i, i + 1) for i in range(count_x - 1)]
    down = [(j, i) for i, j in up]
    shape = jax.ShapeDtypeStruct

    def exchange(chunks):
        return lax.all_to_all(chunks, both, split_axis=0, concat_axis=0, tiled=True)

    def to_owners(rows):
        chunks = rows.reshape(slot_groups, 4, per_group, capacity).transpose(0, 2, 1, 3)
        back = exchange(chunks.reshape(devices, 4, capacity)).reshape(slot_groups, per_group, 4, capacity)
        return back.transpose(0, 2, 1, 3).reshape(slot_groups * 4, LANES)

    trimmed = shape((14 * depth * RIM, cols_y), F32)
    fields, high, low, edges = call_kernel(
        pack_body,
        "pack_edges",
        [shape((14 * cells_row, cols_y), F32), trimmed, trimmed, shape((devices, 1, 2 * RIM * LANES), F32)],
        [
            pltpu.VMEM((14 * cells_row, cols_y), F32),
            pltpu.VMEM(trimmed.shape, F32),
            pltpu.VMEM(trimmed.shape, F32),
            pltpu.VMEM((2, 1, 2 * RIM * LANES), F32),
            pltpu.VMEM((1, source_cells.shape[0]), I32),
            pltpu.VMEM(source_wavelet.shape, F32),
            pltpu.SemaphoreType.DMA((6,)),
            pltpu.SemaphoreType.DMA((3,)),
            pltpu.SemaphoreType.DMA((6,)),
        ],
        *[values.reshape(-1, cols_y) for values in (initial_state, lame_lambda, shear_modulus, buoyancy)],
        source_cells.reshape(1, -1),
        source_wavelet,
        place=pl.ANY,
        place_out=pl.ANY,
        room=60 * 1024 * 1024,
    )
    lower = lax.ppermute(high, "gx", up)
    higher = lax.ppermute(low, "gx", down)
    rims = exchange(edges)
    channels = partial_channel.reshape(blocks, LANES)
    slot, row, cover, place = call_kernel(
        functools.partial(slots_body, capacity, devices, cols_y),
        "segment_slots",
        [
            shape((blocks, LANES), I32),
            shape((blocks, LANES), I32),
            shape((cols_y, part_count), BF16),
            shape((LANES, part_count), BF16),
        ],
        [pltpu.VMEM((blocks, LANES), F32)],
        partial_owner.reshape(blocks, LANES),
        segment_start.reshape(blocks, LANES),
    )
    partials, strains, medium = call_kernel(
        forward_body,
        "forward_run",
        [
            shape((slot_groups * 4, LANES), F32),
            shape((18 * cells_row, cols_y), F32),
            shape((3 * depth, SPAN_X, SPAN_Y), F32),
        ],
        [
            pltpu.VMEM((12 * depth, SPAN_X, SPAN_Y), F32),
            pltpu.VMEM((2 * depth, SPAN_NEAR, SPAN_Y), F32),
            pltpu.VMEM((9 * depth, SPAN_NEAR, SPAN_Y), F32),
            pltpu.VMEM((3 * depth, SPAN_NEAR, SPAN_Y), F32),
            pltpu.VMEM((3, LANES, 2 * LANES), F32),
            pltpu.VMEM((2, 14 * cells_row, cols_y), F32),
            pltpu.VMEM((3 * LANES, part_count), BF16),
        ],
        fields,
        lower,
        higher,
        rims,
        slot,
        row,
        segment_weight,
        channels,
        cover,
        place,
    )
    parts = observed_data.shape[1] // LANES
    residuals, reply = call_kernel(
        owner_body,
        "channel_sums",
        [shape(observed_data.shape, F32), shape((slot_groups * 4, LANES), F32)],
        [
            pltpu.VMEM((10 * parts, slot_groups * LANES), BF16),
            pltpu.VMEM((LANES, slot_groups * LANES), BF16),
            pltpu.VMEM((4 * parts, LANES), F32),
        ],
        to_owners(partials),
        observed_data,
    )
    loads, load_edges = call_kernel(
        load_body,
        "segment_loads",
        [shape((6 * cells_row, cols_y), F32), shape((devices, 1, RIM * LANES), F32)],
        [
            pltpu.VMEM((12 * cells_row, part_count), BF16),
            pltpu.VMEM((2, 1, RIM * LANES), F32),
            pltpu.SemaphoreType.DMA((6,)),
        ],
        to_owners(reply),
        slot,
        row,
        segment_weight,
        cover,
        place,
        place_out=(pltpu.VMEM, pl.ANY),
    )
    load_lower = lax.ppermute(loads, "gx", up)
    load_higher = lax.ppermute(loads, "gx", down)
    load_rims = exchange(load_edges)
    gradients, residuals = call_kernel(
        adjoint_body,
        "adjoint_run",
        [shape((2 * cells_row, cols_y), F32), shape(observed_data.shape, F32)],
        [
            pltpu.VMEM((2 * depth, SPAN_X, SPAN_Y), F32),
            pltpu.VMEM((4 * depth, SPAN_NEAR, SPAN_Y), F32),
            pltpu.VMEM((2 * depth, SPAN_X, SPAN_Y), F32),
            pltpu.VMEM((9 * depth, SPAN_NEAR, SPAN_Y), F32),
            pltpu.VMEM((3 * depth, SPAN_NEAR, SPAN_Y), F32),
            pltpu.VMEM((3, LANES, LANES), F32),
        ],
        loads,
        load_higher,
        load_lower,
        load_rims,
        strains,
        medium,
        residuals,
    )
    return (residuals, gradients.reshape(2, depth, rows_x, cols_y))


def solution(mesh):
    in_specs = (
        P(None, None, "gx", "gy"),
        P(None, "gx", "gy"),
        P(None, "gx", "gy"),
        P(None, "gx", "gy"),
        P(("gx", "gy")),
        P(None, ("gx", "gy")),
        P(("gx", "gy")),
        P(None, ("gx", "gy")),
        P(("gx", "gy"), None),
        P(("gx", "gy")),
        P(None, ("gx", "gy")),
    )
    out_specs = (P(None, ("gx", "gy")), P(None, None, "gx", "gy"))
    return jax.shard_map(shards, mesh=mesh, in_specs=in_specs, out_specs=out_specs, check_vma=False)
```

```python
import functools

import jax
import jax.numpy as jnp
from jax import lax
from jax.experimental import pallas as pl
from jax.experimental.pallas import tpu as pltpu
from jax.sharding import Mesh, PartitionSpec as P

GAUGE = 8
STEP = 0.25
RIM = 3
LANES = 128
TILE_X = 4
SPAN_X = 16
SPAN_NEAR = 8
SPAN_Y = 256
F32, BF16, I32 = jnp.float32, jnp.bfloat16, jnp.int32
NEAR = tuple((dx, dy) for dx in (-1, 0, 1) for dy in (-1, 0, 1))


def call_kernel(
    body, name, outs, scratch, *args, place=pltpu.VMEM, place_out=pltpu.VMEM, room=24 * 1024 * 1024
):
    spaces = place_out if isinstance(place_out, tuple) else (place_out,) * len(outs)
    return pl.pallas_call(
        body,
        name=name,
        out_shape=outs,
        in_specs=[pl.BlockSpec(memory_space=place)] * len(args),
        out_specs=[pl.BlockSpec(memory_space=space) for space in spaces],
        scratch_shapes=scratch,
        compiler_params=pltpu.CompilerParams(vmem_limit_bytes=room),
    )(*args)


def pieces(values):
    high = values.astype(BF16).astype(F32)
    rest = values - high
    middle = rest.astype(BF16).astype(F32)
    return high, middle, rest - middle


def iota(shape, dim):
    return lax.broadcasted_iota(I32, shape, dim)


def times(left, right):
    return lax.dot_general(left, right, (((1,), (0,)), ((), ())), preferred_element_type=F32)


def times_turned(left, right):
    return lax.dot_general(left, right, (((1,), (1,)), ((), ())), preferred_element_type=F32)


def packed_rows(row, height):
    tile = jnp.broadcast_to(row.astype(F32), (16, row.shape[1])).astype(BF16)
    return jnp.concatenate([tile] * (height // 16), axis=0) if height > 16 else tile


def packed_iota(height, shift=0):
    return (iota((height, LANES), 0) >> shift).astype(F32).astype(BF16)


def two_pieces(values):
    high = values.astype(BF16).astype(F32)
    return high, values - high


def sum_halves(values):
    half = values.shape[0] // 2
    return values[:half] + values[half:]


def sum_thirds(values):
    third = values.shape[0] // 3
    return values[:third] + values[third : 2 * third] + values[2 * third :]


def neighbour(dx, dy):
    count_x, count_y = lax.axis_size("gx"), lax.axis_size("gz") * lax.axis_size("core")
    at_x = lax.axis_index("gx") + dx
    at_y = lax.axis_index("gz") * lax.axis_size("core") + lax.axis_index("core") + dy
    inside = (at_x >= 0) & (at_x < count_x) & (at_y >= 0) & (at_y < count_y)
    return jnp.where(inside, at_x * count_y + at_y, 0), inside


def edge_columns(rows, side_ref):
    width = rows.shape[0]
    turned = rows.T
    for side, base in ((0, 0), (1, LANES - RIM)):
        for column in range(RIM):
            side_ref[side, 0:1, column * width : (column + 1) * width] = turned[base + column : base + column + 1, :]


def start_sides(side_ref, out_ref, sent):
    sides = []
    for number, (dx, dy) in enumerate((dx, dy) for dx, dy in NEAR if dy):
        index, inside = neighbour(dx, dy)
        source, target = side_ref.at[1 if dy > 0 else 0], out_ref.at[index]
        sides.append((inside, pltpu.make_async_copy(source, target, sent.at[number])))
    for inside, copy in sides:
        pl.when(inside)(copy.start)
    return sides


def wait_sides(sides):
    for inside, copy in sides:
        pl.when(inside)(copy.wait)


def arrived_chunk(recv_ref, dx, dy):
    index, inside = neighbour(dx, dy)
    return jnp.where(inside, recv_ref[index], 0.0)


def rim_rows(recv_ref, turn_ref):
    width = turn_ref.shape[2]
    turn_ref[...] = jnp.zeros_like(turn_ref)
    for block, dx in enumerate((0, 1, -1)):
        for dy, first in ((1, 0), (-1, LANES - RIM)):
            chunk = arrived_chunk(recv_ref, dx, dy)
            for column in range(RIM):
                turn_ref[block, first + column : first + column + 1, :] = chunk[
                    :, column * width : (column + 1) * width
                ]
    return [turn_ref[block].T for block in range(3)]


def lay_planes(wide_ref, narrow_ref, lane, centre, higher, lower):
    row = iota((8, LANES), 0)
    wide = wide_ref.shape[0]
    lanes = slice(lane, lane + LANES)
    for plane in range(wide + narrow_ref.shape[0]):
        rows = slice(8 * (plane // 2), 8 * (plane // 2) + 8)
        mid, high, low = centre[rows], higher[rows], lower[rows]
        if plane % 2:
            mid = pltpu.roll(mid, TILE_X, 0)
        else:
            high, low = pltpu.roll(high, TILE_X, 0), pltpu.roll(low, TILE_X, 0)
        near = jnp.where(row < TILE_X, mid, high)
        if plane < wide:
            wide_ref[plane, 0:8, lanes] = near
            wide_ref[plane, 8:16, lanes] = jnp.where(row < TILE_X, 0.0, low)
        else:
            narrow_ref[plane - wide, :, lanes] = jnp.where(row < SPAN_NEAR - 2, near, low)


def narrowed(plane):
    row = iota((SPAN_NEAR, plane.shape[1]), 0)
    return jnp.where(row < SPAN_NEAR - 2, plane[:SPAN_NEAR], plane[SPAN_NEAR:])


def ahead_x(plane):
    return pltpu.roll(plane, plane.shape[0] - 1, 0) - plane


def behind_x(plane):
    return plane - pltpu.roll(plane, 1, 0)


def ahead_y(plane):
    return pltpu.roll(plane, SPAN_Y - 1, 1) - plane


def behind_y(plane):
    return plane - pltpu.roll(plane, 1, 1)


def ahead_z(planes, z):
    return planes[z + 1] - planes[z] if z + 1 < len(planes) else -planes[z]


def behind_z(planes, z):
    return planes[z] - planes[z - 1] if z else planes[z]


class Planes:
    def __init__(self, ref, first, depth):
        self.ref, self.first, self.depth = ref, first, depth

    def __len__(self):
        return self.depth

    def __getitem__(self, z):
        return self.ref[self.first + z]

    def __setitem__(self, z, plane):
        self.ref[self.first + z] = plane


def fields_of(ref, count, depth, first=0):
    return [Planes(ref, (first + number) * depth, depth) for number in range(count)]


def strain_rates(velocity, z):
    along_x, along_y, along_z = [field[z] for field in velocity]
    return (
        behind_x(along_x),
        behind_y(along_y),
        behind_z(velocity[2], z),
        ahead_y(along_x) + ahead_x(along_y),
        ahead_z(velocity[0], z) + ahead_x(along_z),
        ahead_z(velocity[1], z) + ahead_y(along_z),
    )


def new_stress(stress, strains, lame_lambda, shear_modulus, z):
    dilated = lame_lambda[z] * (strains[0] + strains[1] + strains[2])
    shear = shear_modulus[z]
    normal = [stress[n][z] + STEP * (dilated + 2.0 * shear * strains[n]) for n in range(3)]
    return normal + [stress[n][z] + STEP * shear * strains[n] for n in range(3, 6)]


def advance(state, medium, emit, target):
    velocity, stress = state[:3], state[3:]
    lame_lambda, shear_modulus, buoyancy = medium
    depth = len(buoyancy)
    wide = target is not None and target is not state
    for z in range(depth):
        scale = STEP * buoyancy[z]
        accel = (
            ahead_x(stress[0][z]) + behind_y(stress[3][z]) + behind_z(stress[4], z),
            behind_x(stress[3][z]) + ahead_y(stress[1][z]) + behind_z(stress[5], z),
            behind_x(stress[4][z]) + behind_y(stress[5][z]) + ahead_z(stress[2], z),
        )
        for number in range(3):
            moved = velocity[number][z] + scale * accel[number]
            velocity[number][z] = moved
            if wide:
                target[number][z] = narrowed(moved)
    for z in range(depth):
        strains = strain_rates(velocity, z)
        emit(z, strains)
        if target is not None:
            for number, plane in enumerate(new_stress(stress, strains, lame_lambda, shear_modulus, z)):
                target[3 + number][z] = narrowed(plane) if wide else plane


def pack_body(*refs):
    inputs, outputs, scratch = refs[:6], refs[6:10], refs[10:]
    fields_ref, high_ref, low_ref, side_ref, cells_ref, wavelet_ref, arrived, sent, sent_sides = scratch
    targets, at = [], 0
    for source in inputs[:4]:
        targets.append(fields_ref.at[at : at + source.shape[0]])
        at = at + source.shape[0]
    copies = [
        pltpu.make_async_copy(source, target, arrived.at[number])
        for number, (source, target) in enumerate(zip(inputs, targets + [cells_ref, wavelet_ref]))
    ]
    for copy in copies[4:] + copies[:4]:
        copy.start()
    copies[4].wait()
    copies[5].wait()
    cells_row = inputs[1].shape[0]
    cells = cells_ref[...]
    count = cells.shape[1]
    at_lane = iota((LANES, count), 0) == (cells & (LANES - 1))
    at_row = iota((cells_row, count), 0) == (cells >> (LANES.bit_length() - 1))
    stack = [
        jnp.where(at_row, third[step : step + 1, :], 0.0) for third in pieces(wavelet_ref[...]) for step in range(3)
    ]
    maps = sum_thirds(
        times_turned(jnp.concatenate(stack, axis=0).astype(BF16), jnp.where(at_lane, 1.0, 0.0).astype(BF16))
    )
    for copy in copies[:4]:
        copy.wait()
    fields_ref[at:, :] = maps[cells_row:]
    for number in range(3, 6):
        rows = slice(number * cells_row, (number + 1) * cells_row)
        fields_ref[rows, :] = fields_ref[rows, :] + maps[:cells_row]
    rows = fields_ref[...]
    spare = 2 * LANES - rows.shape[0]
    edge_columns(jnp.concatenate([rows, jnp.zeros((spare, LANES), F32)], axis=0), side_ref)
    sides = start_sides(side_ref, outputs[3], sent_sides)
    height = fields_ref.shape[0] // TILE_X
    for x in range(TILE_X):
        slab = fields_ref[pl.ds(x, height, stride=TILE_X), :]
        if x < RIM:
            low_ref[x * height : (x + 1) * height, :] = slab
        if x >= TILE_X - RIM:
            at = x - TILE_X + RIM
            high_ref[at * height : (at + 1) * height, :] = slab
    writes = [
        pltpu.make_async_copy(source, target, sent.at[number])
        for number, (source, target) in enumerate(zip((fields_ref, high_ref, low_ref), outputs))
    ]
    for copy in writes:
        copy.start()
    for copy in writes:
        copy.wait()
    wait_sides(sides)


def slots_body(capacity, devices, cols_y, owner_ref, start_ref, slot_ref, row_ref, cover_ref, place_ref, rank_ref):
    blocks = owner_ref.shape[0]
    group = 32
    before = jnp.where(iota((LANES, 2 * LANES), 0) < iota((LANES, 2 * LANES), 1), 1.0, 0.0).astype(BF16)
    rank_ref[...] = jnp.zeros_like(rank_ref)

    def count_group(number, carry):
        names = iota((group, LANES), 0) + number * group
        hot = [names == owner_ref[b : b + 1, :] for b in range(blocks)]
        marks = jnp.concatenate([jnp.where(h, 1.0, 0.0) for h in hot], axis=0).astype(BF16)
        counts = times(marks, before)
        total = jnp.zeros((group, LANES), F32)
        for b in range(blocks):
            part = counts[b * group : (b + 1) * group]
            rank_ref[b : b + 1, :] = rank_ref[b : b + 1, :] + jnp.sum(
                jnp.where(hot[b], part[:, :LANES] + total, 0.0), axis=0, keepdims=True
            )
            total = total + part[:, LANES:]
        return carry

    if devices == group:
        count_group(0, 0)
    else:
        lax.fori_loop(0, devices // group, count_group, 0)
    slot = owner_ref[...] * capacity + rank_ref[...].astype(I32)
    slot_ref[...] = slot >> 7
    low = slot & (LANES - 1)
    span = cols_y - GAUGE + 1
    start = start_ref[...]
    row = ((start.astype(F32) + 0.5) * (1.0 / span)).astype(I32)
    row_ref[...] = row
    first = start - row * span
    down = iota((LANES, LANES), 0)
    for b in range(blocks):
        lanes = slice(b * LANES, (b + 1) * LANES)
        offset = down - first[b : b + 1, :]
        cover_ref[:, lanes] = jnp.where((offset >= 0) & (offset < GAUGE), 1.0, 0.0).astype(BF16)
        place_ref[:, lanes] = jnp.where(down == low[b : b + 1, :], 1.0, 0.0).astype(BF16)


def forward_body(
    fields_ref,
    lower_ref,
    higher_ref,
    recv_ref,
    slot_ref,
    row_ref,
    weight_ref,
    channel_ref,
    cover_ref,
    place_ref,
    out_ref,
    strain_ref,
    medium_ref,
    wide_ref,
    source_ref,
    state_ref,
    near_ref,
    turn_ref,
    sides_ref,
    spread_ref,
):
    depth = medium_ref.shape[0] // 3
    cells_row = depth * TILE_X
    rims = rim_rows(recv_ref, turn_ref)
    height = fields_ref.shape[0] // TILE_X
    sides_ref[...] = jnp.zeros_like(sides_ref)
    for x in range(RIM):
        slab = slice(x * height, (x + 1) * height)
        sides_ref[0, pl.ds(x, height, stride=TILE_X), :] = higher_ref[slab, :]
        sides_ref[1, pl.ds(x + TILE_X - RIM, height, stride=TILE_X), :] = lower_ref[slab, :]
    lay_planes(wide_ref, source_ref, 0, fields_ref, sides_ref.at[0], sides_ref.at[1])
    lay_planes(wide_ref, source_ref, LANES, *rims)
    first = 9 * depth
    medium_ref[...] = wide_ref[first:]
    for plane in range(3 * depth):
        near_ref[plane] = narrowed(wide_ref[first + plane])
    state, near = fields_of(state_ref, 9, depth), fields_of(near_ref, 3, depth)
    for step in range(3):

        def emit(z, strains, step=step):
            for number, strain in enumerate(strains):
                base = ((step * 6 + number) * depth + z) * TILE_X
                strain_ref[base : base + TILE_X, :] = strain[0:TILE_X, 0:LANES]

        if step == 0:
            advance(fields_of(wide_ref, 9, depth), fields_of(wide_ref, 3, depth, 9), emit, state)
            continue
        for z in range(depth):
            load = source_ref[(step - 1) * depth + z]
            for number in range(3, 6):
                state[number][z] = state[number][z] + load
        advance(state, near, emit, state if step == 1 else None)
    axial = jnp.concatenate(
        [strain_ref[step * 6 * cells_row : (step * 6 + 2) * cells_row, :] for step in range(3)], axis=0
    )
    axial = jnp.concatenate(pieces(axial), axis=0).astype(BF16)
    rows_down = iota((cells_row, LANES), 0)
    slots_down = packed_iota(LANES, 2)
    for block in range(slot_ref.shape[0]):
        lanes = slice(block * LANES, (block + 1) * LANES)
        if block % 2 == 0:
            both = sum_thirds(times(axial, cover_ref[:, block * LANES : (block + 2) * LANES]))
        windows = both[:, :LANES] if block % 2 == 0 else both[:, LANES:]
        at_row = rows_down == row_ref[block : block + 1, :]
        weight_x, weight_y = weight_ref[0:1, lanes], weight_ref[1:2, lanes]
        sums = []
        for step in range(3):
            base = 2 * step * cells_row
            axial_sum = (
                weight_x * windows[base : base + cells_row]
                + weight_y * windows[base + cells_row : base + 2 * cells_row]
            )
            sums.append(jnp.sum(jnp.where(at_row, axial_sum, 0.0), axis=0, keepdims=True))
        sums.append(channel_ref[block : block + 1, :].astype(F32))
        values = jnp.concatenate(sums + sums, axis=0)
        in_slot = slots_down == packed_rows(slot_ref[block : block + 1, :], LANES)
        for third, piece in enumerate(pieces(values)):
            tile = jnp.concatenate([piece, piece], axis=0).astype(BF16)
            spread_ref[third * LANES : (third + 1) * LANES, lanes] = jnp.where(
                in_slot, jnp.concatenate([tile] * (LANES // 16), axis=0), jnp.zeros((), BF16)
            )
    out_ref[...] = sum_thirds(times_turned(spread_ref[...], place_ref[...]))


def sums_body(arrived_ref, observed_ref, message_ref, place_ref, values_ref, held_ref):
    groups = arrived_ref.shape[0] // 4
    parts = observed_ref.shape[1] // LANES
    rows = 3 * parts
    down = packed_iota(LANES)
    part_down = iota((parts, LANES), 0)
    nothing = jnp.zeros((parts, LANES), F32)
    for s in range(groups):
        block = s % 2 * (groups // 2) + s // 2
        lanes = slice(block * LANES, (block + 1) * LANES)
        number = arrived_ref[4 * s + 3 : 4 * s + 4, :].astype(I32)
        place_ref[:, lanes] = jnp.where(
            down == packed_rows(number & (LANES - 1), LANES), jnp.ones((), BF16), jnp.zeros((), BF16)
        )
        at_part = part_down == (number >> 7)
        thirds = pieces(arrived_ref[4 * s : 4 * s + 3, :])
        stack = []
        for third in thirds:
            for step in range(3):
                stack.append(jnp.where(at_part, third[step : step + 1, :], 0.0))
        stack.append(nothing)
        values_ref[:, lanes] = jnp.concatenate(stack, axis=0).astype(BF16)
    for step in range(3):
        for part in range(parts):
            at = step * parts + part
            held_ref[at : at + 1, :] = observed_ref[step : step + 1, part * LANES : (part + 1) * LANES]
    half = groups // 2 * LANES
    sums = [
        sum_thirds(
            times_turned(values_ref[:, core * half : (core + 1) * half], place_ref[:, core * half : (core + 1) * half])[
                : 3 * rows
            ]
        )
        for core in range(2)
    ]
    first = lax.axis_index("core") == 0
    message_ref[0:rows, :] = jnp.where(first, sums[1], sums[0])
    message_ref[rows:, :] = jnp.where(first, sums[0], sums[1]) - held_ref[...]


def reply_body(arrived_ref, place_ref, message_ref, swapped_ref, residual_ref, reply_ref, held_ref):
    groups = arrived_ref.shape[0] // 4
    rows = message_ref.shape[0] // 2
    parts = rows // 3
    part_down = iota((parts, LANES), 0)
    own = message_ref[rows:, :] + swapped_ref[0:rows, :]
    other = message_ref[0:rows, :] + swapped_ref[rows:, :]
    held_ref[...] = own
    for step in range(3):
        for part in range(parts):
            at = step * parts + part
            residual_ref[step : step + 1, part * LANES : (part + 1) * LANES] = held_ref[at : at + 1, :]
    first = lax.axis_index("core") == 0
    for core, residual in enumerate((jnp.where(first, own, other), jnp.where(first, other, own))):
        halves = jnp.concatenate(two_pieces(residual), axis=0).astype(BF16)
        for k in range(groups // 2):
            block = core * (groups // 2) + k
            if k % 2 == 0:
                both = sum_halves(times(halves, place_ref[:, block * LANES : (block + 2) * LANES]))
            found = both[:, :LANES] if k % 2 == 0 else both[:, LANES:]
            base = 4 * (2 * k + core)
            at_part = part_down == (arrived_ref[base + 3 : base + 4, :].astype(I32) >> 7)
            for step in range(3):
                reply_ref[base + step : base + step + 1, :] = jnp.sum(
                    jnp.where(at_part, found[step * parts : (step + 1) * parts], 0.0), axis=0, keepdims=True
                )
            reply_ref[base + 3 : base + 4, :] = jnp.zeros((1, LANES), F32)


def load_body(
    arrived_ref,
    slot_ref,
    row_ref,
    weight_ref,
    cover_ref,
    place_ref,
    load_ref,
    out_ref,
    spread_ref,
    side_ref,
    sent_sides,
):
    cells_row = load_ref.shape[0] // 6
    stack_rows = load_ref.shape[0]
    arrived = jnp.concatenate(two_pieces(arrived_ref[...]), axis=0).astype(BF16)
    slots_down = iota((LANES, LANES), 0) >> 2
    rows_down = packed_iota(cells_row)
    for block in range(slot_ref.shape[0]):
        lanes = slice(block * LANES, (block + 1) * LANES)
        if block % 2 == 0:
            both = sum_halves(times(arrived, place_ref[:, block * LANES : (block + 2) * LANES]))
        found = both[:, :LANES] if block % 2 == 0 else both[:, LANES:]
        found = jnp.where(slots_down == slot_ref[block : block + 1, :], found, 0.0)
        folded = found[0:8]
        for part in range(1, LANES // 8):
            folded = folded + found[8 * part : 8 * part + 8]
        folded = folded + pltpu.roll(folded, 4, 0)
        at_row = rows_down == packed_rows(row_ref[block : block + 1, :], cells_row)
        for turn in range(3):
            back = folded[2 - turn : 3 - turn, :]
            for part in range(2):
                for half, piece in enumerate(two_pieces(weight_ref[part : part + 1, lanes] * back)):
                    base = half * stack_rows + (2 * turn + part) * cells_row
                    spread_ref[base : base + cells_row, lanes] = jnp.where(
                        at_row, packed_rows(piece, cells_row), jnp.zeros((), BF16)
                    )
    cover = jnp.concatenate([cover_ref[0:16, :], cover_ref[LANES - 16 :, :]], axis=0)
    edges = times_turned(cover, spread_ref[0:stack_rows, :]) + times_turned(cover, spread_ref[stack_rows:, :])
    side_ref[...] = jnp.zeros_like(side_ref)
    for side, base in ((0, 0), (1, 32 - RIM)):
        for column in range(RIM):
            lanes = slice(column * LANES, column * LANES + stack_rows)
            side_ref[side, 0:1, lanes] = edges[base + column : base + column + 1, :]
    sides = start_sides(side_ref, out_ref, sent_sides)
    load_ref[...] = sum_halves(times_turned(spread_ref[...], cover_ref[...]))
    wait_sides(sides)


def adjoint_body(
    load_ref,
    higher_ref,
    lower_ref,
    recv_ref,
    strain_ref,
    medium_ref,
    residual_ref,
    gradient_ref,
    residual_out_ref,
    first_ref,
    later_ref,
    velocity_ref,
    state_ref,
    near_ref,
    turn_ref,
):
    depth = medium_ref.shape[0] // 3
    rims = rim_rows(recv_ref, turn_ref)
    lay_planes(first_ref, later_ref, 0, load_ref, higher_ref, lower_ref)
    lay_planes(first_ref, later_ref, LANES, *rims)
    for plane in range(3 * depth):
        near_ref[plane] = narrowed(medium_ref[plane])
    gradient_ref[...] = jnp.zeros_like(gradient_ref)
    residual_out_ref[...] = residual_ref[...]
    state, near, medium = (
        fields_of(state_ref, 9, depth),
        fields_of(near_ref, 3, depth),
        fields_of(medium_ref, 3, depth),
    )

    def add_terms(turn, z, strains):
        dilation, dilation_back, doubled, product = None, None, None, None
        for number, strain in enumerate(strains):
            base = (((2 - turn) * 6 + number) * depth + z) * TILE_X
            forward = strain_ref[base : base + TILE_X, :]
            if number < 3:
                dilation = forward if dilation is None else dilation + forward
            if strain is None:
                continue
            back = strain[0:TILE_X, 0:LANES]
            term = forward * back
            if number < 3:
                dilation_back = back if dilation_back is None else dilation_back + back
                doubled = term if doubled is None else doubled + term
            else:
                product = term if product is None else product + term
        for part, term in enumerate((dilation * dilation_back, 2.0 * doubled + product)):
            base = (part * depth + z) * TILE_X
            gradient_ref[base : base + TILE_X, :] = gradient_ref[base : base + TILE_X, :] + term

    loads, velocity = fields_of(first_ref, 2, depth), fields_of(velocity_ref, 2, depth)
    for z in range(depth):
        scale = STEP * medium[2][z]
        velocity[0][z] = scale * ahead_x(loads[0][z])
        velocity[1][z] = scale * ahead_y(loads[1][z])
        state[0][z] = narrowed(velocity[0][z])
        state[1][z] = narrowed(velocity[1][z])
        state[2][z] = jnp.zeros((SPAN_NEAR, SPAN_Y), F32)
    for z in range(depth):
        along_x, along_y = velocity[0][z], velocity[1][z]
        strain_x, strain_y = behind_x(along_x), behind_y(along_y)
        sheared = (
            ahead_y(along_x) + ahead_x(along_y),
            ahead_z(velocity[0], z),
            ahead_z(velocity[1], z),
        )
        add_terms(0, z, (strain_x, strain_y, None) + sheared)
        dilated = medium[0][z] * (strain_x + strain_y)
        shear = medium[1][z]
        state[3][z] = narrowed(loads[0][z] + STEP * (dilated + 2.0 * shear * strain_x))
        state[4][z] = narrowed(loads[1][z] + STEP * (dilated + 2.0 * shear * strain_y))
        state[5][z] = narrowed(STEP * dilated)
        for number, strain in enumerate(sheared):
            state[6 + number][z] = narrowed(STEP * shear * strain)
    for turn in (1, 2):
        for part in range(2):
            for z in range(depth):
                load = later_ref[(2 * (turn - 1) + part) * depth + z]
                state[3 + part][z] = state[3 + part][z] + load
        advance(state, near, functools.partial(add_terms, turn), state if turn == 1 else None)


def shards(
    initial_state,
    lame_lambda,
    shear_modulus,
    buoyancy,
    source_cells,
    source_wavelet,
    segment_start,
    segment_weight,
    partial_owner,
    partial_channel,
    observed_data,
):
    depth, rows_x, cols_y = lame_lambda.shape
    part_count = segment_start.shape[0]
    count_x, pairs = lax.axis_size("gx"), lax.axis_size("gx") * lax.axis_size("gz")
    devices = pairs * lax.axis_size("core")
    capacity = max(2, 2 * part_count // devices)
    slot_groups = devices * capacity // LANES
    blocks = part_count // LANES
    per_group = LANES // capacity
    cells_row = depth * rows_x
    up = [(i, i + 1) for i in range(count_x - 1)]
    down = [(j, i) for i, j in up]
    shape = jax.ShapeDtypeStruct

    def exchange(chunks, axes=("gx", "gz", "core")):
        return lax.all_to_all(chunks, axes, split_axis=0, concat_axis=0, tiled=True)

    def to_owners(rows):
        chunks = rows.reshape(slot_groups, 4, per_group, capacity).transpose(0, 2, 1, 3).reshape(pairs, 8, capacity)
        back = exchange(chunks, ("gx", "gz")).reshape(-1, per_group, 2, 4, capacity)
        return back.transpose(0, 2, 3, 1, 4).reshape(slot_groups * 4, LANES)

    def from_owners(rows):
        chunks = rows.reshape(-1, 2, 4, per_group, capacity).transpose(0, 3, 1, 2, 4).reshape(pairs, 8, capacity)
        back = exchange(chunks, ("gx", "gz")).reshape(slot_groups, per_group, 4, capacity)
        return back.transpose(0, 2, 1, 3).reshape(slot_groups * 4, LANES)

    trimmed = shape((14 * depth * RIM, cols_y), F32)
    fields, high, low, edges = call_kernel(
        pack_body,
        "pack_edges",
        [shape((14 * cells_row, cols_y), F32), trimmed, trimmed, shape((devices, 1, 2 * RIM * LANES), F32)],
        [
            pltpu.VMEM((14 * cells_row, cols_y), F32),
            pltpu.VMEM(trimmed.shape, F32),
            pltpu.VMEM(trimmed.shape, F32),
            pltpu.VMEM((2, 1, 2 * RIM * LANES), F32),
            pltpu.VMEM((1, source_cells.shape[0]), I32),
            pltpu.VMEM(source_wavelet.shape, F32),
            pltpu.SemaphoreType.DMA((6,)),
            pltpu.SemaphoreType.DMA((3,)),
            pltpu.SemaphoreType.DMA((6,)),
        ],
        *[values.reshape(-1, cols_y) for values in (initial_state, lame_lambda, shear_modulus, buoyancy)],
        source_cells.reshape(1, -1),
        source_wavelet,
        place=pl.ANY,
        place_out=pl.ANY,
        room=60 * 1024 * 1024,
    )
    lower = lax.ppermute(high, "gx", up)
    higher = lax.ppermute(low, "gx", down)
    rims = exchange(edges)
    channels = partial_channel.reshape(blocks, LANES)
    slot, row, cover, place = call_kernel(
        functools.partial(slots_body, capacity, devices, cols_y),
        "segment_slots",
        [
            shape((blocks, LANES), I32),
            shape((blocks, LANES), I32),
            shape((cols_y, part_count), BF16),
            shape((LANES, part_count), BF16),
        ],
        [pltpu.VMEM((blocks, LANES), F32)],
        partial_owner.reshape(blocks, LANES),
        segment_start.reshape(blocks, LANES),
    )
    partials, strains, medium = call_kernel(
        forward_body,
        "forward_run",
        [
            shape((slot_groups * 4, LANES), F32),
            shape((18 * cells_row, cols_y), F32),
            shape((3 * depth, SPAN_X, SPAN_Y), F32),
        ],
        [
            pltpu.VMEM((12 * depth, SPAN_X, SPAN_Y), F32),
            pltpu.VMEM((2 * depth, SPAN_NEAR, SPAN_Y), F32),
            pltpu.VMEM((9 * depth, SPAN_NEAR, SPAN_Y), F32),
            pltpu.VMEM((3 * depth, SPAN_NEAR, SPAN_Y), F32),
            pltpu.VMEM((3, LANES, 2 * LANES), F32),
            pltpu.VMEM((2, 14 * cells_row, cols_y), F32),
            pltpu.VMEM((3 * LANES, part_count), BF16),
        ],
        fields,
        lower,
        higher,
        rims,
        slot,
        row,
        segment_weight,
        channels,
        cover,
        place,
    )
    parts = observed_data.shape[1] // LANES
    arrived = to_owners(partials)
    message, channel_place = call_kernel(
        sums_body,
        "channel_sums",
        [shape((6 * parts, LANES), F32), shape((LANES, slot_groups * LANES), BF16)],
        [pltpu.VMEM((10 * parts, slot_groups * LANES), BF16), pltpu.VMEM((3 * parts, LANES), F32)],
        arrived,
        observed_data,
    )
    residuals, reply = call_kernel(
        reply_body,
        "channel_replies",
        [shape(observed_data.shape, F32), shape((slot_groups * 4, LANES), F32)],
        [pltpu.VMEM((3 * parts, LANES), F32)],
        arrived,
        channel_place,
        message,
        lax.ppermute(message, "core", [(0, 1), (1, 0)]),
    )
    loads, load_edges = call_kernel(
        load_body,
        "segment_loads",
        [shape((6 * cells_row, cols_y), F32), shape((devices, 1, RIM * LANES), F32)],
        [
            pltpu.VMEM((12 * cells_row, part_count), BF16),
            pltpu.VMEM((2, 1, RIM * LANES), F32),
            pltpu.SemaphoreType.DMA((6,)),
        ],
        from_owners(reply),
        slot,
        row,
        segment_weight,
        cover,
        place,
        place_out=(pltpu.VMEM, pl.ANY),
    )
    load_lower = lax.ppermute(loads, "gx", up)
    load_higher = lax.ppermute(loads, "gx", down)
    load_rims = exchange(load_edges)
    gradients, residuals = call_kernel(
        adjoint_body,
        "adjoint_run",
        [shape((2 * cells_row, cols_y), F32), shape(observed_data.shape, F32)],
        [
            pltpu.VMEM((2 * depth, SPAN_X, SPAN_Y), F32),
            pltpu.VMEM((4 * depth, SPAN_NEAR, SPAN_Y), F32),
            pltpu.VMEM((2 * depth, SPAN_X, SPAN_Y), F32),
            pltpu.VMEM((9 * depth, SPAN_NEAR, SPAN_Y), F32),
            pltpu.VMEM((3 * depth, SPAN_NEAR, SPAN_Y), F32),
            pltpu.VMEM((3, LANES, LANES), F32),
        ],
        loads,
        load_higher,
        load_lower,
        load_rims,
        strains,
        medium,
        residuals,
    )
    return (residuals, gradients.reshape(2, depth, rows_x, cols_y))


def solution(mesh):
    rows_gx, cols_gy = mesh.devices.shape
    split = Mesh(mesh.devices.reshape(rows_gx, cols_gy // 2, 2), ("gx", "gz", "core"))
    column, tile = ("gz", "core"), ("gx", "gz", "core")
    in_specs = (
        P(None, None, "gx", column),
        P(None, "gx", column),
        P(None, "gx", column),
        P(None, "gx", column),
        P(tile),
        P(None, tile),
        P(tile),
        P(None, tile),
        P(tile, None),
        P(tile),
        P(None, tile),
    )
    out_specs = (P(None, tile), P(None, None, "gx", column))
    return jax.shard_map(shards, mesh=split, in_specs=in_specs, out_specs=out_specs, check_vma=False)
```

```python
import functools

import jax
import jax.numpy as jnp
from jax import lax
from jax.experimental import pallas as pl
from jax.experimental.pallas import tpu as pltpu
from jax.sharding import PartitionSpec as P

GAUGE = 8
STEP = 0.25
RIM = 3
LANES = 128
TILE_X = 4
SPAN_X = 16
SPAN_NEAR = 8
SPAN_Y = 256
F32, BF16, I32 = jnp.float32, jnp.bfloat16, jnp.int32
NEAR = tuple((dx, dy) for dx in (-1, 0, 1) for dy in (-1, 0, 1))


def call_kernel(
    body, name, outs, scratch, *args, place=pltpu.VMEM, place_out=pltpu.VMEM, room=24 * 1024 * 1024
):
    spaces = place_out if isinstance(place_out, tuple) else (place_out,) * len(outs)
    return pl.pallas_call(
        body,
        name=name,
        out_shape=outs,
        in_specs=[pl.BlockSpec(memory_space=place)] * len(args),
        out_specs=[pl.BlockSpec(memory_space=space) for space in spaces],
        scratch_shapes=scratch,
        compiler_params=pltpu.CompilerParams(vmem_limit_bytes=room),
    )(*args)


def pieces(values):
    high = values.astype(BF16).astype(F32)
    rest = values - high
    middle = rest.astype(BF16).astype(F32)
    return high, middle, rest - middle


def iota(shape, dim):
    return lax.broadcasted_iota(I32, shape, dim)


def times(left, right):
    return lax.dot_general(left, right, (((1,), (0,)), ((), ())), preferred_element_type=F32)


def times_turned(left, right):
    return lax.dot_general(left, right, (((1,), (1,)), ((), ())), preferred_element_type=F32)


def packed_rows(row, height):
    tile = jnp.broadcast_to(row.astype(F32), (16, row.shape[1])).astype(BF16)
    return jnp.concatenate([tile] * (height // 16), axis=0) if height > 16 else tile


def packed_iota(height, shift=0):
    return (iota((height, LANES), 0) >> shift).astype(F32).astype(BF16)


def two_pieces(values):
    high = values.astype(BF16).astype(F32)
    return high, values - high


def sum_halves(values):
    half = values.shape[0] // 2
    return values[:half] + values[half:]


def sum_thirds(values):
    third = values.shape[0] // 3
    return values[:third] + values[third : 2 * third] + values[2 * third :]


def neighbour(dx, dy):
    count_x, count_y = lax.axis_size("gx"), lax.axis_size("gy")
    at_x, at_y = lax.axis_index("gx") + dx, lax.axis_index("gy") + dy
    inside = (at_x >= 0) & (at_x < count_x) & (at_y >= 0) & (at_y < count_y)
    return jnp.where(inside, at_x * count_y + at_y, 0), inside


def edge_columns(rows, side_ref):
    width = rows.shape[0]
    turned = rows.T
    for side, base in ((0, 0), (1, LANES - RIM)):
        for column in range(RIM):
            side_ref[side, 0:1, column * width : (column + 1) * width] = turned[base + column : base + column + 1, :]


def start_sides(side_ref, out_ref, sent):
    sides = []
    for number, (dx, dy) in enumerate((dx, dy) for dx, dy in NEAR if dy):
        index, inside = neighbour(dx, dy)
        source, target = side_ref.at[1 if dy > 0 else 0], out_ref.at[index]
        sides.append((inside, pltpu.make_async_copy(source, target, sent.at[number])))
    for inside, copy in sides:
        pl.when(inside)(copy.start)
    return sides


def wait_sides(sides):
    for inside, copy in sides:
        pl.when(inside)(copy.wait)


def arrived_chunk(recv_ref, dx, dy):
    index, inside = neighbour(dx, dy)
    return jnp.where(inside, recv_ref[index], 0.0)


def rim_rows(recv_ref, turn_ref):
    width = turn_ref.shape[2]
    turn_ref[...] = jnp.zeros_like(turn_ref)
    for block, dx in enumerate((0, 1, -1)):
        for dy, first in ((1, 0), (-1, LANES - RIM)):
            chunk = arrived_chunk(recv_ref, dx, dy)
            for column in range(RIM):
                turn_ref[block, first + column : first + column + 1, :] = chunk[
                    :, column * width : (column + 1) * width
                ]
    return [turn_ref[block].T for block in range(3)]


def lay_planes(wide_ref, narrow_ref, lane, centre, higher, lower):
    row = iota((8, LANES), 0)
    wide = wide_ref.shape[0]
    lanes = slice(lane, lane + LANES)
    for plane in range(wide + narrow_ref.shape[0]):
        rows = slice(8 * (plane // 2), 8 * (plane // 2) + 8)
        mid, high, low = centre[rows], higher[rows], lower[rows]
        if plane % 2:
            mid = pltpu.roll(mid, TILE_X, 0)
        else:
            high, low = pltpu.roll(high, TILE_X, 0), pltpu.roll(low, TILE_X, 0)
        near = jnp.where(row < TILE_X, mid, high)
        if plane < wide:
            wide_ref[plane, 0:8, lanes] = near
            wide_ref[plane, 8:16, lanes] = jnp.where(row < TILE_X, 0.0, low)
        else:
            narrow_ref[plane - wide, :, lanes] = jnp.where(row < SPAN_NEAR - 2, near, low)


def narrowed(plane):
    row = iota((SPAN_NEAR, plane.shape[1]), 0)
    return jnp.where(row < SPAN_NEAR - 2, plane[:SPAN_NEAR], plane[SPAN_NEAR:])


def ahead_x(plane):
    return pltpu.roll(plane, plane.shape[0] - 1, 0) - plane


def behind_x(plane):
    return plane - pltpu.roll(plane, 1, 0)


def ahead_y(plane):
    return pltpu.roll(plane, SPAN_Y - 1, 1) - plane


def behind_y(plane):
    return plane - pltpu.roll(plane, 1, 1)


def ahead_z(planes, z):
    return planes[z + 1] - planes[z] if z + 1 < len(planes) else -planes[z]


def behind_z(planes, z):
    return planes[z] - planes[z - 1] if z else planes[z]


class Planes:
    def __init__(self, ref, first, depth):
        self.ref, self.first, self.depth = ref, first, depth

    def __len__(self):
        return self.depth

    def __getitem__(self, z):
        return self.ref[self.first + z]

    def __setitem__(self, z, plane):
        self.ref[self.first + z] = plane


def fields_of(ref, count, depth, first=0):
    return [Planes(ref, (first + number) * depth, depth) for number in range(count)]


def strain_rates(velocity, z):
    along_x, along_y, along_z = [field[z] for field in velocity]
    return (
        behind_x(along_x),
        behind_y(along_y),
        behind_z(velocity[2], z),
        ahead_y(along_x) + ahead_x(along_y),
        ahead_z(velocity[0], z) + ahead_x(along_z),
        ahead_z(velocity[1], z) + ahead_y(along_z),
    )


def new_stress(stress, strains, lame_lambda, shear_modulus, z):
    dilated = lame_lambda[z] * (strains[0] + strains[1] + strains[2])
    shear = shear_modulus[z]
    normal = [stress[n][z] + STEP * (dilated + 2.0 * shear * strains[n]) for n in range(3)]
    return normal + [stress[n][z] + STEP * shear * strains[n] for n in range(3, 6)]


def advance(state, medium, emit, target):
    velocity, stress = state[:3], state[3:]
    lame_lambda, shear_modulus, buoyancy = medium
    depth = len(buoyancy)
    wide = target is not None and target is not state
    for z in range(depth):
        scale = STEP * buoyancy[z]
        accel = (
            ahead_x(stress[0][z]) + behind_y(stress[3][z]) + behind_z(stress[4], z),
            behind_x(stress[3][z]) + ahead_y(stress[1][z]) + behind_z(stress[5], z),
            behind_x(stress[4][z]) + behind_y(stress[5][z]) + ahead_z(stress[2], z),
        )
        for number in range(3):
            moved = velocity[number][z] + scale * accel[number]
            velocity[number][z] = moved
            if wide:
                target[number][z] = narrowed(moved)
    for z in range(depth):
        strains = strain_rates(velocity, z)
        emit(z, strains)
        if target is not None:
            for number, plane in enumerate(new_stress(stress, strains, lame_lambda, shear_modulus, z)):
                target[3 + number][z] = narrowed(plane) if wide else plane


def pack_body(*refs):
    inputs, outputs, scratch = refs[:6], refs[6:10], refs[10:]
    fields_ref, high_ref, low_ref, side_ref, cells_ref, wavelet_ref, arrived, sent, sent_sides = scratch
    targets, at = [], 0
    for source in inputs[:4]:
        targets.append(fields_ref.at[at : at + source.shape[0]])
        at = at + source.shape[0]
    copies = [
        pltpu.make_async_copy(source, target, arrived.at[number])
        for number, (source, target) in enumerate(zip(inputs, targets + [cells_ref, wavelet_ref]))
    ]
    for copy in copies[4:] + copies[:4]:
        copy.start()
    copies[4].wait()
    copies[5].wait()
    cells_row = inputs[1].shape[0]
    cells = cells_ref[...]
    count = cells.shape[1]
    at_lane = iota((LANES, count), 0) == (cells & (LANES - 1))
    at_row = iota((cells_row, count), 0) == (cells >> (LANES.bit_length() - 1))
    stack = [
        jnp.where(at_row, third[step : step + 1, :], 0.0) for third in pieces(wavelet_ref[...]) for step in range(3)
    ]
    maps = sum_thirds(
        times_turned(jnp.concatenate(stack, axis=0).astype(BF16), jnp.where(at_lane, 1.0, 0.0).astype(BF16))
    )
    for copy in copies[:4]:
        copy.wait()
    fields_ref[at:, :] = maps[cells_row:]
    for number in range(3, 6):
        rows = slice(number * cells_row, (number + 1) * cells_row)
        fields_ref[rows, :] = fields_ref[rows, :] + maps[:cells_row]
    rows = fields_ref[...]
    spare = 2 * LANES - rows.shape[0]
    edge_columns(jnp.concatenate([rows, jnp.zeros((spare, LANES), F32)], axis=0), side_ref)
    sides = start_sides(side_ref, outputs[3], sent_sides)
    height = fields_ref.shape[0] // TILE_X
    for x in range(TILE_X):
        slab = fields_ref[pl.ds(x, height, stride=TILE_X), :]
        if x < RIM:
            low_ref[x * height : (x + 1) * height, :] = slab
        if x >= TILE_X - RIM:
            at = x - TILE_X + RIM
            high_ref[at * height : (at + 1) * height, :] = slab
    writes = [
        pltpu.make_async_copy(source, target, sent.at[number])
        for number, (source, target) in enumerate(zip((fields_ref, high_ref, low_ref), outputs))
    ]
    for copy in writes:
        copy.start()
    for copy in writes:
        copy.wait()
    wait_sides(sides)


def slots_body(capacity, devices, cols_y, owner_ref, start_ref, slot_ref, row_ref, cover_ref, place_ref, rank_ref):
    blocks = owner_ref.shape[0]
    group = 32
    before = jnp.where(iota((LANES, 2 * LANES), 0) < iota((LANES, 2 * LANES), 1), 1.0, 0.0).astype(BF16)
    rank_ref[...] = jnp.zeros_like(rank_ref)

    def count_group(number, carry):
        names = iota((group, LANES), 0) + number * group
        hot = [names == owner_ref[b : b + 1, :] for b in range(blocks)]
        marks = jnp.concatenate([jnp.where(h, 1.0, 0.0) for h in hot], axis=0).astype(BF16)
        counts = times(marks, before)
        total = jnp.zeros((group, LANES), F32)
        for b in range(blocks):
            part = counts[b * group : (b + 1) * group]
            rank_ref[b : b + 1, :] = rank_ref[b : b + 1, :] + jnp.sum(
                jnp.where(hot[b], part[:, :LANES] + total, 0.0), axis=0, keepdims=True
            )
            total = total + part[:, LANES:]
        return carry

    if devices == group:
        count_group(0, 0)
    else:
        lax.fori_loop(0, devices // group, count_group, 0)
    slot = owner_ref[...] * capacity + rank_ref[...].astype(I32)
    slot_ref[...] = slot >> 7
    low = slot & (LANES - 1)
    span = cols_y - GAUGE + 1
    start = start_ref[...]
    row = ((start.astype(F32) + 0.5) * (1.0 / span)).astype(I32)
    row_ref[...] = row
    first = start - row * span
    down = iota((LANES, LANES), 0)
    for b in range(blocks):
        lanes = slice(b * LANES, (b + 1) * LANES)
        offset = down - first[b : b + 1, :]
        cover_ref[:, lanes] = jnp.where((offset >= 0) & (offset < GAUGE), 1.0, 0.0).astype(BF16)
        place_ref[:, lanes] = jnp.where(down == low[b : b + 1, :], 1.0, 0.0).astype(BF16)


def forward_body(
    fields_ref,
    lower_ref,
    higher_ref,
    recv_ref,
    slot_ref,
    row_ref,
    weight_ref,
    channel_ref,
    cover_ref,
    place_ref,
    out_ref,
    strain_ref,
    medium_ref,
    wide_ref,
    source_ref,
    state_ref,
    near_ref,
    turn_ref,
    sides_ref,
    spread_ref,
):
    depth = medium_ref.shape[0] // 3
    cells_row = depth * TILE_X
    rims = rim_rows(recv_ref, turn_ref)
    height = fields_ref.shape[0] // TILE_X
    sides_ref[...] = jnp.zeros_like(sides_ref)
    for x in range(RIM):
        slab = slice(x * height, (x + 1) * height)
        sides_ref[0, pl.ds(x, height, stride=TILE_X), :] = higher_ref[slab, :]
        sides_ref[1, pl.ds(x + TILE_X - RIM, height, stride=TILE_X), :] = lower_ref[slab, :]
    lay_planes(wide_ref, source_ref, 0, fields_ref, sides_ref.at[0], sides_ref.at[1])
    lay_planes(wide_ref, source_ref, LANES, *rims)
    first = 9 * depth
    medium_ref[...] = wide_ref[first:]
    for plane in range(3 * depth):
        near_ref[plane] = narrowed(wide_ref[first + plane])
    state, near = fields_of(state_ref, 9, depth), fields_of(near_ref, 3, depth)
    for step in range(3):

        def emit(z, strains, step=step):
            for number, strain in enumerate(strains):
                base = ((step * 6 + number) * depth + z) * TILE_X
                strain_ref[base : base + TILE_X, :] = strain[0:TILE_X, 0:LANES]

        if step == 0:
            advance(fields_of(wide_ref, 9, depth), fields_of(wide_ref, 3, depth, 9), emit, state)
            continue
        for z in range(depth):
            load = source_ref[(step - 1) * depth + z]
            for number in range(3, 6):
                state[number][z] = state[number][z] + load
        advance(state, near, emit, state if step == 1 else None)
    axial = jnp.concatenate(
        [strain_ref[step * 6 * cells_row : (step * 6 + 2) * cells_row, :] for step in range(3)], axis=0
    )
    axial = jnp.concatenate(pieces(axial), axis=0).astype(BF16)
    rows_down = iota((cells_row, LANES), 0)
    slots_down = packed_iota(LANES, 2)
    for block in range(slot_ref.shape[0]):
        lanes = slice(block * LANES, (block + 1) * LANES)
        if block % 2 == 0:
            both = sum_thirds(times(axial, cover_ref[:, block * LANES : (block + 2) * LANES]))
        windows = both[:, :LANES] if block % 2 == 0 else both[:, LANES:]
        at_row = rows_down == row_ref[block : block + 1, :]
        weight_x, weight_y = weight_ref[0:1, lanes], weight_ref[1:2, lanes]
        sums = []
        for step in range(3):
            base = 2 * step * cells_row
            axial_sum = (
                weight_x * windows[base : base + cells_row]
                + weight_y * windows[base + cells_row : base + 2 * cells_row]
            )
            sums.append(jnp.sum(jnp.where(at_row, axial_sum, 0.0), axis=0, keepdims=True))
        sums.append(channel_ref[block : block + 1, :].astype(F32))
        values = jnp.concatenate(sums + sums, axis=0)
        in_slot = slots_down == packed_rows(slot_ref[block : block + 1, :], LANES)
        for third, piece in enumerate(pieces(values)):
            tile = jnp.concatenate([piece, piece], axis=0).astype(BF16)
            spread_ref[third * LANES : (third + 1) * LANES, lanes] = jnp.where(
                in_slot, jnp.concatenate([tile] * (LANES // 16), axis=0), jnp.zeros((), BF16)
            )
    out_ref[...] = sum_thirds(times_turned(spread_ref[...], place_ref[...]))


def owner_body(arrived_ref, observed_ref, residual_ref, reply_ref, values_ref, place_ref, held_ref):
    groups = arrived_ref.shape[0] // 4
    parts = observed_ref.shape[1] // LANES
    down = packed_iota(LANES)
    part_down = iota((parts, LANES), 0)
    nothing = jnp.zeros((parts, LANES), F32)
    numbers = [arrived_ref[4 * s + 3 : 4 * s + 4, :].astype(I32) for s in range(groups)]
    for s in range(groups):
        lanes = slice(s * LANES, (s + 1) * LANES)
        place_ref[:, lanes] = jnp.where(
            down == packed_rows(numbers[s] & (LANES - 1), LANES), jnp.ones((), BF16), jnp.zeros((), BF16)
        )
        at_part = part_down == (numbers[s] >> 7)
        thirds = pieces(arrived_ref[4 * s : 4 * s + 3, :])
        stack = []
        for third in thirds:
            for step in range(3):
                stack.append(jnp.where(at_part, third[step : step + 1, :], 0.0))
        stack.append(nothing)
        values_ref[:, lanes] = jnp.concatenate(stack, axis=0).astype(BF16)
    rows = 3 * parts
    sums = sum_thirds(times_turned(values_ref[...], place_ref[...])[: 3 * rows])
    for step in range(3):
        for part in range(parts):
            at = step * parts + part
            held_ref[at : at + 1, :] = observed_ref[step : step + 1, part * LANES : (part + 1) * LANES]
    held_ref[rows:, :] = nothing
    held_ref[0:rows, :] = sums - held_ref[0:rows, :]
    for step in range(3):
        for part in range(parts):
            at = step * parts + part
            residual_ref[step : step + 1, part * LANES : (part + 1) * LANES] = held_ref[at : at + 1, :]
    residual = jnp.concatenate(two_pieces(held_ref[...]), axis=0).astype(BF16)
    for s in range(groups):
        if s % 2 == 0:
            both = sum_halves(times(residual, place_ref[:, s * LANES : (s + 2) * LANES]))
        found = both[:, :LANES] if s % 2 == 0 else both[:, LANES:]
        at_part = part_down == (numbers[s] >> 7)
        for step in range(3):
            reply_ref[4 * s + step : 4 * s + step + 1, :] = jnp.sum(
                jnp.where(at_part, found[step * parts : (step + 1) * parts], 0.0), axis=0, keepdims=True
            )
        reply_ref[4 * s + 3 : 4 * s + 4, :] = jnp.zeros((1, LANES), F32)


def reached():
    return [(turn, distance) for turn in range(3) for distance in range(RIM - turn)]


def load_body(
    arrived_ref,
    slot_ref,
    row_ref,
    weight_ref,
    cover_ref,
    place_ref,
    load_ref,
    high_ref,
    low_ref,
    out_ref,
    spread_ref,
    side_ref,
    sent_sides,
):
    cells_row = load_ref.shape[0] // 6
    stack_rows = load_ref.shape[0]
    arrived = jnp.concatenate(two_pieces(arrived_ref[...]), axis=0).astype(BF16)
    slots_down = iota((LANES, LANES), 0) >> 2
    rows_down = packed_iota(cells_row)
    for block in range(slot_ref.shape[0]):
        lanes = slice(block * LANES, (block + 1) * LANES)
        if block % 2 == 0:
            both = sum_halves(times(arrived, place_ref[:, block * LANES : (block + 2) * LANES]))
        found = both[:, :LANES] if block % 2 == 0 else both[:, LANES:]
        found = jnp.where(slots_down == slot_ref[block : block + 1, :], found, 0.0)
        folded = found[0:8]
        for part in range(1, LANES // 8):
            folded = folded + found[8 * part : 8 * part + 8]
        folded = folded + pltpu.roll(folded, 4, 0)
        at_row = rows_down == packed_rows(row_ref[block : block + 1, :], cells_row)
        for turn in range(3):
            back = folded[2 - turn : 3 - turn, :]
            for part in range(2):
                for half, piece in enumerate(two_pieces(weight_ref[part : part + 1, lanes] * back)):
                    base = half * stack_rows + (2 * turn + part) * cells_row
                    spread_ref[base : base + cells_row, lanes] = jnp.where(
                        at_row, packed_rows(piece, cells_row), jnp.zeros((), BF16)
                    )
    cover = jnp.concatenate([cover_ref[0:16, :], cover_ref[LANES - 16 :, :]], axis=0)
    edges = times_turned(cover, spread_ref[0:stack_rows, :]) + times_turned(cover, spread_ref[stack_rows:, :])
    side_ref[...] = jnp.zeros_like(side_ref)
    for side, base in ((0, 0), (1, 32 - RIM)):
        for column in range(RIM):
            lanes = slice(column * LANES, column * LANES + stack_rows)
            side_ref[side, 0:1, lanes] = edges[base + column : base + column + 1, :]
    sides = start_sides(side_ref, out_ref, sent_sides)
    load_ref[...] = sum_halves(times_turned(spread_ref[...], cover_ref[...]))
    count = stack_rows // (3 * TILE_X)
    for at, (turn, distance) in enumerate(reached()):
        rows = slice(at * count, (at + 1) * count)
        first = turn * count * TILE_X
        low_ref[rows, :] = load_ref[pl.ds(first + distance, count, stride=TILE_X), :]
        high_ref[rows, :] = load_ref[pl.ds(first + TILE_X - 1 - distance, count, stride=TILE_X), :]
    wait_sides(sides)


def adjoint_body(
    load_ref,
    lower_ref,
    higher_ref,
    recv_ref,
    strain_ref,
    medium_ref,
    residual_ref,
    gradient_ref,
    residual_out_ref,
    first_ref,
    later_ref,
    velocity_ref,
    state_ref,
    near_ref,
    turn_ref,
    sides_ref,
):
    depth = medium_ref.shape[0] // 3
    rims = rim_rows(recv_ref, turn_ref)
    sides_ref[...] = jnp.zeros_like(sides_ref)
    count = load_ref.shape[0] // (3 * TILE_X)
    for at, (turn, distance) in enumerate(reached()):
        rows = slice(at * count, (at + 1) * count)
        first = turn * count * TILE_X
        sides_ref[0, pl.ds(first + distance, count, stride=TILE_X), :] = higher_ref[rows, :]
        sides_ref[1, pl.ds(first + TILE_X - 1 - distance, count, stride=TILE_X), :] = lower_ref[rows, :]
    lay_planes(first_ref, later_ref, 0, load_ref, sides_ref.at[0], sides_ref.at[1])
    lay_planes(first_ref, later_ref, LANES, *rims)
    for plane in range(3 * depth):
        near_ref[plane] = narrowed(medium_ref[plane])
    gradient_ref[...] = jnp.zeros_like(gradient_ref)
    residual_out_ref[...] = residual_ref[...]
    state, near, medium = (
        fields_of(state_ref, 9, depth),
        fields_of(near_ref, 3, depth),
        fields_of(medium_ref, 3, depth),
    )

    def add_terms(turn, z, strains):
        dilation, dilation_back, doubled, product = None, None, None, None
        for number, strain in enumerate(strains):
            base = (((2 - turn) * 6 + number) * depth + z) * TILE_X
            forward = strain_ref[base : base + TILE_X, :]
            if number < 3:
                dilation = forward if dilation is None else dilation + forward
            if strain is None:
                continue
            back = strain[0:TILE_X, 0:LANES]
            term = forward * back
            if number < 3:
                dilation_back = back if dilation_back is None else dilation_back + back
                doubled = term if doubled is None else doubled + term
            else:
                product = term if product is None else product + term
        for part, term in enumerate((dilation * dilation_back, 2.0 * doubled + product)):
            base = (part * depth + z) * TILE_X
            gradient_ref[base : base + TILE_X, :] = gradient_ref[base : base + TILE_X, :] + term

    loads, velocity = fields_of(first_ref, 2, depth), fields_of(velocity_ref, 2, depth)
    for z in range(depth):
        scale = STEP * medium[2][z]
        velocity[0][z] = scale * ahead_x(loads[0][z])
        velocity[1][z] = scale * ahead_y(loads[1][z])
        state[0][z] = narrowed(velocity[0][z])
        state[1][z] = narrowed(velocity[1][z])
        state[2][z] = jnp.zeros((SPAN_NEAR, SPAN_Y), F32)
    for z in range(depth):
        along_x, along_y = velocity[0][z], velocity[1][z]
        strain_x, strain_y = behind_x(along_x), behind_y(along_y)
        sheared = (
            ahead_y(along_x) + ahead_x(along_y),
            ahead_z(velocity[0], z),
            ahead_z(velocity[1], z),
        )
        add_terms(0, z, (strain_x, strain_y, None) + sheared)
        dilated = medium[0][z] * (strain_x + strain_y)
        shear = medium[1][z]
        state[3][z] = narrowed(loads[0][z] + STEP * (dilated + 2.0 * shear * strain_x))
        state[4][z] = narrowed(loads[1][z] + STEP * (dilated + 2.0 * shear * strain_y))
        state[5][z] = narrowed(STEP * dilated)
        for number, strain in enumerate(sheared):
            state[6 + number][z] = narrowed(STEP * shear * strain)
    for turn in (1, 2):
        for part in range(2):
            for z in range(depth):
                load = later_ref[(2 * (turn - 1) + part) * depth + z]
                state[3 + part][z] = state[3 + part][z] + load
        advance(state, near, functools.partial(add_terms, turn), state if turn == 1 else None)


def shards(
    initial_state,
    lame_lambda,
    shear_modulus,
    buoyancy,
    source_cells,
    source_wavelet,
    segment_start,
    segment_weight,
    partial_owner,
    partial_channel,
    observed_data,
):
    depth, rows_x, cols_y = lame_lambda.shape
    part_count = segment_start.shape[0]
    count_x, count_y = lax.axis_size("gx"), lax.axis_size("gy")
    devices = count_x * count_y
    capacity = max(2, 2 * part_count // devices)
    slot_groups = devices * capacity // LANES
    blocks = part_count // LANES
    per_group = LANES // capacity
    cells_row = depth * rows_x
    both = ("gx", "gy")
    up = [(i, i + 1) for i in range(count_x - 1)]
    down = [(j, i) for i, j in up]
    shape = jax.ShapeDtypeStruct

    def exchange(chunks):
        return lax.all_to_all(chunks, both, split_axis=0, concat_axis=0, tiled=True)

    def to_owners(rows):
        chunks = rows.reshape(slot_groups, 4, per_group, capacity).transpose(0, 2, 1, 3)
        back = exchange(chunks.reshape(devices, 4, capacity)).reshape(slot_groups, per_group, 4, capacity)
        return back.transpose(0, 2, 1, 3).reshape(slot_groups * 4, LANES)

    trimmed = shape((14 * depth * RIM, cols_y), F32)
    fields, high, low, edges = call_kernel(
        pack_body,
        "pack_edges",
        [shape((14 * cells_row, cols_y), F32), trimmed, trimmed, shape((devices, 1, 2 * RIM * LANES), F32)],
        [
            pltpu.VMEM((14 * cells_row, cols_y), F32),
            pltpu.VMEM(trimmed.shape, F32),
            pltpu.VMEM(trimmed.shape, F32),
            pltpu.VMEM((2, 1, 2 * RIM * LANES), F32),
            pltpu.VMEM((1, source_cells.shape[0]), I32),
            pltpu.VMEM(source_wavelet.shape, F32),
            pltpu.SemaphoreType.DMA((6,)),
            pltpu.SemaphoreType.DMA((3,)),
            pltpu.SemaphoreType.DMA((6,)),
        ],
        *[values.reshape(-1, cols_y) for values in (initial_state, lame_lambda, shear_modulus, buoyancy)],
        source_cells.reshape(1, -1),
        source_wavelet,
        place=pl.ANY,
        place_out=pl.ANY,
        room=60 * 1024 * 1024,
    )
    lower = lax.ppermute(high, "gx", up)
    higher = lax.ppermute(low, "gx", down)
    rims = exchange(edges)
    channels = partial_channel.reshape(blocks, LANES)
    slot, row, cover, place = call_kernel(
        functools.partial(slots_body, capacity, devices, cols_y),
        "segment_slots",
        [
            shape((blocks, LANES), I32),
            shape((blocks, LANES), I32),
            shape((cols_y, part_count), BF16),
            shape((LANES, part_count), BF16),
        ],
        [pltpu.VMEM((blocks, LANES), F32)],
        partial_owner.reshape(blocks, LANES),
        segment_start.reshape(blocks, LANES),
    )
    partials, strains, medium = call_kernel(
        forward_body,
        "forward_run",
        [
            shape((slot_groups * 4, LANES), F32),
            shape((18 * cells_row, cols_y), F32),
            shape((3 * depth, SPAN_X, SPAN_Y), F32),
        ],
        [
            pltpu.VMEM((12 * depth, SPAN_X, SPAN_Y), F32),
            pltpu.VMEM((2 * depth, SPAN_NEAR, SPAN_Y), F32),
            pltpu.VMEM((9 * depth, SPAN_NEAR, SPAN_Y), F32),
            pltpu.VMEM((3 * depth, SPAN_NEAR, SPAN_Y), F32),
            pltpu.VMEM((3, LANES, 2 * LANES), F32),
            pltpu.VMEM((2, 14 * cells_row, cols_y), F32),
            pltpu.VMEM((3 * LANES, part_count), BF16),
        ],
        fields,
        lower,
        higher,
        rims,
        slot,
        row,
        segment_weight,
        channels,
        cover,
        place,
    )
    parts = observed_data.shape[1] // LANES
    residuals, reply = call_kernel(
        owner_body,
        "channel_sums",
        [shape(observed_data.shape, F32), shape((slot_groups * 4, LANES), F32)],
        [
            pltpu.VMEM((10 * parts, slot_groups * LANES), BF16),
            pltpu.VMEM((LANES, slot_groups * LANES), BF16),
            pltpu.VMEM((4 * parts, LANES), F32),
        ],
        to_owners(partials),
        observed_data,
    )
    reach = shape((len(reached()) * 2 * depth, cols_y), F32)
    loads, load_high, load_low, load_edges = call_kernel(
        load_body,
        "segment_loads",
        [shape((6 * cells_row, cols_y), F32), reach, reach, shape((devices, 1, RIM * LANES), F32)],
        [
            pltpu.VMEM((12 * cells_row, part_count), BF16),
            pltpu.VMEM((2, 1, RIM * LANES), F32),
            pltpu.SemaphoreType.DMA((6,)),
        ],
        to_owners(reply),
        slot,
        row,
        segment_weight,
        cover,
        place,
        place_out=(pltpu.VMEM, pltpu.VMEM, pltpu.VMEM, pl.ANY),
    )
    load_lower = lax.ppermute(load_high, "gx", up)
    load_higher = lax.ppermute(load_low, "gx", down)
    load_rims = exchange(load_edges)
    gradients, residuals = call_kernel(
        adjoint_body,
        "adjoint_run",
        [shape((2 * cells_row, cols_y), F32), shape(observed_data.shape, F32)],
        [
            pltpu.VMEM((2 * depth, SPAN_X, SPAN_Y), F32),
            pltpu.VMEM((4 * depth, SPAN_NEAR, SPAN_Y), F32),
            pltpu.VMEM((2 * depth, SPAN_X, SPAN_Y), F32),
            pltpu.VMEM((9 * depth, SPAN_NEAR, SPAN_Y), F32),
            pltpu.VMEM((3 * depth, SPAN_NEAR, SPAN_Y), F32),
            pltpu.VMEM((3, LANES, LANES), F32),
            pltpu.VMEM((2, 6 * cells_row, cols_y), F32),
        ],
        loads,
        load_lower,
        load_higher,
        load_rims,
        strains,
        medium,
        residuals,
    )
    return (residuals, gradients.reshape(2, depth, rows_x, cols_y))


def solution(mesh):
    in_specs = (
        P(None, None, "gx", "gy"),
        P(None, "gx", "gy"),
        P(None, "gx", "gy"),
        P(None, "gx", "gy"),
        P(("gx", "gy")),
        P(None, ("gx", "gy")),
        P(("gx", "gy")),
        P(None, ("gx", "gy")),
        P(("gx", "gy"), None),
        P(("gx", "gy")),
        P(None, ("gx", "gy")),
    )
    out_specs = (P(None, ("gx", "gy")), P(None, None, "gx", "gy"))
    return jax.shard_map(shards, mesh=mesh, in_specs=in_specs, out_specs=out_specs, check_vma=False)
```

```python
import functools

import jax
import jax.numpy as jnp
from jax import lax
from jax.experimental import pallas as pl
from jax.experimental.pallas import tpu as pltpu
from jax.sharding import PartitionSpec as P

GAUGE = 8
STEP = 0.25
RIM = 3
LANES = 128
TILE_X = 4
SPAN_X = 16
SPAN_NEAR = 8
SPAN_Y = 256
F32, BF16, I32 = jnp.float32, jnp.bfloat16, jnp.int32
NEAR = tuple((dx, dy) for dx in (-1, 0, 1) for dy in (-1, 0, 1))


def call_kernel(
    body, name, outs, scratch, *args, place=pltpu.VMEM, place_out=pltpu.VMEM, room=24 * 1024 * 1024
):
    spaces = place_out if isinstance(place_out, tuple) else (place_out,) * len(outs)
    return pl.pallas_call(
        body,
        name=name,
        out_shape=outs,
        in_specs=[pl.BlockSpec(memory_space=place)] * len(args),
        out_specs=[pl.BlockSpec(memory_space=space) for space in spaces],
        scratch_shapes=scratch,
        compiler_params=pltpu.CompilerParams(vmem_limit_bytes=room),
    )(*args)


def pieces(values):
    high = values.astype(BF16).astype(F32)
    rest = values - high
    middle = rest.astype(BF16).astype(F32)
    return high, middle, rest - middle


def iota(shape, dim):
    return lax.broadcasted_iota(I32, shape, dim)


def times(left, right):
    return lax.dot_general(left, right, (((1,), (0,)), ((), ())), preferred_element_type=F32)


def times_turned(left, right):
    return lax.dot_general(left, right, (((1,), (1,)), ((), ())), preferred_element_type=F32)


def packed_rows(row, height):
    tile = jnp.broadcast_to(row.astype(F32), (16, row.shape[1])).astype(BF16)
    return jnp.concatenate([tile] * (height // 16), axis=0) if height > 16 else tile


def packed_iota(height, shift=0):
    return (iota((height, LANES), 0) >> shift).astype(F32).astype(BF16)


def two_pieces(values):
    high = values.astype(BF16).astype(F32)
    return high, values - high


def sum_halves(values):
    half = values.shape[0] // 2
    return values[:half] + values[half:]


def sum_thirds(values):
    third = values.shape[0] // 3
    return values[:third] + values[third : 2 * third] + values[2 * third :]


def neighbour(dx, dy):
    count_x, count_y = lax.axis_size("gx"), lax.axis_size("gy")
    at_x, at_y = lax.axis_index("gx") + dx, lax.axis_index("gy") + dy
    inside = (at_x >= 0) & (at_x < count_x) & (at_y >= 0) & (at_y < count_y)
    return jnp.where(inside, at_x * count_y + at_y, 0), inside


def edge_columns(rows, side_ref):
    width = rows.shape[0]
    turned = rows.T
    for side, base in ((0, 0), (1, LANES - RIM)):
        for column in range(RIM):
            side_ref[side, 0:1, column * width : (column + 1) * width] = turned[base + column : base + column + 1, :]


def start_sides(side_ref, out_ref, sent):
    sides = []
    for number, (dx, dy) in enumerate((dx, dy) for dx, dy in NEAR if dy):
        index, inside = neighbour(dx, dy)
        source, target = side_ref.at[1 if dy > 0 else 0], out_ref.at[index]
        sides.append((inside, pltpu.make_async_copy(source, target, sent.at[number])))
    for inside, copy in sides:
        pl.when(inside)(copy.start)
    return sides


def wait_sides(sides):
    for inside, copy in sides:
        pl.when(inside)(copy.wait)


def arrived_chunk(recv_ref, dx, dy):
    index, inside = neighbour(dx, dy)
    return jnp.where(inside, recv_ref[index], 0.0)


def rim_rows(recv_ref, turn_ref):
    width = turn_ref.shape[2]
    turn_ref[...] = jnp.zeros_like(turn_ref)
    for block, dx in enumerate((0, 1, -1)):
        for dy, first in ((1, 0), (-1, LANES - RIM)):
            chunk = arrived_chunk(recv_ref, dx, dy)
            for column in range(RIM):
                turn_ref[block, first + column : first + column + 1, :] = chunk[
                    :, column * width : (column + 1) * width
                ]
    return [turn_ref[block].T for block in range(3)]


def lay_planes(wide_ref, narrow_ref, lane, centre, higher, lower):
    row = iota((8, LANES), 0)
    wide = wide_ref.shape[0]
    lanes = slice(lane, lane + LANES)
    for plane in range(wide + narrow_ref.shape[0]):
        rows = slice(8 * (plane // 2), 8 * (plane // 2) + 8)
        mid, high, low = centre[rows], higher[rows], lower[rows]
        if plane % 2:
            mid = pltpu.roll(mid, TILE_X, 0)
        else:
            high, low = pltpu.roll(high, TILE_X, 0), pltpu.roll(low, TILE_X, 0)
        near = jnp.where(row < TILE_X, mid, high)
        if plane < wide:
            wide_ref[plane, 0:8, lanes] = near
            wide_ref[plane, 8:16, lanes] = jnp.where(row < TILE_X, 0.0, low)
        else:
            narrow_ref[plane - wide, :, lanes] = jnp.where(row < SPAN_NEAR - 2, near, low)


def narrowed(plane):
    row = iota((SPAN_NEAR, plane.shape[1]), 0)
    return jnp.where(row < SPAN_NEAR - 2, plane[:SPAN_NEAR], plane[SPAN_NEAR:])


def ahead_x(plane):
    return pltpu.roll(plane, plane.shape[0] - 1, 0) - plane


def behind_x(plane):
    return plane - pltpu.roll(plane, 1, 0)


def ahead_y(plane):
    return pltpu.roll(plane, SPAN_Y - 1, 1) - plane


def behind_y(plane):
    return plane - pltpu.roll(plane, 1, 1)


def ahead_z(planes, z):
    return planes[z + 1] - planes[z] if z + 1 < len(planes) else -planes[z]


def behind_z(planes, z):
    return planes[z] - planes[z - 1] if z else planes[z]


class Planes:
    def __init__(self, ref, first, depth):
        self.ref, self.first, self.depth = ref, first, depth

    def __len__(self):
        return self.depth

    def __getitem__(self, z):
        return self.ref[self.first + z]

    def __setitem__(self, z, plane):
        self.ref[self.first + z] = plane


def fields_of(ref, count, depth, first=0):
    return [Planes(ref, (first + number) * depth, depth) for number in range(count)]


def strain_rates(velocity, z):
    along_x, along_y, along_z = [field[z] for field in velocity]
    return (
        behind_x(along_x),
        behind_y(along_y),
        behind_z(velocity[2], z),
        ahead_y(along_x) + ahead_x(along_y),
        ahead_z(velocity[0], z) + ahead_x(along_z),
        ahead_z(velocity[1], z) + ahead_y(along_z),
    )


def new_stress(stress, strains, lame_lambda, shear_modulus, z):
    dilated = lame_lambda[z] * (strains[0] + strains[1] + strains[2])
    shear = shear_modulus[z]
    normal = [stress[n][z] + STEP * (dilated + 2.0 * shear * strains[n]) for n in range(3)]
    return normal + [stress[n][z] + STEP * shear * strains[n] for n in range(3, 6)]


def advance(state, medium, emit, target):
    velocity, stress = state[:3], state[3:]
    lame_lambda, shear_modulus, buoyancy = medium
    depth = len(buoyancy)
    wide = target is not None and target is not state
    for z in range(depth):
        scale = STEP * buoyancy[z]
        accel = (
            ahead_x(stress[0][z]) + behind_y(stress[3][z]) + behind_z(stress[4], z),
            behind_x(stress[3][z]) + ahead_y(stress[1][z]) + behind_z(stress[5], z),
            behind_x(stress[4][z]) + behind_y(stress[5][z]) + ahead_z(stress[2], z),
        )
        for number in range(3):
            moved = velocity[number][z] + scale * accel[number]
            velocity[number][z] = moved
            if wide:
                target[number][z] = narrowed(moved)
    for z in range(depth):
        strains = strain_rates(velocity, z)
        emit(z, strains)
        if target is not None:
            for number, plane in enumerate(new_stress(stress, strains, lame_lambda, shear_modulus, z)):
                target[3 + number][z] = narrowed(plane) if wide else plane


def pack_body(*refs):
    inputs, outputs, scratch = refs[:6], refs[6:10], refs[10:]
    fields_ref, high_ref, low_ref, side_ref, cells_ref, wavelet_ref, arrived, sent, sent_sides = scratch
    targets, at = [], 0
    for source in inputs[:4]:
        targets.append(fields_ref.at[at : at + source.shape[0]])
        at = at + source.shape[0]
    copies = [
        pltpu.make_async_copy(source, target, arrived.at[number])
        for number, (source, target) in enumerate(zip(inputs, targets + [cells_ref, wavelet_ref]))
    ]
    for copy in copies[4:] + copies[:4]:
        copy.start()
    copies[4].wait()
    copies[5].wait()
    cells_row = inputs[1].shape[0]
    cells = cells_ref[...]
    count = cells.shape[1]
    at_lane = iota((LANES, count), 0) == (cells & (LANES - 1))
    at_row = iota((cells_row, count), 0) == (cells >> (LANES.bit_length() - 1))
    stack = [
        jnp.where(at_row, third[step : step + 1, :], 0.0) for third in pieces(wavelet_ref[...]) for step in range(3)
    ]
    maps = sum_thirds(
        times_turned(jnp.concatenate(stack, axis=0).astype(BF16), jnp.where(at_lane, 1.0, 0.0).astype(BF16))
    )
    for copy in copies[:4]:
        copy.wait()
    fields_ref[at:, :] = maps[cells_row:]
    for number in range(3, 6):
        rows = slice(number * cells_row, (number + 1) * cells_row)
        fields_ref[rows, :] = fields_ref[rows, :] + maps[:cells_row]
    rows = fields_ref[...]
    spare = 2 * LANES - rows.shape[0]
    edge_columns(jnp.concatenate([rows, jnp.zeros((spare, LANES), F32)], axis=0), side_ref)
    sides = start_sides(side_ref, outputs[3], sent_sides)
    height = fields_ref.shape[0] // TILE_X
    for x in range(TILE_X):
        slab = fields_ref[pl.ds(x, height, stride=TILE_X), :]
        if x < RIM:
            low_ref[x * height : (x + 1) * height, :] = slab
        if x >= TILE_X - RIM:
            at = x - TILE_X + RIM
            high_ref[at * height : (at + 1) * height, :] = slab
    writes = [
        pltpu.make_async_copy(source, target, sent.at[number])
        for number, (source, target) in enumerate(zip((fields_ref, high_ref, low_ref), outputs))
    ]
    for copy in writes:
        copy.start()
    for copy in writes:
        copy.wait()
    wait_sides(sides)


def slots_body(capacity, devices, cols_y, owner_ref, start_ref, slot_ref, row_ref, cover_ref, place_ref, rank_ref):
    blocks = owner_ref.shape[0]
    group = 32
    before = jnp.where(iota((LANES, 2 * LANES), 0) < iota((LANES, 2 * LANES), 1), 1.0, 0.0).astype(BF16)
    rank_ref[...] = jnp.zeros_like(rank_ref)

    def count_group(number, carry):
        names = iota((group, LANES), 0) + number * group
        hot = [names == owner_ref[b : b + 1, :] for b in range(blocks)]
        marks = jnp.concatenate([jnp.where(h, 1.0, 0.0) for h in hot], axis=0).astype(BF16)
        counts = times(marks, before)
        total = jnp.zeros((group, LANES), F32)
        for b in range(blocks):
            part = counts[b * group : (b + 1) * group]
            rank_ref[b : b + 1, :] = rank_ref[b : b + 1, :] + jnp.sum(
                jnp.where(hot[b], part[:, :LANES] + total, 0.0), axis=0, keepdims=True
            )
            total = total + part[:, LANES:]
        return carry

    if devices == group:
        count_group(0, 0)
    else:
        lax.fori_loop(0, devices // group, count_group, 0)
    slot = owner_ref[...] * capacity + rank_ref[...].astype(I32)
    slot_ref[...] = slot >> 7
    low = slot & (LANES - 1)
    span = cols_y - GAUGE + 1
    start = start_ref[...]
    row = ((start.astype(F32) + 0.5) * (1.0 / span)).astype(I32)
    row_ref[...] = row
    first = start - row * span
    down = iota((LANES, LANES), 0)
    for b in range(blocks):
        lanes = slice(b * LANES, (b + 1) * LANES)
        offset = down - first[b : b + 1, :]
        cover_ref[:, lanes] = jnp.where((offset >= 0) & (offset < GAUGE), 1.0, 0.0).astype(BF16)
        place_ref[:, lanes] = jnp.where(down == low[b : b + 1, :], 1.0, 0.0).astype(BF16)


def forward_body(
    fields_ref,
    lower_ref,
    higher_ref,
    recv_ref,
    slot_ref,
    row_ref,
    weight_ref,
    channel_ref,
    cover_ref,
    place_ref,
    out_ref,
    strain_ref,
    medium_ref,
    wide_ref,
    source_ref,
    state_ref,
    near_ref,
    turn_ref,
    sides_ref,
    spread_ref,
):
    depth = medium_ref.shape[0] // 3
    cells_row = depth * TILE_X
    rims = rim_rows(recv_ref, turn_ref)
    height = fields_ref.shape[0] // TILE_X
    sides_ref[...] = jnp.zeros_like(sides_ref)
    for x in range(RIM):
        slab = slice(x * height, (x + 1) * height)
        sides_ref[0, pl.ds(x, height, stride=TILE_X), :] = higher_ref[slab, :]
        sides_ref[1, pl.ds(x + TILE_X - RIM, height, stride=TILE_X), :] = lower_ref[slab, :]
    lay_planes(wide_ref, source_ref, 0, fields_ref, sides_ref.at[0], sides_ref.at[1])
    lay_planes(wide_ref, source_ref, LANES, *rims)
    first = 9 * depth
    medium_ref[...] = wide_ref[first:]
    for plane in range(3 * depth):
        near_ref[plane] = narrowed(wide_ref[first + plane])
    state, near = fields_of(state_ref, 9, depth), fields_of(near_ref, 3, depth)
    for step in range(3):

        def emit(z, strains, step=step):
            for number, strain in enumerate(strains):
                base = ((step * 6 + number) * depth + z) * TILE_X
                strain_ref[base : base + TILE_X, :] = strain[0:TILE_X, 0:LANES]

        if step == 0:
            advance(fields_of(wide_ref, 9, depth), fields_of(wide_ref, 3, depth, 9), emit, state)
            continue
        for z in range(depth):
            load = source_ref[(step - 1) * depth + z]
            for number in range(3, 6):
                state[number][z] = state[number][z] + load
        advance(state, near, emit, state if step == 1 else None)
    axial = jnp.concatenate(
        [strain_ref[step * 6 * cells_row : (step * 6 + 2) * cells_row, :] for step in range(3)], axis=0
    )
    axial = jnp.concatenate(pieces(axial), axis=0).astype(BF16)
    rows_down = iota((cells_row, LANES), 0)
    slots_down = packed_iota(LANES, 2)
    for block in range(slot_ref.shape[0]):
        lanes = slice(block * LANES, (block + 1) * LANES)
        if block % 2 == 0:
            both = sum_thirds(times(axial, cover_ref[:, block * LANES : (block + 2) * LANES]))
        windows = both[:, :LANES] if block % 2 == 0 else both[:, LANES:]
        at_row = rows_down == row_ref[block : block + 1, :]
        weight_x, weight_y = weight_ref[0:1, lanes], weight_ref[1:2, lanes]
        sums = []
        for step in range(3):
            base = 2 * step * cells_row
            axial_sum = (
                weight_x * windows[base : base + cells_row]
                + weight_y * windows[base + cells_row : base + 2 * cells_row]
            )
            sums.append(jnp.sum(jnp.where(at_row, axial_sum, 0.0), axis=0, keepdims=True))
        sums.append(channel_ref[block : block + 1, :].astype(F32))
        values = jnp.concatenate(sums + sums, axis=0)
        in_slot = slots_down == packed_rows(slot_ref[block : block + 1, :], LANES)
        for third, piece in enumerate(pieces(values)):
            tile = jnp.concatenate([piece, piece], axis=0).astype(BF16)
            spread_ref[third * LANES : (third + 1) * LANES, lanes] = jnp.where(
                in_slot, jnp.concatenate([tile] * (LANES // 16), axis=0), jnp.zeros((), BF16)
            )
    out_ref[...] = sum_thirds(times_turned(spread_ref[...], place_ref[...]))


def owner_body(arrived_ref, observed_ref, residual_ref, reply_ref, values_ref, place_ref, held_ref):
    groups = arrived_ref.shape[0] // 4
    parts = observed_ref.shape[1] // LANES
    down = packed_iota(LANES)
    part_down = iota((parts, LANES), 0)
    nothing = jnp.zeros((parts, LANES), F32)
    numbers = [arrived_ref[4 * s + 3 : 4 * s + 4, :].astype(I32) for s in range(groups)]
    for s in range(groups):
        lanes = slice(s * LANES, (s + 1) * LANES)
        place_ref[:, lanes] = jnp.where(
            down == packed_rows(numbers[s] & (LANES - 1), LANES), jnp.ones((), BF16), jnp.zeros((), BF16)
        )
        at_part = part_down == (numbers[s] >> 7)
        thirds = pieces(arrived_ref[4 * s : 4 * s + 3, :])
        stack = []
        for third in thirds:
            for step in range(3):
                stack.append(jnp.where(at_part, third[step : step + 1, :], 0.0))
        stack.append(nothing)
        values_ref[:, lanes] = jnp.concatenate(stack, axis=0).astype(BF16)
    rows = 3 * parts
    sums = sum_thirds(times_turned(values_ref[...], place_ref[...])[: 3 * rows])
    for step in range(3):
        for part in range(parts):
            at = step * parts + part
            held_ref[at : at + 1, :] = observed_ref[step : step + 1, part * LANES : (part + 1) * LANES]
    held_ref[rows:, :] = nothing
    held_ref[0:rows, :] = sums - held_ref[0:rows, :]
    for step in range(3):
        for part in range(parts):
            at = step * parts + part
            residual_ref[step : step + 1, part * LANES : (part + 1) * LANES] = held_ref[at : at + 1, :]
    residual = jnp.concatenate(two_pieces(held_ref[...]), axis=0).astype(BF16)
    for s in range(groups):
        if s % 2 == 0:
            both = sum_halves(times(residual, place_ref[:, s * LANES : (s + 2) * LANES]))
        found = both[:, :LANES] if s % 2 == 0 else both[:, LANES:]
        at_part = part_down == (numbers[s] >> 7)
        for step in range(3):
            reply_ref[4 * s + step : 4 * s + step + 1, :] = jnp.sum(
                jnp.where(at_part, found[step * parts : (step + 1) * parts], 0.0), axis=0, keepdims=True
            )
        reply_ref[4 * s + 3 : 4 * s + 4, :] = jnp.zeros((1, LANES), F32)


def reached():
    return [(turn, distance) for turn in range(3) for distance in range(RIM - turn)]


def load_body(
    arrived_ref,
    slot_ref,
    row_ref,
    weight_ref,
    cover_ref,
    place_ref,
    load_ref,
    high_ref,
    low_ref,
    out_ref,
    spread_ref,
    side_ref,
    sent_sides,
):
    cells_row = load_ref.shape[0] // 6
    stack_rows = load_ref.shape[0]
    arrived = jnp.concatenate(two_pieces(arrived_ref[...]), axis=0).astype(BF16)
    slots_down = iota((LANES, LANES), 0) >> 2
    rows_down = packed_iota(cells_row)
    for block in range(slot_ref.shape[0]):
        lanes = slice(block * LANES, (block + 1) * LANES)
        if block % 2 == 0:
            both = sum_halves(times(arrived, place_ref[:, block * LANES : (block + 2) * LANES]))
        found = both[:, :LANES] if block % 2 == 0 else both[:, LANES:]
        found = jnp.where(slots_down == slot_ref[block : block + 1, :], found, 0.0)
        folded = found[0:8]
        for part in range(1, LANES // 8):
            folded = folded + found[8 * part : 8 * part + 8]
        folded = folded + pltpu.roll(folded, 4, 0)
        at_row = rows_down == packed_rows(row_ref[block : block + 1, :], cells_row)
        for turn in range(3):
            back = folded[2 - turn : 3 - turn, :]
            for part in range(2):
                for half, piece in enumerate(two_pieces(weight_ref[part : part + 1, lanes] * back)):
                    base = half * stack_rows + (2 * turn + part) * cells_row
                    spread_ref[base : base + cells_row, lanes] = jnp.where(
                        at_row, packed_rows(piece, cells_row), jnp.zeros((), BF16)
                    )
    cover = jnp.concatenate([cover_ref[0:16, :], cover_ref[LANES - 16 :, :]], axis=0)
    edges = times_turned(cover, spread_ref[0:stack_rows, :]) + times_turned(cover, spread_ref[stack_rows:, :])
    side_ref[...] = jnp.zeros_like(side_ref)
    for side, base in ((0, 0), (1, 32 - RIM)):
        for column in range(RIM):
            lanes = slice(column * LANES, column * LANES + stack_rows)
            side_ref[side, 0:1, lanes] = edges[base + column : base + column + 1, :]
    sides = start_sides(side_ref, out_ref, sent_sides)
    load_ref[...] = sum_halves(times_turned(spread_ref[...], cover_ref[...]))
    count = stack_rows // (3 * TILE_X)
    for at, (turn, distance) in enumerate(reached()):
        rows = slice(at * count, (at + 1) * count)
        first = turn * count * TILE_X
        low_ref[rows, :] = load_ref[pl.ds(first + distance, count, stride=TILE_X), :]
        high_ref[rows, :] = load_ref[pl.ds(first + TILE_X - 1 - distance, count, stride=TILE_X), :]
    wait_sides(sides)


def adjoint_body(
    load_ref,
    higher_ref,
    lower_ref,
    recv_ref,
    strain_ref,
    medium_ref,
    residual_ref,
    gradient_ref,
    residual_out_ref,
    first_ref,
    later_ref,
    velocity_ref,
    state_ref,
    near_ref,
    turn_ref,
    sides_ref,
):
    depth = medium_ref.shape[0] // 3
    rims = rim_rows(recv_ref, turn_ref)
    sides_ref[...] = jnp.zeros_like(sides_ref)
    count = load_ref.shape[0] // (3 * TILE_X)
    for at, (turn, distance) in enumerate(reached()):
        rows = slice(at * count, (at + 1) * count)
        first = turn * count * TILE_X
        sides_ref[0, pl.ds(first + distance, count, stride=TILE_X), :] = higher_ref[rows, :]
        sides_ref[1, pl.ds(first + TILE_X - 1 - distance, count, stride=TILE_X), :] = lower_ref[rows, :]
    lay_planes(first_ref, later_ref, 0, load_ref, sides_ref.at[0], sides_ref.at[1])
    lay_planes(first_ref, later_ref, LANES, *rims)
    for plane in range(3 * depth):
        near_ref[plane] = narrowed(medium_ref[plane])
    gradient_ref[...] = jnp.zeros_like(gradient_ref)
    residual_out_ref[...] = residual_ref[...]
    state, near, medium = (
        fields_of(state_ref, 9, depth),
        fields_of(near_ref, 3, depth),
        fields_of(medium_ref, 3, depth),
    )

    def add_terms(turn, z, strains):
        dilation, dilation_back, doubled, product = None, None, None, None
        for number, strain in enumerate(strains):
            base = (((2 - turn) * 6 + number) * depth + z) * TILE_X
            forward = strain_ref[base : base + TILE_X, :]
            if number < 3:
                dilation = forward if dilation is None else dilation + forward
            if strain is None:
                continue
            back = strain[0:TILE_X, 0:LANES]
            term = forward * back
            if number < 3:
                dilation_back = back if dilation_back is None else dilation_back + back
                doubled = term if doubled is None else doubled + term
            else:
                product = term if product is None else product + term
        for part, term in enumerate((dilation * dilation_back, 2.0 * doubled + product)):
            base = (part * depth + z) * TILE_X
            gradient_ref[base : base + TILE_X, :] = gradient_ref[base : base + TILE_X, :] + term

    loads, velocity = fields_of(first_ref, 2, depth), fields_of(velocity_ref, 2, depth)
    for z in range(depth):
        scale = STEP * medium[2][z]
        velocity[0][z] = scale * ahead_x(loads[0][z])
        velocity[1][z] = scale * ahead_y(loads[1][z])
        state[0][z] = narrowed(velocity[0][z])
        state[1][z] = narrowed(velocity[1][z])
        state[2][z] = jnp.zeros((SPAN_NEAR, SPAN_Y), F32)
    for z in range(depth):
        along_x, along_y = velocity[0][z], velocity[1][z]
        strain_x, strain_y = behind_x(along_x), behind_y(along_y)
        sheared = (
            ahead_y(along_x) + ahead_x(along_y),
            ahead_z(velocity[0], z),
            ahead_z(velocity[1], z),
        )
        add_terms(0, z, (strain_x, strain_y, None) + sheared)
        dilated = medium[0][z] * (strain_x + strain_y)
        shear = medium[1][z]
        state[3][z] = narrowed(loads[0][z] + STEP * (dilated + 2.0 * shear * strain_x))
        state[4][z] = narrowed(loads[1][z] + STEP * (dilated + 2.0 * shear * strain_y))
        state[5][z] = narrowed(STEP * dilated)
        for number, strain in enumerate(sheared):
            state[6 + number][z] = narrowed(STEP * shear * strain)
    for turn in (1, 2):
        for part in range(2):
            for z in range(depth):
                load = later_ref[(2 * (turn - 1) + part) * depth + z]
                state[3 + part][z] = state[3 + part][z] + load
        advance(state, near, functools.partial(add_terms, turn), state if turn == 1 else None)


def shards(
    initial_state,
    lame_lambda,
    shear_modulus,
    buoyancy,
    source_cells,
    source_wavelet,
    segment_start,
    segment_weight,
    partial_owner,
    partial_channel,
    observed_data,
):
    depth, rows_x, cols_y = lame_lambda.shape
    part_count = segment_start.shape[0]
    count_x, count_y = lax.axis_size("gx"), lax.axis_size("gy")
    devices = count_x * count_y
    capacity = max(2, 2 * part_count // devices)
    slot_groups = devices * capacity // LANES
    blocks = part_count // LANES
    per_group = LANES // capacity
    cells_row = depth * rows_x
    both = ("gx", "gy")
    up = [(i, i + 1) for i in range(count_x - 1)]
    down = [(j, i) for i, j in up]
    shape = jax.ShapeDtypeStruct

    def exchange(chunks):
        return lax.all_to_all(chunks, both, split_axis=0, concat_axis=0, tiled=True)

    def to_owners(rows):
        chunks = rows.reshape(slot_groups, 4, per_group, capacity).transpose(0, 2, 1, 3)
        back = exchange(chunks.reshape(devices, 4, capacity)).reshape(slot_groups, per_group, 4, capacity)
        return back.transpose(0, 2, 1, 3).reshape(slot_groups * 4, LANES)

    trimmed = shape((14 * depth * RIM, cols_y), F32)
    fields, high, low, edges = call_kernel(
        pack_body,
        "pack_edges",
        [shape((14 * cells_row, cols_y), F32), trimmed, trimmed, shape((devices, 1, 2 * RIM * LANES), F32)],
        [
            pltpu.VMEM((14 * cells_row, cols_y), F32),
            pltpu.VMEM(trimmed.shape, F32),
            pltpu.VMEM(trimmed.shape, F32),
            pltpu.VMEM((2, 1, 2 * RIM * LANES), F32),
            pltpu.VMEM((1, source_cells.shape[0]), I32),
            pltpu.VMEM(source_wavelet.shape, F32),
            pltpu.SemaphoreType.DMA((6,)),
            pltpu.SemaphoreType.DMA((3,)),
            pltpu.SemaphoreType.DMA((6,)),
        ],
        *[values.reshape(-1, cols_y) for values in (initial_state, lame_lambda, shear_modulus, buoyancy)],
        source_cells.reshape(1, -1),
        source_wavelet,
        place=pl.ANY,
        place_out=pl.ANY,
        room=60 * 1024 * 1024,
    )
    lower = lax.ppermute(high, "gx", up)
    higher = lax.ppermute(low, "gx", down)
    rims = exchange(edges)
    channels = partial_channel.reshape(blocks, LANES)
    slot, row, cover, place = call_kernel(
        functools.partial(slots_body, capacity, devices, cols_y),
        "segment_slots",
        [
            shape((blocks, LANES), I32),
            shape((blocks, LANES), I32),
            shape((cols_y, part_count), BF16),
            shape((LANES, part_count), BF16),
        ],
        [pltpu.VMEM((blocks, LANES), F32)],
        partial_owner.reshape(blocks, LANES),
        segment_start.reshape(blocks, LANES),
    )
    partials, strains, medium = call_kernel(
        forward_body,
        "forward_run",
        [
            shape((slot_groups * 4, LANES), F32),
            shape((18 * cells_row, cols_y), F32),
            shape((3 * depth, SPAN_X, SPAN_Y), F32),
        ],
        [
            pltpu.VMEM((12 * depth, SPAN_X, SPAN_Y), F32),
            pltpu.VMEM((2 * depth, SPAN_NEAR, SPAN_Y), F32),
            pltpu.VMEM((9 * depth, SPAN_NEAR, SPAN_Y), F32),
            pltpu.VMEM((3 * depth, SPAN_NEAR, SPAN_Y), F32),
            pltpu.VMEM((3, LANES, 2 * LANES), F32),
            pltpu.VMEM((2, 14 * cells_row, cols_y), F32),
            pltpu.VMEM((3 * LANES, part_count), BF16),
        ],
        fields,
        lower,
        higher,
        rims,
        slot,
        row,
        segment_weight,
        channels,
        cover,
        place,
    )
    parts = observed_data.shape[1] // LANES
    residuals, reply = call_kernel(
        owner_body,
        "channel_sums",
        [shape(observed_data.shape, F32), shape((slot_groups * 4, LANES), F32)],
        [
            pltpu.VMEM((10 * parts, slot_groups * LANES), BF16),
            pltpu.VMEM((LANES, slot_groups * LANES), BF16),
            pltpu.VMEM((4 * parts, LANES), F32),
        ],
        to_owners(partials),
        observed_data,
    )
    reach = shape((len(reached()) * 2 * depth, cols_y), F32)
    loads, load_high, load_low, load_edges = call_kernel(
        load_body,
        "segment_loads",
        [shape((6 * cells_row, cols_y), F32), reach, reach, shape((devices, 1, RIM * LANES), F32)],
        [
            pltpu.VMEM((12 * cells_row, part_count), BF16),
            pltpu.VMEM((2, 1, RIM * LANES), F32),
            pltpu.SemaphoreType.DMA((6,)),
        ],
        to_owners(reply),
        slot,
        row,
        segment_weight,
        cover,
        place,
        place_out=(pltpu.VMEM, pltpu.VMEM, pltpu.VMEM, pl.ANY),
    )
    load_lower = lax.ppermute(load_high, "gx", up)
    load_higher = lax.ppermute(load_low, "gx", down)
    load_rims = exchange(load_edges)
    gradients, residuals = call_kernel(
        adjoint_body,
        "adjoint_run",
        [shape((2 * cells_row, cols_y), F32), shape(observed_data.shape, F32)],
        [
            pltpu.VMEM((2 * depth, SPAN_X, SPAN_Y), F32),
            pltpu.VMEM((4 * depth, SPAN_NEAR, SPAN_Y), F32),
            pltpu.VMEM((2 * depth, SPAN_X, SPAN_Y), F32),
            pltpu.VMEM((9 * depth, SPAN_NEAR, SPAN_Y), F32),
            pltpu.VMEM((3 * depth, SPAN_NEAR, SPAN_Y), F32),
            pltpu.VMEM((3, LANES, LANES), F32),
            pltpu.VMEM((2, 6 * cells_row, cols_y), F32),
        ],
        loads,
        load_higher,
        load_lower,
        load_rims,
        strains,
        medium,
        residuals,
    )
    return (residuals, gradients.reshape(2, depth, rows_x, cols_y))


def solution(mesh):
    in_specs = (
        P(None, None, "gx", "gy"),
        P(None, "gx", "gy"),
        P(None, "gx", "gy"),
        P(None, "gx", "gy"),
        P(("gx", "gy")),
        P(None, ("gx", "gy")),
        P(("gx", "gy")),
        P(None, ("gx", "gy")),
        P(("gx", "gy"), None),
        P(("gx", "gy")),
        P(None, ("gx", "gy")),
    )
    out_specs = (P(None, ("gx", "gy")), P(None, None, "gx", "gy"))
    return jax.shard_map(shards, mesh=mesh, in_specs=in_specs, out_specs=out_specs, check_vma=False)
```

```python
import functools

import jax
import jax.numpy as jnp
from jax import lax
from jax.experimental import pallas as pl
from jax.experimental.pallas import tpu as pltpu
from jax.sharding import PartitionSpec as P

GAUGE = 8
STEP = 0.25
RIM = 3
LANES = 128
TILE_X = 4
SPAN_X = 16
SPAN_NEAR = 8
SPAN_Y = 256
F32, BF16, I32 = jnp.float32, jnp.bfloat16, jnp.int32
NEAR = tuple((dx, dy) for dx in (-1, 0, 1) for dy in (-1, 0, 1))


def call_kernel(
    body, name, outs, scratch, *args, place=pltpu.VMEM, place_out=pltpu.VMEM, room=24 * 1024 * 1024
):
    spaces = place_out if isinstance(place_out, tuple) else (place_out,) * len(outs)
    return pl.pallas_call(
        body,
        name=name,
        out_shape=outs,
        in_specs=[pl.BlockSpec(memory_space=place)] * len(args),
        out_specs=[pl.BlockSpec(memory_space=space) for space in spaces],
        scratch_shapes=scratch,
        compiler_params=pltpu.CompilerParams(vmem_limit_bytes=room),
    )(*args)


def pieces(values):
    high = values.astype(BF16).astype(F32)
    rest = values - high
    middle = rest.astype(BF16).astype(F32)
    return high, middle, rest - middle


def iota(shape, dim):
    return lax.broadcasted_iota(I32, shape, dim)


def times(left, right):
    return lax.dot_general(left, right, (((1,), (0,)), ((), ())), preferred_element_type=F32)


def times_turned(left, right):
    return lax.dot_general(left, right, (((1,), (1,)), ((), ())), preferred_element_type=F32)


def packed_rows(row, height):
    tile = jnp.broadcast_to(row.astype(F32), (16, row.shape[1])).astype(BF16)
    return jnp.concatenate([tile] * (height // 16), axis=0) if height > 16 else tile


def packed_iota(height, shift=0):
    return (iota((height, LANES), 0) >> shift).astype(F32).astype(BF16)


def two_pieces(values):
    high = values.astype(BF16).astype(F32)
    return high, values - high


def sum_halves(values):
    half = values.shape[0] // 2
    return values[:half] + values[half:]


def sum_thirds(values):
    third = values.shape[0] // 3
    return values[:third] + values[third : 2 * third] + values[2 * third :]


def neighbour(dx, dy):
    count_x, count_y = lax.axis_size("gx"), lax.axis_size("gy")
    at_x, at_y = lax.axis_index("gx") + dx, lax.axis_index("gy") + dy
    inside = (at_x >= 0) & (at_x < count_x) & (at_y >= 0) & (at_y < count_y)
    return jnp.where(inside, at_x * count_y + at_y, 0), inside


def edge_columns(rows, side_ref):
    width = rows.shape[0]
    turned = rows.T
    for side, base in ((0, 0), (1, LANES - RIM)):
        for column in range(RIM):
            side_ref[side, 0:1, column * width : (column + 1) * width] = turned[base + column : base + column + 1, :]


def start_sides(side_ref, out_ref, sent):
    sides = []
    for number, (dx, dy) in enumerate((dx, dy) for dx, dy in NEAR if dy):
        index, inside = neighbour(dx, dy)
        source, target = side_ref.at[1 if dy > 0 else 0], out_ref.at[index]
        sides.append((inside, pltpu.make_async_copy(source, target, sent.at[number])))
    for inside, copy in sides:
        pl.when(inside)(copy.start)
    return sides


def wait_sides(sides):
    for inside, copy in sides:
        pl.when(inside)(copy.wait)


def arrived_chunk(recv_ref, dx, dy):
    index, inside = neighbour(dx, dy)
    return jnp.where(inside, recv_ref[index], 0.0)


def rim_rows(recv_ref, turn_ref):
    width = turn_ref.shape[2]
    turn_ref[...] = jnp.zeros_like(turn_ref)
    for block, dx in enumerate((0, 1, -1)):
        for dy, first in ((1, 0), (-1, LANES - RIM)):
            chunk = arrived_chunk(recv_ref, dx, dy)
            for column in range(RIM):
                turn_ref[block, first + column : first + column + 1, :] = chunk[
                    :, column * width : (column + 1) * width
                ]
    return [turn_ref[block].T for block in range(3)]


def lay_planes(wide_ref, narrow_ref, lane, centre, higher, lower):
    row = iota((8, LANES), 0)
    wide = wide_ref.shape[0]
    lanes = slice(lane, lane + LANES)
    for plane in range(wide + narrow_ref.shape[0]):
        rows = slice(8 * (plane // 2), 8 * (plane // 2) + 8)
        mid, high, low = centre[rows], higher[rows], lower[rows]
        if plane % 2:
            mid = pltpu.roll(mid, TILE_X, 0)
        else:
            high, low = pltpu.roll(high, TILE_X, 0), pltpu.roll(low, TILE_X, 0)
        near = jnp.where(row < TILE_X, mid, high)
        if plane < wide:
            wide_ref[plane, 0:8, lanes] = near
            wide_ref[plane, 8:16, lanes] = jnp.where(row < TILE_X, 0.0, low)
        else:
            narrow_ref[plane - wide, :, lanes] = jnp.where(row < SPAN_NEAR - 2, near, low)


def narrowed(plane):
    row = iota((SPAN_NEAR, plane.shape[1]), 0)
    return jnp.where(row < SPAN_NEAR - 2, plane[:SPAN_NEAR], plane[SPAN_NEAR:])


def ahead_x(plane):
    return pltpu.roll(plane, plane.shape[0] - 1, 0) - plane


def behind_x(plane):
    return plane - pltpu.roll(plane, 1, 0)


def ahead_y(plane):
    return pltpu.roll(plane, SPAN_Y - 1, 1) - plane


def behind_y(plane):
    return plane - pltpu.roll(plane, 1, 1)


def ahead_z(planes, z):
    return planes[z + 1] - planes[z] if z + 1 < len(planes) else -planes[z]


def behind_z(planes, z):
    return planes[z] - planes[z - 1] if z else planes[z]


class Planes:
    def __init__(self, ref, first, depth):
        self.ref, self.first, self.depth = ref, first, depth

    def __len__(self):
        return self.depth

    def __getitem__(self, z):
        return self.ref[self.first + z]

    def __setitem__(self, z, plane):
        self.ref[self.first + z] = plane


def fields_of(ref, count, depth, first=0):
    return [Planes(ref, (first + number) * depth, depth) for number in range(count)]


def strain_rates(velocity, z):
    along_x, along_y, along_z = [field[z] for field in velocity]
    return (
        behind_x(along_x),
        behind_y(along_y),
        behind_z(velocity[2], z),
        ahead_y(along_x) + ahead_x(along_y),
        ahead_z(velocity[0], z) + ahead_x(along_z),
        ahead_z(velocity[1], z) + ahead_y(along_z),
    )


def new_stress(stress, strains, lame_lambda, shear_modulus, z):
    dilated = lame_lambda[z] * (strains[0] + strains[1] + strains[2])
    shear = shear_modulus[z]
    normal = [stress[n][z] + STEP * (dilated + 2.0 * shear * strains[n]) for n in range(3)]
    return normal + [stress[n][z] + STEP * shear * strains[n] for n in range(3, 6)]


def advance(state, medium, emit, target):
    velocity, stress = state[:3], state[3:]
    lame_lambda, shear_modulus, buoyancy = medium
    depth = len(buoyancy)
    wide = target is not None and target is not state
    for z in range(depth):
        scale = STEP * buoyancy[z]
        accel = (
            ahead_x(stress[0][z]) + behind_y(stress[3][z]) + behind_z(stress[4], z),
            behind_x(stress[3][z]) + ahead_y(stress[1][z]) + behind_z(stress[5], z),
            behind_x(stress[4][z]) + behind_y(stress[5][z]) + ahead_z(stress[2], z),
        )
        for number in range(3):
            moved = velocity[number][z] + scale * accel[number]
            velocity[number][z] = moved
            if wide:
                target[number][z] = narrowed(moved)
    for z in range(depth):
        strains = strain_rates(velocity, z)
        emit(z, strains)
        if target is not None:
            for number, plane in enumerate(new_stress(stress, strains, lame_lambda, shear_modulus, z)):
                target[3 + number][z] = narrowed(plane) if wide else plane


def slabs_of(depth):
    whole, inner, first = 14 * depth, 10 * depth, 2 * depth
    low = ((0, 0, whole), (1, 0, whole), (2, first, inner))
    high = ((1, first, inner), (2, 0, whole), (3, 0, whole))
    return low, high


def pack_body(*refs):
    inputs, outputs, scratch = refs[:6], refs[6:10], refs[10:]
    fields_ref, high_ref, low_ref, side_ref, cells_ref, wavelet_ref, arrived, sent, sent_sides = scratch
    state, lame_lambda, shear_modulus, buoyancy, cells, wavelet = inputs
    third = state.shape[0] // 3
    sources, at = [lame_lambda, shear_modulus], 0
    sources += [state.at[part * third : (part + 1) * third] for part in range(3)] + [buoyancy]
    copies = [(cells, cells_ref), (wavelet, wavelet_ref)]
    for source in sources:
        copies.append((source, fields_ref.at[at : at + source.shape[0]]))
        at = at + source.shape[0]
    copies = [
        pltpu.make_async_copy(source, target, arrived.at[number]) for number, (source, target) in enumerate(copies)
    ]
    for copy in copies:
        copy.start()
    copies[0].wait()
    copies[1].wait()
    cells_row = inputs[1].shape[0]
    cells = cells_ref[...]
    count = cells.shape[1]
    at_lane = iota((LANES, count), 0) == (cells & (LANES - 1))
    at_row = iota((cells_row, count), 0) == (cells >> (LANES.bit_length() - 1))
    stack = [
        jnp.where(at_row, third[step : step + 1, :], 0.0) for third in pieces(wavelet_ref[...]) for step in range(3)
    ]
    maps = sum_thirds(
        times_turned(jnp.concatenate(stack, axis=0).astype(BF16), jnp.where(at_lane, 1.0, 0.0).astype(BF16))
    )
    for copy in copies[2:]:
        copy.wait()
    fields_ref[at:, :] = maps[cells_row:]
    for number in range(5, 8):
        rows = slice(number * cells_row, (number + 1) * cells_row)
        fields_ref[rows, :] = fields_ref[rows, :] + maps[:cells_row]
    rows = fields_ref[...]
    spare = 2 * LANES - rows.shape[0]
    edge_columns(jnp.concatenate([rows, jnp.zeros((spare, LANES), F32)], axis=0), side_ref)
    sides = start_sides(side_ref, outputs[3], sent_sides)
    for target, slabs in zip((low_ref, high_ref), slabs_of(cells_row // TILE_X)):
        at = 0
        for x, first, count in slabs:
            target[at : at + count, :] = fields_ref[pl.ds(first * TILE_X + x, count, stride=TILE_X), :]
            at = at + count
    writes = [
        pltpu.make_async_copy(source, target, sent.at[number])
        for number, (source, target) in enumerate(zip((fields_ref, high_ref, low_ref), outputs))
    ]
    for copy in writes:
        copy.start()
    for copy in writes:
        copy.wait()
    wait_sides(sides)


def slots_body(capacity, devices, cols_y, owner_ref, start_ref, slot_ref, row_ref, cover_ref, place_ref, rank_ref):
    blocks = owner_ref.shape[0]
    group = 32
    before = jnp.where(iota((LANES, 2 * LANES), 0) < iota((LANES, 2 * LANES), 1), 1.0, 0.0).astype(BF16)
    rank_ref[...] = jnp.zeros_like(rank_ref)

    def count_group(number, carry):
        names = iota((group, LANES), 0) + number * group
        hot = [names == owner_ref[b : b + 1, :] for b in range(blocks)]
        marks = jnp.concatenate([jnp.where(h, 1.0, 0.0) for h in hot], axis=0).astype(BF16)
        counts = times(marks, before)
        total = jnp.zeros((group, LANES), F32)
        for b in range(blocks):
            part = counts[b * group : (b + 1) * group]
            rank_ref[b : b + 1, :] = rank_ref[b : b + 1, :] + jnp.sum(
                jnp.where(hot[b], part[:, :LANES] + total, 0.0), axis=0, keepdims=True
            )
            total = total + part[:, LANES:]
        return carry

    if devices == group:
        count_group(0, 0)
    else:
        lax.fori_loop(0, devices // group, count_group, 0)
    slot = owner_ref[...] * capacity + rank_ref[...].astype(I32)
    slot_ref[...] = slot >> 7
    low = slot & (LANES - 1)
    span = cols_y - GAUGE + 1
    start = start_ref[...]
    row = ((start.astype(F32) + 0.5) * (1.0 / span)).astype(I32)
    row_ref[...] = row
    first = start - row * span
    down = iota((LANES, LANES), 0)
    for b in range(blocks):
        lanes = slice(b * LANES, (b + 1) * LANES)
        offset = down - first[b : b + 1, :]
        cover_ref[:, lanes] = jnp.where((offset >= 0) & (offset < GAUGE), 1.0, 0.0).astype(BF16)
        place_ref[:, lanes] = jnp.where(down == low[b : b + 1, :], 1.0, 0.0).astype(BF16)


def forward_body(
    fields_ref,
    lower_ref,
    higher_ref,
    recv_ref,
    slot_ref,
    row_ref,
    weight_ref,
    channel_ref,
    cover_ref,
    place_ref,
    out_ref,
    strain_ref,
    medium_ref,
    wide_ref,
    source_ref,
    state_ref,
    near_ref,
    turn_ref,
    sides_ref,
    spread_ref,
):
    depth = medium_ref.shape[0] // 3
    cells_row = depth * TILE_X
    rims = rim_rows(recv_ref, turn_ref)
    sides_ref[...] = jnp.zeros_like(sides_ref)
    for side, (source, slabs) in enumerate(zip((higher_ref, lower_ref), slabs_of(depth))):
        at = 0
        for x, first, count in slabs:
            sides_ref[side, pl.ds(first * TILE_X + x, count, stride=TILE_X), :] = source[at : at + count, :]
            at = at + count
    lay_planes(wide_ref, source_ref, 0, fields_ref, sides_ref.at[0], sides_ref.at[1])
    lay_planes(wide_ref, source_ref, LANES, *rims)
    medium_ref[0 : 2 * depth] = wide_ref[0 : 2 * depth]
    medium_ref[2 * depth :] = wide_ref[11 * depth :]
    for plane in range(3 * depth):
        near_ref[plane] = narrowed(medium_ref[plane])
    state, near = fields_of(state_ref, 9, depth), fields_of(near_ref, 3, depth)
    for step in range(3):

        def emit(z, strains, step=step):
            for number, strain in enumerate(strains):
                base = ((step * 6 + number) * depth + z) * TILE_X
                strain_ref[base : base + TILE_X, :] = strain[0:TILE_X, 0:LANES]

        if step == 0:
            advance(fields_of(wide_ref, 9, depth, 2), fields_of(medium_ref, 3, depth), emit, state)
            continue
        for z in range(depth):
            load = source_ref[(step - 1) * depth + z]
            for number in range(3, 6):
                state[number][z] = state[number][z] + load
        advance(state, near, emit, state if step == 1 else None)
    axial = jnp.concatenate(
        [strain_ref[step * 6 * cells_row : (step * 6 + 2) * cells_row, :] for step in range(3)], axis=0
    )
    axial = jnp.concatenate(pieces(axial), axis=0).astype(BF16)
    rows_down = iota((cells_row, LANES), 0)
    slots_down = packed_iota(LANES, 2)
    for block in range(slot_ref.shape[0]):
        lanes = slice(block * LANES, (block + 1) * LANES)
        if block % 2 == 0:
            both = sum_thirds(times(axial, cover_ref[:, block * LANES : (block + 2) * LANES]))
        windows = both[:, :LANES] if block % 2 == 0 else both[:, LANES:]
        at_row = rows_down == row_ref[block : block + 1, :]
        weight_x, weight_y = weight_ref[0:1, lanes], weight_ref[1:2, lanes]
        sums = []
        for step in range(3):
            base = 2 * step * cells_row
            axial_sum = (
                weight_x * windows[base : base + cells_row]
                + weight_y * windows[base + cells_row : base + 2 * cells_row]
            )
            sums.append(jnp.sum(jnp.where(at_row, axial_sum, 0.0), axis=0, keepdims=True))
        sums.append(channel_ref[block : block + 1, :].astype(F32))
        values = jnp.concatenate(sums + sums, axis=0)
        in_slot = slots_down == packed_rows(slot_ref[block : block + 1, :], LANES)
        for third, piece in enumerate(pieces(values)):
            tile = jnp.concatenate([piece, piece], axis=0).astype(BF16)
            spread_ref[third * LANES : (third + 1) * LANES, lanes] = jnp.where(
                in_slot, jnp.concatenate([tile] * (LANES // 16), axis=0), jnp.zeros((), BF16)
            )
    out_ref[...] = sum_thirds(times_turned(spread_ref[...], place_ref[...]))


def owner_body(arrived_ref, observed_ref, residual_ref, reply_ref, values_ref, place_ref, held_ref):
    groups = arrived_ref.shape[0] // 4
    parts = observed_ref.shape[1] // LANES
    down = packed_iota(LANES)
    part_down = iota((parts, LANES), 0)
    nothing = jnp.zeros((parts, LANES), F32)
    numbers = [arrived_ref[4 * s + 3 : 4 * s + 4, :].astype(I32) for s in range(groups)]
    for s in range(groups):
        lanes = slice(s * LANES, (s + 1) * LANES)
        place_ref[:, lanes] = jnp.where(
            down == packed_rows(numbers[s] & (LANES - 1), LANES), jnp.ones((), BF16), jnp.zeros((), BF16)
        )
        at_part = part_down == (numbers[s] >> 7)
        thirds = pieces(arrived_ref[4 * s : 4 * s + 3, :])
        stack = []
        for third in thirds:
            for step in range(3):
                stack.append(jnp.where(at_part, third[step : step + 1, :], 0.0))
        stack.append(nothing)
        values_ref[:, lanes] = jnp.concatenate(stack, axis=0).astype(BF16)
    rows = 3 * parts
    sums = sum_thirds(times_turned(values_ref[...], place_ref[...])[: 3 * rows])
    for step in range(3):
        for part in range(parts):
            at = step * parts + part
            held_ref[at : at + 1, :] = observed_ref[step : step + 1, part * LANES : (part + 1) * LANES]
    held_ref[rows:, :] = nothing
    held_ref[0:rows, :] = sums - held_ref[0:rows, :]
    for step in range(3):
        for part in range(parts):
            at = step * parts + part
            residual_ref[step : step + 1, part * LANES : (part + 1) * LANES] = held_ref[at : at + 1, :]
    residual = jnp.concatenate(two_pieces(held_ref[...]), axis=0).astype(BF16)
    for s in range(groups):
        if s % 2 == 0:
            both = sum_halves(times(residual, place_ref[:, s * LANES : (s + 2) * LANES]))
        found = both[:, :LANES] if s % 2 == 0 else both[:, LANES:]
        at_part = part_down == (numbers[s] >> 7)
        for step in range(3):
            reply_ref[4 * s + step : 4 * s + step + 1, :] = jnp.sum(
                jnp.where(at_part, found[step * parts : (step + 1) * parts], 0.0), axis=0, keepdims=True
            )
        reply_ref[4 * s + 3 : 4 * s + 4, :] = jnp.zeros((1, LANES), F32)


def reached():
    return [(turn, distance) for turn in range(3) for distance in range(RIM - turn)]


def load_body(
    arrived_ref,
    slot_ref,
    row_ref,
    weight_ref,
    cover_ref,
    place_ref,
    load_ref,
    high_ref,
    low_ref,
    out_ref,
    spread_ref,
    side_ref,
    sent_sides,
):
    cells_row = load_ref.shape[0] // 6
    stack_rows = load_ref.shape[0]
    arrived = jnp.concatenate(two_pieces(arrived_ref[...]), axis=0).astype(BF16)
    slots_down = iota((LANES, LANES), 0) >> 2
    rows_down = packed_iota(cells_row)
    for block in range(slot_ref.shape[0]):
        lanes = slice(block * LANES, (block + 1) * LANES)
        if block % 2 == 0:
            both = sum_halves(times(arrived, place_ref[:, block * LANES : (block + 2) * LANES]))
        found = both[:, :LANES] if block % 2 == 0 else both[:, LANES:]
        found = jnp.where(slots_down == slot_ref[block : block + 1, :], found, 0.0)
        folded = found[0:8]
        for part in range(1, LANES // 8):
            folded = folded + found[8 * part : 8 * part + 8]
        folded = folded + pltpu.roll(folded, 4, 0)
        at_row = rows_down == packed_rows(row_ref[block : block + 1, :], cells_row)
        for turn in range(3):
            back = folded[2 - turn : 3 - turn, :]
            for part in range(2):
                for half, piece in enumerate(two_pieces(weight_ref[part : part + 1, lanes] * back)):
                    base = half * stack_rows + (2 * turn + part) * cells_row
                    spread_ref[base : base + cells_row, lanes] = jnp.where(
                        at_row, packed_rows(piece, cells_row), jnp.zeros((), BF16)
                    )
    cover = jnp.concatenate([cover_ref[0:16, :], cover_ref[LANES - 16 :, :]], axis=0)
    edges = times_turned(cover, spread_ref[0:stack_rows, :]) + times_turned(cover, spread_ref[stack_rows:, :])
    side_ref[...] = jnp.zeros_like(side_ref)
    for side, base in ((0, 0), (1, 32 - RIM)):
        for column in range(RIM):
            lanes = slice(column * LANES, column * LANES + stack_rows)
            side_ref[side, 0:1, lanes] = edges[base + column : base + column + 1, :]
    sides = start_sides(side_ref, out_ref, sent_sides)
    load_ref[...] = sum_halves(times_turned(spread_ref[...], cover_ref[...]))
    count = stack_rows // (3 * TILE_X)
    for at, (turn, distance) in enumerate(reached()):
        rows = slice(at * count, (at + 1) * count)
        first = turn * count * TILE_X
        low_ref[rows, :] = load_ref[pl.ds(first + distance, count, stride=TILE_X), :]
        high_ref[rows, :] = load_ref[pl.ds(first + TILE_X - 1 - distance, count, stride=TILE_X), :]
    wait_sides(sides)


def adjoint_body(
    load_ref,
    higher_ref,
    lower_ref,
    recv_ref,
    strain_ref,
    medium_ref,
    residual_ref,
    gradient_ref,
    residual_out_ref,
    first_ref,
    later_ref,
    velocity_ref,
    state_ref,
    near_ref,
    turn_ref,
    sides_ref,
):
    depth = medium_ref.shape[0] // 3
    rims = rim_rows(recv_ref, turn_ref)
    sides_ref[...] = jnp.zeros_like(sides_ref)
    count = load_ref.shape[0] // (3 * TILE_X)
    for at, (turn, distance) in enumerate(reached()):
        rows = slice(at * count, (at + 1) * count)
        first = turn * count * TILE_X
        sides_ref[0, pl.ds(first + distance, count, stride=TILE_X), :] = higher_ref[rows, :]
        sides_ref[1, pl.ds(first + TILE_X - 1 - distance, count, stride=TILE_X), :] = lower_ref[rows, :]
    lay_planes(first_ref, later_ref, 0, load_ref, sides_ref.at[0], sides_ref.at[1])
    lay_planes(first_ref, later_ref, LANES, *rims)
    for plane in range(3 * depth):
        near_ref[plane] = narrowed(medium_ref[plane])
    gradient_ref[...] = jnp.zeros_like(gradient_ref)
    residual_out_ref[...] = residual_ref[...]
    state, near, medium = (
        fields_of(state_ref, 9, depth),
        fields_of(near_ref, 3, depth),
        fields_of(medium_ref, 3, depth),
    )

    def add_terms(turn, z, strains):
        dilation, dilation_back, doubled, product = None, None, None, None
        for number, strain in enumerate(strains):
            base = (((2 - turn) * 6 + number) * depth + z) * TILE_X
            forward = strain_ref[base : base + TILE_X, :]
            if number < 3:
                dilation = forward if dilation is None else dilation + forward
            if strain is None:
                continue
            back = strain[0:TILE_X, 0:LANES]
            term = forward * back
            if number < 3:
                dilation_back = back if dilation_back is None else dilation_back + back
                doubled = term if doubled is None else doubled + term
            else:
                product = term if product is None else product + term
        for part, term in enumerate((dilation * dilation_back, 2.0 * doubled + product)):
            base = (part * depth + z) * TILE_X
            gradient_ref[base : base + TILE_X, :] = gradient_ref[base : base + TILE_X, :] + term

    loads, velocity = fields_of(first_ref, 2, depth), fields_of(velocity_ref, 2, depth)
    for z in range(depth):
        scale = STEP * medium[2][z]
        velocity[0][z] = scale * ahead_x(loads[0][z])
        velocity[1][z] = scale * ahead_y(loads[1][z])
        state[0][z] = narrowed(velocity[0][z])
        state[1][z] = narrowed(velocity[1][z])
        state[2][z] = jnp.zeros((SPAN_NEAR, SPAN_Y), F32)
    for z in range(depth):
        along_x, along_y = velocity[0][z], velocity[1][z]
        strain_x, strain_y = behind_x(along_x), behind_y(along_y)
        sheared = (
            ahead_y(along_x) + ahead_x(along_y),
            ahead_z(velocity[0], z),
            ahead_z(velocity[1], z),
        )
        add_terms(0, z, (strain_x, strain_y, None) + sheared)
        dilated = medium[0][z] * (strain_x + strain_y)
        shear = medium[1][z]
        state[3][z] = narrowed(loads[0][z] + STEP * (dilated + 2.0 * shear * strain_x))
        state[4][z] = narrowed(loads[1][z] + STEP * (dilated + 2.0 * shear * strain_y))
        state[5][z] = narrowed(STEP * dilated)
        for number, strain in enumerate(sheared):
            state[6 + number][z] = narrowed(STEP * shear * strain)
    for turn in (1, 2):
        for part in range(2):
            for z in range(depth):
                load = later_ref[(2 * (turn - 1) + part) * depth + z]
                state[3 + part][z] = state[3 + part][z] + load
        advance(state, near, functools.partial(add_terms, turn), state if turn == 1 else None)


def shards(
    initial_state,
    lame_lambda,
    shear_modulus,
    buoyancy,
    source_cells,
    source_wavelet,
    segment_start,
    segment_weight,
    partial_owner,
    partial_channel,
    observed_data,
):
    depth, rows_x, cols_y = lame_lambda.shape
    part_count = segment_start.shape[0]
    count_x, count_y = lax.axis_size("gx"), lax.axis_size("gy")
    devices = count_x * count_y
    capacity = max(2, 2 * part_count // devices)
    slot_groups = devices * capacity // LANES
    blocks = part_count // LANES
    per_group = LANES // capacity
    cells_row = depth * rows_x
    both = ("gx", "gy")
    up = [(i, i + 1) for i in range(count_x - 1)]
    down = [(j, i) for i, j in up]
    shape = jax.ShapeDtypeStruct

    def exchange(chunks):
        return lax.all_to_all(chunks, both, split_axis=0, concat_axis=0, tiled=True)

    def to_owners(rows):
        chunks = rows.reshape(slot_groups, 4, per_group, capacity).transpose(0, 2, 1, 3)
        back = exchange(chunks.reshape(devices, 4, capacity)).reshape(slot_groups, per_group, 4, capacity)
        return back.transpose(0, 2, 1, 3).reshape(slot_groups * 4, LANES)

    trimmed = shape((sum(count for _, _, count in slabs_of(depth)[0]), cols_y), F32)
    fields, high, low, edges = call_kernel(
        pack_body,
        "pack_edges",
        [shape((14 * cells_row, cols_y), F32), trimmed, trimmed, shape((devices, 1, 2 * RIM * LANES), F32)],
        [
            pltpu.VMEM((14 * cells_row, cols_y), F32),
            pltpu.VMEM(trimmed.shape, F32),
            pltpu.VMEM(trimmed.shape, F32),
            pltpu.VMEM((2, 1, 2 * RIM * LANES), F32),
            pltpu.VMEM((1, source_cells.shape[0]), I32),
            pltpu.VMEM(source_wavelet.shape, F32),
            pltpu.SemaphoreType.DMA((8,)),
            pltpu.SemaphoreType.DMA((3,)),
            pltpu.SemaphoreType.DMA((6,)),
        ],
        *[values.reshape(-1, cols_y) for values in (initial_state, lame_lambda, shear_modulus, buoyancy)],
        source_cells.reshape(1, -1),
        source_wavelet,
        place=pl.ANY,
        place_out=pl.ANY,
        room=60 * 1024 * 1024,
    )
    lower = lax.ppermute(high, "gx", up)
    higher = lax.ppermute(low, "gx", down)
    rims = exchange(edges)
    channels = partial_channel.reshape(blocks, LANES)
    slot, row, cover, place = call_kernel(
        functools.partial(slots_body, capacity, devices, cols_y),
        "segment_slots",
        [
            shape((blocks, LANES), I32),
            shape((blocks, LANES), I32),
            shape((cols_y, part_count), BF16),
            shape((LANES, part_count), BF16),
        ],
        [pltpu.VMEM((blocks, LANES), F32)],
        partial_owner.reshape(blocks, LANES),
        segment_start.reshape(blocks, LANES),
    )
    partials, strains, medium = call_kernel(
        forward_body,
        "forward_run",
        [
            shape((slot_groups * 4, LANES), F32),
            shape((18 * cells_row, cols_y), F32),
            shape((3 * depth, SPAN_X, SPAN_Y), F32),
        ],
        [
            pltpu.VMEM((12 * depth, SPAN_X, SPAN_Y), F32),
            pltpu.VMEM((2 * depth, SPAN_NEAR, SPAN_Y), F32),
            pltpu.VMEM((9 * depth, SPAN_NEAR, SPAN_Y), F32),
            pltpu.VMEM((3 * depth, SPAN_NEAR, SPAN_Y), F32),
            pltpu.VMEM((3, LANES, 2 * LANES), F32),
            pltpu.VMEM((2, 14 * cells_row, cols_y), F32),
            pltpu.VMEM((3 * LANES, part_count), BF16),
        ],
        fields,
        lower,
        higher,
        rims,
        slot,
        row,
        segment_weight,
        channels,
        cover,
        place,
    )
    parts = observed_data.shape[1] // LANES
    residuals, reply = call_kernel(
        owner_body,
        "channel_sums",
        [shape(observed_data.shape, F32), shape((slot_groups * 4, LANES), F32)],
        [
            pltpu.VMEM((10 * parts, slot_groups * LANES), BF16),
            pltpu.VMEM((LANES, slot_groups * LANES), BF16),
            pltpu.VMEM((4 * parts, LANES), F32),
        ],
        to_owners(partials),
        observed_data,
    )
    reach = shape((len(reached()) * 2 * depth, cols_y), F32)
    loads, load_high, load_low, load_edges = call_kernel(
        load_body,
        "segment_loads",
        [shape((6 * cells_row, cols_y), F32), reach, reach, shape((devices, 1, RIM * LANES), F32)],
        [
            pltpu.VMEM((12 * cells_row, part_count), BF16),
            pltpu.VMEM((2, 1, RIM * LANES), F32),
            pltpu.SemaphoreType.DMA((6,)),
        ],
        to_owners(reply),
        slot,
        row,
        segment_weight,
        cover,
        place,
        place_out=(pltpu.VMEM, pltpu.VMEM, pltpu.VMEM, pl.ANY),
    )
    load_lower = lax.ppermute(load_high, "gx", up)
    load_higher = lax.ppermute(load_low, "gx", down)
    load_rims = exchange(load_edges)
    gradients, residuals = call_kernel(
        adjoint_body,
        "adjoint_run",
        [shape((2 * cells_row, cols_y), F32), shape(observed_data.shape, F32)],
        [
            pltpu.VMEM((2 * depth, SPAN_X, SPAN_Y), F32),
            pltpu.VMEM((4 * depth, SPAN_NEAR, SPAN_Y), F32),
            pltpu.VMEM((2 * depth, SPAN_X, SPAN_Y), F32),
            pltpu.VMEM((9 * depth, SPAN_NEAR, SPAN_Y), F32),
            pltpu.VMEM((3 * depth, SPAN_NEAR, SPAN_Y), F32),
            pltpu.VMEM((3, LANES, LANES), F32),
            pltpu.VMEM((2, 6 * cells_row, cols_y), F32),
        ],
        loads,
        load_higher,
        load_lower,
        load_rims,
        strains,
        medium,
        residuals,
    )
    return (residuals, gradients.reshape(2, depth, rows_x, cols_y))


def solution(mesh):
    in_specs = (
        P(None, None, "gx", "gy"),
        P(None, "gx", "gy"),
        P(None, "gx", "gy"),
        P(None, "gx", "gy"),
        P(("gx", "gy")),
        P(None, ("gx", "gy")),
        P(("gx", "gy")),
        P(None, ("gx", "gy")),
        P(("gx", "gy"), None),
        P(("gx", "gy")),
        P(None, ("gx", "gy")),
    )
    out_specs = (P(None, ("gx", "gy")), P(None, None, "gx", "gy"))
    return jax.shard_map(shards, mesh=mesh, in_specs=in_specs, out_specs=out_specs, check_vma=False)
```

```python
import functools

import jax
import jax.numpy as jnp
from jax import lax
from jax.experimental import pallas as pl
from jax.experimental.pallas import tpu as pltpu
from jax.sharding import PartitionSpec as P

GAUGE = 8
STEP = 0.25
RIM = 3
LANES = 128
TILE_X = 4
SPARE = 8
SPAN_X = 16
SPAN_NEAR = 8
SPAN_Y = 256
F32, BF16, I32 = jnp.float32, jnp.bfloat16, jnp.int32
NEAR = tuple((dx, dy) for dx in (-1, 0, 1) for dy in (-1, 0, 1))


def call_kernel(
    body, name, outs, scratch, *args, place=pltpu.VMEM, place_out=pltpu.VMEM, room=24 * 1024 * 1024
):
    spaces = place_out if isinstance(place_out, tuple) else (place_out,) * len(outs)
    return pl.pallas_call(
        body,
        name=name,
        out_shape=outs,
        in_specs=[pl.BlockSpec(memory_space=place)] * len(args),
        out_specs=[pl.BlockSpec(memory_space=space) for space in spaces],
        scratch_shapes=scratch,
        compiler_params=pltpu.CompilerParams(vmem_limit_bytes=room),
    )(*args)


def pieces(values):
    high = values.astype(BF16).astype(F32)
    rest = values - high
    middle = rest.astype(BF16).astype(F32)
    return high, middle, rest - middle


def iota(shape, dim):
    return lax.broadcasted_iota(I32, shape, dim)


def times(left, right):
    return lax.dot_general(left, right, (((1,), (0,)), ((), ())), preferred_element_type=F32)


def times_turned(left, right):
    return lax.dot_general(left, right, (((1,), (1,)), ((), ())), preferred_element_type=F32)


def packed_rows(row, height):
    tile = jnp.broadcast_to(row.astype(F32), (16, row.shape[1])).astype(BF16)
    return jnp.concatenate([tile] * (height // 16), axis=0) if height > 16 else tile


def packed_iota(height, shift=0):
    return (iota((height, LANES), 0) >> shift).astype(F32).astype(BF16)


def two_pieces(values):
    high = values.astype(BF16).astype(F32)
    return high, values - high


def sum_halves(values):
    half = values.shape[0] // 2
    return values[:half] + values[half:]


def sum_thirds(values):
    third = values.shape[0] // 3
    return values[:third] + values[third : 2 * third] + values[2 * third :]


def neighbour(dx, dy):
    count_x, count_y = lax.axis_size("gx"), lax.axis_size("gy")
    at_x, at_y = lax.axis_index("gx") + dx, lax.axis_index("gy") + dy
    inside = (at_x >= 0) & (at_x < count_x) & (at_y >= 0) & (at_y < count_y)
    return jnp.where(inside, at_x * count_y + at_y, 0), inside


def edge_columns(rows, side_ref):
    width = rows.shape[0]
    turned = rows.T
    for side, base in ((0, 0), (1, LANES - RIM)):
        for column in range(RIM):
            side_ref[side, 0:1, column * width : (column + 1) * width] = turned[base + column : base + column + 1, :]


def start_sides(side_ref, out_ref, sent):
    sides = []
    for number, (dx, dy) in enumerate((dx, dy) for dx, dy in NEAR if dy):
        index, inside = neighbour(dx, dy)
        source, target = side_ref.at[1 if dy > 0 else 0], out_ref.at[index]
        sides.append((inside, pltpu.make_async_copy(source, target, sent.at[number])))
    for inside, copy in sides:
        pl.when(inside)(copy.start)
    return sides


def wait_sides(sides):
    for inside, copy in sides:
        pl.when(inside)(copy.wait)


def arrived_chunk(recv_ref, dx, dy):
    index, inside = neighbour(dx, dy)
    return jnp.where(inside, recv_ref[index], 0.0)


def rim_rows(recv_ref, turn_ref):
    width = turn_ref.shape[2]
    turn_ref[...] = jnp.zeros_like(turn_ref)
    for block, dx in enumerate((0, 1, -1)):
        for dy, first in ((1, 0), (-1, LANES - RIM)):
            chunk = arrived_chunk(recv_ref, dx, dy)
            for column in range(RIM):
                turn_ref[block, first + column : first + column + 1, :] = chunk[
                    :, column * width : (column + 1) * width
                ]
    return [turn_ref[block].T for block in range(3)]


def lay_planes(wide_ref, narrow_ref, lane, centre, higher, lower):
    row = iota((8, LANES), 0)
    wide = wide_ref.shape[0]
    lanes = slice(lane, lane + LANES)
    for plane in range(wide + narrow_ref.shape[0]):
        rows = slice(8 * (plane // 2), 8 * (plane // 2) + 8)
        mid, high, low = centre[rows], higher[rows], lower[rows]
        if plane % 2:
            mid = pltpu.roll(mid, TILE_X, 0)
        else:
            high, low = pltpu.roll(high, TILE_X, 0), pltpu.roll(low, TILE_X, 0)
        near = jnp.where(row < TILE_X, mid, high)
        if plane < wide:
            wide_ref[plane, 0:8, lanes] = near
            wide_ref[plane, 8:16, lanes] = jnp.where(row < TILE_X, 0.0, low)
        else:
            narrow_ref[plane - wide, :, lanes] = jnp.where(row < SPAN_NEAR - 2, near, low)


def narrowed(plane):
    row = iota((SPAN_NEAR, plane.shape[1]), 0)
    return jnp.where(row < SPAN_NEAR - 2, plane[:SPAN_NEAR], plane[SPAN_NEAR:])


def ahead_x(plane):
    return pltpu.roll(plane, plane.shape[0] - 1, 0) - plane


def behind_x(plane):
    return plane - pltpu.roll(plane, 1, 0)


def ahead_y(plane):
    return pltpu.roll(plane, SPAN_Y - 1, 1) - plane


def behind_y(plane):
    return plane - pltpu.roll(plane, 1, 1)


def ahead_z(planes, z):
    return planes[z + 1] - planes[z] if z + 1 < len(planes) else -planes[z]


def behind_z(planes, z):
    return planes[z] - planes[z - 1] if z else planes[z]


class Planes:
    def __init__(self, ref, first, depth):
        self.ref, self.first, self.depth = ref, first, depth

    def __len__(self):
        return self.depth

    def __getitem__(self, z):
        return self.ref[self.first + z]

    def __setitem__(self, z, plane):
        self.ref[self.first + z] = plane


def fields_of(ref, count, depth, first=0):
    return [Planes(ref, (first + number) * depth, depth) for number in range(count)]


def strain_rates(velocity, z):
    along_x, along_y, along_z = [field[z] for field in velocity]
    return (
        behind_x(along_x),
        behind_y(along_y),
        behind_z(velocity[2], z),
        ahead_y(along_x) + ahead_x(along_y),
        ahead_z(velocity[0], z) + ahead_x(along_z),
        ahead_z(velocity[1], z) + ahead_y(along_z),
    )


def new_stress(stress, strains, lame_lambda, shear_modulus, z):
    dilated = lame_lambda[z] * (strains[0] + strains[1] + strains[2])
    shear = shear_modulus[z]
    normal = [stress[n][z] + STEP * (dilated + 2.0 * shear * strains[n]) for n in range(3)]
    return normal + [stress[n][z] + STEP * shear * strains[n] for n in range(3, 6)]


def advance(state, medium, emit, target):
    velocity, stress = state[:3], state[3:]
    lame_lambda, shear_modulus, buoyancy = medium
    depth = len(buoyancy)
    wide = target is not None and target is not state
    for z in range(depth):
        scale = STEP * buoyancy[z]
        accel = (
            ahead_x(stress[0][z]) + behind_y(stress[3][z]) + behind_z(stress[4], z),
            behind_x(stress[3][z]) + ahead_y(stress[1][z]) + behind_z(stress[5], z),
            behind_x(stress[4][z]) + behind_y(stress[5][z]) + ahead_z(stress[2], z),
        )
        for number in range(3):
            moved = velocity[number][z] + scale * accel[number]
            velocity[number][z] = moved
            if wide:
                target[number][z] = narrowed(moved)
    for z in range(depth):
        strains = strain_rates(velocity, z)
        emit(z, strains)
        if target is not None:
            for number, plane in enumerate(new_stress(stress, strains, lame_lambda, shear_modulus, z)):
                target[3 + number][z] = narrowed(plane) if wide else plane


def pack_body(*refs):
    inputs, outputs, scratch = refs[:6], refs[6:10], refs[10:]
    fields_ref, high_ref, low_ref, side_ref, cells_ref, wavelet_ref, arrived, sent, sent_sides = scratch
    targets, at = [], 0
    for source in inputs[:4]:
        targets.append(fields_ref.at[at : at + source.shape[0]])
        at = at + source.shape[0]
    copies = [
        pltpu.make_async_copy(source, target, arrived.at[number])
        for number, (source, target) in enumerate(zip(inputs, targets + [cells_ref, wavelet_ref]))
    ]
    for copy in copies[4:] + copies[:4]:
        copy.start()
    copies[4].wait()
    copies[5].wait()
    cells_row = inputs[1].shape[0]
    cells = cells_ref[...]
    count = cells.shape[1]
    at_lane = iota((LANES, count), 0) == (cells & (LANES - 1))
    at_row = iota((cells_row, count), 0) == (cells >> (LANES.bit_length() - 1))
    stack = [
        jnp.where(at_row, third[step : step + 1, :], 0.0) for third in pieces(wavelet_ref[...]) for step in range(3)
    ]
    maps = sum_thirds(
        times_turned(jnp.concatenate(stack, axis=0).astype(BF16), jnp.where(at_lane, 1.0, 0.0).astype(BF16))
    )
    for copy in copies[:4]:
        copy.wait()
    total = at + 2 * cells_row
    fields_ref[at:total, :] = maps[cells_row:]
    for number in range(3, 6):
        rows = slice(number * cells_row, (number + 1) * cells_row)
        fields_ref[rows, :] = fields_ref[rows, :] + maps[:cells_row]
    rows = fields_ref[0:total, :]
    spare = 2 * LANES - total
    edge_columns(jnp.concatenate([rows, jnp.zeros((spare, LANES), F32)], axis=0), side_ref)
    sides = start_sides(side_ref, outputs[3], sent_sides)
    height = total // TILE_X
    for x in range(TILE_X):
        slab = fields_ref[pl.ds(x, height, stride=TILE_X), :]
        if x < RIM:
            low_ref[x * height : (x + 1) * height, :] = slab
        if x >= TILE_X - RIM:
            at = x - TILE_X + RIM
            high_ref[at * height : (at + 1) * height, :] = slab
    writes = [
        pltpu.make_async_copy(source, target, sent.at[number])
        for number, (source, target) in enumerate(zip((fields_ref.at[0:total], high_ref, low_ref), outputs))
    ]
    for copy in writes:
        copy.start()
    for copy in writes:
        copy.wait()
    wait_sides(sides)


def slots_body(capacity, devices, cols_y, owner_ref, start_ref, slot_ref, row_ref, cover_ref, place_ref, rank_ref):
    blocks = owner_ref.shape[0]
    group = 32
    before = jnp.where(iota((LANES, 2 * LANES), 0) < iota((LANES, 2 * LANES), 1), 1.0, 0.0).astype(BF16)
    rank_ref[...] = jnp.zeros_like(rank_ref)

    def count_group(number, carry):
        names = iota((group, LANES), 0) + number * group
        hot = [names == owner_ref[b : b + 1, :] for b in range(blocks)]
        marks = jnp.concatenate([jnp.where(h, 1.0, 0.0) for h in hot], axis=0).astype(BF16)
        counts = times(marks, before)
        total = jnp.zeros((group, LANES), F32)
        for b in range(blocks):
            part = counts[b * group : (b + 1) * group]
            rank_ref[b : b + 1, :] = rank_ref[b : b + 1, :] + jnp.sum(
                jnp.where(hot[b], part[:, :LANES] + total, 0.0), axis=0, keepdims=True
            )
            total = total + part[:, LANES:]
        return carry

    if devices == group:
        count_group(0, 0)
    else:
        lax.fori_loop(0, devices // group, count_group, 0)
    slot = owner_ref[...] * capacity + rank_ref[...].astype(I32)
    slot_ref[...] = slot >> 7
    low = slot & (LANES - 1)
    span = cols_y - GAUGE + 1
    start = start_ref[...]
    row = ((start.astype(F32) + 0.5) * (1.0 / span)).astype(I32)
    row_ref[...] = row
    first = start - row * span
    down = iota((LANES, LANES), 0)
    for b in range(blocks):
        lanes = slice(b * LANES, (b + 1) * LANES)
        offset = down - first[b : b + 1, :]
        cover_ref[:, lanes] = jnp.where((offset >= 0) & (offset < GAUGE), 1.0, 0.0).astype(BF16)
        place_ref[:, lanes] = jnp.where(down == low[b : b + 1, :], 1.0, 0.0).astype(BF16)


def forward_body(
    fields_ref,
    lower_ref,
    higher_ref,
    recv_ref,
    slot_ref,
    row_ref,
    weight_ref,
    channel_ref,
    cover_ref,
    place_ref,
    out_ref,
    strain_ref,
    medium_ref,
    wide_ref,
    source_ref,
    state_ref,
    near_ref,
    turn_ref,
    sides_ref,
    spread_ref,
):
    depth = medium_ref.shape[0] // 3
    cells_row = depth * TILE_X
    rims = rim_rows(recv_ref, turn_ref)
    height = fields_ref.shape[0] // TILE_X
    sides_ref[...] = jnp.zeros_like(sides_ref)
    for x in range(RIM):
        slab = slice(x * height, (x + 1) * height)
        sides_ref[0, pl.ds(x, height, stride=TILE_X), :] = higher_ref[slab, :]
        sides_ref[1, pl.ds(x + TILE_X - RIM, height, stride=TILE_X), :] = lower_ref[slab, :]
    lay_planes(wide_ref, source_ref, 0, fields_ref, sides_ref.at[0], sides_ref.at[1])
    lay_planes(wide_ref, source_ref, LANES, *rims)
    first = 9 * depth
    medium_ref[...] = wide_ref[first:]
    for plane in range(3 * depth):
        near_ref[plane] = narrowed(wide_ref[first + plane])
    state, near = fields_of(state_ref, 9, depth), fields_of(near_ref, 3, depth)
    for step in range(3):

        def emit(z, strains, step=step):
            for number, strain in enumerate(strains):
                base = ((step * 6 + number) * depth + z) * TILE_X
                strain_ref[base : base + TILE_X, :] = strain[0:TILE_X, 0:LANES]

        if step == 0:
            advance(fields_of(wide_ref, 9, depth), fields_of(wide_ref, 3, depth, 9), emit, state)
            continue
        for z in range(depth):
            load = source_ref[(step - 1) * depth + z]
            for number in range(3, 6):
                state[number][z] = state[number][z] + load
        advance(state, near, emit, state if step == 1 else None)
    axial = jnp.concatenate(
        [strain_ref[step * 6 * cells_row : (step * 6 + 2) * cells_row, :] for step in range(3)], axis=0
    )
    axial = jnp.concatenate(pieces(axial), axis=0).astype(BF16)
    rows_down = iota((cells_row, LANES), 0)
    slots_down = packed_iota(LANES, 2)
    for block in range(slot_ref.shape[0]):
        lanes = slice(block * LANES, (block + 1) * LANES)
        if block % 2 == 0:
            both = sum_thirds(times(axial, cover_ref[:, block * LANES : (block + 2) * LANES]))
        windows = both[:, :LANES] if block % 2 == 0 else both[:, LANES:]
        at_row = rows_down == row_ref[block : block + 1, :]
        weight_x, weight_y = weight_ref[0:1, lanes], weight_ref[1:2, lanes]
        sums = []
        for step in range(3):
            base = 2 * step * cells_row
            axial_sum = (
                weight_x * windows[base : base + cells_row]
                + weight_y * windows[base + cells_row : base + 2 * cells_row]
            )
            sums.append(jnp.sum(jnp.where(at_row, axial_sum, 0.0), axis=0, keepdims=True))
        sums.append(channel_ref[block : block + 1, :].astype(F32))
        values = jnp.concatenate(sums + sums, axis=0)
        in_slot = slots_down == packed_rows(slot_ref[block : block + 1, :], LANES)
        for third, piece in enumerate(pieces(values)):
            tile = jnp.concatenate([piece, piece], axis=0).astype(BF16)
            spread_ref[third * LANES : (third + 1) * LANES, lanes] = jnp.where(
                in_slot, jnp.concatenate([tile] * (LANES // 16), axis=0), jnp.zeros((), BF16)
            )
    out_ref[...] = sum_thirds(times_turned(spread_ref[...], place_ref[...]))


def owner_body(arrived_ref, observed_ref, residual_ref, reply_ref, values_ref, place_ref, held_ref):
    groups = arrived_ref.shape[0] // 4
    parts = observed_ref.shape[1] // LANES
    down = packed_iota(LANES)
    part_down = iota((parts, LANES), 0)
    nothing = jnp.zeros((parts, LANES), F32)
    numbers = [arrived_ref[4 * s + 3 : 4 * s + 4, :].astype(I32) for s in range(groups)]
    for s in range(groups):
        lanes = slice(s * LANES, (s + 1) * LANES)
        place_ref[:, lanes] = jnp.where(
            down == packed_rows(numbers[s] & (LANES - 1), LANES), jnp.ones((), BF16), jnp.zeros((), BF16)
        )
        at_part = part_down == (numbers[s] >> 7)
        thirds = pieces(arrived_ref[4 * s : 4 * s + 3, :])
        stack = []
        for third in thirds:
            for step in range(3):
                stack.append(jnp.where(at_part, third[step : step + 1, :], 0.0))
        stack.append(nothing)
        values_ref[:, lanes] = jnp.concatenate(stack, axis=0).astype(BF16)
    rows = 3 * parts
    sums = sum_thirds(times_turned(values_ref[...], place_ref[...])[: 3 * rows])
    for step in range(3):
        for part in range(parts):
            at = step * parts + part
            held_ref[at : at + 1, :] = observed_ref[step : step + 1, part * LANES : (part + 1) * LANES]
    held_ref[rows:, :] = nothing
    held_ref[0:rows, :] = sums - held_ref[0:rows, :]
    for step in range(3):
        for part in range(parts):
            at = step * parts + part
            residual_ref[step : step + 1, part * LANES : (part + 1) * LANES] = held_ref[at : at + 1, :]
    residual = jnp.concatenate(two_pieces(held_ref[...]), axis=0).astype(BF16)
    for s in range(groups):
        if s % 2 == 0:
            both = sum_halves(times(residual, place_ref[:, s * LANES : (s + 2) * LANES]))
        found = both[:, :LANES] if s % 2 == 0 else both[:, LANES:]
        at_part = part_down == (numbers[s] >> 7)
        for step in range(3):
            reply_ref[4 * s + step : 4 * s + step + 1, :] = jnp.sum(
                jnp.where(at_part, found[step * parts : (step + 1) * parts], 0.0), axis=0, keepdims=True
            )
        reply_ref[4 * s + 3 : 4 * s + 4, :] = jnp.zeros((1, LANES), F32)


def reached():
    return [(turn, distance) for turn in range(3) for distance in range(RIM - turn)]


def load_body(
    arrived_ref,
    slot_ref,
    row_ref,
    weight_ref,
    cover_ref,
    place_ref,
    load_ref,
    high_ref,
    low_ref,
    out_ref,
    spread_ref,
    side_ref,
    held_ref,
    sent_sides,
):
    cells_row = load_ref.shape[0] // 6
    stack_rows = load_ref.shape[0]
    arrived = jnp.concatenate(two_pieces(arrived_ref[...]), axis=0).astype(BF16)
    slots_down = iota((LANES, LANES), 0) >> 2
    rows_down = packed_iota(cells_row)
    for block in range(slot_ref.shape[0]):
        lanes = slice(block * LANES, (block + 1) * LANES)
        if block % 2 == 0:
            both = sum_halves(times(arrived, place_ref[:, block * LANES : (block + 2) * LANES]))
        found = both[:, :LANES] if block % 2 == 0 else both[:, LANES:]
        found = jnp.where(slots_down == slot_ref[block : block + 1, :], found, 0.0)
        folded = found[0:8]
        for part in range(1, LANES // 8):
            folded = folded + found[8 * part : 8 * part + 8]
        folded = folded + pltpu.roll(folded, 4, 0)
        at_row = rows_down == packed_rows(row_ref[block : block + 1, :], cells_row)
        for turn in range(3):
            back = folded[2 - turn : 3 - turn, :]
            for part in range(2):
                for half, piece in enumerate(two_pieces(weight_ref[part : part + 1, lanes] * back)):
                    base = half * stack_rows + (2 * turn + part) * cells_row
                    spread_ref[base : base + cells_row, lanes] = jnp.where(
                        at_row, packed_rows(piece, cells_row), jnp.zeros((), BF16)
                    )
    cover = jnp.concatenate([cover_ref[0:16, :], cover_ref[LANES - 16 :, :]], axis=0)
    edges = times_turned(cover, spread_ref[0:stack_rows, :]) + times_turned(cover, spread_ref[stack_rows:, :])
    side_ref[...] = jnp.zeros_like(side_ref)
    for side, base in ((0, 0), (1, 32 - RIM)):
        for column in range(RIM):
            lanes = slice(column * LANES, column * LANES + stack_rows)
            side_ref[side, 0:1, lanes] = edges[base + column : base + column + 1, :]
    sides = start_sides(side_ref, out_ref, sent_sides)
    load = sum_halves(times_turned(spread_ref[...], cover_ref[...]))
    load_ref[...] = load
    held_ref[0:stack_rows, :] = load
    count = stack_rows // (3 * TILE_X)
    for at, (turn, distance) in enumerate(reached()):
        rows = slice(at * count, (at + 1) * count)
        first = turn * count * TILE_X
        low_ref[rows, :] = held_ref[pl.ds(first + distance, count, stride=TILE_X), :]
        high_ref[rows, :] = held_ref[pl.ds(first + TILE_X - 1 - distance, count, stride=TILE_X), :]
    wait_sides(sides)


def adjoint_body(
    load_ref,
    higher_ref,
    lower_ref,
    recv_ref,
    strain_ref,
    medium_ref,
    residual_ref,
    gradient_ref,
    residual_out_ref,
    first_ref,
    later_ref,
    velocity_ref,
    state_ref,
    near_ref,
    turn_ref,
    sides_ref,
):
    depth = medium_ref.shape[0] // 3
    rims = rim_rows(recv_ref, turn_ref)
    sides_ref[...] = jnp.zeros_like(sides_ref)
    count = load_ref.shape[0] // (3 * TILE_X)
    for at, (turn, distance) in enumerate(reached()):
        rows = slice(at * count, (at + 1) * count)
        first = turn * count * TILE_X
        sides_ref[0, pl.ds(first + distance, count, stride=TILE_X), :] = higher_ref[rows, :]
        sides_ref[1, pl.ds(first + TILE_X - 1 - distance, count, stride=TILE_X), :] = lower_ref[rows, :]
    lay_planes(first_ref, later_ref, 0, load_ref, sides_ref.at[0], sides_ref.at[1])
    lay_planes(first_ref, later_ref, LANES, *rims)
    for plane in range(3 * depth):
        near_ref[plane] = narrowed(medium_ref[plane])
    gradient_ref[...] = jnp.zeros_like(gradient_ref)
    residual_out_ref[...] = residual_ref[...]
    state, near, medium = (
        fields_of(state_ref, 9, depth),
        fields_of(near_ref, 3, depth),
        fields_of(medium_ref, 3, depth),
    )

    def add_terms(turn, z, strains):
        dilation, dilation_back, doubled, product = None, None, None, None
        for number, strain in enumerate(strains):
            base = (((2 - turn) * 6 + number) * depth + z) * TILE_X
            forward = strain_ref[base : base + TILE_X, :]
            if number < 3:
                dilation = forward if dilation is None else dilation + forward
            if strain is None:
                continue
            back = strain[0:TILE_X, 0:LANES]
            term = forward * back
            if number < 3:
                dilation_back = back if dilation_back is None else dilation_back + back
                doubled = term if doubled is None else doubled + term
            else:
                product = term if product is None else product + term
        for part, term in enumerate((dilation * dilation_back, 2.0 * doubled + product)):
            base = (part * depth + z) * TILE_X
            gradient_ref[base : base + TILE_X, :] = gradient_ref[base : base + TILE_X, :] + term

    loads, velocity = fields_of(first_ref, 2, depth), fields_of(velocity_ref, 2, depth)
    for z in range(depth):
        scale = STEP * medium[2][z]
        velocity[0][z] = scale * ahead_x(loads[0][z])
        velocity[1][z] = scale * ahead_y(loads[1][z])
        state[0][z] = narrowed(velocity[0][z])
        state[1][z] = narrowed(velocity[1][z])
        state[2][z] = jnp.zeros((SPAN_NEAR, SPAN_Y), F32)
    for z in range(depth):
        along_x, along_y = velocity[0][z], velocity[1][z]
        strain_x, strain_y = behind_x(along_x), behind_y(along_y)
        sheared = (
            ahead_y(along_x) + ahead_x(along_y),
            ahead_z(velocity[0], z),
            ahead_z(velocity[1], z),
        )
        add_terms(0, z, (strain_x, strain_y, None) + sheared)
        dilated = medium[0][z] * (strain_x + strain_y)
        shear = medium[1][z]
        state[3][z] = narrowed(loads[0][z] + STEP * (dilated + 2.0 * shear * strain_x))
        state[4][z] = narrowed(loads[1][z] + STEP * (dilated + 2.0 * shear * strain_y))
        state[5][z] = narrowed(STEP * dilated)
        for number, strain in enumerate(sheared):
            state[6 + number][z] = narrowed(STEP * shear * strain)
    for turn in (1, 2):
        for part in range(2):
            for z in range(depth):
                load = later_ref[(2 * (turn - 1) + part) * depth + z]
                state[3 + part][z] = state[3 + part][z] + load
        advance(state, near, functools.partial(add_terms, turn), state if turn == 1 else None)


def shards(
    initial_state,
    lame_lambda,
    shear_modulus,
    buoyancy,
    source_cells,
    source_wavelet,
    segment_start,
    segment_weight,
    partial_owner,
    partial_channel,
    observed_data,
):
    depth, rows_x, cols_y = lame_lambda.shape
    part_count = segment_start.shape[0]
    count_x, count_y = lax.axis_size("gx"), lax.axis_size("gy")
    devices = count_x * count_y
    capacity = max(2, 2 * part_count // devices)
    slot_groups = devices * capacity // LANES
    blocks = part_count // LANES
    per_group = LANES // capacity
    cells_row = depth * rows_x
    both = ("gx", "gy")
    up = [(i, i + 1) for i in range(count_x - 1)]
    down = [(j, i) for i, j in up]
    shape = jax.ShapeDtypeStruct

    def exchange(chunks):
        return lax.all_to_all(chunks, both, split_axis=0, concat_axis=0, tiled=True)

    def to_owners(rows):
        chunks = rows.reshape(slot_groups, 4, per_group, capacity).transpose(0, 2, 1, 3)
        back = exchange(chunks.reshape(devices, 4, capacity)).reshape(slot_groups, per_group, 4, capacity)
        return back.transpose(0, 2, 1, 3).reshape(slot_groups * 4, LANES)

    trimmed = shape((14 * depth * RIM, cols_y), F32)
    fields, high, low, edges = call_kernel(
        pack_body,
        "pack_edges",
        [shape((14 * cells_row, cols_y), F32), trimmed, trimmed, shape((devices, 1, 2 * RIM * LANES), F32)],
        [
            pltpu.VMEM((14 * cells_row + SPARE, cols_y), F32),
            pltpu.VMEM(trimmed.shape, F32),
            pltpu.VMEM(trimmed.shape, F32),
            pltpu.VMEM((2, 1, 2 * RIM * LANES), F32),
            pltpu.VMEM((1, source_cells.shape[0]), I32),
            pltpu.VMEM(source_wavelet.shape, F32),
            pltpu.SemaphoreType.DMA((6,)),
            pltpu.SemaphoreType.DMA((3,)),
            pltpu.SemaphoreType.DMA((6,)),
        ],
        *[values.reshape(-1, cols_y) for values in (initial_state, lame_lambda, shear_modulus, buoyancy)],
        source_cells.reshape(1, -1),
        source_wavelet,
        place=pl.ANY,
        place_out=pl.ANY,
        room=60 * 1024 * 1024,
    )
    lower = lax.ppermute(high, "gx", up)
    higher = lax.ppermute(low, "gx", down)
    rims = exchange(edges)
    channels = partial_channel.reshape(blocks, LANES)
    slot, row, cover, place = call_kernel(
        functools.partial(slots_body, capacity, devices, cols_y),
        "segment_slots",
        [
            shape((blocks, LANES), I32),
            shape((blocks, LANES), I32),
            shape((cols_y, part_count), BF16),
            shape((LANES, part_count), BF16),
        ],
        [pltpu.VMEM((blocks, LANES), F32)],
        partial_owner.reshape(blocks, LANES),
        segment_start.reshape(blocks, LANES),
    )
    partials, strains, medium = call_kernel(
        forward_body,
        "forward_run",
        [
            shape((slot_groups * 4, LANES), F32),
            shape((18 * cells_row, cols_y), F32),
            shape((3 * depth, SPAN_X, SPAN_Y), F32),
        ],
        [
            pltpu.VMEM((12 * depth, SPAN_X, SPAN_Y), F32),
            pltpu.VMEM((2 * depth, SPAN_NEAR, SPAN_Y), F32),
            pltpu.VMEM((9 * depth, SPAN_NEAR, SPAN_Y), F32),
            pltpu.VMEM((3 * depth, SPAN_NEAR, SPAN_Y), F32),
            pltpu.VMEM((3, LANES, 2 * LANES), F32),
            pltpu.VMEM((2, 14 * cells_row + SPARE, cols_y), F32),
            pltpu.VMEM((3 * LANES, part_count), BF16),
        ],
        fields,
        lower,
        higher,
        rims,
        slot,
        row,
        segment_weight,
        channels,
        cover,
        place,
    )
    parts = observed_data.shape[1] // LANES
    residuals, reply = call_kernel(
        owner_body,
        "channel_sums",
        [shape(observed_data.shape, F32), shape((slot_groups * 4, LANES), F32)],
        [
            pltpu.VMEM((10 * parts, slot_groups * LANES), BF16),
            pltpu.VMEM((LANES, slot_groups * LANES), BF16),
            pltpu.VMEM((4 * parts, LANES), F32),
        ],
        to_owners(partials),
        observed_data,
    )
    reach = shape((len(reached()) * 2 * depth, cols_y), F32)
    loads, load_high, load_low, load_edges = call_kernel(
        load_body,
        "segment_loads",
        [shape((6 * cells_row, cols_y), F32), reach, reach, shape((devices, 1, RIM * LANES), F32)],
        [
            pltpu.VMEM((12 * cells_row, part_count), BF16),
            pltpu.VMEM((2, 1, RIM * LANES), F32),
            pltpu.VMEM((6 * cells_row + SPARE, cols_y), F32),
            pltpu.SemaphoreType.DMA((6,)),
        ],
        to_owners(reply),
        slot,
        row,
        segment_weight,
        cover,
        place,
        place_out=(pltpu.VMEM, pltpu.VMEM, pltpu.VMEM, pl.ANY),
    )
    load_lower = lax.ppermute(load_high, "gx", up)
    load_higher = lax.ppermute(load_low, "gx", down)
    load_rims = exchange(load_edges)
    gradients, residuals = call_kernel(
        adjoint_body,
        "adjoint_run",
        [shape((2 * cells_row, cols_y), F32), shape(observed_data.shape, F32)],
        [
            pltpu.VMEM((2 * depth, SPAN_X, SPAN_Y), F32),
            pltpu.VMEM((4 * depth, SPAN_NEAR, SPAN_Y), F32),
            pltpu.VMEM((2 * depth, SPAN_X, SPAN_Y), F32),
            pltpu.VMEM((9 * depth, SPAN_NEAR, SPAN_Y), F32),
            pltpu.VMEM((3 * depth, SPAN_NEAR, SPAN_Y), F32),
            pltpu.VMEM((3, LANES, LANES), F32),
            pltpu.VMEM((2, 6 * cells_row + SPARE, cols_y), F32),
        ],
        loads,
        load_higher,
        load_lower,
        load_rims,
        strains,
        medium,
        residuals,
    )
    return (residuals, gradients.reshape(2, depth, rows_x, cols_y))


def solution(mesh):
    in_specs = (
        P(None, None, "gx", "gy"),
        P(None, "gx", "gy"),
        P(None, "gx", "gy"),
        P(None, "gx", "gy"),
        P(("gx", "gy")),
        P(None, ("gx", "gy")),
        P(("gx", "gy")),
        P(None, ("gx", "gy")),
        P(("gx", "gy"), None),
        P(("gx", "gy")),
        P(None, ("gx", "gy")),
    )
    out_specs = (P(None, ("gx", "gy")), P(None, None, "gx", "gy"))
    return jax.shard_map(shards, mesh=mesh, in_specs=in_specs, out_specs=out_specs, check_vma=False)
```

```python
import functools

import jax
import jax.numpy as jnp
from jax import lax
from jax.experimental import pallas as pl
from jax.experimental.pallas import tpu as pltpu
from jax.sharding import PartitionSpec as P

GAUGE = 8
STEP = 0.25
RIM = 3
LANES = 128
TILE_X = 4
SPARE = 8
SPAN_X = 16
SPAN_NEAR = 8
SPAN_Y = 256
F32, BF16, I32 = jnp.float32, jnp.bfloat16, jnp.int32
NEAR = tuple((dx, dy) for dx in (-1, 0, 1) for dy in (-1, 0, 1))


def call_kernel(
    body, name, outs, scratch, *args, place=pltpu.VMEM, place_out=pltpu.VMEM, room=24 * 1024 * 1024
):
    spaces = place_out if isinstance(place_out, tuple) else (place_out,) * len(outs)
    return pl.pallas_call(
        body,
        name=name,
        out_shape=outs,
        in_specs=[pl.BlockSpec(memory_space=place)] * len(args),
        out_specs=[pl.BlockSpec(memory_space=space) for space in spaces],
        scratch_shapes=scratch,
        compiler_params=pltpu.CompilerParams(vmem_limit_bytes=room),
    )(*args)


def pieces(values):
    high = values.astype(BF16).astype(F32)
    rest = values - high
    middle = rest.astype(BF16).astype(F32)
    return high, middle, rest - middle


def iota(shape, dim):
    return lax.broadcasted_iota(I32, shape, dim)


def times(left, right):
    return lax.dot_general(left, right, (((1,), (0,)), ((), ())), preferred_element_type=F32)


def times_turned(left, right):
    return lax.dot_general(left, right, (((1,), (1,)), ((), ())), preferred_element_type=F32)


def packed_rows(row, height):
    tile = jnp.broadcast_to(row.astype(F32), (16, row.shape[1])).astype(BF16)
    return jnp.concatenate([tile] * (height // 16), axis=0) if height > 16 else tile


def packed_iota(height, shift=0):
    return (iota((height, LANES), 0) >> shift).astype(F32).astype(BF16)


def two_pieces(values):
    high = values.astype(BF16).astype(F32)
    return high, values - high


def sum_halves(values):
    half = values.shape[0] // 2
    return values[:half] + values[half:]


def sum_thirds(values):
    third = values.shape[0] // 3
    return values[:third] + values[third : 2 * third] + values[2 * third :]


def neighbour(dx, dy):
    count_x, count_y = lax.axis_size("gx"), lax.axis_size("gy")
    at_x, at_y = lax.axis_index("gx") + dx, lax.axis_index("gy") + dy
    inside = (at_x >= 0) & (at_x < count_x) & (at_y >= 0) & (at_y < count_y)
    return jnp.where(inside, at_x * count_y + at_y, 0), inside


def odd_column():
    return lax.axis_index("gy") % 2 == 1


def opposed(rows_up):
    count_x, count_y = lax.axis_size("gx"), lax.axis_size("gy")
    pairs = []
    for x in range(count_x):
        for y in range(count_y):
            there = x + 1 if y % 2 == rows_up else x - 1
            if 0 <= there < count_x:
                pairs.append((x * count_y + y, there * count_y + y))
    return pairs


def edge_columns(rows, side_ref):
    width = rows.shape[0]
    turned = rows.T
    for side, base in ((0, 0), (1, LANES - RIM)):
        for column in range(RIM):
            side_ref[side, 0:1, column * width : (column + 1) * width] = turned[base + column : base + column + 1, :]


def start_sides(side_ref, out_ref, sent):
    sides = []
    for number, (dx, dy) in enumerate((dx, dy) for dx, dy in NEAR if dy):
        index, inside = neighbour(dx, dy)
        source, target = side_ref.at[1 if dy > 0 else 0], out_ref.at[index]
        sides.append((inside, pltpu.make_async_copy(source, target, sent.at[number])))
    for inside, copy in sides:
        pl.when(inside)(copy.start)
    return sides


def wait_sides(sides):
    for inside, copy in sides:
        pl.when(inside)(copy.wait)


def arrived_chunk(recv_ref, dx, dy):
    index, inside = neighbour(dx, dy)
    return jnp.where(inside, recv_ref[index], 0.0)


def rim_rows(recv_ref, turn_ref):
    width = turn_ref.shape[2]
    turn_ref[...] = jnp.zeros_like(turn_ref)
    for block, dx in enumerate((0, 1, -1)):
        for dy, first in ((1, 0), (-1, LANES - RIM)):
            chunk = arrived_chunk(recv_ref, dx, dy)
            for column in range(RIM):
                turn_ref[block, first + column : first + column + 1, :] = chunk[
                    :, column * width : (column + 1) * width
                ]
    return [turn_ref[block].T for block in range(3)]


def lay_planes(wide_ref, narrow_ref, lane, centre, higher, lower):
    row = iota((8, LANES), 0)
    wide = wide_ref.shape[0]
    lanes = slice(lane, lane + LANES)
    for plane in range(wide + narrow_ref.shape[0]):
        rows = slice(8 * (plane // 2), 8 * (plane // 2) + 8)
        mid, high, low = centre[rows], higher[rows], lower[rows]
        if plane % 2:
            mid = pltpu.roll(mid, TILE_X, 0)
        else:
            high, low = pltpu.roll(high, TILE_X, 0), pltpu.roll(low, TILE_X, 0)
        near = jnp.where(row < TILE_X, mid, high)
        if plane < wide:
            wide_ref[plane, 0:8, lanes] = near
            wide_ref[plane, 8:16, lanes] = jnp.where(row < TILE_X, 0.0, low)
        else:
            narrow_ref[plane - wide, :, lanes] = jnp.where(row < SPAN_NEAR - 2, near, low)


def narrowed(plane):
    row = iota((SPAN_NEAR, plane.shape[1]), 0)
    return jnp.where(row < SPAN_NEAR - 2, plane[:SPAN_NEAR], plane[SPAN_NEAR:])


def ahead_x(plane):
    return pltpu.roll(plane, plane.shape[0] - 1, 0) - plane


def behind_x(plane):
    return plane - pltpu.roll(plane, 1, 0)


def ahead_y(plane):
    return pltpu.roll(plane, SPAN_Y - 1, 1) - plane


def behind_y(plane):
    return plane - pltpu.roll(plane, 1, 1)


def ahead_z(planes, z):
    return planes[z + 1] - planes[z] if z + 1 < len(planes) else -planes[z]


def behind_z(planes, z):
    return planes[z] - planes[z - 1] if z else planes[z]


class Planes:
    def __init__(self, ref, first, depth):
        self.ref, self.first, self.depth = ref, first, depth

    def __len__(self):
        return self.depth

    def __getitem__(self, z):
        return self.ref[self.first + z]

    def __setitem__(self, z, plane):
        self.ref[self.first + z] = plane


def fields_of(ref, count, depth, first=0):
    return [Planes(ref, (first + number) * depth, depth) for number in range(count)]


def strain_rates(velocity, z):
    along_x, along_y, along_z = [field[z] for field in velocity]
    return (
        behind_x(along_x),
        behind_y(along_y),
        behind_z(velocity[2], z),
        ahead_y(along_x) + ahead_x(along_y),
        ahead_z(velocity[0], z) + ahead_x(along_z),
        ahead_z(velocity[1], z) + ahead_y(along_z),
    )


def new_stress(stress, strains, lame_lambda, shear_modulus, z):
    dilated = lame_lambda[z] * (strains[0] + strains[1] + strains[2])
    shear = shear_modulus[z]
    normal = [stress[n][z] + STEP * (dilated + 2.0 * shear * strains[n]) for n in range(3)]
    return normal + [stress[n][z] + STEP * shear * strains[n] for n in range(3, 6)]


def advance(state, medium, emit, target):
    velocity, stress = state[:3], state[3:]
    lame_lambda, shear_modulus, buoyancy = medium
    depth = len(buoyancy)
    wide = target is not None and target is not state
    for z in range(depth):
        scale = STEP * buoyancy[z]
        accel = (
            ahead_x(stress[0][z]) + behind_y(stress[3][z]) + behind_z(stress[4], z),
            behind_x(stress[3][z]) + ahead_y(stress[1][z]) + behind_z(stress[5], z),
            behind_x(stress[4][z]) + behind_y(stress[5][z]) + ahead_z(stress[2], z),
        )
        for number in range(3):
            moved = velocity[number][z] + scale * accel[number]
            velocity[number][z] = moved
            if wide:
                target[number][z] = narrowed(moved)
    for z in range(depth):
        strains = strain_rates(velocity, z)
        emit(z, strains)
        if target is not None:
            for number, plane in enumerate(new_stress(stress, strains, lame_lambda, shear_modulus, z)):
                target[3 + number][z] = narrowed(plane) if wide else plane


def pack_body(*refs):
    inputs, outputs, scratch = refs[:6], refs[6:10], refs[10:]
    fields_ref, first_ref, second_ref, side_ref, cells_ref, wavelet_ref, arrived, sent, sent_sides = scratch
    targets, at = [], 0
    for source in inputs[:4]:
        targets.append(fields_ref.at[at : at + source.shape[0]])
        at = at + source.shape[0]
    copies = [
        pltpu.make_async_copy(source, target, arrived.at[number])
        for number, (source, target) in enumerate(zip(inputs, targets + [cells_ref, wavelet_ref]))
    ]
    for copy in copies[4:] + copies[:4]:
        copy.start()
    copies[4].wait()
    copies[5].wait()
    cells_row = inputs[1].shape[0]
    cells = cells_ref[...]
    count = cells.shape[1]
    at_lane = iota((LANES, count), 0) == (cells & (LANES - 1))
    at_row = iota((cells_row, count), 0) == (cells >> (LANES.bit_length() - 1))
    stack = [
        jnp.where(at_row, third[step : step + 1, :], 0.0) for third in pieces(wavelet_ref[...]) for step in range(3)
    ]
    maps = sum_thirds(
        times_turned(jnp.concatenate(stack, axis=0).astype(BF16), jnp.where(at_lane, 1.0, 0.0).astype(BF16))
    )
    for copy in copies[:4]:
        copy.wait()
    total = at + 2 * cells_row
    fields_ref[at:total, :] = maps[cells_row:]
    for number in range(3, 6):
        rows = slice(number * cells_row, (number + 1) * cells_row)
        fields_ref[rows, :] = fields_ref[rows, :] + maps[:cells_row]
    rows = fields_ref[0:total, :]
    spare = 2 * LANES - total
    edge_columns(jnp.concatenate([rows, jnp.zeros((spare, LANES), F32)], axis=0), side_ref)
    sides = start_sides(side_ref, outputs[3], sent_sides)
    height = total // TILE_X
    odd = odd_column()
    for distance in range(RIM):
        rows = slice(distance * height, (distance + 1) * height)
        low = fields_ref[pl.ds(distance, height, stride=TILE_X), :]
        high = fields_ref[pl.ds(distance + TILE_X - RIM, height, stride=TILE_X), :]
        first_ref[rows, :] = jnp.where(odd, low, high)
        second_ref[rows, :] = jnp.where(odd, high, low)
    writes = [
        pltpu.make_async_copy(source, target, sent.at[number])
        for number, (source, target) in enumerate(zip((fields_ref.at[0:total], first_ref, second_ref), outputs))
    ]
    for copy in writes:
        copy.start()
    for copy in writes:
        copy.wait()
    wait_sides(sides)


def slots_body(capacity, devices, cols_y, owner_ref, start_ref, slot_ref, row_ref, cover_ref, place_ref, rank_ref):
    blocks = owner_ref.shape[0]
    group = 32
    before = jnp.where(iota((LANES, 2 * LANES), 0) < iota((LANES, 2 * LANES), 1), 1.0, 0.0).astype(BF16)
    rank_ref[...] = jnp.zeros_like(rank_ref)

    def count_group(number, carry):
        names = iota((group, LANES), 0) + number * group
        hot = [names == owner_ref[b : b + 1, :] for b in range(blocks)]
        marks = jnp.concatenate([jnp.where(h, 1.0, 0.0) for h in hot], axis=0).astype(BF16)
        counts = times(marks, before)
        total = jnp.zeros((group, LANES), F32)
        for b in range(blocks):
            part = counts[b * group : (b + 1) * group]
            rank_ref[b : b + 1, :] = rank_ref[b : b + 1, :] + jnp.sum(
                jnp.where(hot[b], part[:, :LANES] + total, 0.0), axis=0, keepdims=True
            )
            total = total + part[:, LANES:]
        return carry

    if devices == group:
        count_group(0, 0)
    else:
        lax.fori_loop(0, devices // group, count_group, 0)
    slot = owner_ref[...] * capacity + rank_ref[...].astype(I32)
    slot_ref[...] = slot >> 7
    low = slot & (LANES - 1)
    span = cols_y - GAUGE + 1
    start = start_ref[...]
    row = ((start.astype(F32) + 0.5) * (1.0 / span)).astype(I32)
    row_ref[...] = row
    first = start - row * span
    down = iota((LANES, LANES), 0)
    for b in range(blocks):
        lanes = slice(b * LANES, (b + 1) * LANES)
        offset = down - first[b : b + 1, :]
        cover_ref[:, lanes] = jnp.where((offset >= 0) & (offset < GAUGE), 1.0, 0.0).astype(BF16)
        place_ref[:, lanes] = jnp.where(down == low[b : b + 1, :], 1.0, 0.0).astype(BF16)


def forward_body(
    fields_ref,
    first_recv_ref,
    second_recv_ref,
    recv_ref,
    slot_ref,
    row_ref,
    weight_ref,
    channel_ref,
    cover_ref,
    place_ref,
    out_ref,
    strain_ref,
    medium_ref,
    wide_ref,
    source_ref,
    state_ref,
    near_ref,
    turn_ref,
    sides_ref,
    spread_ref,
):
    depth = medium_ref.shape[0] // 3
    cells_row = depth * TILE_X
    rims = rim_rows(recv_ref, turn_ref)
    height = fields_ref.shape[0] // TILE_X
    sides_ref[...] = jnp.zeros_like(sides_ref)
    odd = odd_column()
    for x in range(RIM):
        slab = slice(x * height, (x + 1) * height)
        one, two = first_recv_ref[slab, :], second_recv_ref[slab, :]
        sides_ref[0, pl.ds(x, height, stride=TILE_X), :] = jnp.where(odd, one, two)
        sides_ref[1, pl.ds(x + TILE_X - RIM, height, stride=TILE_X), :] = jnp.where(odd, two, one)
    lay_planes(wide_ref, source_ref, 0, fields_ref, sides_ref.at[0], sides_ref.at[1])
    lay_planes(wide_ref, source_ref, LANES, *rims)
    first = 9 * depth
    medium_ref[...] = wide_ref[first:]
    for plane in range(3 * depth):
        near_ref[plane] = narrowed(wide_ref[first + plane])
    state, near = fields_of(state_ref, 9, depth), fields_of(near_ref, 3, depth)
    for step in range(3):

        def emit(z, strains, step=step):
            for number, strain in enumerate(strains):
                base = ((step * 6 + number) * depth + z) * TILE_X
                strain_ref[base : base + TILE_X, :] = strain[0:TILE_X, 0:LANES]

        if step == 0:
            advance(fields_of(wide_ref, 9, depth), fields_of(wide_ref, 3, depth, 9), emit, state)
            continue
        for z in range(depth):
            load = source_ref[(step - 1) * depth + z]
            for number in range(3, 6):
                state[number][z] = state[number][z] + load
        advance(state, near, emit, state if step == 1 else None)
    axial = jnp.concatenate(
        [strain_ref[step * 6 * cells_row : (step * 6 + 2) * cells_row, :] for step in range(3)], axis=0
    )
    axial = jnp.concatenate(pieces(axial), axis=0).astype(BF16)
    rows_down = iota((cells_row, LANES), 0)
    slots_down = packed_iota(LANES, 2)
    for block in range(slot_ref.shape[0]):
        lanes = slice(block * LANES, (block + 1) * LANES)
        if block % 2 == 0:
            both = sum_thirds(times(axial, cover_ref[:, block * LANES : (block + 2) * LANES]))
        windows = both[:, :LANES] if block % 2 == 0 else both[:, LANES:]
        at_row = rows_down == row_ref[block : block + 1, :]
        weight_x, weight_y = weight_ref[0:1, lanes], weight_ref[1:2, lanes]
        sums = []
        for step in range(3):
            base = 2 * step * cells_row
            axial_sum = (
                weight_x * windows[base : base + cells_row]
                + weight_y * windows[base + cells_row : base + 2 * cells_row]
            )
            sums.append(jnp.sum(jnp.where(at_row, axial_sum, 0.0), axis=0, keepdims=True))
        sums.append(channel_ref[block : block + 1, :].astype(F32))
        values = jnp.concatenate(sums + sums, axis=0)
        in_slot = slots_down == packed_rows(slot_ref[block : block + 1, :], LANES)
        for third, piece in enumerate(pieces(values)):
            tile = jnp.concatenate([piece, piece], axis=0).astype(BF16)
            spread_ref[third * LANES : (third + 1) * LANES, lanes] = jnp.where(
                in_slot, jnp.concatenate([tile] * (LANES // 16), axis=0), jnp.zeros((), BF16)
            )
    out_ref[...] = sum_thirds(times_turned(spread_ref[...], place_ref[...]))


def owner_body(arrived_ref, observed_ref, residual_ref, reply_ref, values_ref, place_ref, held_ref):
    groups = arrived_ref.shape[0] // 4
    parts = observed_ref.shape[1] // LANES
    down = packed_iota(LANES)
    part_down = iota((parts, LANES), 0)
    nothing = jnp.zeros((parts, LANES), F32)
    numbers = [arrived_ref[4 * s + 3 : 4 * s + 4, :].astype(I32) for s in range(groups)]
    for s in range(groups):
        lanes = slice(s * LANES, (s + 1) * LANES)
        place_ref[:, lanes] = jnp.where(
            down == packed_rows(numbers[s] & (LANES - 1), LANES), jnp.ones((), BF16), jnp.zeros((), BF16)
        )
        at_part = part_down == (numbers[s] >> 7)
        thirds = pieces(arrived_ref[4 * s : 4 * s + 3, :])
        stack = []
        for third in thirds:
            for step in range(3):
                stack.append(jnp.where(at_part, third[step : step + 1, :], 0.0))
        stack.append(nothing)
        values_ref[:, lanes] = jnp.concatenate(stack, axis=0).astype(BF16)
    rows = 3 * parts
    sums = sum_thirds(times_turned(values_ref[...], place_ref[...])[: 3 * rows])
    for step in range(3):
        for part in range(parts):
            at = step * parts + part
            held_ref[at : at + 1, :] = observed_ref[step : step + 1, part * LANES : (part + 1) * LANES]
    held_ref[rows:, :] = nothing
    held_ref[0:rows, :] = sums - held_ref[0:rows, :]
    for step in range(3):
        for part in range(parts):
            at = step * parts + part
            residual_ref[step : step + 1, part * LANES : (part + 1) * LANES] = held_ref[at : at + 1, :]
    residual = jnp.concatenate(two_pieces(held_ref[...]), axis=0).astype(BF16)
    for s in range(groups):
        if s % 2 == 0:
            both = sum_halves(times(residual, place_ref[:, s * LANES : (s + 2) * LANES]))
        found = both[:, :LANES] if s % 2 == 0 else both[:, LANES:]
        at_part = part_down == (numbers[s] >> 7)
        for step in range(3):
            reply_ref[4 * s + step : 4 * s + step + 1, :] = jnp.sum(
                jnp.where(at_part, found[step * parts : (step + 1) * parts], 0.0), axis=0, keepdims=True
            )
        reply_ref[4 * s + 3 : 4 * s + 4, :] = jnp.zeros((1, LANES), F32)


def reached():
    return [(turn, distance) for turn in range(3) for distance in range(RIM - turn)]


def load_body(
    arrived_ref,
    slot_ref,
    row_ref,
    weight_ref,
    cover_ref,
    place_ref,
    load_ref,
    first_ref,
    second_ref,
    out_ref,
    spread_ref,
    side_ref,
    held_ref,
    sent_sides,
):
    cells_row = load_ref.shape[0] // 6
    stack_rows = load_ref.shape[0]
    arrived = jnp.concatenate(two_pieces(arrived_ref[...]), axis=0).astype(BF16)
    slots_down = iota((LANES, LANES), 0) >> 2
    rows_down = packed_iota(cells_row)
    for block in range(slot_ref.shape[0]):
        lanes = slice(block * LANES, (block + 1) * LANES)
        if block % 2 == 0:
            both = sum_halves(times(arrived, place_ref[:, block * LANES : (block + 2) * LANES]))
        found = both[:, :LANES] if block % 2 == 0 else both[:, LANES:]
        found = jnp.where(slots_down == slot_ref[block : block + 1, :], found, 0.0)
        folded = found[0:8]
        for part in range(1, LANES // 8):
            folded = folded + found[8 * part : 8 * part + 8]
        folded = folded + pltpu.roll(folded, 4, 0)
        at_row = rows_down == packed_rows(row_ref[block : block + 1, :], cells_row)
        for turn in range(3):
            back = folded[2 - turn : 3 - turn, :]
            for part in range(2):
                for half, piece in enumerate(two_pieces(weight_ref[part : part + 1, lanes] * back)):
                    base = half * stack_rows + (2 * turn + part) * cells_row
                    spread_ref[base : base + cells_row, lanes] = jnp.where(
                        at_row, packed_rows(piece, cells_row), jnp.zeros((), BF16)
                    )
    cover = jnp.concatenate([cover_ref[0:16, :], cover_ref[LANES - 16 :, :]], axis=0)
    edges = times_turned(cover, spread_ref[0:stack_rows, :]) + times_turned(cover, spread_ref[stack_rows:, :])
    side_ref[...] = jnp.zeros_like(side_ref)
    for side, base in ((0, 0), (1, 32 - RIM)):
        for column in range(RIM):
            lanes = slice(column * LANES, column * LANES + stack_rows)
            side_ref[side, 0:1, lanes] = edges[base + column : base + column + 1, :]
    sides = start_sides(side_ref, out_ref, sent_sides)
    load = sum_halves(times_turned(spread_ref[...], cover_ref[...]))
    load_ref[...] = load
    held_ref[0:stack_rows, :] = load
    count = stack_rows // (3 * TILE_X)
    odd = odd_column()
    for at, (turn, distance) in enumerate(reached()):
        rows = slice(at * count, (at + 1) * count)
        first = turn * count * TILE_X
        low = held_ref[pl.ds(first + distance, count, stride=TILE_X), :]
        high = held_ref[pl.ds(first + TILE_X - 1 - distance, count, stride=TILE_X), :]
        first_ref[rows, :] = jnp.where(odd, high, low)
        second_ref[rows, :] = jnp.where(odd, low, high)
    wait_sides(sides)


def adjoint_body(
    load_ref,
    first_recv_ref,
    second_recv_ref,
    recv_ref,
    strain_ref,
    medium_ref,
    residual_ref,
    gradient_ref,
    residual_out_ref,
    first_ref,
    later_ref,
    velocity_ref,
    state_ref,
    near_ref,
    turn_ref,
    sides_ref,
):
    depth = medium_ref.shape[0] // 3
    rims = rim_rows(recv_ref, turn_ref)
    sides_ref[...] = jnp.zeros_like(sides_ref)
    count = load_ref.shape[0] // (3 * TILE_X)
    odd = odd_column()
    for at, (turn, distance) in enumerate(reached()):
        rows = slice(at * count, (at + 1) * count)
        first = turn * count * TILE_X
        one, two = first_recv_ref[rows, :], second_recv_ref[rows, :]
        sides_ref[0, pl.ds(first + distance, count, stride=TILE_X), :] = jnp.where(odd, two, one)
        sides_ref[1, pl.ds(first + TILE_X - 1 - distance, count, stride=TILE_X), :] = jnp.where(odd, one, two)
    lay_planes(first_ref, later_ref, 0, load_ref, sides_ref.at[0], sides_ref.at[1])
    lay_planes(first_ref, later_ref, LANES, *rims)
    for plane in range(3 * depth):
        near_ref[plane] = narrowed(medium_ref[plane])
    gradient_ref[...] = jnp.zeros_like(gradient_ref)
    residual_out_ref[...] = residual_ref[...]
    state, near, medium = (
        fields_of(state_ref, 9, depth),
        fields_of(near_ref, 3, depth),
        fields_of(medium_ref, 3, depth),
    )

    def add_terms(turn, z, strains):
        dilation, dilation_back, doubled, product = None, None, None, None
        for number, strain in enumerate(strains):
            base = (((2 - turn) * 6 + number) * depth + z) * TILE_X
            forward = strain_ref[base : base + TILE_X, :]
            if number < 3:
                dilation = forward if dilation is None else dilation + forward
            if strain is None:
                continue
            back = strain[0:TILE_X, 0:LANES]
            term = forward * back
            if number < 3:
                dilation_back = back if dilation_back is None else dilation_back + back
                doubled = term if doubled is None else doubled + term
            else:
                product = term if product is None else product + term
        for part, term in enumerate((dilation * dilation_back, 2.0 * doubled + product)):
            base = (part * depth + z) * TILE_X
            gradient_ref[base : base + TILE_X, :] = gradient_ref[base : base + TILE_X, :] + term

    loads, velocity = fields_of(first_ref, 2, depth), fields_of(velocity_ref, 2, depth)
    for z in range(depth):
        scale = STEP * medium[2][z]
        velocity[0][z] = scale * ahead_x(loads[0][z])
        velocity[1][z] = scale * ahead_y(loads[1][z])
        state[0][z] = narrowed(velocity[0][z])
        state[1][z] = narrowed(velocity[1][z])
        state[2][z] = jnp.zeros((SPAN_NEAR, SPAN_Y), F32)
    for z in range(depth):
        along_x, along_y = velocity[0][z], velocity[1][z]
        strain_x, strain_y = behind_x(along_x), behind_y(along_y)
        sheared = (
            ahead_y(along_x) + ahead_x(along_y),
            ahead_z(velocity[0], z),
            ahead_z(velocity[1], z),
        )
        add_terms(0, z, (strain_x, strain_y, None) + sheared)
        dilated = medium[0][z] * (strain_x + strain_y)
        shear = medium[1][z]
        state[3][z] = narrowed(loads[0][z] + STEP * (dilated + 2.0 * shear * strain_x))
        state[4][z] = narrowed(loads[1][z] + STEP * (dilated + 2.0 * shear * strain_y))
        state[5][z] = narrowed(STEP * dilated)
        for number, strain in enumerate(sheared):
            state[6 + number][z] = narrowed(STEP * shear * strain)
    for turn in (1, 2):
        for part in range(2):
            for z in range(depth):
                load = later_ref[(2 * (turn - 1) + part) * depth + z]
                state[3 + part][z] = state[3 + part][z] + load
        advance(state, near, functools.partial(add_terms, turn), state if turn == 1 else None)


def shards(
    initial_state,
    lame_lambda,
    shear_modulus,
    buoyancy,
    source_cells,
    source_wavelet,
    segment_start,
    segment_weight,
    partial_owner,
    partial_channel,
    observed_data,
):
    depth, rows_x, cols_y = lame_lambda.shape
    part_count = segment_start.shape[0]
    count_x, count_y = lax.axis_size("gx"), lax.axis_size("gy")
    devices = count_x * count_y
    capacity = max(2, 2 * part_count // devices)
    slot_groups = devices * capacity // LANES
    blocks = part_count // LANES
    per_group = LANES // capacity
    cells_row = depth * rows_x
    both = ("gx", "gy")
    shape = jax.ShapeDtypeStruct

    def exchange(chunks):
        return lax.all_to_all(chunks, both, split_axis=0, concat_axis=0, tiled=True)

    def to_owners(rows):
        chunks = rows.reshape(slot_groups, 4, per_group, capacity).transpose(0, 2, 1, 3)
        back = exchange(chunks.reshape(devices, 4, capacity)).reshape(slot_groups, per_group, 4, capacity)
        return back.transpose(0, 2, 1, 3).reshape(slot_groups * 4, LANES)

    trimmed = shape((14 * depth * RIM, cols_y), F32)
    fields, first_slabs, second_slabs, edges = call_kernel(
        pack_body,
        "pack_edges",
        [shape((14 * cells_row, cols_y), F32), trimmed, trimmed, shape((devices, 1, 2 * RIM * LANES), F32)],
        [
            pltpu.VMEM((14 * cells_row + SPARE, cols_y), F32),
            pltpu.VMEM(trimmed.shape, F32),
            pltpu.VMEM(trimmed.shape, F32),
            pltpu.VMEM((2, 1, 2 * RIM * LANES), F32),
            pltpu.VMEM((1, source_cells.shape[0]), I32),
            pltpu.VMEM(source_wavelet.shape, F32),
            pltpu.SemaphoreType.DMA((6,)),
            pltpu.SemaphoreType.DMA((3,)),
            pltpu.SemaphoreType.DMA((6,)),
        ],
        *[values.reshape(-1, cols_y) for values in (initial_state, lame_lambda, shear_modulus, buoyancy)],
        source_cells.reshape(1, -1),
        source_wavelet,
        place=pl.ANY,
        place_out=pl.ANY,
        room=60 * 1024 * 1024,
    )
    first_fields = lax.ppermute(first_slabs, both, opposed(0))
    second_fields = lax.ppermute(second_slabs, both, opposed(1))
    rims = exchange(edges)
    channels = partial_channel.reshape(blocks, LANES)
    slot, row, cover, place = call_kernel(
        functools.partial(slots_body, capacity, devices, cols_y),
        "segment_slots",
        [
            shape((blocks, LANES), I32),
            shape((blocks, LANES), I32),
            shape((cols_y, part_count), BF16),
            shape((LANES, part_count), BF16),
        ],
        [pltpu.VMEM((blocks, LANES), F32)],
        partial_owner.reshape(blocks, LANES),
        segment_start.reshape(blocks, LANES),
    )
    partials, strains, medium = call_kernel(
        forward_body,
        "forward_run",
        [
            shape((slot_groups * 4, LANES), F32),
            shape((18 * cells_row, cols_y), F32),
            shape((3 * depth, SPAN_X, SPAN_Y), F32),
        ],
        [
            pltpu.VMEM((12 * depth, SPAN_X, SPAN_Y), F32),
            pltpu.VMEM((2 * depth, SPAN_NEAR, SPAN_Y), F32),
            pltpu.VMEM((9 * depth, SPAN_NEAR, SPAN_Y), F32),
            pltpu.VMEM((3 * depth, SPAN_NEAR, SPAN_Y), F32),
            pltpu.VMEM((3, LANES, 2 * LANES), F32),
            pltpu.VMEM((2, 14 * cells_row + SPARE, cols_y), F32),
            pltpu.VMEM((3 * LANES, part_count), BF16),
        ],
        fields,
        first_fields,
        second_fields,
        rims,
        slot,
        row,
        segment_weight,
        channels,
        cover,
        place,
    )
    parts = observed_data.shape[1] // LANES
    residuals, reply = call_kernel(
        owner_body,
        "channel_sums",
        [shape(observed_data.shape, F32), shape((slot_groups * 4, LANES), F32)],
        [
            pltpu.VMEM((10 * parts, slot_groups * LANES), BF16),
            pltpu.VMEM((LANES, slot_groups * LANES), BF16),
            pltpu.VMEM((4 * parts, LANES), F32),
        ],
        to_owners(partials),
        observed_data,
    )
    reach = shape((len(reached()) * 2 * depth, cols_y), F32)
    loads, first_loads, second_loads, load_edges = call_kernel(
        load_body,
        "segment_loads",
        [shape((6 * cells_row, cols_y), F32), reach, reach, shape((devices, 1, RIM * LANES), F32)],
        [
            pltpu.VMEM((12 * cells_row, part_count), BF16),
            pltpu.VMEM((2, 1, RIM * LANES), F32),
            pltpu.VMEM((6 * cells_row + SPARE, cols_y), F32),
            pltpu.SemaphoreType.DMA((6,)),
        ],
        to_owners(reply),
        slot,
        row,
        segment_weight,
        cover,
        place,
        place_out=(pltpu.VMEM, pltpu.VMEM, pltpu.VMEM, pl.ANY),
    )
    first_arrived = lax.ppermute(first_loads, both, opposed(1))
    second_arrived = lax.ppermute(second_loads, both, opposed(0))
    load_rims = exchange(load_edges)
    gradients, residuals = call_kernel(
        adjoint_body,
        "adjoint_run",
        [shape((2 * cells_row, cols_y), F32), shape(observed_data.shape, F32)],
        [
            pltpu.VMEM((2 * depth, SPAN_X, SPAN_Y), F32),
            pltpu.VMEM((4 * depth, SPAN_NEAR, SPAN_Y), F32),
            pltpu.VMEM((2 * depth, SPAN_X, SPAN_Y), F32),
            pltpu.VMEM((9 * depth, SPAN_NEAR, SPAN_Y), F32),
            pltpu.VMEM((3 * depth, SPAN_NEAR, SPAN_Y), F32),
            pltpu.VMEM((3, LANES, LANES), F32),
            pltpu.VMEM((2, 6 * cells_row + SPARE, cols_y), F32),
        ],
        loads,
        first_arrived,
        second_arrived,
        load_rims,
        strains,
        medium,
        residuals,
    )
    return (residuals, gradients.reshape(2, depth, rows_x, cols_y))


def solution(mesh):
    in_specs = (
        P(None, None, "gx", "gy"),
        P(None, "gx", "gy"),
        P(None, "gx", "gy"),
        P(None, "gx", "gy"),
        P(("gx", "gy")),
        P(None, ("gx", "gy")),
        P(("gx", "gy")),
        P(None, ("gx", "gy")),
        P(("gx", "gy"), None),
        P(("gx", "gy")),
        P(None, ("gx", "gy")),
    )
    out_specs = (P(None, ("gx", "gy")), P(None, None, "gx", "gy"))
    return jax.shard_map(shards, mesh=mesh, in_specs=in_specs, out_specs=out_specs, check_vma=False)
```

```python
import functools

import jax
import jax.numpy as jnp
from jax import lax
from jax.experimental import pallas as pl
from jax.experimental.pallas import tpu as pltpu
from jax.sharding import PartitionSpec as P

GAUGE = 8
STEP = 0.25
RIM = 3
LANES = 128
TILE_X = 4
SPARE = 8
SPAN_X = 16
SPAN_NEAR = 8
SPAN_Y = 256
F32, BF16, I32 = jnp.float32, jnp.bfloat16, jnp.int32
NEAR = tuple((dx, dy) for dx in (-1, 0, 1) for dy in (-1, 0, 1))


def call_kernel(
    body, name, outs, scratch, *args, place=pltpu.VMEM, place_out=pltpu.VMEM, room=24 * 1024 * 1024
):
    spaces = place_out if isinstance(place_out, tuple) else (place_out,) * len(outs)
    return pl.pallas_call(
        body,
        name=name,
        out_shape=outs,
        in_specs=[pl.BlockSpec(memory_space=place)] * len(args),
        out_specs=[pl.BlockSpec(memory_space=space) for space in spaces],
        scratch_shapes=scratch,
        compiler_params=pltpu.CompilerParams(vmem_limit_bytes=room),
    )(*args)


def pieces(values):
    high = values.astype(BF16).astype(F32)
    rest = values - high
    middle = rest.astype(BF16).astype(F32)
    return high, middle, rest - middle


def iota(shape, dim):
    return lax.broadcasted_iota(I32, shape, dim)


def times(left, right):
    return lax.dot_general(left, right, (((1,), (0,)), ((), ())), preferred_element_type=F32)


def times_turned(left, right):
    return lax.dot_general(left, right, (((1,), (1,)), ((), ())), preferred_element_type=F32)


def packed_rows(row, height):
    tile = jnp.broadcast_to(row.astype(F32), (16, row.shape[1])).astype(BF16)
    return jnp.concatenate([tile] * (height // 16), axis=0) if height > 16 else tile


def packed_iota(height, shift=0):
    return (iota((height, LANES), 0) >> shift).astype(F32).astype(BF16)


def two_pieces(values):
    high = values.astype(BF16).astype(F32)
    return high, values - high


def sum_halves(values):
    half = values.shape[0] // 2
    return values[:half] + values[half:]


def sum_thirds(values):
    third = values.shape[0] // 3
    return values[:third] + values[third : 2 * third] + values[2 * third :]


def neighbour(dx, dy):
    count_x, count_y = lax.axis_size("gx"), lax.axis_size("gy")
    at_x, at_y = lax.axis_index("gx") + dx, lax.axis_index("gy") + dy
    inside = (at_x >= 0) & (at_x < count_x) & (at_y >= 0) & (at_y < count_y)
    return jnp.where(inside, at_x * count_y + at_y, 0), inside


def edge_columns(rows, side_ref):
    width = rows.shape[0]
    turned = rows.T
    for side, base in ((0, 0), (1, LANES - RIM)):
        for column in range(RIM):
            side_ref[side, 0:1, column * width : (column + 1) * width] = turned[base + column : base + column + 1, :]


def start_sides(side_ref, out_ref, sent):
    sides = []
    for number, (dx, dy) in enumerate((dx, dy) for dx, dy in NEAR if dy):
        index, inside = neighbour(dx, dy)
        source, target = side_ref.at[1 if dy > 0 else 0], out_ref.at[index]
        sides.append((inside, pltpu.make_async_copy(source, target, sent.at[number])))
    for inside, copy in sides:
        pl.when(inside)(copy.start)
    return sides


def wait_sides(sides):
    for inside, copy in sides:
        pl.when(inside)(copy.wait)


def arrived_chunk(recv_ref, dx, dy):
    index, inside = neighbour(dx, dy)
    return jnp.where(inside, recv_ref[index], 0.0)


def rim_rows(recv_ref, turn_ref):
    width = turn_ref.shape[2]
    turn_ref[...] = jnp.zeros_like(turn_ref)
    for block, dx in enumerate((0, 1, -1)):
        for dy, first in ((1, 0), (-1, LANES - RIM)):
            chunk = arrived_chunk(recv_ref, dx, dy)
            for column in range(RIM):
                turn_ref[block, first + column : first + column + 1, :] = chunk[
                    :, column * width : (column + 1) * width
                ]
    return [turn_ref[block].T for block in range(3)]


def lay_planes(wide_ref, narrow_ref, lane, centre, higher, lower):
    row = iota((8, LANES), 0)
    wide = wide_ref.shape[0]
    lanes = slice(lane, lane + LANES)
    for plane in range(wide + narrow_ref.shape[0]):
        rows = slice(8 * (plane // 2), 8 * (plane // 2) + 8)
        mid, high, low = centre[rows], higher[rows], lower[rows]
        if plane % 2:
            mid = pltpu.roll(mid, TILE_X, 0)
        else:
            high, low = pltpu.roll(high, TILE_X, 0), pltpu.roll(low, TILE_X, 0)
        near = jnp.where(row < TILE_X, mid, high)
        if plane < wide:
            wide_ref[plane, 0:8, lanes] = near
            wide_ref[plane, 8:16, lanes] = jnp.where(row < TILE_X, 0.0, low)
        else:
            narrow_ref[plane - wide, :, lanes] = jnp.where(row < SPAN_NEAR - 2, near, low)


def narrowed(plane):
    row = iota((SPAN_NEAR, plane.shape[1]), 0)
    return jnp.where(row < SPAN_NEAR - 2, plane[:SPAN_NEAR], plane[SPAN_NEAR:])


def ahead_x(plane):
    return pltpu.roll(plane, plane.shape[0] - 1, 0) - plane


def behind_x(plane):
    return plane - pltpu.roll(plane, 1, 0)


def ahead_y(plane):
    return pltpu.roll(plane, SPAN_Y - 1, 1) - plane


def behind_y(plane):
    return plane - pltpu.roll(plane, 1, 1)


def ahead_z(planes, z):
    return planes[z + 1] - planes[z] if z + 1 < len(planes) else -planes[z]


def behind_z(planes, z):
    return planes[z] - planes[z - 1] if z else planes[z]


class Planes:
    def __init__(self, ref, first, depth):
        self.ref, self.first, self.depth = ref, first, depth

    def __len__(self):
        return self.depth

    def __getitem__(self, z):
        return self.ref[self.first + z]

    def __setitem__(self, z, plane):
        self.ref[self.first + z] = plane


def fields_of(ref, count, depth, first=0):
    return [Planes(ref, (first + number) * depth, depth) for number in range(count)]


def strain_rates(velocity, z):
    along_x, along_y, along_z = [field[z] for field in velocity]
    return (
        behind_x(along_x),
        behind_y(along_y),
        behind_z(velocity[2], z),
        ahead_y(along_x) + ahead_x(along_y),
        ahead_z(velocity[0], z) + ahead_x(along_z),
        ahead_z(velocity[1], z) + ahead_y(along_z),
    )


def new_stress(stress, strains, lame_lambda, shear_modulus, z):
    dilated = lame_lambda[z] * (strains[0] + strains[1] + strains[2])
    shear = shear_modulus[z]
    normal = [stress[n][z] + STEP * (dilated + 2.0 * shear * strains[n]) for n in range(3)]
    return normal + [stress[n][z] + STEP * shear * strains[n] for n in range(3, 6)]


def advance(state, medium, emit, target):
    velocity, stress = state[:3], state[3:]
    lame_lambda, shear_modulus, buoyancy = medium
    depth = len(buoyancy)
    wide = target is not None and target is not state
    for z in range(depth):
        scale = STEP * buoyancy[z]
        accel = (
            ahead_x(stress[0][z]) + behind_y(stress[3][z]) + behind_z(stress[4], z),
            behind_x(stress[3][z]) + ahead_y(stress[1][z]) + behind_z(stress[5], z),
            behind_x(stress[4][z]) + behind_y(stress[5][z]) + ahead_z(stress[2], z),
        )
        for number in range(3):
            moved = velocity[number][z] + scale * accel[number]
            velocity[number][z] = moved
            if wide:
                target[number][z] = narrowed(moved)
    for z in range(depth):
        strains = strain_rates(velocity, z)
        emit(z, strains)
        if target is not None:
            for number, plane in enumerate(new_stress(stress, strains, lame_lambda, shear_modulus, z)):
                target[3 + number][z] = narrowed(plane) if wide else plane


def pack_body(*refs):
    inputs, outputs, scratch = refs[:6], refs[6:10], refs[10:]
    fields_ref, high_ref, low_ref, side_ref, cells_ref, wavelet_ref, arrived, sent, sent_sides = scratch
    targets, at = [], 0
    for source in inputs[:4]:
        targets.append(fields_ref.at[at : at + source.shape[0]])
        at = at + source.shape[0]
    copies = [
        pltpu.make_async_copy(source, target, arrived.at[number])
        for number, (source, target) in enumerate(zip(inputs, targets + [cells_ref, wavelet_ref]))
    ]
    for copy in copies[4:] + copies[:4]:
        copy.start()
    copies[4].wait()
    copies[5].wait()
    cells_row = inputs[1].shape[0]
    cells = cells_ref[...]
    count = cells.shape[1]
    at_lane = iota((LANES, count), 0) == (cells & (LANES - 1))
    at_row = iota((cells_row, count), 0) == (cells >> (LANES.bit_length() - 1))
    stack = [
        jnp.where(at_row, third[step : step + 1, :], 0.0) for third in pieces(wavelet_ref[...]) for step in range(3)
    ]
    maps = sum_thirds(
        times_turned(jnp.concatenate(stack, axis=0).astype(BF16), jnp.where(at_lane, 1.0, 0.0).astype(BF16))
    )
    for copy in copies[:4]:
        copy.wait()
    total = at + 2 * cells_row
    fields_ref[at:total, :] = maps[cells_row:]
    for number in range(3, 6):
        rows = slice(number * cells_row, (number + 1) * cells_row)
        fields_ref[rows, :] = fields_ref[rows, :] + maps[:cells_row]
    rows = fields_ref[0:total, :]
    spare = 2 * LANES - total
    edge_columns(jnp.concatenate([rows, jnp.zeros((spare, LANES), F32)], axis=0), side_ref)
    sides = start_sides(side_ref, outputs[3], sent_sides)
    height = total // TILE_X
    for x in range(TILE_X):
        slab = fields_ref[pl.ds(x, height, stride=TILE_X), :]
        if x < RIM:
            low_ref[x * height : (x + 1) * height, :] = slab
        if x >= TILE_X - RIM:
            at = x - TILE_X + RIM
            high_ref[at * height : (at + 1) * height, :] = slab
    writes = [
        pltpu.make_async_copy(source, target, sent.at[number])
        for number, (source, target) in enumerate(zip((fields_ref.at[0:total], high_ref, low_ref), outputs))
    ]
    for copy in writes:
        copy.start()
    for copy in writes:
        copy.wait()
    wait_sides(sides)


def slots_body(capacity, devices, cols_y, owner_ref, start_ref, slot_ref, row_ref, cover_ref, place_ref, rank_ref):
    blocks = owner_ref.shape[0]
    group = 32
    before = jnp.where(iota((LANES, 2 * LANES), 0) < iota((LANES, 2 * LANES), 1), 1.0, 0.0).astype(BF16)
    rank_ref[...] = jnp.zeros_like(rank_ref)

    def count_group(number, carry):
        names = iota((group, LANES), 0) + number * group
        hot = [names == owner_ref[b : b + 1, :] for b in range(blocks)]
        marks = jnp.concatenate([jnp.where(h, 1.0, 0.0) for h in hot], axis=0).astype(BF16)
        counts = times(marks, before)
        total = jnp.zeros((group, LANES), F32)
        for b in range(blocks):
            part = counts[b * group : (b + 1) * group]
            rank_ref[b : b + 1, :] = rank_ref[b : b + 1, :] + jnp.sum(
                jnp.where(hot[b], part[:, :LANES] + total, 0.0), axis=0, keepdims=True
            )
            total = total + part[:, LANES:]
        return carry

    if devices == group:
        count_group(0, 0)
    else:
        lax.fori_loop(0, devices // group, count_group, 0)
    slot = owner_ref[...] * capacity + rank_ref[...].astype(I32)
    slot_ref[...] = slot >> 7
    low = slot & (LANES - 1)
    span = cols_y - GAUGE + 1
    start = start_ref[...]
    row = ((start.astype(F32) + 0.5) * (1.0 / span)).astype(I32)
    row_ref[...] = row
    first = start - row * span
    down = iota((LANES, LANES), 0)
    for b in range(blocks):
        lanes = slice(b * LANES, (b + 1) * LANES)
        offset = down - first[b : b + 1, :]
        cover_ref[:, lanes] = jnp.where((offset >= 0) & (offset < GAUGE), 1.0, 0.0).astype(BF16)
        place_ref[:, lanes] = jnp.where(down == low[b : b + 1, :], 1.0, 0.0).astype(BF16)


def forward_body(
    fields_ref,
    higher_ref,
    lower_ref,
    recv_ref,
    slot_ref,
    row_ref,
    weight_ref,
    channel_ref,
    cover_ref,
    place_ref,
    out_ref,
    strain_ref,
    medium_ref,
    wide_ref,
    source_ref,
    state_ref,
    near_ref,
    turn_ref,
    sides_ref,
    spread_ref,
):
    depth = medium_ref.shape[0] // 3
    cells_row = depth * TILE_X
    rims = rim_rows(recv_ref, turn_ref)
    height = fields_ref.shape[0] // TILE_X
    sides_ref[...] = jnp.zeros_like(sides_ref)
    for x in range(RIM):
        slab = slice(x * height, (x + 1) * height)
        sides_ref[0, pl.ds(x, height, stride=TILE_X), :] = higher_ref[slab, :]
        sides_ref[1, pl.ds(x + TILE_X - RIM, height, stride=TILE_X), :] = lower_ref[slab, :]
    lay_planes(wide_ref, source_ref, 0, fields_ref, sides_ref.at[0], sides_ref.at[1])
    lay_planes(wide_ref, source_ref, LANES, *rims)
    first = 9 * depth
    medium_ref[...] = wide_ref[first:]
    for plane in range(3 * depth):
        near_ref[plane] = narrowed(wide_ref[first + plane])
    state, near = fields_of(state_ref, 9, depth), fields_of(near_ref, 3, depth)
    for step in range(3):

        def emit(z, strains, step=step):
            for number, strain in enumerate(strains):
                base = ((step * 6 + number) * depth + z) * TILE_X
                strain_ref[base : base + TILE_X, :] = strain[0:TILE_X, 0:LANES]

        if step == 0:
            advance(fields_of(wide_ref, 9, depth), fields_of(wide_ref, 3, depth, 9), emit, state)
            continue
        for z in range(depth):
            load = source_ref[(step - 1) * depth + z]
            for number in range(3, 6):
                state[number][z] = state[number][z] + load
        advance(state, near, emit, state if step == 1 else None)
    axial = jnp.concatenate(
        [strain_ref[step * 6 * cells_row : (step * 6 + 2) * cells_row, :] for step in range(3)], axis=0
    )
    axial = jnp.concatenate(pieces(axial), axis=0).astype(BF16)
    rows_down = iota((cells_row, LANES), 0)
    slots_down = packed_iota(LANES, 2)
    for block in range(slot_ref.shape[0]):
        lanes = slice(block * LANES, (block + 1) * LANES)
        if block % 2 == 0:
            both = sum_thirds(times(axial, cover_ref[:, block * LANES : (block + 2) * LANES]))
        windows = both[:, :LANES] if block % 2 == 0 else both[:, LANES:]
        at_row = rows_down == row_ref[block : block + 1, :]
        weight_x, weight_y = weight_ref[0:1, lanes], weight_ref[1:2, lanes]
        sums = []
        for step in range(3):
            base = 2 * step * cells_row
            axial_sum = (
                weight_x * windows[base : base + cells_row]
                + weight_y * windows[base + cells_row : base + 2 * cells_row]
            )
            sums.append(jnp.sum(jnp.where(at_row, axial_sum, 0.0), axis=0, keepdims=True))
        sums.append(channel_ref[block : block + 1, :].astype(F32))
        values = jnp.concatenate(sums + sums, axis=0)
        in_slot = slots_down == packed_rows(slot_ref[block : block + 1, :], LANES)
        for third, piece in enumerate(pieces(values)):
            tile = jnp.concatenate([piece, piece], axis=0).astype(BF16)
            spread_ref[third * LANES : (third + 1) * LANES, lanes] = jnp.where(
                in_slot, jnp.concatenate([tile] * (LANES // 16), axis=0), jnp.zeros((), BF16)
            )
    out_ref[...] = sum_thirds(times_turned(spread_ref[...], place_ref[...]))


def owner_body(arrived_ref, observed_ref, residual_ref, reply_ref, values_ref, place_ref, held_ref):
    groups = arrived_ref.shape[0] // 4
    parts = observed_ref.shape[1] // LANES
    down = packed_iota(LANES)
    part_down = iota((parts, LANES), 0)
    nothing = jnp.zeros((parts, LANES), F32)
    numbers = [arrived_ref[4 * s + 3 : 4 * s + 4, :].astype(I32) for s in range(groups)]
    for s in range(groups):
        lanes = slice(s * LANES, (s + 1) * LANES)
        place_ref[:, lanes] = jnp.where(
            down == packed_rows(numbers[s] & (LANES - 1), LANES), jnp.ones((), BF16), jnp.zeros((), BF16)
        )
        at_part = part_down == (numbers[s] >> 7)
        thirds = pieces(arrived_ref[4 * s : 4 * s + 3, :])
        stack = []
        for third in thirds:
            for step in range(3):
                stack.append(jnp.where(at_part, third[step : step + 1, :], 0.0))
        stack.append(nothing)
        values_ref[:, lanes] = jnp.concatenate(stack, axis=0).astype(BF16)
    rows = 3 * parts
    sums = sum_thirds(times_turned(values_ref[...], place_ref[...])[: 3 * rows])
    for step in range(3):
        for part in range(parts):
            at = step * parts + part
            held_ref[at : at + 1, :] = observed_ref[step : step + 1, part * LANES : (part + 1) * LANES]
    held_ref[rows:, :] = nothing
    held_ref[0:rows, :] = sums - held_ref[0:rows, :]
    for step in range(3):
        for part in range(parts):
            at = step * parts + part
            residual_ref[step : step + 1, part * LANES : (part + 1) * LANES] = held_ref[at : at + 1, :]
    residual = jnp.concatenate(two_pieces(held_ref[...]), axis=0).astype(BF16)
    for s in range(groups):
        if s % 2 == 0:
            both = sum_halves(times(residual, place_ref[:, s * LANES : (s + 2) * LANES]))
        found = both[:, :LANES] if s % 2 == 0 else both[:, LANES:]
        at_part = part_down == (numbers[s] >> 7)
        for step in range(3):
            reply_ref[4 * s + step : 4 * s + step + 1, :] = jnp.sum(
                jnp.where(at_part, found[step * parts : (step + 1) * parts], 0.0), axis=0, keepdims=True
            )
        reply_ref[4 * s + 3 : 4 * s + 4, :] = jnp.zeros((1, LANES), F32)


def reached():
    return [(turn, distance) for turn in range(3) for distance in range(RIM - turn)]


def load_body(
    arrived_ref,
    slot_ref,
    row_ref,
    weight_ref,
    cover_ref,
    place_ref,
    load_ref,
    high_ref,
    low_ref,
    out_ref,
    spread_ref,
    side_ref,
    held_ref,
    sent_sides,
):
    cells_row = load_ref.shape[0] // 6
    stack_rows = load_ref.shape[0]
    arrived = jnp.concatenate(two_pieces(arrived_ref[...]), axis=0).astype(BF16)
    slots_down = iota((LANES, LANES), 0) >> 2
    rows_down = packed_iota(cells_row)
    for block in range(slot_ref.shape[0]):
        lanes = slice(block * LANES, (block + 1) * LANES)
        if block % 2 == 0:
            both = sum_halves(times(arrived, place_ref[:, block * LANES : (block + 2) * LANES]))
        found = both[:, :LANES] if block % 2 == 0 else both[:, LANES:]
        found = jnp.where(slots_down == slot_ref[block : block + 1, :], found, 0.0)
        folded = found[0:8]
        for part in range(1, LANES // 8):
            folded = folded + found[8 * part : 8 * part + 8]
        folded = folded + pltpu.roll(folded, 4, 0)
        at_row = rows_down == packed_rows(row_ref[block : block + 1, :], cells_row)
        for turn in range(3):
            back = folded[2 - turn : 3 - turn, :]
            for part in range(2):
                for half, piece in enumerate(two_pieces(weight_ref[part : part + 1, lanes] * back)):
                    base = half * stack_rows + (2 * turn + part) * cells_row
                    spread_ref[base : base + cells_row, lanes] = jnp.where(
                        at_row, packed_rows(piece, cells_row), jnp.zeros((), BF16)
                    )
    cover = jnp.concatenate([cover_ref[0:16, :], cover_ref[LANES - 16 :, :]], axis=0)
    edges = times_turned(cover, spread_ref[0:stack_rows, :]) + times_turned(cover, spread_ref[stack_rows:, :])
    side_ref[...] = jnp.zeros_like(side_ref)
    for side, base in ((0, 0), (1, 32 - RIM)):
        for column in range(RIM):
            lanes = slice(column * LANES, column * LANES + stack_rows)
            side_ref[side, 0:1, lanes] = edges[base + column : base + column + 1, :]
    sides = start_sides(side_ref, out_ref, sent_sides)
    load = sum_halves(times_turned(spread_ref[...], cover_ref[...]))
    load_ref[...] = load
    held_ref[0:stack_rows, :] = load
    count = stack_rows // (3 * TILE_X)
    for at, (turn, distance) in enumerate(reached()):
        rows = slice(at * count, (at + 1) * count)
        first = turn * count * TILE_X
        low_ref[rows, :] = held_ref[pl.ds(first + distance, count, stride=TILE_X), :]
        high_ref[rows, :] = held_ref[pl.ds(first + TILE_X - 1 - distance, count, stride=TILE_X), :]
    wait_sides(sides)


def adjoint_body(
    load_ref,
    higher_ref,
    lower_ref,
    recv_ref,
    strain_ref,
    medium_ref,
    residual_ref,
    gradient_ref,
    residual_out_ref,
    first_ref,
    later_ref,
    velocity_ref,
    state_ref,
    near_ref,
    turn_ref,
    sides_ref,
):
    depth = medium_ref.shape[0] // 3
    rims = rim_rows(recv_ref, turn_ref)
    sides_ref[...] = jnp.zeros_like(sides_ref)
    count = load_ref.shape[0] // (3 * TILE_X)
    for at, (turn, distance) in enumerate(reached()):
        rows = slice(at * count, (at + 1) * count)
        first = turn * count * TILE_X
        sides_ref[0, pl.ds(first + distance, count, stride=TILE_X), :] = higher_ref[rows, :]
        sides_ref[1, pl.ds(first + TILE_X - 1 - distance, count, stride=TILE_X), :] = lower_ref[rows, :]
    lay_planes(first_ref, later_ref, 0, load_ref, sides_ref.at[0], sides_ref.at[1])
    lay_planes(first_ref, later_ref, LANES, *rims)
    for plane in range(3 * depth):
        near_ref[plane] = narrowed(medium_ref[plane])
    gradient_ref[...] = jnp.zeros_like(gradient_ref)
    residual_out_ref[...] = residual_ref[...]
    state, near, medium = (
        fields_of(state_ref, 9, depth),
        fields_of(near_ref, 3, depth),
        fields_of(medium_ref, 3, depth),
    )

    def add_terms(turn, z, strains):
        dilation, dilation_back, doubled, product = None, None, None, None
        for number, strain in enumerate(strains):
            base = (((2 - turn) * 6 + number) * depth + z) * TILE_X
            forward = strain_ref[base : base + TILE_X, :]
            if number < 3:
                dilation = forward if dilation is None else dilation + forward
            if strain is None:
                continue
            back = strain[0:TILE_X, 0:LANES]
            term = forward * back
            if number < 3:
                dilation_back = back if dilation_back is None else dilation_back + back
                doubled = term if doubled is None else doubled + term
            else:
                product = term if product is None else product + term
        for part, term in enumerate((dilation * dilation_back, 2.0 * doubled + product)):
            base = (part * depth + z) * TILE_X
            gradient_ref[base : base + TILE_X, :] = gradient_ref[base : base + TILE_X, :] + term

    loads, velocity = fields_of(first_ref, 2, depth), fields_of(velocity_ref, 2, depth)
    for z in range(depth):
        scale = STEP * medium[2][z]
        velocity[0][z] = scale * ahead_x(loads[0][z])
        velocity[1][z] = scale * ahead_y(loads[1][z])
        state[0][z] = narrowed(velocity[0][z])
        state[1][z] = narrowed(velocity[1][z])
        state[2][z] = jnp.zeros((SPAN_NEAR, SPAN_Y), F32)
    for z in range(depth):
        along_x, along_y = velocity[0][z], velocity[1][z]
        strain_x, strain_y = behind_x(along_x), behind_y(along_y)
        sheared = (
            ahead_y(along_x) + ahead_x(along_y),
            ahead_z(velocity[0], z),
            ahead_z(velocity[1], z),
        )
        add_terms(0, z, (strain_x, strain_y, None) + sheared)
        dilated = medium[0][z] * (strain_x + strain_y)
        shear = medium[1][z]
        state[3][z] = narrowed(loads[0][z] + STEP * (dilated + 2.0 * shear * strain_x))
        state[4][z] = narrowed(loads[1][z] + STEP * (dilated + 2.0 * shear * strain_y))
        state[5][z] = narrowed(STEP * dilated)
        for number, strain in enumerate(sheared):
            state[6 + number][z] = narrowed(STEP * shear * strain)
    for turn in (1, 2):
        for part in range(2):
            for z in range(depth):
                load = later_ref[(2 * (turn - 1) + part) * depth + z]
                state[3 + part][z] = state[3 + part][z] + load
        advance(state, near, functools.partial(add_terms, turn), state if turn == 1 else None)


def shards(
    initial_state,
    lame_lambda,
    shear_modulus,
    buoyancy,
    source_cells,
    source_wavelet,
    segment_start,
    segment_weight,
    partial_owner,
    partial_channel,
    observed_data,
):
    depth, rows_x, cols_y = lame_lambda.shape
    part_count = segment_start.shape[0]
    count_x, count_y = lax.axis_size("gx"), lax.axis_size("gy")
    devices = count_x * count_y
    capacity = max(2, 2 * part_count // devices)
    slot_groups = devices * capacity // LANES
    blocks = part_count // LANES
    per_group = LANES // capacity
    cells_row = depth * rows_x
    both = ("gx", "gy")
    up = [(i, i + 1) for i in range(count_x - 1)]
    down = [(j, i) for i, j in up]
    shape = jax.ShapeDtypeStruct

    def exchange(chunks):
        return lax.all_to_all(chunks, both, split_axis=0, concat_axis=0, tiled=True)

    def to_owners(rows):
        chunks = rows.reshape(slot_groups, 4, per_group, capacity).transpose(0, 2, 1, 3)
        back = exchange(chunks.reshape(devices, 4, capacity)).reshape(slot_groups, per_group, 4, capacity)
        return back.transpose(0, 2, 1, 3).reshape(slot_groups * 4, LANES)

    trimmed = shape((14 * depth * RIM, cols_y), F32)
    fields, high, low, edges = call_kernel(
        pack_body,
        "pack_edges",
        [shape((14 * cells_row, cols_y), F32), trimmed, trimmed, shape((devices, 1, 2 * RIM * LANES), F32)],
        [
            pltpu.VMEM((14 * cells_row + SPARE, cols_y), F32),
            pltpu.VMEM(trimmed.shape, F32),
            pltpu.VMEM(trimmed.shape, F32),
            pltpu.VMEM((2, 1, 2 * RIM * LANES), F32),
            pltpu.VMEM((1, source_cells.shape[0]), I32),
            pltpu.VMEM(source_wavelet.shape, F32),
            pltpu.SemaphoreType.DMA((6,)),
            pltpu.SemaphoreType.DMA((3,)),
            pltpu.SemaphoreType.DMA((6,)),
        ],
        *[values.reshape(-1, cols_y) for values in (initial_state, lame_lambda, shear_modulus, buoyancy)],
        source_cells.reshape(1, -1),
        source_wavelet,
        place=pl.ANY,
        place_out=pl.ANY,
        room=60 * 1024 * 1024,
    )
    lower = lax.ppermute(high, "gx", up)
    higher = lax.ppermute(low, "gx", down)
    rims = exchange(edges)
    channels = partial_channel.reshape(blocks, LANES)
    slot, row, cover, place = call_kernel(
        functools.partial(slots_body, capacity, devices, cols_y),
        "segment_slots",
        [
            shape((blocks, LANES), I32),
            shape((blocks, LANES), I32),
            shape((cols_y, part_count), BF16),
            shape((LANES, part_count), BF16),
        ],
        [pltpu.VMEM((blocks, LANES), F32)],
        partial_owner.reshape(blocks, LANES),
        segment_start.reshape(blocks, LANES),
    )
    partials, strains, medium = call_kernel(
        forward_body,
        "forward_run",
        [
            shape((slot_groups * 4, LANES), F32),
            shape((18 * cells_row, cols_y), F32),
            shape((3 * depth, SPAN_X, SPAN_Y), F32),
        ],
        [
            pltpu.VMEM((12 * depth, SPAN_X, SPAN_Y), F32),
            pltpu.VMEM((2 * depth, SPAN_NEAR, SPAN_Y), F32),
            pltpu.VMEM((9 * depth, SPAN_NEAR, SPAN_Y), F32),
            pltpu.VMEM((3 * depth, SPAN_NEAR, SPAN_Y), F32),
            pltpu.VMEM((3, LANES, 2 * LANES), F32),
            pltpu.VMEM((2, 14 * cells_row + SPARE, cols_y), F32),
            pltpu.VMEM((3 * LANES, part_count), BF16),
        ],
        fields,
        higher,
        lower,
        rims,
        slot,
        row,
        segment_weight,
        channels,
        cover,
        place,
    )
    parts = observed_data.shape[1] // LANES
    residuals, reply = call_kernel(
        owner_body,
        "channel_sums",
        [shape(observed_data.shape, F32), shape((slot_groups * 4, LANES), F32)],
        [
            pltpu.VMEM((10 * parts, slot_groups * LANES), BF16),
            pltpu.VMEM((LANES, slot_groups * LANES), BF16),
            pltpu.VMEM((4 * parts, LANES), F32),
        ],
        to_owners(partials),
        observed_data,
    )
    reach = shape((len(reached()) * 2 * depth, cols_y), F32)
    loads, load_high, load_low, load_edges = call_kernel(
        load_body,
        "segment_loads",
        [shape((6 * cells_row, cols_y), F32), reach, reach, shape((devices, 1, RIM * LANES), F32)],
        [
            pltpu.VMEM((12 * cells_row, part_count), BF16),
            pltpu.VMEM((2, 1, RIM * LANES), F32),
            pltpu.VMEM((6 * cells_row + SPARE, cols_y), F32),
            pltpu.SemaphoreType.DMA((6,)),
        ],
        to_owners(reply),
        slot,
        row,
        segment_weight,
        cover,
        place,
        place_out=(pltpu.VMEM, pltpu.VMEM, pltpu.VMEM, pl.ANY),
    )
    load_lower = lax.ppermute(load_high, "gx", up)
    load_higher = lax.ppermute(load_low, "gx", down)
    load_rims = exchange(load_edges)
    gradients, residuals = call_kernel(
        adjoint_body,
        "adjoint_run",
        [shape((2 * cells_row, cols_y), F32), shape(observed_data.shape, F32)],
        [
            pltpu.VMEM((2 * depth, SPAN_X, SPAN_Y), F32),
            pltpu.VMEM((4 * depth, SPAN_NEAR, SPAN_Y), F32),
            pltpu.VMEM((2 * depth, SPAN_X, SPAN_Y), F32),
            pltpu.VMEM((9 * depth, SPAN_NEAR, SPAN_Y), F32),
            pltpu.VMEM((3 * depth, SPAN_NEAR, SPAN_Y), F32),
            pltpu.VMEM((3, LANES, LANES), F32),
            pltpu.VMEM((2, 6 * cells_row + SPARE, cols_y), F32),
        ],
        loads,
        load_higher,
        load_lower,
        load_rims,
        strains,
        medium,
        residuals,
    )
    return (residuals, gradients.reshape(2, depth, rows_x, cols_y))


def solution(mesh):
    in_specs = (
        P(None, None, "gx", "gy"),
        P(None, "gx", "gy"),
        P(None, "gx", "gy"),
        P(None, "gx", "gy"),
        P(("gx", "gy")),
        P(None, ("gx", "gy")),
        P(("gx", "gy")),
        P(None, ("gx", "gy")),
        P(("gx", "gy"), None),
        P(("gx", "gy")),
        P(None, ("gx", "gy")),
    )
    out_specs = (P(None, ("gx", "gy")), P(None, None, "gx", "gy"))
    return jax.shard_map(shards, mesh=mesh, in_specs=in_specs, out_specs=out_specs, check_vma=False)
```

```python
import functools

import jax
import jax.numpy as jnp
from jax import lax
from jax.experimental import pallas as pl
from jax.experimental.pallas import tpu as pltpu
from jax.sharding import PartitionSpec as P

GAUGE = 8
STEP = 0.25
RIM = 3
LANES = 128
TILE_X = 4
SPARE = 8
SPAN_X = 16
SPAN_NEAR = 8
SPAN_Y = 256
F32, BF16, I32 = jnp.float32, jnp.bfloat16, jnp.int32
NEAR = tuple((dx, dy) for dx in (-1, 0, 1) for dy in (-1, 0, 1))


def call_kernel(
    body, name, outs, scratch, *args, place=pltpu.VMEM, place_out=pltpu.VMEM, room=24 * 1024 * 1024
):
    spaces = place_out if isinstance(place_out, tuple) else (place_out,) * len(outs)
    return pl.pallas_call(
        body,
        name=name,
        out_shape=outs,
        in_specs=[pl.BlockSpec(memory_space=place)] * len(args),
        out_specs=[pl.BlockSpec(memory_space=space) for space in spaces],
        scratch_shapes=scratch,
        compiler_params=pltpu.CompilerParams(vmem_limit_bytes=room),
    )(*args)


def pieces(values):
    high = values.astype(BF16).astype(F32)
    rest = values - high
    middle = rest.astype(BF16).astype(F32)
    return high, middle, rest - middle


def iota(shape, dim):
    return lax.broadcasted_iota(I32, shape, dim)


def times(left, right):
    return lax.dot_general(left, right, (((1,), (0,)), ((), ())), preferred_element_type=F32)


def times_turned(left, right):
    return lax.dot_general(left, right, (((1,), (1,)), ((), ())), preferred_element_type=F32)


def packed_rows(row, height):
    tile = jnp.broadcast_to(row.astype(F32), (16, row.shape[1])).astype(BF16)
    return jnp.concatenate([tile] * (height // 16), axis=0) if height > 16 else tile


def packed_iota(height, shift=0):
    return (iota((height, LANES), 0) >> shift).astype(F32).astype(BF16)


def two_pieces(values):
    high = values.astype(BF16).astype(F32)
    return high, values - high


def sum_halves(values):
    half = values.shape[0] // 2
    return values[:half] + values[half:]


def sum_thirds(values):
    third = values.shape[0] // 3
    return values[:third] + values[third : 2 * third] + values[2 * third :]


def neighbour(dx, dy):
    count_x, count_y = lax.axis_size("gx"), lax.axis_size("gy")
    at_x, at_y = lax.axis_index("gx") + dx, lax.axis_index("gy") + dy
    inside = (at_x >= 0) & (at_x < count_x) & (at_y >= 0) & (at_y < count_y)
    return jnp.where(inside, at_x * count_y + at_y, 0), inside


def edge_columns(rows, side_ref):
    width = rows.shape[0]
    turned = rows.T
    for side, base in ((0, 0), (1, LANES - RIM)):
        for column in range(RIM):
            side_ref[side, 0:1, column * width : (column + 1) * width] = turned[base + column : base + column + 1, :]


def start_sides(side_ref, out_ref, sent):
    sides = []
    for number, (dx, dy) in enumerate((dx, dy) for dx, dy in NEAR if dy):
        index, inside = neighbour(dx, dy)
        source, target = side_ref.at[1 if dy > 0 else 0], out_ref.at[index]
        sides.append((inside, pltpu.make_async_copy(source, target, sent.at[number])))
    for inside, copy in sides:
        pl.when(inside)(copy.start)
    return sides


def wait_sides(sides):
    for inside, copy in sides:
        pl.when(inside)(copy.wait)


def arrived_chunk(recv_ref, dx, dy):
    index, inside = neighbour(dx, dy)
    return jnp.where(inside, recv_ref[index], 0.0)


def rim_rows(recv_ref, turn_ref):
    width = turn_ref.shape[2]
    turn_ref[...] = jnp.zeros_like(turn_ref)
    for block, dx in enumerate((0, 1, -1)):
        for dy, first in ((1, 0), (-1, LANES - RIM)):
            chunk = arrived_chunk(recv_ref, dx, dy)
            for column in range(RIM):
                turn_ref[block, first + column : first + column + 1, :] = chunk[
                    :, column * width : (column + 1) * width
                ]
    return [turn_ref[block].T for block in range(3)]


def lay_planes(wide_ref, narrow_ref, lane, centre, higher, lower):
    row = iota((8, LANES), 0)
    wide = wide_ref.shape[0]
    lanes = slice(lane, lane + LANES)
    for plane in range(wide + narrow_ref.shape[0]):
        rows = slice(8 * (plane // 2), 8 * (plane // 2) + 8)
        mid, high, low = centre[rows], higher[rows], lower[rows]
        if plane % 2:
            mid = pltpu.roll(mid, TILE_X, 0)
        else:
            high, low = pltpu.roll(high, TILE_X, 0), pltpu.roll(low, TILE_X, 0)
        near = jnp.where(row < TILE_X, mid, high)
        if plane < wide:
            wide_ref[plane, 0:8, lanes] = near
            wide_ref[plane, 8:16, lanes] = jnp.where(row < TILE_X, 0.0, low)
        else:
            narrow_ref[plane - wide, :, lanes] = jnp.where(row < SPAN_NEAR - 2, near, low)


def narrowed(plane):
    row = iota((SPAN_NEAR, plane.shape[1]), 0)
    return jnp.where(row < SPAN_NEAR - 2, plane[:SPAN_NEAR], plane[SPAN_NEAR:])


def ahead_x(plane):
    return pltpu.roll(plane, plane.shape[0] - 1, 0) - plane


def behind_x(plane):
    return plane - pltpu.roll(plane, 1, 0)


def ahead_y(plane):
    return pltpu.roll(plane, SPAN_Y - 1, 1) - plane


def behind_y(plane):
    return plane - pltpu.roll(plane, 1, 1)


def ahead_z(planes, z):
    return planes[z + 1] - planes[z] if z + 1 < len(planes) else -planes[z]


def behind_z(planes, z):
    return planes[z] - planes[z - 1] if z else planes[z]


class Planes:
    def __init__(self, ref, first, depth):
        self.ref, self.first, self.depth = ref, first, depth

    def __len__(self):
        return self.depth

    def __getitem__(self, z):
        return self.ref[self.first + z]

    def __setitem__(self, z, plane):
        self.ref[self.first + z] = plane


def fields_of(ref, count, depth, first=0):
    return [Planes(ref, (first + number) * depth, depth) for number in range(count)]


def strain_rates(velocity, z):
    along_x, along_y, along_z = [field[z] for field in velocity]
    return (
        behind_x(along_x),
        behind_y(along_y),
        behind_z(velocity[2], z),
        ahead_y(along_x) + ahead_x(along_y),
        ahead_z(velocity[0], z) + ahead_x(along_z),
        ahead_z(velocity[1], z) + ahead_y(along_z),
    )


def new_stress(stress, strains, lame_lambda, shear_modulus, z):
    dilated = lame_lambda[z] * (strains[0] + strains[1] + strains[2])
    shear = shear_modulus[z]
    normal = [stress[n][z] + STEP * (dilated + 2.0 * shear * strains[n]) for n in range(3)]
    return normal + [stress[n][z] + STEP * shear * strains[n] for n in range(3, 6)]


def advance(state, medium, emit, target):
    velocity, stress = state[:3], state[3:]
    lame_lambda, shear_modulus, buoyancy = medium
    depth = len(buoyancy)
    wide = target is not None and target is not state
    for z in range(depth):
        scale = STEP * buoyancy[z]
        accel = (
            ahead_x(stress[0][z]) + behind_y(stress[3][z]) + behind_z(stress[4], z),
            behind_x(stress[3][z]) + ahead_y(stress[1][z]) + behind_z(stress[5], z),
            behind_x(stress[4][z]) + behind_y(stress[5][z]) + ahead_z(stress[2], z),
        )
        for number in range(3):
            moved = velocity[number][z] + scale * accel[number]
            velocity[number][z] = moved
            if wide:
                target[number][z] = narrowed(moved)
    for z in range(depth):
        strains = strain_rates(velocity, z)
        emit(z, strains)
        if target is not None:
            for number, plane in enumerate(new_stress(stress, strains, lame_lambda, shear_modulus, z)):
                target[3 + number][z] = narrowed(plane) if wide else plane


def pack_body(*refs):
    inputs, outputs, scratch = refs[:6], refs[6:10], refs[10:]
    fields_ref, high_ref, low_ref, side_ref, cells_ref, wavelet_ref, arrived, sent, sent_sides = scratch
    targets, at = [], 0
    for source in inputs[:4]:
        targets.append(fields_ref.at[at : at + source.shape[0]])
        at = at + source.shape[0]
    copies = [
        pltpu.make_async_copy(source, target, arrived.at[number])
        for number, (source, target) in enumerate(zip(inputs, targets + [cells_ref, wavelet_ref]))
    ]
    for copy in copies[4:] + copies[:4]:
        copy.start()
    copies[4].wait()
    copies[5].wait()
    cells_row = inputs[1].shape[0]
    cells = cells_ref[...]
    count = cells.shape[1]
    at_lane = iota((LANES, count), 0) == (cells & (LANES - 1))
    at_row = iota((cells_row, count), 0) == (cells >> (LANES.bit_length() - 1))
    stack = [
        jnp.where(at_row, third[step : step + 1, :], 0.0) for third in pieces(wavelet_ref[...]) for step in range(3)
    ]
    maps = sum_thirds(
        times_turned(jnp.concatenate(stack, axis=0).astype(BF16), jnp.where(at_lane, 1.0, 0.0).astype(BF16))
    )
    for copy in copies[:4]:
        copy.wait()
    total = at + 2 * cells_row
    fields_ref[at:total, :] = maps[cells_row:]
    for number in range(3, 6):
        rows = slice(number * cells_row, (number + 1) * cells_row)
        fields_ref[rows, :] = fields_ref[rows, :] + maps[:cells_row]
    rows = fields_ref[0:total, :]
    spare = 2 * LANES - total
    edge_columns(jnp.concatenate([rows, jnp.zeros((spare, LANES), F32)], axis=0), side_ref)
    sides = start_sides(side_ref, outputs[3], sent_sides)
    height = total // TILE_X
    for x in range(TILE_X):
        slab = fields_ref[pl.ds(x, height, stride=TILE_X), :]
        if x < RIM:
            low_ref[x * height : (x + 1) * height, :] = slab
        if x >= TILE_X - RIM:
            at = x - TILE_X + RIM
            high_ref[at * height : (at + 1) * height, :] = slab
    writes = [
        pltpu.make_async_copy(source, target, sent.at[number])
        for number, (source, target) in enumerate(zip((fields_ref.at[0:total], high_ref, low_ref), outputs))
    ]
    for copy in writes:
        copy.start()
    for copy in writes:
        copy.wait()
    wait_sides(sides)


def slots_body(capacity, devices, cols_y, owner_ref, start_ref, slot_ref, row_ref, cover_ref, place_ref, rank_ref):
    blocks = owner_ref.shape[0]
    group = 32
    before = jnp.where(iota((LANES, 2 * LANES), 0) < iota((LANES, 2 * LANES), 1), 1.0, 0.0).astype(BF16)
    rank_ref[...] = jnp.zeros_like(rank_ref)

    def count_group(number, carry):
        names = iota((group, LANES), 0) + number * group
        hot = [names == owner_ref[b : b + 1, :] for b in range(blocks)]
        marks = jnp.concatenate([jnp.where(h, 1.0, 0.0) for h in hot], axis=0).astype(BF16)
        counts = times(marks, before)
        total = jnp.zeros((group, LANES), F32)
        for b in range(blocks):
            part = counts[b * group : (b + 1) * group]
            rank_ref[b : b + 1, :] = rank_ref[b : b + 1, :] + jnp.sum(
                jnp.where(hot[b], part[:, :LANES] + total, 0.0), axis=0, keepdims=True
            )
            total = total + part[:, LANES:]
        return carry

    if devices == group:
        count_group(0, 0)
    else:
        lax.fori_loop(0, devices // group, count_group, 0)
    slot = owner_ref[...] * capacity + rank_ref[...].astype(I32)
    slot_ref[...] = slot >> 7
    low = slot & (LANES - 1)
    span = cols_y - GAUGE + 1
    start = start_ref[...]
    row = ((start.astype(F32) + 0.5) * (1.0 / span)).astype(I32)
    row_ref[...] = row
    first = start - row * span
    down = iota((LANES, LANES), 0)
    for b in range(blocks):
        lanes = slice(b * LANES, (b + 1) * LANES)
        offset = down - first[b : b + 1, :]
        cover_ref[:, lanes] = jnp.where((offset >= 0) & (offset < GAUGE), 1.0, 0.0).astype(BF16)
        place_ref[:, lanes] = jnp.where(down == low[b : b + 1, :], 1.0, 0.0).astype(BF16)


def forward_body(
    fields_ref,
    higher_ref,
    lower_ref,
    recv_ref,
    slot_ref,
    row_ref,
    weight_ref,
    channel_ref,
    cover_ref,
    place_ref,
    out_ref,
    strain_ref,
    medium_ref,
    wide_ref,
    source_ref,
    state_ref,
    near_ref,
    turn_ref,
    sides_ref,
    spread_ref,
):
    depth = medium_ref.shape[0] // 3
    cells_row = depth * TILE_X
    rims = rim_rows(recv_ref, turn_ref)
    height = fields_ref.shape[0] // TILE_X
    sides_ref[...] = jnp.zeros_like(sides_ref)
    for x in range(RIM):
        slab = slice(x * height, (x + 1) * height)
        sides_ref[0, pl.ds(x, height, stride=TILE_X), :] = higher_ref[slab, :]
        sides_ref[1, pl.ds(x + TILE_X - RIM, height, stride=TILE_X), :] = lower_ref[slab, :]
    lay_planes(wide_ref, source_ref, 0, fields_ref, sides_ref.at[0], sides_ref.at[1])
    lay_planes(wide_ref, source_ref, LANES, *rims)
    first = 9 * depth
    medium_ref[...] = wide_ref[first:]
    for plane in range(3 * depth):
        near_ref[plane] = narrowed(wide_ref[first + plane])
    state, near = fields_of(state_ref, 9, depth), fields_of(near_ref, 3, depth)
    for step in range(3):

        def emit(z, strains, step=step):
            for number, strain in enumerate(strains):
                base = ((step * 6 + number) * depth + z) * TILE_X
                strain_ref[base : base + TILE_X, :] = strain[0:TILE_X, 0:LANES]

        if step == 0:
            advance(fields_of(wide_ref, 9, depth), fields_of(wide_ref, 3, depth, 9), emit, state)
            continue
        for z in range(depth):
            load = source_ref[(step - 1) * depth + z]
            for number in range(3, 6):
                state[number][z] = state[number][z] + load
        advance(state, near, emit, state if step == 1 else None)
    axial = jnp.concatenate(
        [strain_ref[step * 6 * cells_row : (step * 6 + 2) * cells_row, :] for step in range(3)], axis=0
    )
    high, middle, low = [piece.astype(BF16) for piece in pieces(axial)]
    upper = jnp.concatenate([high, middle], axis=1)
    rows_down = iota((cells_row, LANES), 0)
    slots_down = packed_iota(LANES, 2)
    for block in range(slot_ref.shape[0]):
        lanes = slice(block * LANES, (block + 1) * LANES)
        if block % 2 == 0:
            cover = cover_ref[:, block * LANES : (block + 2) * LANES]
            both = times(upper, jnp.concatenate([cover, cover], axis=0)) + times(low, cover)
        windows = both[:, :LANES] if block % 2 == 0 else both[:, LANES:]
        at_row = rows_down == row_ref[block : block + 1, :]
        weight_x, weight_y = weight_ref[0:1, lanes], weight_ref[1:2, lanes]
        sums = []
        for step in range(3):
            base = 2 * step * cells_row
            axial_sum = (
                weight_x * windows[base : base + cells_row]
                + weight_y * windows[base + cells_row : base + 2 * cells_row]
            )
            sums.append(jnp.sum(jnp.where(at_row, axial_sum, 0.0), axis=0, keepdims=True))
        sums.append(channel_ref[block : block + 1, :].astype(F32))
        values = jnp.concatenate(sums + sums, axis=0)
        in_slot = slots_down == packed_rows(slot_ref[block : block + 1, :], LANES)
        for third, piece in enumerate(pieces(values)):
            tile = jnp.concatenate([piece, piece], axis=0).astype(BF16)
            spread_ref[third * LANES : (third + 1) * LANES, lanes] = jnp.where(
                in_slot, jnp.concatenate([tile] * (LANES // 16), axis=0), jnp.zeros((), BF16)
            )
    out_ref[...] = sum_thirds(times_turned(spread_ref[...], place_ref[...]))


def owner_body(arrived_ref, observed_ref, residual_ref, reply_ref, values_ref, place_ref, held_ref):
    groups = arrived_ref.shape[0] // 4
    parts = observed_ref.shape[1] // LANES
    down = packed_iota(LANES)
    part_down = iota((parts, LANES), 0)
    nothing = jnp.zeros((parts, LANES), F32)
    numbers = [arrived_ref[4 * s + 3 : 4 * s + 4, :].astype(I32) for s in range(groups)]
    for s in range(groups):
        lanes = slice(s * LANES, (s + 1) * LANES)
        place_ref[:, lanes] = jnp.where(
            down == packed_rows(numbers[s] & (LANES - 1), LANES), jnp.ones((), BF16), jnp.zeros((), BF16)
        )
        at_part = part_down == (numbers[s] >> 7)
        thirds = pieces(arrived_ref[4 * s : 4 * s + 3, :])
        stack = []
        for third in thirds:
            for step in range(3):
                stack.append(jnp.where(at_part, third[step : step + 1, :], 0.0))
        stack.append(nothing)
        values_ref[:, lanes] = jnp.concatenate(stack, axis=0).astype(BF16)
    rows = 3 * parts
    sums = sum_thirds(times_turned(values_ref[...], place_ref[...])[: 3 * rows])
    for step in range(3):
        for part in range(parts):
            at = step * parts + part
            held_ref[at : at + 1, :] = observed_ref[step : step + 1, part * LANES : (part + 1) * LANES]
    held_ref[rows:, :] = nothing
    held_ref[0:rows, :] = sums - held_ref[0:rows, :]
    for step in range(3):
        for part in range(parts):
            at = step * parts + part
            residual_ref[step : step + 1, part * LANES : (part + 1) * LANES] = held_ref[at : at + 1, :]
    residual = jnp.concatenate(two_pieces(held_ref[...]), axis=1).astype(BF16)
    for s in range(groups):
        if s % 2 == 0:
            place = place_ref[:, s * LANES : (s + 2) * LANES]
            both = times(residual, jnp.concatenate([place, place], axis=0))
        found = both[:, :LANES] if s % 2 == 0 else both[:, LANES:]
        at_part = part_down == (numbers[s] >> 7)
        for step in range(3):
            reply_ref[4 * s + step : 4 * s + step + 1, :] = jnp.sum(
                jnp.where(at_part, found[step * parts : (step + 1) * parts], 0.0), axis=0, keepdims=True
            )
        reply_ref[4 * s + 3 : 4 * s + 4, :] = jnp.zeros((1, LANES), F32)


def reached():
    return [(turn, distance) for turn in range(3) for distance in range(RIM - turn)]


def load_body(
    arrived_ref,
    slot_ref,
    row_ref,
    weight_ref,
    cover_ref,
    place_ref,
    load_ref,
    high_ref,
    low_ref,
    out_ref,
    spread_ref,
    side_ref,
    held_ref,
    sent_sides,
):
    cells_row = load_ref.shape[0] // 6
    stack_rows = load_ref.shape[0]
    arrived = jnp.concatenate(two_pieces(arrived_ref[...]), axis=1).astype(BF16)
    slots_down = iota((LANES, LANES), 0) >> 2
    rows_down = packed_iota(cells_row)
    for block in range(slot_ref.shape[0]):
        lanes = slice(block * LANES, (block + 1) * LANES)
        if block % 2 == 0:
            place = place_ref[:, block * LANES : (block + 2) * LANES]
            both = times(arrived, jnp.concatenate([place, place], axis=0))
        found = both[:, :LANES] if block % 2 == 0 else both[:, LANES:]
        found = jnp.where(slots_down == slot_ref[block : block + 1, :], found, 0.0)
        folded = found[0:8]
        for part in range(1, LANES // 8):
            folded = folded + found[8 * part : 8 * part + 8]
        folded = folded + pltpu.roll(folded, 4, 0)
        at_row = rows_down == packed_rows(row_ref[block : block + 1, :], cells_row)
        for turn in range(3):
            back = folded[2 - turn : 3 - turn, :]
            for part in range(2):
                for half, piece in enumerate(two_pieces(weight_ref[part : part + 1, lanes] * back)):
                    base = half * stack_rows + (2 * turn + part) * cells_row
                    spread_ref[base : base + cells_row, lanes] = jnp.where(
                        at_row, packed_rows(piece, cells_row), jnp.zeros((), BF16)
                    )
    cover = jnp.concatenate([cover_ref[0:16, :], cover_ref[LANES - 16 :, :]], axis=0)
    edges = times_turned(cover, spread_ref[0:stack_rows, :]) + times_turned(cover, spread_ref[stack_rows:, :])
    side_ref[...] = jnp.zeros_like(side_ref)
    for side, base in ((0, 0), (1, 32 - RIM)):
        for column in range(RIM):
            lanes = slice(column * LANES, column * LANES + stack_rows)
            side_ref[side, 0:1, lanes] = edges[base + column : base + column + 1, :]
    sides = start_sides(side_ref, out_ref, sent_sides)
    load = sum_halves(times_turned(spread_ref[...], cover_ref[...]))
    load_ref[...] = load
    held_ref[0:stack_rows, :] = load
    count = stack_rows // (3 * TILE_X)
    for at, (turn, distance) in enumerate(reached()):
        rows = slice(at * count, (at + 1) * count)
        first = turn * count * TILE_X
        low_ref[rows, :] = held_ref[pl.ds(first + distance, count, stride=TILE_X), :]
        high_ref[rows, :] = held_ref[pl.ds(first + TILE_X - 1 - distance, count, stride=TILE_X), :]
    wait_sides(sides)


def adjoint_body(
    load_ref,
    higher_ref,
    lower_ref,
    recv_ref,
    strain_ref,
    medium_ref,
    residual_ref,
    gradient_ref,
    residual_out_ref,
    first_ref,
    later_ref,
    velocity_ref,
    state_ref,
    near_ref,
    turn_ref,
    sides_ref,
):
    depth = medium_ref.shape[0] // 3
    rims = rim_rows(recv_ref, turn_ref)
    sides_ref[...] = jnp.zeros_like(sides_ref)
    count = load_ref.shape[0] // (3 * TILE_X)
    for at, (turn, distance) in enumerate(reached()):
        rows = slice(at * count, (at + 1) * count)
        first = turn * count * TILE_X
        sides_ref[0, pl.ds(first + distance, count, stride=TILE_X), :] = higher_ref[rows, :]
        sides_ref[1, pl.ds(first + TILE_X - 1 - distance, count, stride=TILE_X), :] = lower_ref[rows, :]
    lay_planes(first_ref, later_ref, 0, load_ref, sides_ref.at[0], sides_ref.at[1])
    lay_planes(first_ref, later_ref, LANES, *rims)
    for plane in range(3 * depth):
        near_ref[plane] = narrowed(medium_ref[plane])
    gradient_ref[...] = jnp.zeros_like(gradient_ref)
    residual_out_ref[...] = residual_ref[...]
    state, near, medium = (
        fields_of(state_ref, 9, depth),
        fields_of(near_ref, 3, depth),
        fields_of(medium_ref, 3, depth),
    )

    def add_terms(turn, z, strains):
        dilation, dilation_back, doubled, product = None, None, None, None
        for number, strain in enumerate(strains):
            base = (((2 - turn) * 6 + number) * depth + z) * TILE_X
            forward = strain_ref[base : base + TILE_X, :]
            if number < 3:
                dilation = forward if dilation is None else dilation + forward
            if strain is None:
                continue
            back = strain[0:TILE_X, 0:LANES]
            term = forward * back
            if number < 3:
                dilation_back = back if dilation_back is None else dilation_back + back
                doubled = term if doubled is None else doubled + term
            else:
                product = term if product is None else product + term
        for part, term in enumerate((dilation * dilation_back, 2.0 * doubled + product)):
            base = (part * depth + z) * TILE_X
            gradient_ref[base : base + TILE_X, :] = gradient_ref[base : base + TILE_X, :] + term

    loads, velocity = fields_of(first_ref, 2, depth), fields_of(velocity_ref, 2, depth)
    for z in range(depth):
        scale = STEP * medium[2][z]
        velocity[0][z] = scale * ahead_x(loads[0][z])
        velocity[1][z] = scale * ahead_y(loads[1][z])
        state[0][z] = narrowed(velocity[0][z])
        state[1][z] = narrowed(velocity[1][z])
        state[2][z] = jnp.zeros((SPAN_NEAR, SPAN_Y), F32)
    for z in range(depth):
        along_x, along_y = velocity[0][z], velocity[1][z]
        strain_x, strain_y = behind_x(along_x), behind_y(along_y)
        sheared = (
            ahead_y(along_x) + ahead_x(along_y),
            ahead_z(velocity[0], z),
            ahead_z(velocity[1], z),
        )
        add_terms(0, z, (strain_x, strain_y, None) + sheared)
        dilated = medium[0][z] * (strain_x + strain_y)
        shear = medium[1][z]
        state[3][z] = narrowed(loads[0][z] + STEP * (dilated + 2.0 * shear * strain_x))
        state[4][z] = narrowed(loads[1][z] + STEP * (dilated + 2.0 * shear * strain_y))
        state[5][z] = narrowed(STEP * dilated)
        for number, strain in enumerate(sheared):
            state[6 + number][z] = narrowed(STEP * shear * strain)
    for turn in (1, 2):
        for part in range(2):
            for z in range(depth):
                load = later_ref[(2 * (turn - 1) + part) * depth + z]
                state[3 + part][z] = state[3 + part][z] + load
        advance(state, near, functools.partial(add_terms, turn), state if turn == 1 else None)


def shards(
    initial_state,
    lame_lambda,
    shear_modulus,
    buoyancy,
    source_cells,
    source_wavelet,
    segment_start,
    segment_weight,
    partial_owner,
    partial_channel,
    observed_data,
):
    depth, rows_x, cols_y = lame_lambda.shape
    part_count = segment_start.shape[0]
    count_x, count_y = lax.axis_size("gx"), lax.axis_size("gy")
    devices = count_x * count_y
    capacity = max(2, 2 * part_count // devices)
    slot_groups = devices * capacity // LANES
    blocks = part_count // LANES
    per_group = LANES // capacity
    cells_row = depth * rows_x
    both = ("gx", "gy")
    up = [(i, i + 1) for i in range(count_x - 1)]
    down = [(j, i) for i, j in up]
    shape = jax.ShapeDtypeStruct

    def exchange(chunks):
        return lax.all_to_all(chunks, both, split_axis=0, concat_axis=0, tiled=True)

    def to_owners(rows):
        chunks = rows.reshape(slot_groups, 4, per_group, capacity).transpose(0, 2, 1, 3)
        back = exchange(chunks.reshape(devices, 4, capacity)).reshape(slot_groups, per_group, 4, capacity)
        return back.transpose(0, 2, 1, 3).reshape(slot_groups * 4, LANES)

    trimmed = shape((14 * depth * RIM, cols_y), F32)
    fields, high, low, edges = call_kernel(
        pack_body,
        "pack_edges",
        [shape((14 * cells_row, cols_y), F32), trimmed, trimmed, shape((devices, 1, 2 * RIM * LANES), F32)],
        [
            pltpu.VMEM((14 * cells_row + SPARE, cols_y), F32),
            pltpu.VMEM(trimmed.shape, F32),
            pltpu.VMEM(trimmed.shape, F32),
            pltpu.VMEM((2, 1, 2 * RIM * LANES), F32),
            pltpu.VMEM((1, source_cells.shape[0]), I32),
            pltpu.VMEM(source_wavelet.shape, F32),
            pltpu.SemaphoreType.DMA((6,)),
            pltpu.SemaphoreType.DMA((3,)),
            pltpu.SemaphoreType.DMA((6,)),
        ],
        *[values.reshape(-1, cols_y) for values in (initial_state, lame_lambda, shear_modulus, buoyancy)],
        source_cells.reshape(1, -1),
        source_wavelet,
        place=pl.ANY,
        place_out=pl.ANY,
        room=60 * 1024 * 1024,
    )
    lower = lax.ppermute(high, "gx", up)
    higher = lax.ppermute(low, "gx", down)
    rims = exchange(edges)
    channels = partial_channel.reshape(blocks, LANES)
    slot, row, cover, place = call_kernel(
        functools.partial(slots_body, capacity, devices, cols_y),
        "segment_slots",
        [
            shape((blocks, LANES), I32),
            shape((blocks, LANES), I32),
            shape((cols_y, part_count), BF16),
            shape((LANES, part_count), BF16),
        ],
        [pltpu.VMEM((blocks, LANES), F32)],
        partial_owner.reshape(blocks, LANES),
        segment_start.reshape(blocks, LANES),
    )
    partials, strains, medium = call_kernel(
        forward_body,
        "forward_run",
        [
            shape((slot_groups * 4, LANES), F32),
            shape((18 * cells_row, cols_y), F32),
            shape((3 * depth, SPAN_X, SPAN_Y), F32),
        ],
        [
            pltpu.VMEM((12 * depth, SPAN_X, SPAN_Y), F32),
            pltpu.VMEM((2 * depth, SPAN_NEAR, SPAN_Y), F32),
            pltpu.VMEM((9 * depth, SPAN_NEAR, SPAN_Y), F32),
            pltpu.VMEM((3 * depth, SPAN_NEAR, SPAN_Y), F32),
            pltpu.VMEM((3, LANES, 2 * LANES), F32),
            pltpu.VMEM((2, 14 * cells_row + SPARE, cols_y), F32),
            pltpu.VMEM((3 * LANES, part_count), BF16),
        ],
        fields,
        higher,
        lower,
        rims,
        slot,
        row,
        segment_weight,
        channels,
        cover,
        place,
    )
    parts = observed_data.shape[1] // LANES
    residuals, reply = call_kernel(
        owner_body,
        "channel_sums",
        [shape(observed_data.shape, F32), shape((slot_groups * 4, LANES), F32)],
        [
            pltpu.VMEM((10 * parts, slot_groups * LANES), BF16),
            pltpu.VMEM((LANES, slot_groups * LANES), BF16),
            pltpu.VMEM((4 * parts, LANES), F32),
        ],
        to_owners(partials),
        observed_data,
    )
    reach = shape((len(reached()) * 2 * depth, cols_y), F32)
    loads, load_high, load_low, load_edges = call_kernel(
        load_body,
        "segment_loads",
        [shape((6 * cells_row, cols_y), F32), reach, reach, shape((devices, 1, RIM * LANES), F32)],
        [
            pltpu.VMEM((12 * cells_row, part_count), BF16),
            pltpu.VMEM((2, 1, RIM * LANES), F32),
            pltpu.VMEM((6 * cells_row + SPARE, cols_y), F32),
            pltpu.SemaphoreType.DMA((6,)),
        ],
        to_owners(reply),
        slot,
        row,
        segment_weight,
        cover,
        place,
        place_out=(pltpu.VMEM, pltpu.VMEM, pltpu.VMEM, pl.ANY),
    )
    load_lower = lax.ppermute(load_high, "gx", up)
    load_higher = lax.ppermute(load_low, "gx", down)
    load_rims = exchange(load_edges)
    gradients, residuals = call_kernel(
        adjoint_body,
        "adjoint_run",
        [shape((2 * cells_row, cols_y), F32), shape(observed_data.shape, F32)],
        [
            pltpu.VMEM((2 * depth, SPAN_X, SPAN_Y), F32),
            pltpu.VMEM((4 * depth, SPAN_NEAR, SPAN_Y), F32),
            pltpu.VMEM((2 * depth, SPAN_X, SPAN_Y), F32),
            pltpu.VMEM((9 * depth, SPAN_NEAR, SPAN_Y), F32),
            pltpu.VMEM((3 * depth, SPAN_NEAR, SPAN_Y), F32),
            pltpu.VMEM((3, LANES, LANES), F32),
            pltpu.VMEM((2, 6 * cells_row + SPARE, cols_y), F32),
        ],
        loads,
        load_higher,
        load_lower,
        load_rims,
        strains,
        medium,
        residuals,
    )
    return (residuals, gradients.reshape(2, depth, rows_x, cols_y))


def solution(mesh):
    in_specs = (
        P(None, None, "gx", "gy"),
        P(None, "gx", "gy"),
        P(None, "gx", "gy"),
        P(None, "gx", "gy"),
        P(("gx", "gy")),
        P(None, ("gx", "gy")),
        P(("gx", "gy")),
        P(None, ("gx", "gy")),
        P(("gx", "gy"), None),
        P(("gx", "gy")),
        P(None, ("gx", "gy")),
    )
    out_specs = (P(None, ("gx", "gy")), P(None, None, "gx", "gy"))
    return jax.shard_map(shards, mesh=mesh, in_specs=in_specs, out_specs=out_specs, check_vma=False)
```

```python
import functools

import jax
import jax.numpy as jnp
from jax import lax
from jax.experimental import pallas as pl
from jax.experimental.pallas import tpu as pltpu
from jax.sharding import PartitionSpec as P

GAUGE = 8
STEP = 0.25
RIM = 3
LANES = 128
TILE_X = 4
SPARE = 8
SPAN_X = 16
SPAN_NEAR = 8
SPAN_Y = 256
F32, BF16, I32 = jnp.float32, jnp.bfloat16, jnp.int32
NEAR = tuple((dx, dy) for dx in (-1, 0, 1) for dy in (-1, 0, 1))


def call_kernel(
    body, name, outs, scratch, *args, place=pltpu.VMEM, place_out=pltpu.VMEM, room=24 * 1024 * 1024
):
    spaces = place_out if isinstance(place_out, tuple) else (place_out,) * len(outs)
    return pl.pallas_call(
        body,
        name=name,
        out_shape=outs,
        in_specs=[pl.BlockSpec(memory_space=place)] * len(args),
        out_specs=[pl.BlockSpec(memory_space=space) for space in spaces],
        scratch_shapes=scratch,
        compiler_params=pltpu.CompilerParams(vmem_limit_bytes=room),
    )(*args)


def pieces(values):
    high = values.astype(BF16).astype(F32)
    rest = values - high
    middle = rest.astype(BF16).astype(F32)
    return high, middle, rest - middle


def iota(shape, dim):
    return lax.broadcasted_iota(I32, shape, dim)


def times(left, right):
    return lax.dot_general(left, right, (((1,), (0,)), ((), ())), preferred_element_type=F32)


def times_turned(left, right):
    return lax.dot_general(left, right, (((1,), (1,)), ((), ())), preferred_element_type=F32)


def packed_rows(row, height):
    tile = jnp.broadcast_to(row.astype(F32), (16, row.shape[1])).astype(BF16)
    return jnp.concatenate([tile] * (height // 16), axis=0) if height > 16 else tile


def packed_iota(height, shift=0):
    return (iota((height, LANES), 0) >> shift).astype(F32).astype(BF16)


def two_pieces(values):
    high = values.astype(BF16).astype(F32)
    return high, values - high


def sum_halves(values):
    half = values.shape[0] // 2
    return values[:half] + values[half:]


def sum_thirds(values):
    third = values.shape[0] // 3
    return values[:third] + values[third : 2 * third] + values[2 * third :]


def neighbour(dx, dy):
    count_x, count_y = lax.axis_size("gx"), lax.axis_size("gy")
    at_x, at_y = lax.axis_index("gx") + dx, lax.axis_index("gy") + dy
    inside = (at_x >= 0) & (at_x < count_x) & (at_y >= 0) & (at_y < count_y)
    return jnp.where(inside, at_x * count_y + at_y, 0), inside


def edge_columns(rows, side_ref):
    width = rows.shape[0]
    turned = rows.T
    for side, base in ((0, 0), (1, LANES - RIM)):
        for column in range(RIM):
            side_ref[side, 0:1, column * width : (column + 1) * width] = turned[base + column : base + column + 1, :]


def start_sides(side_ref, out_ref, sent):
    sides = []
    for number, (dx, dy) in enumerate((dx, dy) for dx, dy in NEAR if dy):
        index, inside = neighbour(dx, dy)
        source, target = side_ref.at[1 if dy > 0 else 0], out_ref.at[index]
        sides.append((inside, pltpu.make_async_copy(source, target, sent.at[number])))
    for inside, copy in sides:
        pl.when(inside)(copy.start)
    return sides


def wait_sides(sides):
    for inside, copy in sides:
        pl.when(inside)(copy.wait)


def arrived_chunk(recv_ref, dx, dy):
    index, inside = neighbour(dx, dy)
    return jnp.where(inside, recv_ref[index], 0.0)


def rim_rows(recv_ref, turn_ref):
    width = turn_ref.shape[2]
    turn_ref[...] = jnp.zeros_like(turn_ref)
    for block, dx in enumerate((0, 1, -1)):
        for dy, first in ((1, 0), (-1, LANES - RIM)):
            chunk = arrived_chunk(recv_ref, dx, dy)
            for column in range(RIM):
                turn_ref[block, first + column : first + column + 1, :] = chunk[
                    :, column * width : (column + 1) * width
                ]
    return [turn_ref[block].T for block in range(3)]


def lay_planes(wide_ref, narrow_ref, lane, centre, higher, lower):
    row = iota((8, LANES), 0)
    wide = wide_ref.shape[0]
    lanes = slice(lane, lane + LANES)
    for plane in range(wide + narrow_ref.shape[0]):
        rows = slice(8 * (plane // 2), 8 * (plane // 2) + 8)
        mid, high, low = centre[rows], higher[rows], lower[rows]
        if plane % 2:
            mid = pltpu.roll(mid, TILE_X, 0)
        else:
            high, low = pltpu.roll(high, TILE_X, 0), pltpu.roll(low, TILE_X, 0)
        near = jnp.where(row < TILE_X, mid, high)
        if plane < wide:
            wide_ref[plane, 0:8, lanes] = near
            wide_ref[plane, 8:16, lanes] = jnp.where(row < TILE_X, 0.0, low)
        else:
            narrow_ref[plane - wide, :, lanes] = jnp.where(row < SPAN_NEAR - 2, near, low)


def narrowed(plane):
    row = iota((SPAN_NEAR, plane.shape[1]), 0)
    return jnp.where(row < SPAN_NEAR - 2, plane[:SPAN_NEAR], plane[SPAN_NEAR:])


def ahead_x(plane):
    return pltpu.roll(plane, plane.shape[0] - 1, 0) - plane


def behind_x(plane):
    return plane - pltpu.roll(plane, 1, 0)


def ahead_y(plane):
    return pltpu.roll(plane, SPAN_Y - 1, 1) - plane


def behind_y(plane):
    return plane - pltpu.roll(plane, 1, 1)


def ahead_z(planes, z):
    return planes[z + 1] - planes[z] if z + 1 < len(planes) else -planes[z]


def behind_z(planes, z):
    return planes[z] - planes[z - 1] if z else planes[z]


class Planes:
    def __init__(self, ref, first, depth):
        self.ref, self.first, self.depth = ref, first, depth

    def __len__(self):
        return self.depth

    def __getitem__(self, z):
        return self.ref[self.first + z]

    def __setitem__(self, z, plane):
        self.ref[self.first + z] = plane


def fields_of(ref, count, depth, first=0):
    return [Planes(ref, (first + number) * depth, depth) for number in range(count)]


def strain_rates(velocity, z):
    along_x, along_y, along_z = [field[z] for field in velocity]
    return (
        behind_x(along_x),
        behind_y(along_y),
        behind_z(velocity[2], z),
        ahead_y(along_x) + ahead_x(along_y),
        ahead_z(velocity[0], z) + ahead_x(along_z),
        ahead_z(velocity[1], z) + ahead_y(along_z),
    )


def new_stress(stress, strains, lame_lambda, shear_modulus, z):
    dilated = lame_lambda[z] * (strains[0] + strains[1] + strains[2])
    shear = shear_modulus[z]
    normal = [stress[n][z] + STEP * (dilated + 2.0 * shear * strains[n]) for n in range(3)]
    return normal + [stress[n][z] + STEP * shear * strains[n] for n in range(3, 6)]


def advance(state, medium, emit, target):
    velocity, stress = state[:3], state[3:]
    lame_lambda, shear_modulus, buoyancy = medium
    depth = len(buoyancy)
    wide = target is not None and target is not state
    for z in range(depth):
        scale = STEP * buoyancy[z]
        accel = (
            ahead_x(stress[0][z]) + behind_y(stress[3][z]) + behind_z(stress[4], z),
            behind_x(stress[3][z]) + ahead_y(stress[1][z]) + behind_z(stress[5], z),
            behind_x(stress[4][z]) + behind_y(stress[5][z]) + ahead_z(stress[2], z),
        )
        for number in range(3):
            moved = velocity[number][z] + scale * accel[number]
            velocity[number][z] = moved
            if wide:
                target[number][z] = narrowed(moved)
    for z in range(depth):
        strains = strain_rates(velocity, z)
        emit(z, strains)
        if target is not None:
            for number, plane in enumerate(new_stress(stress, strains, lame_lambda, shear_modulus, z)):
                target[3 + number][z] = narrowed(plane) if wide else plane


def pack_body(*refs):
    inputs, outputs, scratch = refs[:6], refs[6:10], refs[10:]
    fields_ref, high_ref, low_ref, side_ref, cells_ref, wavelet_ref, arrived, sent, sent_sides = scratch
    targets, at = [], 0
    for source in inputs[:4]:
        targets.append(fields_ref.at[at : at + source.shape[0]])
        at = at + source.shape[0]
    copies = [
        pltpu.make_async_copy(source, target, arrived.at[number])
        for number, (source, target) in enumerate(zip(inputs, targets + [cells_ref, wavelet_ref]))
    ]
    for copy in copies[4:] + copies[:4]:
        copy.start()
    copies[4].wait()
    copies[5].wait()
    cells_row = inputs[1].shape[0]
    cells = cells_ref[...]
    count = cells.shape[1]
    at_lane = iota((LANES, count), 0) == (cells & (LANES - 1))
    at_row = iota((cells_row, count), 0) == (cells >> (LANES.bit_length() - 1))
    stack = [
        jnp.where(at_row, third[step : step + 1, :], 0.0) for third in pieces(wavelet_ref[...]) for step in range(3)
    ]
    maps = sum_thirds(
        times_turned(jnp.concatenate(stack, axis=0).astype(BF16), jnp.where(at_lane, 1.0, 0.0).astype(BF16))
    )
    for copy in copies[:4]:
        copy.wait()
    total = at + 2 * cells_row
    fields_ref[at:total, :] = maps[cells_row:]
    for number in range(3, 6):
        rows = slice(number * cells_row, (number + 1) * cells_row)
        fields_ref[rows, :] = fields_ref[rows, :] + maps[:cells_row]
    rows = fields_ref[0:total, :]
    spare = 2 * LANES - total
    edge_columns(jnp.concatenate([rows, jnp.zeros((spare, LANES), F32)], axis=0), side_ref)
    sides = start_sides(side_ref, outputs[3], sent_sides)
    height = total // TILE_X
    for x in range(TILE_X):
        slab = fields_ref[pl.ds(x, height, stride=TILE_X), :]
        if x < RIM:
            low_ref[x * height : (x + 1) * height, :] = slab
        if x >= TILE_X - RIM:
            at = x - TILE_X + RIM
            high_ref[at * height : (at + 1) * height, :] = slab
    writes = [
        pltpu.make_async_copy(source, target, sent.at[number])
        for number, (source, target) in enumerate(zip((fields_ref.at[0:total], high_ref, low_ref), outputs))
    ]
    for copy in writes:
        copy.start()
    for copy in writes:
        copy.wait()
    wait_sides(sides)


def slots_body(capacity, devices, cols_y, owner_ref, start_ref, slot_ref, row_ref, cover_ref, place_ref, rank_ref):
    blocks = owner_ref.shape[0]
    group = 32
    before = jnp.where(iota((LANES, 2 * LANES), 0) < iota((LANES, 2 * LANES), 1), 1.0, 0.0).astype(BF16)
    rank_ref[...] = jnp.zeros_like(rank_ref)

    def count_group(number, carry):
        names = iota((group, LANES), 0) + number * group
        hot = [names == owner_ref[b : b + 1, :] for b in range(blocks)]
        marks = jnp.concatenate([jnp.where(h, 1.0, 0.0) for h in hot], axis=0).astype(BF16)
        counts = times(marks, before)
        total = jnp.zeros((group, LANES), F32)
        for b in range(blocks):
            part = counts[b * group : (b + 1) * group]
            rank_ref[b : b + 1, :] = rank_ref[b : b + 1, :] + jnp.sum(
                jnp.where(hot[b], part[:, :LANES] + total, 0.0), axis=0, keepdims=True
            )
            total = total + part[:, LANES:]
        return carry

    if devices == group:
        count_group(0, 0)
    else:
        lax.fori_loop(0, devices // group, count_group, 0)
    slot = owner_ref[...] * capacity + rank_ref[...].astype(I32)
    slot_ref[...] = slot >> 7
    low = slot & (LANES - 1)
    span = cols_y - GAUGE + 1
    start = start_ref[...]
    row = ((start.astype(F32) + 0.5) * (1.0 / span)).astype(I32)
    row_ref[...] = row
    first = start - row * span
    down = iota((LANES, LANES), 0)
    for b in range(blocks):
        lanes = slice(b * LANES, (b + 1) * LANES)
        offset = down - first[b : b + 1, :]
        cover_ref[:, lanes] = jnp.where((offset >= 0) & (offset < GAUGE), 1.0, 0.0).astype(BF16)
        place_ref[:, lanes] = jnp.where(down == low[b : b + 1, :], 1.0, 0.0).astype(BF16)


def forward_body(
    fields_ref,
    higher_ref,
    lower_ref,
    recv_ref,
    slot_ref,
    row_ref,
    weight_ref,
    channel_ref,
    cover_ref,
    place_ref,
    out_ref,
    strain_ref,
    medium_ref,
    wide_ref,
    source_ref,
    state_ref,
    near_ref,
    turn_ref,
    sides_ref,
    spread_ref,
):
    depth = medium_ref.shape[0] // 3
    cells_row = depth * TILE_X
    rims = rim_rows(recv_ref, turn_ref)
    height = fields_ref.shape[0] // TILE_X
    sides_ref[...] = jnp.zeros_like(sides_ref)
    for x in range(RIM):
        slab = slice(x * height, (x + 1) * height)
        sides_ref[0, pl.ds(x, height, stride=TILE_X), :] = higher_ref[slab, :]
        sides_ref[1, pl.ds(x + TILE_X - RIM, height, stride=TILE_X), :] = lower_ref[slab, :]
    lay_planes(wide_ref, source_ref, 0, fields_ref, sides_ref.at[0], sides_ref.at[1])
    lay_planes(wide_ref, source_ref, LANES, *rims)
    first = 9 * depth
    medium_ref[...] = wide_ref[first:]
    for plane in range(3 * depth):
        near_ref[plane] = narrowed(wide_ref[first + plane])
    state, near = fields_of(state_ref, 9, depth), fields_of(near_ref, 3, depth)
    for step in range(3):

        def emit(z, strains, step=step):
            for number, strain in enumerate(strains):
                base = ((step * 6 + number) * depth + z) * TILE_X
                strain_ref[base : base + TILE_X, :] = strain[0:TILE_X, 0:LANES]

        if step == 0:
            advance(fields_of(wide_ref, 9, depth), fields_of(wide_ref, 3, depth, 9), emit, state)
            continue
        for z in range(depth):
            load = source_ref[(step - 1) * depth + z]
            for number in range(3, 6):
                state[number][z] = state[number][z] + load
        advance(state, near, emit, state if step == 1 else None)
    axial = jnp.concatenate(
        [strain_ref[step * 6 * cells_row : (step * 6 + 2) * cells_row, :] for step in range(3)], axis=0
    )
    axial = jnp.concatenate(pieces(axial), axis=0).astype(BF16)
    rows_down = iota((cells_row, LANES), 0)
    slots_down = packed_iota(LANES, 2)
    for block in range(slot_ref.shape[0]):
        lanes = slice(block * LANES, (block + 1) * LANES)
        if block % 2 == 0:
            both = sum_thirds(times(axial, cover_ref[:, block * LANES : (block + 2) * LANES]))
        windows = both[:, :LANES] if block % 2 == 0 else both[:, LANES:]
        at_row = rows_down == row_ref[block : block + 1, :]
        weight_x, weight_y = weight_ref[0:1, lanes], weight_ref[1:2, lanes]
        sums = []
        for step in range(3):
            base = 2 * step * cells_row
            axial_sum = (
                weight_x * windows[base : base + cells_row]
                + weight_y * windows[base + cells_row : base + 2 * cells_row]
            )
            sums.append(jnp.sum(jnp.where(at_row, axial_sum, 0.0), axis=0, keepdims=True))
        sums.append(channel_ref[block : block + 1, :].astype(F32))
        values = jnp.concatenate(sums + sums, axis=0)
        in_slot = slots_down == packed_rows(slot_ref[block : block + 1, :], LANES)
        for third, piece in enumerate(pieces(values)):
            tile = jnp.concatenate([piece, piece], axis=0).astype(BF16)
            spread_ref[third * LANES : (third + 1) * LANES, lanes] = jnp.where(
                in_slot, jnp.concatenate([tile] * (LANES // 16), axis=0), jnp.zeros((), BF16)
            )
    out_ref[...] = sum_thirds(times_turned(spread_ref[...], place_ref[...]))


def owner_body(arrived_ref, observed_ref, residual_ref, reply_ref, values_ref, place_ref, held_ref):
    groups = arrived_ref.shape[0] // 4
    parts = observed_ref.shape[1] // LANES
    down = packed_iota(LANES)
    part_down = iota((parts, LANES), 0)
    nothing = jnp.zeros((parts, LANES), F32)
    numbers = [arrived_ref[4 * s + 3 : 4 * s + 4, :].astype(I32) for s in range(groups)]
    for s in range(groups):
        lanes = slice(s * LANES, (s + 1) * LANES)
        place_ref[:, lanes] = jnp.where(
            down == packed_rows(numbers[s] & (LANES - 1), LANES), jnp.ones((), BF16), jnp.zeros((), BF16)
        )
        at_part = part_down == (numbers[s] >> 7)
        thirds = pieces(arrived_ref[4 * s : 4 * s + 3, :])
        stack = []
        for third in thirds:
            for step in range(3):
                stack.append(jnp.where(at_part, third[step : step + 1, :], 0.0))
        stack.append(nothing)
        values_ref[:, lanes] = jnp.concatenate(stack, axis=0).astype(BF16)
    rows = 3 * parts
    sums = sum_thirds(times_turned(values_ref[...], place_ref[...])[: 3 * rows])
    for step in range(3):
        for part in range(parts):
            at = step * parts + part
            held_ref[at : at + 1, :] = observed_ref[step : step + 1, part * LANES : (part + 1) * LANES]
    held_ref[rows:, :] = nothing
    held_ref[0:rows, :] = sums - held_ref[0:rows, :]
    for step in range(3):
        for part in range(parts):
            at = step * parts + part
            residual_ref[step : step + 1, part * LANES : (part + 1) * LANES] = held_ref[at : at + 1, :]
    residual = jnp.concatenate(two_pieces(held_ref[...]), axis=0).astype(BF16)
    for s in range(groups):
        if s % 2 == 0:
            both = sum_halves(times(residual, place_ref[:, s * LANES : (s + 2) * LANES]))
        found = both[:, :LANES] if s % 2 == 0 else both[:, LANES:]
        at_part = part_down == (numbers[s] >> 7)
        for step in range(3):
            reply_ref[4 * s + step : 4 * s + step + 1, :] = jnp.sum(
                jnp.where(at_part, found[step * parts : (step + 1) * parts], 0.0), axis=0, keepdims=True
            )
        reply_ref[4 * s + 3 : 4 * s + 4, :] = jnp.zeros((1, LANES), F32)


def reached():
    return [(turn, distance) for turn in range(3) for distance in range(RIM - turn)]


def load_body(
    arrived_ref,
    slot_ref,
    row_ref,
    weight_ref,
    cover_ref,
    place_ref,
    load_ref,
    high_ref,
    low_ref,
    out_ref,
    spread_ref,
    side_ref,
    held_ref,
    sent_sides,
):
    cells_row = load_ref.shape[0] // 6
    stack_rows = load_ref.shape[0]
    arrived = jnp.concatenate(two_pieces(arrived_ref[...]), axis=0).astype(BF16)
    slots_down = iota((LANES, LANES), 0) >> 2
    rows_down = packed_iota(cells_row)
    for block in range(slot_ref.shape[0]):
        lanes = slice(block * LANES, (block + 1) * LANES)
        if block % 2 == 0:
            both = sum_halves(times(arrived, place_ref[:, block * LANES : (block + 2) * LANES]))
        found = both[:, :LANES] if block % 2 == 0 else both[:, LANES:]
        found = jnp.where(slots_down == slot_ref[block : block + 1, :], found, 0.0)
        folded = found[0:8]
        for part in range(1, LANES // 8):
            folded = folded + found[8 * part : 8 * part + 8]
        folded = folded + pltpu.roll(folded, 4, 0)
        at_row = rows_down == packed_rows(row_ref[block : block + 1, :], cells_row)
        for turn in range(3):
            back = folded[2 - turn : 3 - turn, :]
            for part in range(2):
                for half, piece in enumerate(two_pieces(weight_ref[part : part + 1, lanes] * back)):
                    base = half * stack_rows + (2 * turn + part) * cells_row
                    spread_ref[base : base + cells_row, lanes] = jnp.where(
                        at_row, packed_rows(piece, cells_row), jnp.zeros((), BF16)
                    )
    load = sum_halves(times_turned(spread_ref[...], cover_ref[...]))
    spare = LANES - stack_rows
    edge_columns(jnp.concatenate([load, jnp.zeros((spare, LANES), F32)], axis=0), side_ref)
    sides = start_sides(side_ref, out_ref, sent_sides)
    load_ref[...] = load
    held_ref[0:stack_rows, :] = load
    count = stack_rows // (3 * TILE_X)
    for at, (turn, distance) in enumerate(reached()):
        rows = slice(at * count, (at + 1) * count)
        first = turn * count * TILE_X
        low_ref[rows, :] = held_ref[pl.ds(first + distance, count, stride=TILE_X), :]
        high_ref[rows, :] = held_ref[pl.ds(first + TILE_X - 1 - distance, count, stride=TILE_X), :]
    wait_sides(sides)


def adjoint_body(
    load_ref,
    higher_ref,
    lower_ref,
    recv_ref,
    strain_ref,
    medium_ref,
    residual_ref,
    gradient_ref,
    residual_out_ref,
    first_ref,
    later_ref,
    velocity_ref,
    state_ref,
    near_ref,
    turn_ref,
    sides_ref,
):
    depth = medium_ref.shape[0] // 3
    rims = rim_rows(recv_ref, turn_ref)
    sides_ref[...] = jnp.zeros_like(sides_ref)
    count = load_ref.shape[0] // (3 * TILE_X)
    for at, (turn, distance) in enumerate(reached()):
        rows = slice(at * count, (at + 1) * count)
        first = turn * count * TILE_X
        sides_ref[0, pl.ds(first + distance, count, stride=TILE_X), :] = higher_ref[rows, :]
        sides_ref[1, pl.ds(first + TILE_X - 1 - distance, count, stride=TILE_X), :] = lower_ref[rows, :]
    lay_planes(first_ref, later_ref, 0, load_ref, sides_ref.at[0], sides_ref.at[1])
    lay_planes(first_ref, later_ref, LANES, *rims)
    for plane in range(3 * depth):
        near_ref[plane] = narrowed(medium_ref[plane])
    gradient_ref[...] = jnp.zeros_like(gradient_ref)
    residual_out_ref[...] = residual_ref[...]
    state, near, medium = (
        fields_of(state_ref, 9, depth),
        fields_of(near_ref, 3, depth),
        fields_of(medium_ref, 3, depth),
    )

    def add_terms(turn, z, strains):
        dilation, dilation_back, doubled, product = None, None, None, None
        for number, strain in enumerate(strains):
            base = (((2 - turn) * 6 + number) * depth + z) * TILE_X
            forward = strain_ref[base : base + TILE_X, :]
            if number < 3:
                dilation = forward if dilation is None else dilation + forward
            if strain is None:
                continue
            back = strain[0:TILE_X, 0:LANES]
            term = forward * back
            if number < 3:
                dilation_back = back if dilation_back is None else dilation_back + back
                doubled = term if doubled is None else doubled + term
            else:
                product = term if product is None else product + term
        for part, term in enumerate((dilation * dilation_back, 2.0 * doubled + product)):
            base = (part * depth + z) * TILE_X
            gradient_ref[base : base + TILE_X, :] = gradient_ref[base : base + TILE_X, :] + term

    loads, velocity = fields_of(first_ref, 2, depth), fields_of(velocity_ref, 2, depth)
    for z in range(depth):
        scale = STEP * medium[2][z]
        velocity[0][z] = scale * ahead_x(loads[0][z])
        velocity[1][z] = scale * ahead_y(loads[1][z])
        state[0][z] = narrowed(velocity[0][z])
        state[1][z] = narrowed(velocity[1][z])
        state[2][z] = jnp.zeros((SPAN_NEAR, SPAN_Y), F32)
    for z in range(depth):
        along_x, along_y = velocity[0][z], velocity[1][z]
        strain_x, strain_y = behind_x(along_x), behind_y(along_y)
        sheared = (
            ahead_y(along_x) + ahead_x(along_y),
            ahead_z(velocity[0], z),
            ahead_z(velocity[1], z),
        )
        add_terms(0, z, (strain_x, strain_y, None) + sheared)
        dilated = medium[0][z] * (strain_x + strain_y)
        shear = medium[1][z]
        state[3][z] = narrowed(loads[0][z] + STEP * (dilated + 2.0 * shear * strain_x))
        state[4][z] = narrowed(loads[1][z] + STEP * (dilated + 2.0 * shear * strain_y))
        state[5][z] = narrowed(STEP * dilated)
        for number, strain in enumerate(sheared):
            state[6 + number][z] = narrowed(STEP * shear * strain)
    for turn in (1, 2):
        for part in range(2):
            for z in range(depth):
                load = later_ref[(2 * (turn - 1) + part) * depth + z]
                state[3 + part][z] = state[3 + part][z] + load
        advance(state, near, functools.partial(add_terms, turn), state if turn == 1 else None)


def shards(
    initial_state,
    lame_lambda,
    shear_modulus,
    buoyancy,
    source_cells,
    source_wavelet,
    segment_start,
    segment_weight,
    partial_owner,
    partial_channel,
    observed_data,
):
    depth, rows_x, cols_y = lame_lambda.shape
    part_count = segment_start.shape[0]
    count_x, count_y = lax.axis_size("gx"), lax.axis_size("gy")
    devices = count_x * count_y
    capacity = max(2, 2 * part_count // devices)
    slot_groups = devices * capacity // LANES
    blocks = part_count // LANES
    per_group = LANES // capacity
    cells_row = depth * rows_x
    both = ("gx", "gy")
    up = [(i, i + 1) for i in range(count_x - 1)]
    down = [(j, i) for i, j in up]
    shape = jax.ShapeDtypeStruct

    def exchange(chunks):
        return lax.all_to_all(chunks, both, split_axis=0, concat_axis=0, tiled=True)

    def to_owners(rows):
        chunks = rows.reshape(slot_groups, 4, per_group, capacity).transpose(0, 2, 1, 3)
        back = exchange(chunks.reshape(devices, 4, capacity)).reshape(slot_groups, per_group, 4, capacity)
        return back.transpose(0, 2, 1, 3).reshape(slot_groups * 4, LANES)

    trimmed = shape((14 * depth * RIM, cols_y), F32)
    fields, high, low, edges = call_kernel(
        pack_body,
        "pack_edges",
        [shape((14 * cells_row, cols_y), F32), trimmed, trimmed, shape((devices, 1, 2 * RIM * LANES), F32)],
        [
            pltpu.VMEM((14 * cells_row + SPARE, cols_y), F32),
            pltpu.VMEM(trimmed.shape, F32),
            pltpu.VMEM(trimmed.shape, F32),
            pltpu.VMEM((2, 1, 2 * RIM * LANES), F32),
            pltpu.VMEM((1, source_cells.shape[0]), I32),
            pltpu.VMEM(source_wavelet.shape, F32),
            pltpu.SemaphoreType.DMA((6,)),
            pltpu.SemaphoreType.DMA((3,)),
            pltpu.SemaphoreType.DMA((6,)),
        ],
        *[values.reshape(-1, cols_y) for values in (initial_state, lame_lambda, shear_modulus, buoyancy)],
        source_cells.reshape(1, -1),
        source_wavelet,
        place=pl.ANY,
        place_out=pl.ANY,
        room=60 * 1024 * 1024,
    )
    lower = lax.ppermute(high, "gx", up)
    higher = lax.ppermute(low, "gx", down)
    rims = exchange(edges)
    channels = partial_channel.reshape(blocks, LANES)
    slot, row, cover, place = call_kernel(
        functools.partial(slots_body, capacity, devices, cols_y),
        "segment_slots",
        [
            shape((blocks, LANES), I32),
            shape((blocks, LANES), I32),
            shape((cols_y, part_count), BF16),
            shape((LANES, part_count), BF16),
        ],
        [pltpu.VMEM((blocks, LANES), F32)],
        partial_owner.reshape(blocks, LANES),
        segment_start.reshape(blocks, LANES),
    )
    partials, strains, medium = call_kernel(
        forward_body,
        "forward_run",
        [
            shape((slot_groups * 4, LANES), F32),
            shape((18 * cells_row, cols_y), F32),
            shape((3 * depth, SPAN_X, SPAN_Y), F32),
        ],
        [
            pltpu.VMEM((12 * depth, SPAN_X, SPAN_Y), F32),
            pltpu.VMEM((2 * depth, SPAN_NEAR, SPAN_Y), F32),
            pltpu.VMEM((9 * depth, SPAN_NEAR, SPAN_Y), F32),
            pltpu.VMEM((3 * depth, SPAN_NEAR, SPAN_Y), F32),
            pltpu.VMEM((3, LANES, 2 * LANES), F32),
            pltpu.VMEM((2, 14 * cells_row + SPARE, cols_y), F32),
            pltpu.VMEM((3 * LANES, part_count), BF16),
        ],
        fields,
        higher,
        lower,
        rims,
        slot,
        row,
        segment_weight,
        channels,
        cover,
        place,
    )
    parts = observed_data.shape[1] // LANES
    residuals, reply = call_kernel(
        owner_body,
        "channel_sums",
        [shape(observed_data.shape, F32), shape((slot_groups * 4, LANES), F32)],
        [
            pltpu.VMEM((10 * parts, slot_groups * LANES), BF16),
            pltpu.VMEM((LANES, slot_groups * LANES), BF16),
            pltpu.VMEM((4 * parts, LANES), F32),
        ],
        to_owners(partials),
        observed_data,
    )
    reach = shape((len(reached()) * 2 * depth, cols_y), F32)
    loads, load_high, load_low, load_edges = call_kernel(
        load_body,
        "segment_loads",
        [shape((6 * cells_row, cols_y), F32), reach, reach, shape((devices, 1, RIM * LANES), F32)],
        [
            pltpu.VMEM((12 * cells_row, part_count), BF16),
            pltpu.VMEM((2, 1, RIM * LANES), F32),
            pltpu.VMEM((6 * cells_row + SPARE, cols_y), F32),
            pltpu.SemaphoreType.DMA((6,)),
        ],
        to_owners(reply),
        slot,
        row,
        segment_weight,
        cover,
        place,
        place_out=(pltpu.VMEM, pltpu.VMEM, pltpu.VMEM, pl.ANY),
    )
    load_lower = lax.ppermute(load_high, "gx", up)
    load_higher = lax.ppermute(load_low, "gx", down)
    load_rims = exchange(load_edges)
    gradients, residuals = call_kernel(
        adjoint_body,
        "adjoint_run",
        [shape((2 * cells_row, cols_y), F32), shape(observed_data.shape, F32)],
        [
            pltpu.VMEM((2 * depth, SPAN_X, SPAN_Y), F32),
            pltpu.VMEM((4 * depth, SPAN_NEAR, SPAN_Y), F32),
            pltpu.VMEM((2 * depth, SPAN_X, SPAN_Y), F32),
            pltpu.VMEM((9 * depth, SPAN_NEAR, SPAN_Y), F32),
            pltpu.VMEM((3 * depth, SPAN_NEAR, SPAN_Y), F32),
            pltpu.VMEM((3, LANES, LANES), F32),
            pltpu.VMEM((2, 6 * cells_row + SPARE, cols_y), F32),
        ],
        loads,
        load_higher,
        load_lower,
        load_rims,
        strains,
        medium,
        residuals,
    )
    return (residuals, gradients.reshape(2, depth, rows_x, cols_y))


def solution(mesh):
    in_specs = (
        P(None, None, "gx", "gy"),
        P(None, "gx", "gy"),
        P(None, "gx", "gy"),
        P(None, "gx", "gy"),
        P(("gx", "gy")),
        P(None, ("gx", "gy")),
        P(("gx", "gy")),
        P(None, ("gx", "gy")),
        P(("gx", "gy"), None),
        P(("gx", "gy")),
        P(None, ("gx", "gy")),
    )
    out_specs = (P(None, ("gx", "gy")), P(None, None, "gx", "gy"))
    return jax.shard_map(shards, mesh=mesh, in_specs=in_specs, out_specs=out_specs, check_vma=False)
```

```python
import functools

import jax
import jax.numpy as jnp
from jax import lax
from jax.experimental import pallas as pl
from jax.experimental.pallas import tpu as pltpu
from jax.sharding import PartitionSpec as P

GAUGE = 8
STEP = 0.25
RIM = 3
LANES = 128
TILE_X = 4
SPARE = 8
SPAN_X = 16
SPAN_NEAR = 8
SPAN_Y = 256
F32, BF16, I32 = jnp.float32, jnp.bfloat16, jnp.int32
NEAR = tuple((dx, dy) for dx in (-1, 0, 1) for dy in (-1, 0, 1))


def call_kernel(
    body, name, outs, scratch, *args, place=pltpu.VMEM, place_out=pltpu.VMEM, room=24 * 1024 * 1024
):
    spaces = place_out if isinstance(place_out, tuple) else (place_out,) * len(outs)
    return pl.pallas_call(
        body,
        name=name,
        out_shape=outs,
        in_specs=[pl.BlockSpec(memory_space=place)] * len(args),
        out_specs=[pl.BlockSpec(memory_space=space) for space in spaces],
        scratch_shapes=scratch,
        compiler_params=pltpu.CompilerParams(vmem_limit_bytes=room),
    )(*args)


def pieces(values):
    high = values.astype(BF16).astype(F32)
    rest = values - high
    middle = rest.astype(BF16).astype(F32)
    return high, middle, rest - middle


def iota(shape, dim):
    return lax.broadcasted_iota(I32, shape, dim)


def times(left, right):
    return lax.dot_general(left, right, (((1,), (0,)), ((), ())), preferred_element_type=F32)


def times_turned(left, right):
    return lax.dot_general(left, right, (((1,), (1,)), ((), ())), preferred_element_type=F32)


def packed_rows(row, height):
    tile = jnp.broadcast_to(row.astype(F32), (16, row.shape[1])).astype(BF16)
    return jnp.concatenate([tile] * (height // 16), axis=0) if height > 16 else tile


def packed_iota(height, shift=0):
    return (iota((height, LANES), 0) >> shift).astype(F32).astype(BF16)


def two_pieces(values):
    high = values.astype(BF16).astype(F32)
    return high, values - high


def sum_halves(values):
    half = values.shape[0] // 2
    return values[:half] + values[half:]


def sum_thirds(values):
    third = values.shape[0] // 3
    return values[:third] + values[third : 2 * third] + values[2 * third :]


def neighbour(dx, dy):
    count_x, count_y = lax.axis_size("gx"), lax.axis_size("gy")
    at_x, at_y = lax.axis_index("gx") + dx, lax.axis_index("gy") + dy
    inside = (at_x >= 0) & (at_x < count_x) & (at_y >= 0) & (at_y < count_y)
    return jnp.where(inside, at_x * count_y + at_y, 0), inside


def edge_columns(rows, side_ref):
    width = rows.shape[0]
    turned = rows.T
    for side, base in ((0, 0), (1, LANES - RIM)):
        for column in range(RIM):
            side_ref[side, 0:1, column * width : (column + 1) * width] = turned[base + column : base + column + 1, :]


def start_sides(side_ref, out_ref, sent):
    sides = []
    for number, (dx, dy) in enumerate((dx, dy) for dx, dy in NEAR if dy):
        index, inside = neighbour(dx, dy)
        source, target = side_ref.at[1 if dy > 0 else 0], out_ref.at[index]
        sides.append((inside, pltpu.make_async_copy(source, target, sent.at[number])))
    for inside, copy in sides:
        pl.when(inside)(copy.start)
    return sides


def wait_sides(sides):
    for inside, copy in sides:
        pl.when(inside)(copy.wait)


def arrived_chunk(recv_ref, dx, dy):
    index, inside = neighbour(dx, dy)
    return jnp.where(inside, recv_ref[index], 0.0)


def rim_rows(recv_ref, turn_ref):
    width = turn_ref.shape[2]
    turn_ref[...] = jnp.zeros_like(turn_ref)
    for block, dx in enumerate((0, 1, -1)):
        for dy, first in ((1, 0), (-1, LANES - RIM)):
            chunk = arrived_chunk(recv_ref, dx, dy)
            for column in range(RIM):
                turn_ref[block, first + column : first + column + 1, :] = chunk[
                    :, column * width : (column + 1) * width
                ]
    return [turn_ref[block].T for block in range(3)]


def lay_planes(wide_ref, narrow_ref, lane, centre, higher, lower):
    row = iota((8, LANES), 0)
    wide = wide_ref.shape[0]
    lanes = slice(lane, lane + LANES)
    for plane in range(wide + narrow_ref.shape[0]):
        rows = slice(8 * (plane // 2), 8 * (plane // 2) + 8)
        mid, high, low = centre[rows], higher[rows], lower[rows]
        if plane % 2:
            mid = pltpu.roll(mid, TILE_X, 0)
        else:
            high, low = pltpu.roll(high, TILE_X, 0), pltpu.roll(low, TILE_X, 0)
        near = jnp.where(row < TILE_X, mid, high)
        if plane < wide:
            wide_ref[plane, 0:8, lanes] = near
            wide_ref[plane, 8:16, lanes] = jnp.where(row < TILE_X, 0.0, low)
        else:
            narrow_ref[plane - wide, :, lanes] = jnp.where(row < SPAN_NEAR - 2, near, low)


def narrowed(plane):
    row = iota((SPAN_NEAR, plane.shape[1]), 0)
    return jnp.where(row < SPAN_NEAR - 2, plane[:SPAN_NEAR], plane[SPAN_NEAR:])


def ahead_x(plane):
    return pltpu.roll(plane, plane.shape[0] - 1, 0) - plane


def behind_x(plane):
    return plane - pltpu.roll(plane, 1, 0)


def ahead_y(plane):
    return pltpu.roll(plane, SPAN_Y - 1, 1) - plane


def behind_y(plane):
    return plane - pltpu.roll(plane, 1, 1)


def ahead_z(planes, z):
    return planes[z + 1] - planes[z] if z + 1 < len(planes) else -planes[z]


def behind_z(planes, z):
    return planes[z] - planes[z - 1] if z else planes[z]


class Planes:
    def __init__(self, ref, first, depth):
        self.ref, self.first, self.depth = ref, first, depth

    def __len__(self):
        return self.depth

    def __getitem__(self, z):
        return self.ref[self.first + z]

    def __setitem__(self, z, plane):
        self.ref[self.first + z] = plane


def fields_of(ref, count, depth, first=0):
    return [Planes(ref, (first + number) * depth, depth) for number in range(count)]


def strain_rates(velocity, z):
    along_x, along_y, along_z = [field[z] for field in velocity]
    return (
        behind_x(along_x),
        behind_y(along_y),
        behind_z(velocity[2], z),
        ahead_y(along_x) + ahead_x(along_y),
        ahead_z(velocity[0], z) + ahead_x(along_z),
        ahead_z(velocity[1], z) + ahead_y(along_z),
    )


def new_stress(stress, strains, lame_lambda, shear_modulus, z):
    dilated = lame_lambda[z] * (strains[0] + strains[1] + strains[2])
    shear = shear_modulus[z]
    normal = [stress[n][z] + STEP * (dilated + 2.0 * shear * strains[n]) for n in range(3)]
    return normal + [stress[n][z] + STEP * shear * strains[n] for n in range(3, 6)]


def advance(state, medium, emit, target):
    velocity, stress = state[:3], state[3:]
    lame_lambda, shear_modulus, buoyancy = medium
    depth = len(buoyancy)
    wide = target is not None and target is not state
    for z in range(depth):
        scale = STEP * buoyancy[z]
        accel = (
            ahead_x(stress[0][z]) + behind_y(stress[3][z]) + behind_z(stress[4], z),
            behind_x(stress[3][z]) + ahead_y(stress[1][z]) + behind_z(stress[5], z),
            behind_x(stress[4][z]) + behind_y(stress[5][z]) + ahead_z(stress[2], z),
        )
        for number in range(3):
            moved = velocity[number][z] + scale * accel[number]
            velocity[number][z] = moved
            if wide:
                target[number][z] = narrowed(moved)
    for z in range(depth):
        strains = strain_rates(velocity, z)
        emit(z, strains)
        if target is not None:
            for number, plane in enumerate(new_stress(stress, strains, lame_lambda, shear_modulus, z)):
                target[3 + number][z] = narrowed(plane) if wide else plane


def pack_body(*refs):
    inputs, outputs, scratch = refs[:6], refs[6:10], refs[10:]
    fields_ref, high_ref, low_ref, side_ref, cells_ref, wavelet_ref, arrived, sent, sent_sides = scratch
    third = inputs[0].shape[0] // 3
    sources = [inputs[0].at[part * third : (part + 1) * third] for part in range(3)] + list(inputs[1:4])
    targets, at = [], 0
    for source in sources:
        targets.append(fields_ref.at[at : at + source.shape[0]])
        at = at + source.shape[0]
    sources += inputs[4:]
    copies = [
        pltpu.make_async_copy(source, target, arrived.at[number])
        for number, (source, target) in enumerate(zip(sources, targets + [cells_ref, wavelet_ref]))
    ]
    for copy in copies[6:] + copies[:6]:
        copy.start()
    copies[6].wait()
    copies[7].wait()
    cells_row = inputs[1].shape[0]
    cells = cells_ref[...]
    count = cells.shape[1]
    at_lane = iota((LANES, count), 0) == (cells & (LANES - 1))
    at_row = iota((cells_row, count), 0) == (cells >> (LANES.bit_length() - 1))
    stack = [
        jnp.where(at_row, third[step : step + 1, :], 0.0) for third in pieces(wavelet_ref[...]) for step in range(3)
    ]
    maps = sum_thirds(
        times_turned(jnp.concatenate(stack, axis=0).astype(BF16), jnp.where(at_lane, 1.0, 0.0).astype(BF16))
    )
    for copy in copies[:6]:
        copy.wait()
    total = at + 2 * cells_row
    fields_ref[at:total, :] = maps[cells_row:]
    for number in range(3, 6):
        rows = slice(number * cells_row, (number + 1) * cells_row)
        fields_ref[rows, :] = fields_ref[rows, :] + maps[:cells_row]
    rows = fields_ref[0:total, :]
    spare = 2 * LANES - total
    edge_columns(jnp.concatenate([rows, jnp.zeros((spare, LANES), F32)], axis=0), side_ref)
    sides = start_sides(side_ref, outputs[3], sent_sides)
    height = total // TILE_X
    for x in range(TILE_X):
        slab = fields_ref[pl.ds(x, height, stride=TILE_X), :]
        if x < RIM:
            low_ref[x * height : (x + 1) * height, :] = slab
        if x >= TILE_X - RIM:
            at = x - TILE_X + RIM
            high_ref[at * height : (at + 1) * height, :] = slab
    writes = [
        pltpu.make_async_copy(source, target, sent.at[number])
        for number, (source, target) in enumerate(zip((fields_ref.at[0:total], high_ref, low_ref), outputs))
    ]
    for copy in writes:
        copy.start()
    for copy in writes:
        copy.wait()
    wait_sides(sides)


def slots_body(capacity, devices, cols_y, owner_ref, start_ref, slot_ref, row_ref, cover_ref, place_ref, rank_ref):
    blocks = owner_ref.shape[0]
    group = 32
    before = jnp.where(iota((LANES, 2 * LANES), 0) < iota((LANES, 2 * LANES), 1), 1.0, 0.0).astype(BF16)
    rank_ref[...] = jnp.zeros_like(rank_ref)

    def count_group(number, carry):
        names = iota((group, LANES), 0) + number * group
        hot = [names == owner_ref[b : b + 1, :] for b in range(blocks)]
        marks = jnp.concatenate([jnp.where(h, 1.0, 0.0) for h in hot], axis=0).astype(BF16)
        counts = times(marks, before)
        total = jnp.zeros((group, LANES), F32)
        for b in range(blocks):
            part = counts[b * group : (b + 1) * group]
            rank_ref[b : b + 1, :] = rank_ref[b : b + 1, :] + jnp.sum(
                jnp.where(hot[b], part[:, :LANES] + total, 0.0), axis=0, keepdims=True
            )
            total = total + part[:, LANES:]
        return carry

    if devices == group:
        count_group(0, 0)
    else:
        lax.fori_loop(0, devices // group, count_group, 0)
    slot = owner_ref[...] * capacity + rank_ref[...].astype(I32)
    slot_ref[...] = slot >> 7
    low = slot & (LANES - 1)
    span = cols_y - GAUGE + 1
    start = start_ref[...]
    row = ((start.astype(F32) + 0.5) * (1.0 / span)).astype(I32)
    row_ref[...] = row
    first = start - row * span
    down = iota((LANES, LANES), 0)
    for b in range(blocks):
        lanes = slice(b * LANES, (b + 1) * LANES)
        offset = down - first[b : b + 1, :]
        cover_ref[:, lanes] = jnp.where((offset >= 0) & (offset < GAUGE), 1.0, 0.0).astype(BF16)
        place_ref[:, lanes] = jnp.where(down == low[b : b + 1, :], 1.0, 0.0).astype(BF16)


def forward_body(
    fields_ref,
    higher_ref,
    lower_ref,
    recv_ref,
    slot_ref,
    row_ref,
    weight_ref,
    channel_ref,
    cover_ref,
    place_ref,
    out_ref,
    strain_ref,
    medium_ref,
    wide_ref,
    source_ref,
    state_ref,
    near_ref,
    turn_ref,
    sides_ref,
    spread_ref,
):
    depth = medium_ref.shape[0] // 3
    cells_row = depth * TILE_X
    rims = rim_rows(recv_ref, turn_ref)
    height = fields_ref.shape[0] // TILE_X
    sides_ref[...] = jnp.zeros_like(sides_ref)
    for x in range(RIM):
        slab = slice(x * height, (x + 1) * height)
        sides_ref[0, pl.ds(x, height, stride=TILE_X), :] = higher_ref[slab, :]
        sides_ref[1, pl.ds(x + TILE_X - RIM, height, stride=TILE_X), :] = lower_ref[slab, :]
    lay_planes(wide_ref, source_ref, 0, fields_ref, sides_ref.at[0], sides_ref.at[1])
    lay_planes(wide_ref, source_ref, LANES, *rims)
    first = 9 * depth
    medium_ref[...] = wide_ref[first:]
    for plane in range(3 * depth):
        near_ref[plane] = narrowed(wide_ref[first + plane])
    state, near = fields_of(state_ref, 9, depth), fields_of(near_ref, 3, depth)
    for step in range(3):

        def emit(z, strains, step=step):
            for number, strain in enumerate(strains):
                base = ((step * 6 + number) * depth + z) * TILE_X
                strain_ref[base : base + TILE_X, :] = strain[0:TILE_X, 0:LANES]

        if step == 0:
            advance(fields_of(wide_ref, 9, depth), fields_of(wide_ref, 3, depth, 9), emit, state)
            continue
        for z in range(depth):
            load = source_ref[(step - 1) * depth + z]
            for number in range(3, 6):
                state[number][z] = state[number][z] + load
        advance(state, near, emit, state if step == 1 else None)
    axial = jnp.concatenate(
        [strain_ref[step * 6 * cells_row : (step * 6 + 2) * cells_row, :] for step in range(3)], axis=0
    )
    axial = jnp.concatenate(pieces(axial), axis=0).astype(BF16)
    rows_down = iota((cells_row, LANES), 0)
    slots_down = packed_iota(LANES, 2)
    for block in range(slot_ref.shape[0]):
        lanes = slice(block * LANES, (block + 1) * LANES)
        if block % 2 == 0:
            both = sum_thirds(times(axial, cover_ref[:, block * LANES : (block + 2) * LANES]))
        windows = both[:, :LANES] if block % 2 == 0 else both[:, LANES:]
        at_row = rows_down == row_ref[block : block + 1, :]
        weight_x, weight_y = weight_ref[0:1, lanes], weight_ref[1:2, lanes]
        sums = []
        for step in range(3):
            base = 2 * step * cells_row
            axial_sum = (
                weight_x * windows[base : base + cells_row]
                + weight_y * windows[base + cells_row : base + 2 * cells_row]
            )
            sums.append(jnp.sum(jnp.where(at_row, axial_sum, 0.0), axis=0, keepdims=True))
        sums.append(channel_ref[block : block + 1, :].astype(F32))
        values = jnp.concatenate(sums + sums, axis=0)
        in_slot = slots_down == packed_rows(slot_ref[block : block + 1, :], LANES)
        for third, piece in enumerate(pieces(values)):
            tile = jnp.concatenate([piece, piece], axis=0).astype(BF16)
            spread_ref[third * LANES : (third + 1) * LANES, lanes] = jnp.where(
                in_slot, jnp.concatenate([tile] * (LANES // 16), axis=0), jnp.zeros((), BF16)
            )
    out_ref[...] = sum_thirds(times_turned(spread_ref[...], place_ref[...]))


def owner_body(arrived_ref, observed_ref, residual_ref, reply_ref, values_ref, place_ref, held_ref):
    groups = arrived_ref.shape[0] // 4
    parts = observed_ref.shape[1] // LANES
    down = packed_iota(LANES)
    part_down = iota((parts, LANES), 0)
    nothing = jnp.zeros((parts, LANES), F32)
    numbers = [arrived_ref[4 * s + 3 : 4 * s + 4, :].astype(I32) for s in range(groups)]
    for s in range(groups):
        lanes = slice(s * LANES, (s + 1) * LANES)
        place_ref[:, lanes] = jnp.where(
            down == packed_rows(numbers[s] & (LANES - 1), LANES), jnp.ones((), BF16), jnp.zeros((), BF16)
        )
        at_part = part_down == (numbers[s] >> 7)
        thirds = pieces(arrived_ref[4 * s : 4 * s + 3, :])
        stack = []
        for third in thirds:
            for step in range(3):
                stack.append(jnp.where(at_part, third[step : step + 1, :], 0.0))
        stack.append(nothing)
        values_ref[:, lanes] = jnp.concatenate(stack, axis=0).astype(BF16)
    rows = 3 * parts
    sums = sum_thirds(times_turned(values_ref[...], place_ref[...])[: 3 * rows])
    for step in range(3):
        for part in range(parts):
            at = step * parts + part
            held_ref[at : at + 1, :] = observed_ref[step : step + 1, part * LANES : (part + 1) * LANES]
    held_ref[rows:, :] = nothing
    held_ref[0:rows, :] = sums - held_ref[0:rows, :]
    for step in range(3):
        for part in range(parts):
            at = step * parts + part
            residual_ref[step : step + 1, part * LANES : (part + 1) * LANES] = held_ref[at : at + 1, :]
    residual = jnp.concatenate(two_pieces(held_ref[...]), axis=0).astype(BF16)
    for s in range(groups):
        if s % 2 == 0:
            both = sum_halves(times(residual, place_ref[:, s * LANES : (s + 2) * LANES]))
        found = both[:, :LANES] if s % 2 == 0 else both[:, LANES:]
        at_part = part_down == (numbers[s] >> 7)
        for step in range(3):
            reply_ref[4 * s + step : 4 * s + step + 1, :] = jnp.sum(
                jnp.where(at_part, found[step * parts : (step + 1) * parts], 0.0), axis=0, keepdims=True
            )
        reply_ref[4 * s + 3 : 4 * s + 4, :] = jnp.zeros((1, LANES), F32)


def reached():
    return [(turn, distance) for turn in range(3) for distance in range(RIM - turn)]


def load_body(
    arrived_ref,
    slot_ref,
    row_ref,
    weight_ref,
    cover_ref,
    place_ref,
    load_ref,
    high_ref,
    low_ref,
    out_ref,
    spread_ref,
    side_ref,
    held_ref,
    sent_sides,
):
    cells_row = load_ref.shape[0] // 6
    stack_rows = load_ref.shape[0]
    arrived = jnp.concatenate(two_pieces(arrived_ref[...]), axis=0).astype(BF16)
    slots_down = iota((LANES, LANES), 0) >> 2
    rows_down = packed_iota(cells_row)
    for block in range(slot_ref.shape[0]):
        lanes = slice(block * LANES, (block + 1) * LANES)
        if block % 2 == 0:
            both = sum_halves(times(arrived, place_ref[:, block * LANES : (block + 2) * LANES]))
        found = both[:, :LANES] if block % 2 == 0 else both[:, LANES:]
        found = jnp.where(slots_down == slot_ref[block : block + 1, :], found, 0.0)
        folded = found[0:8]
        for part in range(1, LANES // 8):
            folded = folded + found[8 * part : 8 * part + 8]
        folded = folded + pltpu.roll(folded, 4, 0)
        at_row = rows_down == packed_rows(row_ref[block : block + 1, :], cells_row)
        for turn in range(3):
            back = folded[2 - turn : 3 - turn, :]
            for part in range(2):
                for half, piece in enumerate(two_pieces(weight_ref[part : part + 1, lanes] * back)):
                    base = half * stack_rows + (2 * turn + part) * cells_row
                    spread_ref[base : base + cells_row, lanes] = jnp.where(
                        at_row, packed_rows(piece, cells_row), jnp.zeros((), BF16)
                    )
    cover = jnp.concatenate([cover_ref[0:16, :], cover_ref[LANES - 16 :, :]], axis=0)
    edges = times_turned(cover, spread_ref[0:stack_rows, :]) + times_turned(cover, spread_ref[stack_rows:, :])
    side_ref[...] = jnp.zeros_like(side_ref)
    for side, base in ((0, 0), (1, 32 - RIM)):
        for column in range(RIM):
            lanes = slice(column * LANES, column * LANES + stack_rows)
            side_ref[side, 0:1, lanes] = edges[base + column : base + column + 1, :]
    sides = start_sides(side_ref, out_ref, sent_sides)
    load = sum_halves(times_turned(spread_ref[...], cover_ref[...]))
    load_ref[...] = load
    held_ref[0:stack_rows, :] = load
    count = stack_rows // (3 * TILE_X)
    for at, (turn, distance) in enumerate(reached()):
        rows = slice(at * count, (at + 1) * count)
        first = turn * count * TILE_X
        low_ref[rows, :] = held_ref[pl.ds(first + distance, count, stride=TILE_X), :]
        high_ref[rows, :] = held_ref[pl.ds(first + TILE_X - 1 - distance, count, stride=TILE_X), :]
    wait_sides(sides)


def adjoint_body(
    load_ref,
    higher_ref,
    lower_ref,
    recv_ref,
    strain_ref,
    medium_ref,
    residual_ref,
    gradient_ref,
    residual_out_ref,
    first_ref,
    later_ref,
    velocity_ref,
    state_ref,
    near_ref,
    turn_ref,
    sides_ref,
):
    depth = medium_ref.shape[0] // 3
    rims = rim_rows(recv_ref, turn_ref)
    sides_ref[...] = jnp.zeros_like(sides_ref)
    count = load_ref.shape[0] // (3 * TILE_X)
    for at, (turn, distance) in enumerate(reached()):
        rows = slice(at * count, (at + 1) * count)
        first = turn * count * TILE_X
        sides_ref[0, pl.ds(first + distance, count, stride=TILE_X), :] = higher_ref[rows, :]
        sides_ref[1, pl.ds(first + TILE_X - 1 - distance, count, stride=TILE_X), :] = lower_ref[rows, :]
    lay_planes(first_ref, later_ref, 0, load_ref, sides_ref.at[0], sides_ref.at[1])
    lay_planes(first_ref, later_ref, LANES, *rims)
    for plane in range(3 * depth):
        near_ref[plane] = narrowed(medium_ref[plane])
    residual_out_ref[...] = residual_ref[...]
    state, near, medium = (
        fields_of(state_ref, 9, depth),
        fields_of(near_ref, 3, depth),
        fields_of(medium_ref, 3, depth),
    )

    def add_terms(turn, z, strains):
        dilation, dilation_back, doubled, product = None, None, None, None
        for number, strain in enumerate(strains):
            base = (((2 - turn) * 6 + number) * depth + z) * TILE_X
            forward = strain_ref[base : base + TILE_X, :]
            if number < 3:
                dilation = forward if dilation is None else dilation + forward
            if strain is None:
                continue
            back = strain[0:TILE_X, 0:LANES]
            term = forward * back
            if number < 3:
                dilation_back = back if dilation_back is None else dilation_back + back
                doubled = term if doubled is None else doubled + term
            else:
                product = term if product is None else product + term
        for part, term in enumerate((dilation * dilation_back, 2.0 * doubled + product)):
            base = (part * depth + z) * TILE_X
            rows = slice(base, base + TILE_X)
            gradient_ref[rows, :] = gradient_ref[rows, :] + term if turn else term

    loads, velocity = fields_of(first_ref, 2, depth), fields_of(velocity_ref, 2, depth)
    for z in range(depth):
        scale = STEP * medium[2][z]
        velocity[0][z] = scale * ahead_x(loads[0][z])
        velocity[1][z] = scale * ahead_y(loads[1][z])
        state[0][z] = narrowed(velocity[0][z])
        state[1][z] = narrowed(velocity[1][z])
        state[2][z] = jnp.zeros((SPAN_NEAR, SPAN_Y), F32)
    for z in range(depth):
        along_x, along_y = velocity[0][z], velocity[1][z]
        strain_x, strain_y = behind_x(along_x), behind_y(along_y)
        sheared = (
            ahead_y(along_x) + ahead_x(along_y),
            ahead_z(velocity[0], z),
            ahead_z(velocity[1], z),
        )
        add_terms(0, z, (strain_x, strain_y, None) + sheared)
        dilated = medium[0][z] * (strain_x + strain_y)
        shear = medium[1][z]
        state[3][z] = narrowed(loads[0][z] + STEP * (dilated + 2.0 * shear * strain_x))
        state[4][z] = narrowed(loads[1][z] + STEP * (dilated + 2.0 * shear * strain_y))
        state[5][z] = narrowed(STEP * dilated)
        for number, strain in enumerate(sheared):
            state[6 + number][z] = narrowed(STEP * shear * strain)
    for turn in (1, 2):
        for part in range(2):
            for z in range(depth):
                load = later_ref[(2 * (turn - 1) + part) * depth + z]
                state[3 + part][z] = state[3 + part][z] + load
        advance(state, near, functools.partial(add_terms, turn), state if turn == 1 else None)


def shards(
    initial_state,
    lame_lambda,
    shear_modulus,
    buoyancy,
    source_cells,
    source_wavelet,
    segment_start,
    segment_weight,
    partial_owner,
    partial_channel,
    observed_data,
):
    depth, rows_x, cols_y = lame_lambda.shape
    part_count = segment_start.shape[0]
    count_x, count_y = lax.axis_size("gx"), lax.axis_size("gy")
    devices = count_x * count_y
    capacity = max(2, 2 * part_count // devices)
    slot_groups = devices * capacity // LANES
    blocks = part_count // LANES
    per_group = LANES // capacity
    cells_row = depth * rows_x
    both = ("gx", "gy")
    up = [(i, i + 1) for i in range(count_x - 1)]
    down = [(j, i) for i, j in up]
    shape = jax.ShapeDtypeStruct

    def exchange(chunks):
        return lax.all_to_all(chunks, both, split_axis=0, concat_axis=0, tiled=True)

    def to_owners(rows):
        chunks = rows.reshape(slot_groups, 4, per_group, capacity).transpose(0, 2, 1, 3)
        back = exchange(chunks.reshape(devices, 4, capacity)).reshape(slot_groups, per_group, 4, capacity)
        return back.transpose(0, 2, 1, 3).reshape(slot_groups * 4, LANES)

    trimmed = shape((14 * depth * RIM, cols_y), F32)
    fields, high, low, edges = call_kernel(
        pack_body,
        "pack_edges",
        [shape((14 * cells_row, cols_y), F32), trimmed, trimmed, shape((devices, 1, 2 * RIM * LANES), F32)],
        [
            pltpu.VMEM((14 * cells_row + SPARE, cols_y), F32),
            pltpu.VMEM(trimmed.shape, F32),
            pltpu.VMEM(trimmed.shape, F32),
            pltpu.VMEM((2, 1, 2 * RIM * LANES), F32),
            pltpu.VMEM((1, source_cells.shape[0]), I32),
            pltpu.VMEM(source_wavelet.shape, F32),
            pltpu.SemaphoreType.DMA((8,)),
            pltpu.SemaphoreType.DMA((3,)),
            pltpu.SemaphoreType.DMA((6,)),
        ],
        *[values.reshape(-1, cols_y) for values in (initial_state, lame_lambda, shear_modulus, buoyancy)],
        source_cells.reshape(1, -1),
        source_wavelet,
        place=pl.ANY,
        place_out=pl.ANY,
        room=60 * 1024 * 1024,
    )
    lower = lax.ppermute(high, "gx", up)
    higher = lax.ppermute(low, "gx", down)
    rims = exchange(edges)
    channels = partial_channel.reshape(blocks, LANES)
    slot, row, cover, place = call_kernel(
        functools.partial(slots_body, capacity, devices, cols_y),
        "segment_slots",
        [
            shape((blocks, LANES), I32),
            shape((blocks, LANES), I32),
            shape((cols_y, part_count), BF16),
            shape((LANES, part_count), BF16),
        ],
        [pltpu.VMEM((blocks, LANES), F32)],
        partial_owner.reshape(blocks, LANES),
        segment_start.reshape(blocks, LANES),
    )
    partials, strains, medium = call_kernel(
        forward_body,
        "forward_run",
        [
            shape((slot_groups * 4, LANES), F32),
            shape((18 * cells_row, cols_y), F32),
            shape((3 * depth, SPAN_X, SPAN_Y), F32),
        ],
        [
            pltpu.VMEM((12 * depth, SPAN_X, SPAN_Y), F32),
            pltpu.VMEM((2 * depth, SPAN_NEAR, SPAN_Y), F32),
            pltpu.VMEM((9 * depth, SPAN_NEAR, SPAN_Y), F32),
            pltpu.VMEM((3 * depth, SPAN_NEAR, SPAN_Y), F32),
            pltpu.VMEM((3, LANES, 2 * LANES), F32),
            pltpu.VMEM((2, 14 * cells_row + SPARE, cols_y), F32),
            pltpu.VMEM((3 * LANES, part_count), BF16),
        ],
        fields,
        higher,
        lower,
        rims,
        slot,
        row,
        segment_weight,
        channels,
        cover,
        place,
    )
    parts = observed_data.shape[1] // LANES
    residuals, reply = call_kernel(
        owner_body,
        "channel_sums",
        [shape(observed_data.shape, F32), shape((slot_groups * 4, LANES), F32)],
        [
            pltpu.VMEM((10 * parts, slot_groups * LANES), BF16),
            pltpu.VMEM((LANES, slot_groups * LANES), BF16),
            pltpu.VMEM((4 * parts, LANES), F32),
        ],
        to_owners(partials),
        observed_data,
    )
    reach = shape((len(reached()) * 2 * depth, cols_y), F32)
    loads, load_high, load_low, load_edges = call_kernel(
        load_body,
        "segment_loads",
        [shape((6 * cells_row, cols_y), F32), reach, reach, shape((devices, 1, RIM * LANES), F32)],
        [
            pltpu.VMEM((12 * cells_row, part_count), BF16),
            pltpu.VMEM((2, 1, RIM * LANES), F32),
            pltpu.VMEM((6 * cells_row + SPARE, cols_y), F32),
            pltpu.SemaphoreType.DMA((6,)),
        ],
        to_owners(reply),
        slot,
        row,
        segment_weight,
        cover,
        place,
        place_out=(pltpu.VMEM, pltpu.VMEM, pltpu.VMEM, pl.ANY),
    )
    load_lower = lax.ppermute(load_high, "gx", up)
    load_higher = lax.ppermute(load_low, "gx", down)
    load_rims = exchange(load_edges)
    gradients, residuals = call_kernel(
        adjoint_body,
        "adjoint_run",
        [shape((2 * cells_row, cols_y), F32), shape(observed_data.shape, F32)],
        [
            pltpu.VMEM((2 * depth, SPAN_X, SPAN_Y), F32),
            pltpu.VMEM((4 * depth, SPAN_NEAR, SPAN_Y), F32),
            pltpu.VMEM((2 * depth, SPAN_X, SPAN_Y), F32),
            pltpu.VMEM((9 * depth, SPAN_NEAR, SPAN_Y), F32),
            pltpu.VMEM((3 * depth, SPAN_NEAR, SPAN_Y), F32),
            pltpu.VMEM((3, LANES, LANES), F32),
            pltpu.VMEM((2, 6 * cells_row + SPARE, cols_y), F32),
        ],
        loads,
        load_higher,
        load_lower,
        load_rims,
        strains,
        medium,
        residuals,
    )
    return (residuals, gradients.reshape(2, depth, rows_x, cols_y))


def solution(mesh):
    in_specs = (
        P(None, None, "gx", "gy"),
        P(None, "gx", "gy"),
        P(None, "gx", "gy"),
        P(None, "gx", "gy"),
        P(("gx", "gy")),
        P(None, ("gx", "gy")),
        P(("gx", "gy")),
        P(None, ("gx", "gy")),
        P(("gx", "gy"), None),
        P(("gx", "gy")),
        P(None, ("gx", "gy")),
    )
    out_specs = (P(None, ("gx", "gy")), P(None, None, "gx", "gy"))
    return jax.shard_map(shards, mesh=mesh, in_specs=in_specs, out_specs=out_specs, check_vma=False)
```

```python
import functools

import jax
import jax.numpy as jnp
from jax import lax
from jax.experimental import pallas as pl
from jax.experimental.pallas import tpu as pltpu
from jax.sharding import PartitionSpec as P

GAUGE = 8
STEP = 0.25
RIM = 3
LANES = 128
TILE_X = 4
SPARE = 8
SPAN_X = 16
SPAN_NEAR = 8
SPAN_Y = 256
F32, BF16, I32 = jnp.float32, jnp.bfloat16, jnp.int32
NEAR = tuple((dx, dy) for dx in (-1, 0, 1) for dy in (-1, 0, 1))


def call_kernel(
    body, name, outs, scratch, *args, place=pltpu.VMEM, place_out=pltpu.VMEM, room=24 * 1024 * 1024
):
    spaces = place_out if isinstance(place_out, tuple) else (place_out,) * len(outs)
    return pl.pallas_call(
        body,
        name=name,
        out_shape=outs,
        in_specs=[pl.BlockSpec(memory_space=place)] * len(args),
        out_specs=[pl.BlockSpec(memory_space=space) for space in spaces],
        scratch_shapes=scratch,
        compiler_params=pltpu.CompilerParams(vmem_limit_bytes=room),
    )(*args)


def pieces(values):
    high = values.astype(BF16).astype(F32)
    rest = values - high
    middle = rest.astype(BF16).astype(F32)
    return high, middle, rest - middle


def iota(shape, dim):
    return lax.broadcasted_iota(I32, shape, dim)


def times(left, right):
    return lax.dot_general(left, right, (((1,), (0,)), ((), ())), preferred_element_type=F32)


def times_turned(left, right):
    return lax.dot_general(left, right, (((1,), (1,)), ((), ())), preferred_element_type=F32)


def packed_rows(row, height):
    tile = jnp.broadcast_to(row.astype(F32), (16, row.shape[1])).astype(BF16)
    return jnp.concatenate([tile] * (height // 16), axis=0) if height > 16 else tile


def packed_iota(height, shift=0):
    return (iota((height, LANES), 0) >> shift).astype(F32).astype(BF16)


def two_pieces(values):
    high = values.astype(BF16).astype(F32)
    return high, values - high


def sum_halves(values):
    half = values.shape[0] // 2
    return values[:half] + values[half:]


def sum_thirds(values):
    third = values.shape[0] // 3
    return values[:third] + values[third : 2 * third] + values[2 * third :]


def neighbour(dx, dy):
    count_x, count_y = lax.axis_size("gx"), lax.axis_size("gy")
    at_x, at_y = lax.axis_index("gx") + dx, lax.axis_index("gy") + dy
    inside = (at_x >= 0) & (at_x < count_x) & (at_y >= 0) & (at_y < count_y)
    return jnp.where(inside, at_x * count_y + at_y, 0), inside


def edge_columns(rows, side_ref):
    width = rows.shape[0]
    turned = rows.T
    for side, base in ((0, 0), (1, LANES - RIM)):
        for column in range(RIM):
            side_ref[side, 0:1, column * width : (column + 1) * width] = turned[base + column : base + column + 1, :]


def start_sides(side_ref, out_ref, sent):
    sides = []
    for number, (dx, dy) in enumerate((dx, dy) for dx, dy in NEAR if dy):
        index, inside = neighbour(dx, dy)
        source, target = side_ref.at[1 if dy > 0 else 0], out_ref.at[index]
        sides.append((inside, pltpu.make_async_copy(source, target, sent.at[number])))
    for inside, copy in sides:
        pl.when(inside)(copy.start)
    return sides


def wait_sides(sides):
    for inside, copy in sides:
        pl.when(inside)(copy.wait)


def arrived_chunk(recv_ref, dx, dy):
    index, inside = neighbour(dx, dy)
    return jnp.where(inside, recv_ref[index], 0.0)


def rim_rows(recv_ref, turn_ref):
    width = turn_ref.shape[2]
    turn_ref[...] = jnp.zeros_like(turn_ref)
    for block, dx in enumerate((0, 1, -1)):
        for dy, first in ((1, 0), (-1, LANES - RIM)):
            chunk = arrived_chunk(recv_ref, dx, dy)
            for column in range(RIM):
                turn_ref[block, first + column : first + column + 1, :] = chunk[
                    :, column * width : (column + 1) * width
                ]
    return [turn_ref[block].T for block in range(3)]


def lay_planes(wide_ref, narrow_ref, lane, centre, higher, lower):
    row = iota((8, LANES), 0)
    wide = wide_ref.shape[0]
    lanes = slice(lane, lane + LANES)
    for plane in range(wide + narrow_ref.shape[0]):
        rows = slice(8 * (plane // 2), 8 * (plane // 2) + 8)
        mid, high, low = centre[rows], higher[rows], lower[rows]
        if plane % 2:
            mid = pltpu.roll(mid, TILE_X, 0)
        else:
            high, low = pltpu.roll(high, TILE_X, 0), pltpu.roll(low, TILE_X, 0)
        near = jnp.where(row < TILE_X, mid, high)
        if plane < wide:
            wide_ref[plane, 0:8, lanes] = near
            wide_ref[plane, 8:16, lanes] = jnp.where(row < TILE_X, 0.0, low)
        else:
            narrow_ref[plane - wide, :, lanes] = jnp.where(row < SPAN_NEAR - 2, near, low)


def narrowed(plane):
    row = iota((SPAN_NEAR, plane.shape[1]), 0)
    return jnp.where(row < SPAN_NEAR - 2, plane[:SPAN_NEAR], plane[SPAN_NEAR:])


def ahead_x(plane):
    return pltpu.roll(plane, plane.shape[0] - 1, 0) - plane


def behind_x(plane):
    return plane - pltpu.roll(plane, 1, 0)


def ahead_y(plane):
    return pltpu.roll(plane, SPAN_Y - 1, 1) - plane


def behind_y(plane):
    return plane - pltpu.roll(plane, 1, 1)


def ahead_z(planes, z):
    return planes[z + 1] - planes[z] if z + 1 < len(planes) else -planes[z]


def behind_z(planes, z):
    return planes[z] - planes[z - 1] if z else planes[z]


class Planes:
    def __init__(self, ref, first, depth):
        self.ref, self.first, self.depth = ref, first, depth

    def __len__(self):
        return self.depth

    def __getitem__(self, z):
        return self.ref[self.first + z]

    def __setitem__(self, z, plane):
        self.ref[self.first + z] = plane


def fields_of(ref, count, depth, first=0):
    return [Planes(ref, (first + number) * depth, depth) for number in range(count)]


def strain_rates(velocity, z):
    along_x, along_y, along_z = [field[z] for field in velocity]
    return (
        behind_x(along_x),
        behind_y(along_y),
        behind_z(velocity[2], z),
        ahead_y(along_x) + ahead_x(along_y),
        ahead_z(velocity[0], z) + ahead_x(along_z),
        ahead_z(velocity[1], z) + ahead_y(along_z),
    )


def new_stress(stress, strains, lame_lambda, shear_modulus, z):
    dilated = lame_lambda[z] * (strains[0] + strains[1] + strains[2])
    shear = shear_modulus[z]
    normal = [stress[n][z] + STEP * (dilated + 2.0 * shear * strains[n]) for n in range(3)]
    return normal + [stress[n][z] + STEP * shear * strains[n] for n in range(3, 6)]


def advance(state, medium, emit, target):
    velocity, stress = state[:3], state[3:]
    lame_lambda, shear_modulus, buoyancy = medium
    depth = len(buoyancy)
    wide = target is not None and target is not state
    for z in range(depth):
        scale = STEP * buoyancy[z]
        accel = (
            ahead_x(stress[0][z]) + behind_y(stress[3][z]) + behind_z(stress[4], z),
            behind_x(stress[3][z]) + ahead_y(stress[1][z]) + behind_z(stress[5], z),
            behind_x(stress[4][z]) + behind_y(stress[5][z]) + ahead_z(stress[2], z),
        )
        for number in range(3):
            moved = velocity[number][z] + scale * accel[number]
            velocity[number][z] = moved
            if wide:
                target[number][z] = narrowed(moved)
    for z in range(depth):
        strains = strain_rates(velocity, z)
        emit(z, strains)
        if target is not None:
            for number, plane in enumerate(new_stress(stress, strains, lame_lambda, shear_modulus, z)):
                target[3 + number][z] = narrowed(plane) if wide else plane


def pack_body(*refs):
    inputs, outputs, scratch = refs[:6], refs[6:10], refs[10:]
    fields_ref, high_ref, low_ref, side_ref, cells_ref, wavelet_ref, arrived, sent, sent_sides = scratch
    third = inputs[0].shape[0] // 3
    sources = [inputs[0].at[part * third : (part + 1) * third] for part in range(3)] + list(inputs[1:4])
    targets, at = [], 0
    for source in sources:
        targets.append(fields_ref.at[at : at + source.shape[0]])
        at = at + source.shape[0]
    sources += inputs[4:]
    copies = [
        pltpu.make_async_copy(source, target, arrived.at[number])
        for number, (source, target) in enumerate(zip(sources, targets + [cells_ref, wavelet_ref]))
    ]
    for copy in copies:
        copy.start()
    copies[6].wait()
    copies[7].wait()
    cells_row = inputs[1].shape[0]
    cells = cells_ref[...]
    count = cells.shape[1]
    at_lane = iota((LANES, count), 0) == (cells & (LANES - 1))
    at_row = iota((cells_row, count), 0) == (cells >> (LANES.bit_length() - 1))
    stack = [
        jnp.where(at_row, third[step : step + 1, :], 0.0) for third in pieces(wavelet_ref[...]) for step in range(3)
    ]
    maps = sum_thirds(
        times_turned(jnp.concatenate(stack, axis=0).astype(BF16), jnp.where(at_lane, 1.0, 0.0).astype(BF16))
    )
    for copy in copies[:6]:
        copy.wait()
    total = at + 2 * cells_row
    fields_ref[at:total, :] = maps[cells_row:]
    for number in range(3, 6):
        rows = slice(number * cells_row, (number + 1) * cells_row)
        fields_ref[rows, :] = fields_ref[rows, :] + maps[:cells_row]
    rows = fields_ref[0:total, :]
    spare = 2 * LANES - total
    edge_columns(jnp.concatenate([rows, jnp.zeros((spare, LANES), F32)], axis=0), side_ref)
    sides = start_sides(side_ref, outputs[3], sent_sides)
    height = total // TILE_X
    for x in range(TILE_X):
        slab = fields_ref[pl.ds(x, height, stride=TILE_X), :]
        if x < RIM:
            low_ref[x * height : (x + 1) * height, :] = slab
        if x >= TILE_X - RIM:
            at = x - TILE_X + RIM
            high_ref[at * height : (at + 1) * height, :] = slab
    writes = [
        pltpu.make_async_copy(source, target, sent.at[number])
        for number, (source, target) in enumerate(zip((fields_ref.at[0:total], high_ref, low_ref), outputs))
    ]
    for copy in writes:
        copy.start()
    for copy in writes:
        copy.wait()
    wait_sides(sides)


def slots_body(capacity, devices, cols_y, owner_ref, start_ref, slot_ref, row_ref, cover_ref, place_ref, rank_ref):
    blocks = owner_ref.shape[0]
    group = 32
    before = jnp.where(iota((LANES, 2 * LANES), 0) < iota((LANES, 2 * LANES), 1), 1.0, 0.0).astype(BF16)
    rank_ref[...] = jnp.zeros_like(rank_ref)

    def count_group(number, carry):
        names = iota((group, LANES), 0) + number * group
        hot = [names == owner_ref[b : b + 1, :] for b in range(blocks)]
        marks = jnp.concatenate([jnp.where(h, 1.0, 0.0) for h in hot], axis=0).astype(BF16)
        counts = times(marks, before)
        total = jnp.zeros((group, LANES), F32)
        for b in range(blocks):
            part = counts[b * group : (b + 1) * group]
            rank_ref[b : b + 1, :] = rank_ref[b : b + 1, :] + jnp.sum(
                jnp.where(hot[b], part[:, :LANES] + total, 0.0), axis=0, keepdims=True
            )
            total = total + part[:, LANES:]
        return carry

    if devices == group:
        count_group(0, 0)
    else:
        lax.fori_loop(0, devices // group, count_group, 0)
    slot = owner_ref[...] * capacity + rank_ref[...].astype(I32)
    slot_ref[...] = slot >> 7
    low = slot & (LANES - 1)
    span = cols_y - GAUGE + 1
    start = start_ref[...]
    row = ((start.astype(F32) + 0.5) * (1.0 / span)).astype(I32)
    row_ref[...] = row
    first = start - row * span
    down = iota((LANES, LANES), 0)
    for b in range(blocks):
        lanes = slice(b * LANES, (b + 1) * LANES)
        offset = down - first[b : b + 1, :]
        cover_ref[:, lanes] = jnp.where((offset >= 0) & (offset < GAUGE), 1.0, 0.0).astype(BF16)
        place_ref[:, lanes] = jnp.where(down == low[b : b + 1, :], 1.0, 0.0).astype(BF16)


def forward_body(
    fields_ref,
    higher_ref,
    lower_ref,
    recv_ref,
    slot_ref,
    row_ref,
    weight_ref,
    channel_ref,
    cover_ref,
    place_ref,
    out_ref,
    strain_ref,
    medium_ref,
    wide_ref,
    source_ref,
    state_ref,
    near_ref,
    turn_ref,
    sides_ref,
    spread_ref,
):
    depth = medium_ref.shape[0] // 3
    cells_row = depth * TILE_X
    rims = rim_rows(recv_ref, turn_ref)
    height = fields_ref.shape[0] // TILE_X
    sides_ref[...] = jnp.zeros_like(sides_ref)
    for x in range(RIM):
        slab = slice(x * height, (x + 1) * height)
        sides_ref[0, pl.ds(x, height, stride=TILE_X), :] = higher_ref[slab, :]
        sides_ref[1, pl.ds(x + TILE_X - RIM, height, stride=TILE_X), :] = lower_ref[slab, :]
    lay_planes(wide_ref, source_ref, 0, fields_ref, sides_ref.at[0], sides_ref.at[1])
    lay_planes(wide_ref, source_ref, LANES, *rims)
    first = 9 * depth
    medium_ref[...] = wide_ref[first:]
    for plane in range(3 * depth):
        near_ref[plane] = narrowed(wide_ref[first + plane])
    state, near = fields_of(state_ref, 9, depth), fields_of(near_ref, 3, depth)
    for step in range(3):

        def emit(z, strains, step=step):
            for number, strain in enumerate(strains):
                base = ((step * 6 + number) * depth + z) * TILE_X
                strain_ref[base : base + TILE_X, :] = strain[0:TILE_X, 0:LANES]

        if step == 0:
            advance(fields_of(wide_ref, 9, depth), fields_of(wide_ref, 3, depth, 9), emit, state)
            continue
        for z in range(depth):
            load = source_ref[(step - 1) * depth + z]
            for number in range(3, 6):
                state[number][z] = state[number][z] + load
        advance(state, near, emit, state if step == 1 else None)
    axial = jnp.concatenate(
        [strain_ref[step * 6 * cells_row : (step * 6 + 2) * cells_row, :] for step in range(3)], axis=0
    )
    axial = jnp.concatenate(pieces(axial), axis=0).astype(BF16)
    rows_down = iota((cells_row, LANES), 0)
    slots_down = packed_iota(LANES, 2)
    for block in range(slot_ref.shape[0]):
        lanes = slice(block * LANES, (block + 1) * LANES)
        if block % 2 == 0:
            both = sum_thirds(times(axial, cover_ref[:, block * LANES : (block + 2) * LANES]))
        windows = both[:, :LANES] if block % 2 == 0 else both[:, LANES:]
        at_row = rows_down == row_ref[block : block + 1, :]
        weight_x, weight_y = weight_ref[0:1, lanes], weight_ref[1:2, lanes]
        sums = []
        for step in range(3):
            base = 2 * step * cells_row
            axial_sum = (
                weight_x * windows[base : base + cells_row]
                + weight_y * windows[base + cells_row : base + 2 * cells_row]
            )
            sums.append(jnp.sum(jnp.where(at_row, axial_sum, 0.0), axis=0, keepdims=True))
        sums.append(channel_ref[block : block + 1, :].astype(F32))
        values = jnp.concatenate(sums + sums, axis=0)
        in_slot = slots_down == packed_rows(slot_ref[block : block + 1, :], LANES)
        for third, piece in enumerate(pieces(values)):
            tile = jnp.concatenate([piece, piece], axis=0).astype(BF16)
            spread_ref[third * LANES : (third + 1) * LANES, lanes] = jnp.where(
                in_slot, jnp.concatenate([tile] * (LANES // 16), axis=0), jnp.zeros((), BF16)
            )
    out_ref[...] = sum_thirds(times_turned(spread_ref[...], place_ref[...]))


def owner_body(arrived_ref, observed_ref, residual_ref, reply_ref, values_ref, place_ref, held_ref):
    groups = arrived_ref.shape[0] // 4
    parts = observed_ref.shape[1] // LANES
    down = packed_iota(LANES)
    part_down = iota((parts, LANES), 0)
    nothing = jnp.zeros((parts, LANES), F32)
    numbers = [arrived_ref[4 * s + 3 : 4 * s + 4, :].astype(I32) for s in range(groups)]
    for s in range(groups):
        lanes = slice(s * LANES, (s + 1) * LANES)
        place_ref[:, lanes] = jnp.where(
            down == packed_rows(numbers[s] & (LANES - 1), LANES), jnp.ones((), BF16), jnp.zeros((), BF16)
        )
        at_part = part_down == (numbers[s] >> 7)
        thirds = pieces(arrived_ref[4 * s : 4 * s + 3, :])
        stack = []
        for third in thirds:
            for step in range(3):
                stack.append(jnp.where(at_part, third[step : step + 1, :], 0.0))
        stack.append(nothing)
        values_ref[:, lanes] = jnp.concatenate(stack, axis=0).astype(BF16)
    rows = 3 * parts
    sums = sum_thirds(times_turned(values_ref[...], place_ref[...])[: 3 * rows])
    for step in range(3):
        for part in range(parts):
            at = step * parts + part
            held_ref[at : at + 1, :] = observed_ref[step : step + 1, part * LANES : (part + 1) * LANES]
    held_ref[rows:, :] = nothing
    held_ref[0:rows, :] = sums - held_ref[0:rows, :]
    for step in range(3):
        for part in range(parts):
            at = step * parts + part
            residual_ref[step : step + 1, part * LANES : (part + 1) * LANES] = held_ref[at : at + 1, :]
    residual = jnp.concatenate(two_pieces(held_ref[...]), axis=0).astype(BF16)
    for s in range(groups):
        if s % 2 == 0:
            both = sum_halves(times(residual, place_ref[:, s * LANES : (s + 2) * LANES]))
        found = both[:, :LANES] if s % 2 == 0 else both[:, LANES:]
        at_part = part_down == (numbers[s] >> 7)
        for step in range(3):
            reply_ref[4 * s + step : 4 * s + step + 1, :] = jnp.sum(
                jnp.where(at_part, found[step * parts : (step + 1) * parts], 0.0), axis=0, keepdims=True
            )
        reply_ref[4 * s + 3 : 4 * s + 4, :] = jnp.zeros((1, LANES), F32)


def reached():
    return [(turn, distance) for turn in range(3) for distance in range(RIM - turn)]


def load_body(
    arrived_ref,
    slot_ref,
    row_ref,
    weight_ref,
    cover_ref,
    place_ref,
    load_ref,
    high_ref,
    low_ref,
    out_ref,
    spread_ref,
    side_ref,
    held_ref,
    sent_sides,
):
    cells_row = load_ref.shape[0] // 6
    stack_rows = load_ref.shape[0]
    arrived = jnp.concatenate(two_pieces(arrived_ref[...]), axis=0).astype(BF16)
    slots_down = iota((LANES, LANES), 0) >> 2
    rows_down = packed_iota(cells_row)
    for block in range(slot_ref.shape[0]):
        lanes = slice(block * LANES, (block + 1) * LANES)
        if block % 2 == 0:
            both = sum_halves(times(arrived, place_ref[:, block * LANES : (block + 2) * LANES]))
        found = both[:, :LANES] if block % 2 == 0 else both[:, LANES:]
        found = jnp.where(slots_down == slot_ref[block : block + 1, :], found, 0.0)
        folded = found[0:8]
        for part in range(1, LANES // 8):
            folded = folded + found[8 * part : 8 * part + 8]
        folded = folded + pltpu.roll(folded, 4, 0)
        at_row = rows_down == packed_rows(row_ref[block : block + 1, :], cells_row)
        for turn in range(3):
            back = folded[2 - turn : 3 - turn, :]
            for part in range(2):
                for half, piece in enumerate(two_pieces(weight_ref[part : part + 1, lanes] * back)):
                    base = half * stack_rows + (2 * turn + part) * cells_row
                    spread_ref[base : base + cells_row, lanes] = jnp.where(
                        at_row, packed_rows(piece, cells_row), jnp.zeros((), BF16)
                    )
    cover = jnp.concatenate([cover_ref[0:16, :], cover_ref[LANES - 16 :, :]], axis=0)
    edges = times_turned(cover, spread_ref[0:stack_rows, :]) + times_turned(cover, spread_ref[stack_rows:, :])
    side_ref[...] = jnp.zeros_like(side_ref)
    for side, base in ((0, 0), (1, 32 - RIM)):
        for column in range(RIM):
            lanes = slice(column * LANES, column * LANES + stack_rows)
            side_ref[side, 0:1, lanes] = edges[base + column : base + column + 1, :]
    sides = start_sides(side_ref, out_ref, sent_sides)
    load = sum_halves(times_turned(spread_ref[...], cover_ref[...]))
    load_ref[...] = load
    held_ref[0:stack_rows, :] = load
    count = stack_rows // (3 * TILE_X)
    for at, (turn, distance) in enumerate(reached()):
        rows = slice(at * count, (at + 1) * count)
        first = turn * count * TILE_X
        low_ref[rows, :] = held_ref[pl.ds(first + distance, count, stride=TILE_X), :]
        high_ref[rows, :] = held_ref[pl.ds(first + TILE_X - 1 - distance, count, stride=TILE_X), :]
    wait_sides(sides)


def adjoint_body(
    load_ref,
    higher_ref,
    lower_ref,
    recv_ref,
    strain_ref,
    medium_ref,
    residual_ref,
    gradient_ref,
    residual_out_ref,
    first_ref,
    later_ref,
    velocity_ref,
    state_ref,
    near_ref,
    turn_ref,
    sides_ref,
):
    depth = medium_ref.shape[0] // 3
    rims = rim_rows(recv_ref, turn_ref)
    sides_ref[...] = jnp.zeros_like(sides_ref)
    count = load_ref.shape[0] // (3 * TILE_X)
    for at, (turn, distance) in enumerate(reached()):
        rows = slice(at * count, (at + 1) * count)
        first = turn * count * TILE_X
        sides_ref[0, pl.ds(first + distance, count, stride=TILE_X), :] = higher_ref[rows, :]
        sides_ref[1, pl.ds(first + TILE_X - 1 - distance, count, stride=TILE_X), :] = lower_ref[rows, :]
    lay_planes(first_ref, later_ref, 0, load_ref, sides_ref.at[0], sides_ref.at[1])
    lay_planes(first_ref, later_ref, LANES, *rims)
    for plane in range(3 * depth):
        near_ref[plane] = narrowed(medium_ref[plane])
    residual_out_ref[...] = residual_ref[...]
    state, near, medium = (
        fields_of(state_ref, 9, depth),
        fields_of(near_ref, 3, depth),
        fields_of(medium_ref, 3, depth),
    )

    def add_terms(turn, z, strains):
        dilation, dilation_back, doubled, product = None, None, None, None
        for number, strain in enumerate(strains):
            base = (((2 - turn) * 6 + number) * depth + z) * TILE_X
            forward = strain_ref[base : base + TILE_X, :]
            if number < 3:
                dilation = forward if dilation is None else dilation + forward
            if strain is None:
                continue
            back = strain[0:TILE_X, 0:LANES]
            term = forward * back
            if number < 3:
                dilation_back = back if dilation_back is None else dilation_back + back
                doubled = term if doubled is None else doubled + term
            else:
                product = term if product is None else product + term
        for part, term in enumerate((dilation * dilation_back, 2.0 * doubled + product)):
            base = (part * depth + z) * TILE_X
            rows = slice(base, base + TILE_X)
            gradient_ref[rows, :] = gradient_ref[rows, :] + term if turn else term

    loads, velocity = fields_of(first_ref, 2, depth), fields_of(velocity_ref, 2, depth)
    for z in range(depth):
        scale = STEP * medium[2][z]
        velocity[0][z] = scale * ahead_x(loads[0][z])
        velocity[1][z] = scale * ahead_y(loads[1][z])
        state[0][z] = narrowed(velocity[0][z])
        state[1][z] = narrowed(velocity[1][z])
        state[2][z] = jnp.zeros((SPAN_NEAR, SPAN_Y), F32)
    for z in range(depth):
        along_x, along_y = velocity[0][z], velocity[1][z]
        strain_x, strain_y = behind_x(along_x), behind_y(along_y)
        sheared = (
            ahead_y(along_x) + ahead_x(along_y),
            ahead_z(velocity[0], z),
            ahead_z(velocity[1], z),
        )
        add_terms(0, z, (strain_x, strain_y, None) + sheared)
        dilated = medium[0][z] * (strain_x + strain_y)
        shear = medium[1][z]
        state[3][z] = narrowed(loads[0][z] + STEP * (dilated + 2.0 * shear * strain_x))
        state[4][z] = narrowed(loads[1][z] + STEP * (dilated + 2.0 * shear * strain_y))
        state[5][z] = narrowed(STEP * dilated)
        for number, strain in enumerate(sheared):
            state[6 + number][z] = narrowed(STEP * shear * strain)
    for turn in (1, 2):
        for part in range(2):
            for z in range(depth):
                load = later_ref[(2 * (turn - 1) + part) * depth + z]
                state[3 + part][z] = state[3 + part][z] + load
        advance(state, near, functools.partial(add_terms, turn), state if turn == 1 else None)


def shards(
    initial_state,
    lame_lambda,
    shear_modulus,
    buoyancy,
    source_cells,
    source_wavelet,
    segment_start,
    segment_weight,
    partial_owner,
    partial_channel,
    observed_data,
):
    depth, rows_x, cols_y = lame_lambda.shape
    part_count = segment_start.shape[0]
    count_x, count_y = lax.axis_size("gx"), lax.axis_size("gy")
    devices = count_x * count_y
    capacity = max(2, 2 * part_count // devices)
    slot_groups = devices * capacity // LANES
    blocks = part_count // LANES
    per_group = LANES // capacity
    cells_row = depth * rows_x
    both = ("gx", "gy")
    up = [(i, i + 1) for i in range(count_x - 1)]
    down = [(j, i) for i, j in up]
    shape = jax.ShapeDtypeStruct

    def exchange(chunks):
        return lax.all_to_all(chunks, both, split_axis=0, concat_axis=0, tiled=True)

    def to_owners(rows):
        chunks = rows.reshape(slot_groups, 4, per_group, capacity).transpose(0, 2, 1, 3)
        back = exchange(chunks.reshape(devices, 4, capacity)).reshape(slot_groups, per_group, 4, capacity)
        return back.transpose(0, 2, 1, 3).reshape(slot_groups * 4, LANES)

    trimmed = shape((14 * depth * RIM, cols_y), F32)
    fields, high, low, edges = call_kernel(
        pack_body,
        "pack_edges",
        [shape((14 * cells_row, cols_y), F32), trimmed, trimmed, shape((devices, 1, 2 * RIM * LANES), F32)],
        [
            pltpu.VMEM((14 * cells_row + SPARE, cols_y), F32),
            pltpu.VMEM(trimmed.shape, F32),
            pltpu.VMEM(trimmed.shape, F32),
            pltpu.VMEM((2, 1, 2 * RIM * LANES), F32),
            pltpu.VMEM((1, source_cells.shape[0]), I32),
            pltpu.VMEM(source_wavelet.shape, F32),
            pltpu.SemaphoreType.DMA((8,)),
            pltpu.SemaphoreType.DMA((3,)),
            pltpu.SemaphoreType.DMA((6,)),
        ],
        *[values.reshape(-1, cols_y) for values in (initial_state, lame_lambda, shear_modulus, buoyancy)],
        source_cells.reshape(1, -1),
        source_wavelet,
        place=pl.ANY,
        place_out=pl.ANY,
        room=60 * 1024 * 1024,
    )
    lower = lax.ppermute(high, "gx", up)
    higher = lax.ppermute(low, "gx", down)
    rims = exchange(edges)
    channels = partial_channel.reshape(blocks, LANES)
    slot, row, cover, place = call_kernel(
        functools.partial(slots_body, capacity, devices, cols_y),
        "segment_slots",
        [
            shape((blocks, LANES), I32),
            shape((blocks, LANES), I32),
            shape((cols_y, part_count), BF16),
            shape((LANES, part_count), BF16),
        ],
        [pltpu.VMEM((blocks, LANES), F32)],
        partial_owner.reshape(blocks, LANES),
        segment_start.reshape(blocks, LANES),
    )
    partials, strains, medium = call_kernel(
        forward_body,
        "forward_run",
        [
            shape((slot_groups * 4, LANES), F32),
            shape((18 * cells_row, cols_y), F32),
            shape((3 * depth, SPAN_X, SPAN_Y), F32),
        ],
        [
            pltpu.VMEM((12 * depth, SPAN_X, SPAN_Y), F32),
            pltpu.VMEM((2 * depth, SPAN_NEAR, SPAN_Y), F32),
            pltpu.VMEM((9 * depth, SPAN_NEAR, SPAN_Y), F32),
            pltpu.VMEM((3 * depth, SPAN_NEAR, SPAN_Y), F32),
            pltpu.VMEM((3, LANES, 2 * LANES), F32),
            pltpu.VMEM((2, 14 * cells_row + SPARE, cols_y), F32),
            pltpu.VMEM((3 * LANES, part_count), BF16),
        ],
        fields,
        higher,
        lower,
        rims,
        slot,
        row,
        segment_weight,
        channels,
        cover,
        place,
    )
    parts = observed_data.shape[1] // LANES
    residuals, reply = call_kernel(
        owner_body,
        "channel_sums",
        [shape(observed_data.shape, F32), shape((slot_groups * 4, LANES), F32)],
        [
            pltpu.VMEM((10 * parts, slot_groups * LANES), BF16),
            pltpu.VMEM((LANES, slot_groups * LANES), BF16),
            pltpu.VMEM((4 * parts, LANES), F32),
        ],
        to_owners(partials),
        observed_data,
    )
    reach = shape((len(reached()) * 2 * depth, cols_y), F32)
    loads, load_high, load_low, load_edges = call_kernel(
        load_body,
        "segment_loads",
        [shape((6 * cells_row, cols_y), F32), reach, reach, shape((devices, 1, RIM * LANES), F32)],
        [
            pltpu.VMEM((12 * cells_row, part_count), BF16),
            pltpu.VMEM((2, 1, RIM * LANES), F32),
            pltpu.VMEM((6 * cells_row + SPARE, cols_y), F32),
            pltpu.SemaphoreType.DMA((6,)),
        ],
        to_owners(reply),
        slot,
        row,
        segment_weight,
        cover,
        place,
        place_out=(pltpu.VMEM, pltpu.VMEM, pltpu.VMEM, pl.ANY),
    )
    load_lower = lax.ppermute(load_high, "gx", up)
    load_higher = lax.ppermute(load_low, "gx", down)
    load_rims = exchange(load_edges)
    gradients, residuals = call_kernel(
        adjoint_body,
        "adjoint_run",
        [shape((2 * cells_row, cols_y), F32), shape(observed_data.shape, F32)],
        [
            pltpu.VMEM((2 * depth, SPAN_X, SPAN_Y), F32),
            pltpu.VMEM((4 * depth, SPAN_NEAR, SPAN_Y), F32),
            pltpu.VMEM((2 * depth, SPAN_X, SPAN_Y), F32),
            pltpu.VMEM((9 * depth, SPAN_NEAR, SPAN_Y), F32),
            pltpu.VMEM((3 * depth, SPAN_NEAR, SPAN_Y), F32),
            pltpu.VMEM((3, LANES, LANES), F32),
            pltpu.VMEM((2, 6 * cells_row + SPARE, cols_y), F32),
        ],
        loads,
        load_higher,
        load_lower,
        load_rims,
        strains,
        medium,
        residuals,
    )
    return (residuals, gradients.reshape(2, depth, rows_x, cols_y))


def solution(mesh):
    in_specs = (
        P(None, None, "gx", "gy"),
        P(None, "gx", "gy"),
        P(None, "gx", "gy"),
        P(None, "gx", "gy"),
        P(("gx", "gy")),
        P(None, ("gx", "gy")),
        P(("gx", "gy")),
        P(None, ("gx", "gy")),
        P(("gx", "gy"), None),
        P(("gx", "gy")),
        P(None, ("gx", "gy")),
    )
    out_specs = (P(None, ("gx", "gy")), P(None, None, "gx", "gy"))
    return jax.shard_map(shards, mesh=mesh, in_specs=in_specs, out_specs=out_specs, check_vma=False)
```
